32 devices in a mesh: dp: 16 (over z, y, core), head: 2 (over x).
Axes of the slice: x: 2, y: 2, z: 4, core: 2. Of those that a mesh axis runs over, the one named last changes fastest.
Arguments:
- tokens: bfloat16 [16384, 768], P(('dp', 'head')), may hold values from -6 to 6
- w_heads: bfloat16 [768, 2304], replicated, may hold values from -0.21875 to 0.21875
- b_heads: bfloat16 [2304], replicated, may hold values from -3 to 3
- w_merge: bfloat16 [768, 768], replicated, may hold values from -3 to 3
- b_merge: bfloat16 [768], replicated, may hold values from -3 to 3
- gain_first: bfloat16 [768], replicated, may hold values from 0.25 to 1.75
- bias_first: bfloat16 [768], replicated, may hold values from -3 to 3
- w_expand: bfloat16 [768, 3072], replicated, may hold values from -0.21875 to 0.21875
- b_expand: bfloat16 [3072], replicated, may hold values from -3 to 3
- w_reduce: bfloat16 [3072, 768], replicated, may hold values from -0.109375 to 0.109375
- b_reduce: bfloat16 [768], replicated, may hold values from -3 to 3
- gain_second: bfloat16 [768], replicated, may hold values from 0.25 to 1.75
- bias_second: bfloat16 [768], replicated, may hold values from -3 to 3
- seq_lengths: int32 [16, 4], P('dp'), may hold values from 1 to 640, 896 in all within a row
- cotangent: bfloat16 [16384, 768], P(('dp', 'head')), may hold values from -6 to 6
Outputs:
- block_output: bfloat16 [16384, 768], P(('dp', 'head'))
- input_grad: float32 [16384, 768], P(('dp', 'head'))
- grad_w_heads: float32 [768, 2304], P(('dp', 'head'))
- grad_b_scores: float32 [1536], P(('dp', 'head'))
- grad_b_values: float32 [768], P(('dp', 'head'))
- grad_w_merge: float32 [768, 768], P(('dp', 'head'))
- grad_b_merge: float32 [768], P(('dp', 'head'))
- grad_gain_first: float32 [768], P(('dp', 'head'))
- grad_bias_first: float32 [768], P(('dp', 'head'))
- grad_w_expand: float32 [768, 3072], P(('dp', 'head'))
- grad_b_expand: float32 [3072], P(('dp', 'head'))
- grad_w_reduce: float32 [3072, 768], P(('dp', 'head'))
- grad_b_reduce: float32 [768], P(('dp', 'head'))
- grad_gain_second: float32 [768], P(('dp', 'head'))
- grad_bias_second: float32 [768], P(('dp', 'head'))
The draws below stay inside these ranges and needn't reach their ends.
Inputs may be any that keep to these rules, and one draw needn't show every extreme that they name: `seq_lengths`: row g lists the lengths of the 4 sequences of token group g in order; each row sums to 896 and its largest entry is 640; the last 128 rows of each group are padding.
All inputs are finite; a program needn't handle non-finite values.
Results may differ from the reference program's by a relative error of at most 0.012.
Values may be sent and summed in bfloat16 or wider, within the bound.
No kernel may reach another device: no remote copies, remote signals or barrier semaphores. Data moves between devices by JAX's collectives and lax.ppermute only.
A program may use at most 192 MiB of HBM per device.

```python
import math
import jax
import jax.numpy as jnp
import numpy as np
from jax import lax

D = 768
HEADS = 12
HEAD_DIM = 64
FF = 3072
SEQS = 4
GROUP = 1024
LIVE = 896
MOST = 640
TOKENS = 16384
N_DP = 16


def spiked(values, stream_key, source, target, parts, factor):
    owner, partner = [(jnp.arange(values.shape[position]) // (values.shape[position] // parts)).reshape([-1 if axis == position else 1 for axis in range(values.ndim)]) for position in (source, target)]
    chosen = jax.random.permutation(stream_key, parts)[partner]
    strong = (owner == chosen) | (owner == (partner + parts // 2) % parts)
    return jnp.where(strong, factor * values, values)


def levels(own_key, dims, cuts, smallest, top_value):
    def one(position, shards_of):
        heights = jax.random.uniform(jax.random.fold_in(jax.random.fold_in(own_key, 6), position), (shards_of,), jnp.float32, smallest / len(cuts), top_value / len(cuts))
        return jnp.repeat(jnp.exp(heights), dims[position] // shards_of).reshape((-1,) + (1,) * (len(dims) - position - 1))

    level = one(*cuts[0])
    for cut in cuts[1:]:
        level = level * one(*cut)
    return level


def split_up(count, total, bound, lean):
    portions = [(1 << 20) // math.isqrt(standing ** lean) + 1 for standing in range(2, count + 1)]
    surplus, given = total - bound - (count - 1), [1] * (count - 1)
    while surplus > 0:
        free = [i for i in range(count - 1) if given[i] < bound]
        mass, remaining = sum([portions[i] for i in free]), surplus
        for i in free:
            addition = min(bound - given[i], max(1, remaining * portions[i] // mass), surplus)
            given[i] = given[i] + addition
            surplus = surplus - addition
    return np.array([bound] + given)


def ragged(key, amount, total, reach, lean):
    if amount == 2:
        one = jax.random.randint(key, (), max(1, total - reach), min(reach, total - 1) + 1)
        return jnp.stack([one, total - one])
    tallies = jnp.asarray(split_up(amount, total, reach, lean), jnp.int32)
    twos = (amount - 1) // 2
    giver, taker = tallies[1:1 + 2 * twos:2], tallies[2:2 + 2 * twos:2]
    room = jnp.minimum(giver - 1, reach - taker)
    moved = jax.random.randint(jax.random.fold_in(key, 1), (twos,), 0, 1 << 20) % (room + 1)
    tallies = tallies.at[1:1 + 2 * twos:2].set(giver - moved).at[2:2 + 2 * twos:2].set(taker + moved)
    return tallies[jax.random.permutation(jax.random.fold_in(key, 2), amount)]


def gaussian(stream_key, extent, scale, reach, split=(), kind=jnp.bfloat16):
    level = levels(stream_key, extent, split, -0.22, 0.18) if split else 1.0
    drawn = jax.random.normal(stream_key, extent, jnp.float32) * scale * level
    return jnp.minimum(jnp.maximum(drawn, -reach), reach).astype(kind)


def gaussian_with(own_key, dims, deviation, most, split, heavy, kind=jnp.bfloat16):
    result = deviation * jax.random.normal(own_key, dims, jnp.float32)
    if split:
        result = result * levels(own_key, dims, split, -0.22, 0.18)
    return jnp.clip(spiked(result, jax.random.fold_in(own_key, 3), *heavy), -most, most).astype(kind)


def setup_inputs(seed: int = 0) -> dict:
    seeds = jax.random.split(jax.random.key(seed), 16)
    return {
        "tokens": gaussian_with(seeds[0], (TOKENS, D), 1.0, 6.0, ((0, 32),), (0, 1, 32, 2.75)),
        "w_heads": gaussian(seeds[1], (D, 3 * D), D ** -0.5, 0.21875),
        "b_heads": gaussian(seeds[2], (3 * D,), 0.5, 3.0),
        "w_merge": gaussian(seeds[3], (D, D), (max(D // 192, 1)) ** -0.5, 3.0),
        "b_merge": gaussian(seeds[4], (D,), 0.5, 3.0),
        "gain_first": jnp.clip(1.0 + 0.15 * jax.random.normal(seeds[5], (D,), jnp.float32), 0.25, 1.75).astype(jnp.bfloat16),
        "bias_first": gaussian(seeds[6], (D,), 0.5, 3.0),
        "w_expand": gaussian(seeds[7], (D, FF), D ** -0.5, 0.21875),
        "b_expand": gaussian(seeds[8], (FF,), 0.5, 3.0),
        "w_reduce": gaussian(seeds[9], (FF, D), FF ** -0.5, 0.109375),
        "b_reduce": gaussian(seeds[10], (D,), 0.5, 3.0),
        "gain_second": jnp.clip(1.0 + 0.15 * jax.random.normal(seeds[11], (D,), jnp.float32), 0.25, 1.75).astype(jnp.bfloat16),
        "bias_second": gaussian(seeds[12], (D,), 0.5, 3.0),
        "seq_lengths": jax.vmap(lambda own: ragged(own, SEQS, LIVE, MOST, 2))(jax.random.split(seeds[13], N_DP)).reshape((N_DP, SEQS)).astype(jnp.int32),
        "cotangent": gaussian_with(seeds[14], (TOKENS, D), 1.0, 6.0, ((0, 32),), (0, 1, 32, 2.75)),
    }


@jax.custom_vjp
def low(v):
    return lax.optimization_barrier(v.astype(jnp.bfloat16)).astype(jnp.float32)

@jax.custom_vjp
def low_back(v):
    return v

def low_keep(v):
    return (low(v), None)

def low_pass(kept, grad):
    return (grad,)

def back_keep(v):
    return (v, None)

def back_low(kept, grad):
    return (low(grad),)
low.defvjp(low_keep, low_pass)
low_back.defvjp(back_keep, back_low)

def seq_tables(lengths, group_rows):
    lengths = lengths.astype(jnp.int32)
    seq_ends = jnp.cumsum(lengths).astype(jnp.int32)
    seq_starts = (seq_ends - lengths).astype(jnp.int32)
    positions = jnp.arange(group_rows, dtype=jnp.int32)
    segment = lax.optimization_barrier(jnp.sum((positions[:, None] >= seq_ends[None, :]).astype(jnp.int32), axis=1)).astype(jnp.int32)
    member = segment[:, None] == jnp.arange(lengths.shape[0], dtype=jnp.int32)[None, :]
    seq_len = lax.optimization_barrier(jnp.sum(jnp.where(member, lengths[None, :], 0), axis=1)).astype(jnp.int32)
    first_row = lax.optimization_barrier(jnp.sum(jnp.where(member, seq_starts[None, :], 0), axis=1)).astype(jnp.int32)
    live_mask = (segment < lengths.shape[0]).astype(jnp.float32)
    phase_angle = 0.5 * math.pi * (positions - first_row).astype(jnp.float32) / jnp.maximum(seq_len, 1).astype(jnp.float32)
    return (segment, jnp.cos(phase_angle) * live_mask, jnp.sin(phase_angle) * live_mask)

def layer_norm(entries, gain, bias):
    average = lax.optimization_barrier(jnp.mean(entries, axis=-1, keepdims=True))
    centred = entries - average
    variance = lax.optimization_barrier(jnp.mean(centred * centred, axis=-1, keepdims=True))
    return centred * lax.rsqrt(variance + 1e-05) * gain + bias

def exact_dot(left, right):
    return jnp.dot(left, right, precision=lax.Precision.HIGHEST, preferred_element_type=jnp.float32)

def features(projected, cos_w, sin_w):
    rectified = jax.nn.relu(projected)
    return jnp.concatenate([rectified * cos_w[:, None, None], rectified * sin_w[:, None, None]], axis=-1)

def attention(query_feat, key_feat, value_low, segment):
    row_count = query_feat.shape[0]
    positions = jnp.arange(row_count, dtype=jnp.int32)
    allowed = (positions[None, :] <= positions[:, None]) & (segment[None, :] == segment[:, None])
    scores = jnp.einsum('iha,jha->hij', query_feat, key_feat, precision=lax.Precision.HIGHEST)
    scores = scores * allowed[None].astype(jnp.float32)
    numerator = jnp.einsum('hij,jhe->ihe', scores, value_low, precision=lax.Precision.HIGHEST)
    denominator = lax.optimization_barrier(jnp.sum(scores, axis=2))
    return numerator / (denominator.T[:, :, None] + 1.0)

def layer_block(inputs, w_heads, b_heads, w_merge, b_merge, gain_first, bias_first, w_expand, b_expand, w_reduce, b_reduce, gain_second, bias_second, cos_w, sin_w, segment):
    row_count = inputs.shape[0]
    projected = low_back(exact_dot(inputs, w_heads) + b_heads)
    queries = projected[:, :D].reshape(row_count, HEADS, HEAD_DIM)
    keys = projected[:, D:2 * D].reshape(row_count, HEADS, HEAD_DIM)
    values = projected[:, 2 * D:].reshape(row_count, HEADS, HEAD_DIM)
    query_feat = low(low_back(features(queries, cos_w, sin_w)))
    key_feat = low(low_back(features(keys, cos_w, sin_w)))
    attended = attention(query_feat, key_feat, low(values), segment)
    attended_low = low(low_back(attended)).reshape(row_count, D)
    branch_attn = low_back(exact_dot(attended_low, w_merge) + b_merge)
    normed = layer_norm(inputs + branch_attn, gain_first, bias_first)
    pre_act = low_back(exact_dot(low(normed), w_expand) + b_expand)
    activated = low(jax.nn.gelu(pre_act, approximate=False))
    branch_ffn = low_back(exact_dot(activated, w_reduce) + b_reduce)
    return layer_norm(normed + branch_ffn, gain_second, bias_second)

def reference(tokens, w_heads, b_heads, w_merge, b_merge, gain_first, bias_first, w_expand, b_expand, w_reduce, b_reduce, gain_second, bias_second, seq_lengths, cotangent):
    params = tuple((param.astype(jnp.float32) for param in (w_heads, b_heads, w_merge, b_merge, gain_first, bias_first, w_expand, b_expand, w_reduce, b_reduce, gain_second, bias_second)))
    input_groups = tokens.astype(jnp.float32).reshape(N_DP, GROUP, D)
    cot_groups = cotangent.astype(jnp.float32).reshape(N_DP, GROUP, D)

    def one_group(totals, slices):
        inputs, cot_rows, lengths = slices
        segment, cos_w, sin_w = seq_tables(lengths, GROUP)

        def forward(entries, *weights):
            return layer_block(entries, *weights, cos_w, sin_w, segment)
        outputs, pullback = jax.vjp(forward, inputs, *params)
        gradients = pullback(cot_rows)
        totals = tuple((total + update for total, update in zip(totals, gradients[1:])))
        return (totals, (outputs.astype(jnp.bfloat16), gradients[0]))
    zero_grads = tuple((jnp.zeros(param.shape, jnp.float32) for param in params))
    totals, (outputs, in_grads) = lax.scan(one_group, zero_grads, (input_groups, cot_groups, seq_lengths))
    return (outputs.reshape(TOKENS, D), in_grads.reshape(TOKENS, D), totals[0], totals[1][:2 * D], totals[1][2 * D:], totals[2], totals[3], totals[4], totals[5], totals[6], totals[7], totals[8], totals[9], totals[10], totals[11])
```

```python
import functools
import math

import jax
import jax.numpy as jnp
from jax import lax
from jax.experimental import pallas as pl
from jax.experimental.pallas import tpu as pltpu
from jax.sharding import PartitionSpec as P

D = 768
PAIRS = 6
FF = 3072
LANES = 128
HALF = 64
BF = jnp.bfloat16
F32 = jnp.float32
AXES = ("dp", "head")
VMEM_LIMIT = 48 * 1024 * 1024
FF_BLOCK = 512
FF_STEPS = FF // FF_BLOCK


def dot(a, b):
    return jnp.dot(a, b, preferred_element_type=F32)


def dot_t(a, b):
    return lax.dot_general(a, b, (((0,), (0,)), ((), ())), preferred_element_type=F32)


def dot_r(a, b):
    return lax.dot_general(a, b, (((1,), (1,)), ((), ())), preferred_element_type=F32)


def call(kernel, name, scal, grid, ins, outs, scratch=(), flops=0, vmem=VMEM_LIMIT):
    whole = lambda n: (lambda *_: (0,) * n)
    in_specs = [
        pl.BlockSpec(b if b is not None else a.shape, m if m is not None else whole(a.ndim))
        for a, b, m in ins
    ]
    out_specs = [
        pl.BlockSpec(b if b is not None else s, m if m is not None else whole(len(s)))
        for s, d, b, m in outs
    ]
    nbytes = sum(a.size * a.dtype.itemsize for a, _, _ in ins)
    nbytes += sum(math.prod(s) * jnp.dtype(d).itemsize for s, d, _, _ in outs)
    return pl.pallas_call(
        kernel,
        name=name,
        grid_spec=pltpu.PrefetchScalarGridSpec(
            num_scalar_prefetch=1,
            grid=grid,
            in_specs=in_specs,
            out_specs=out_specs,
            scratch_shapes=list(scratch),
        ),
        out_shape=[jax.ShapeDtypeStruct(s, d) for s, d, _, _ in outs],
        compiler_params=pltpu.CompilerParams(vmem_limit_bytes=vmem),
        cost_estimate=pl.CostEstimate(flops=int(flops), bytes_accessed=int(nbytes), transcendentals=0),
    )(scal, *[a for a, _, _ in ins])


def lane_masks():
    lane = lax.broadcasted_iota(jnp.int32, (1, LANES), 1)
    even = (lane < HALF).astype(F32)
    return lane, even, even.astype(BF), (1.0 - even).astype(BF)


def square_masks():
    row = lax.broadcasted_iota(jnp.int32, (LANES, LANES), 0)
    lane = lax.broadcasted_iota(jnp.int32, (LANES, LANES), 1)
    upper = row < HALF
    return lane, upper, upper == (lane < HALF)


def high_low(v):
    high = v.astype(BF).astype(F32)
    return high, v - high


def tables(scal, rows, seqs, tcol, trow):
    pos = lax.broadcasted_iota(jnp.int32, (1, rows), 1) + scal[seqs] * rows
    seg = jnp.zeros((1, rows), jnp.int32)
    first = jnp.zeros((1, rows), jnp.int32)
    length = jnp.ones((1, rows), jnp.int32)
    at_boundary = jnp.int32(0)
    begin = jnp.int32(0)
    for s in range(seqs):
        end = begin + scal[s]
        inside = (pos >= begin) & (pos < end)
        first = jnp.where(inside, begin, first)
        length = jnp.where(inside, jnp.maximum(scal[s], 1), length)
        seg = seg + (pos >= end).astype(jnp.int32)
        at_boundary = at_boundary + (rows - 1 >= end).astype(jnp.int32)
        begin = end
    live = (seg < seqs).astype(F32)
    angle = 0.5 * math.pi * (pos - first).astype(F32) / length.astype(F32)
    cos_w = jnp.cos(angle) * live
    sin_w = jnp.sin(angle) * live
    crossing = (seg == at_boundary).astype(F32)
    which = lax.broadcasted_iota(jnp.int32, (LANES, rows), 0)
    table = jnp.zeros((LANES, rows), F32)
    for n, entry in enumerate((cos_w, sin_w, seg.astype(F32), cos_w * crossing, sin_w * crossing)):
        table = jnp.where(which == n, entry, table)
    trow[...] = table[:8]
    tcol[...] = table.T


def pack_state(total_cos, total_sin, norm_cos, norm_sin, pair, norms):
    lane, upper, diag = square_masks()
    packed = jnp.where(diag, total_cos, pltpu.roll(total_sin, HALF, 1))
    cos_high, cos_low = high_low(norm_cos)
    sin_high, sin_low = high_low(norm_sin)
    for n, part in enumerate((cos_high, cos_low, sin_high, sin_low)):
        norms = jnp.where(lane == 4 * pair + n, part, norms)
    return packed.astype(BF), norms


def unpack_state(state_ref, pair):
    lane, upper, diag = square_masks()
    packed = state_ref[pair].astype(F32)
    norms = state_ref[PAIRS].astype(F32)
    of_cos = jnp.where(diag, packed, 0.0)
    of_sin = jnp.where(diag, pltpu.roll(packed, HALF, 1), 0.0)
    pick = lambda n: jnp.sum(
        jnp.where((lane == 4 * pair + n) | (lane == 4 * pair + n + 1), norms, 0.0), axis=1, keepdims=True
    )
    return of_cos, of_sin, pick(0), pick(2)


def kv_kernel(seqs, scal, tok, wk, wv, bk, bv, rk_o, v_o, st_o, tcol, trow, norms):
    step = pl.program_id(0)
    rows = tok.shape[0]

    @pl.when(step == 0)
    def _():
        tables(scal, rows, seqs, tcol, trow)
        norms[...] = jnp.zeros_like(norms)

    rk = jnp.maximum(dot(tok[...], wk[...]) + bk[...].astype(F32), 0.0).astype(BF)
    v = (dot(tok[...], wv[...]) + bv[...].astype(F32)).astype(BF)
    rk_o[...] = rk
    v_o[...] = v
    cos_b, sin_b = tcol[:, 3:4], tcol[:, 4:5]
    lane, even, even_b, odd_b = lane_masks()
    sq_lane, upper, diag = square_masks()
    for n in range(2):
        pair = 2 * step + n
        kp = rk[:, n * LANES : (n + 1) * LANES].astype(F32)
        vp = v[:, n * LANES : (n + 1) * LANES]
        left = jnp.concatenate([(kp * cos_b).astype(BF), (kp * sin_b).astype(BF)], axis=1)
        right = jnp.concatenate([vp * even_b + odd_b, vp * odd_b + even_b], axis=1)
        both = dot_t(left, right)
        of_cos = jnp.where(upper, both[:LANES, :LANES], both[:LANES, LANES:])
        of_sin = jnp.where(upper, both[LANES:, :LANES], both[LANES:, LANES:])
        norm_cos = jnp.where(diag, pltpu.roll(of_cos, HALF, 1), of_cos)
        norm_sin = jnp.where(diag, pltpu.roll(of_sin, HALF, 1), of_sin)
        packed, new_norms = pack_state(of_cos, of_sin, norm_cos, norm_sin, pair, norms[...])
        st_o[pair] = packed
        norms[...] = new_norms

    st_o[PAIRS] = norms[...].astype(BF)


def weights_block(tcol, trow, transposed):
    rows = tcol.shape[0]
    down = lax.broadcasted_iota(jnp.int32, (rows, rows), 0)
    along = lax.broadcasted_iota(jnp.int32, (rows, rows), 1)
    same = tcol[:, 2:3] == trow[2:3, :]
    causal = (down <= along) if transposed else (along <= down)
    value = tcol[:, 0:1] * trow[0:1, :] + tcol[:, 1:2] * trow[1:2, :]
    return jnp.where(same & causal, value, 0.0)


def local_kernel(scal, tok, wq, bq, rk, v, tcol, trow, rq_o, num_o, den_o, weights):
    step = pl.program_id(0)
    rows = tok.shape[0]
    mid = rows // 2

    @pl.when(step == 0)
    def _():
        weights[...] = weights_block(tcol, trow, False)

    rq = jnp.maximum(dot(tok[...], wq[...]) + bq[...].astype(F32), 0.0).astype(BF)
    rq_o[...] = rq
    lane, even, even_b, odd_b = lane_masks()
    is_even = lane < HALF
    for n in range(2):
        cols = slice(n * LANES, (n + 1) * LANES)
        qp, kp, vp = rq[:, cols], rk[:, cols], v[:, cols]
        for lo, hi in ((0, mid), (mid, rows)):
            outs = []
            for own, other in ((even_b, odd_b), (odd_b, even_b)):
                scores = dot_r(qp[lo:hi] * own, kp[:hi]) * weights[lo:hi, :hi]
                outs.append(dot(scores.astype(BF), vp[:hi] * own + other))
            num_o[lo:hi, cols] = jnp.where(is_even, outs[0], outs[1])
            den_o[lo:hi, cols] = pltpu.roll(jnp.where(is_even, outs[1], outs[0]), HALF, 1)


def normalise(entries):
    mean = jnp.mean(entries, axis=1, keepdims=True)
    centred = entries - mean
    var = jnp.mean(centred * centred, axis=1, keepdims=True)
    scale = lax.rsqrt(var + 1e-05)
    return centred * scale, scale


def ffn_kernel(
    scal, rq, num, den, st, tcol, tok, w_merge, b_merge, gain, bias, w_exp, b_exp, w_red, b_red,
    att_o, inv_o, mixed_o, xhat_o, scale_o, normed_o, act_o, slope_o, second_o,
    acc, head_at,
):
    step = pl.program_id(0)

    @pl.when(step == 0)
    def _():
        cross = (scal[head_at] == 1).astype(F32)
        cos_b, sin_b = tcol[:, 3:4] * cross, tcol[:, 4:5] * cross
        sq_lane, upper, diag = square_masks()
        for pair in range(PAIRS):
            cols = slice(pair * LANES, (pair + 1) * LANES)
            qp = rq[:, cols].astype(F32)
            of_cos, of_sin, norm_cos, norm_sin = unpack_state(st, pair)
            top = jnp.concatenate([of_cos, jnp.where(diag, norm_cos, 0.0)], axis=1)
            low = jnp.concatenate([of_sin, jnp.where(diag, norm_sin, 0.0)], axis=1)
            right = jnp.concatenate([top, low], axis=0).astype(BF)
            left = jnp.concatenate([(qp * cos_b).astype(BF), (qp * sin_b).astype(BF)], axis=1)
            prior = dot(left, right)
            inverse = 1.0 / (den[:, cols] + prior[:, LANES:] + 1.0)
            attended = (num[:, cols] + prior[:, :LANES]) * inverse
            att_o[:, cols] = attended
            inv_o[:, cols] = inverse
            mixed_o[:, cols] = attended.astype(BF)
        first_in = tok[...].astype(F32) + dot(mixed_o[...], w_merge[...]) + b_merge[...].astype(F32)
        xhat, scale = normalise(first_in)
        normed = xhat * gain[...].astype(F32) + bias[...].astype(F32)
        xhat_o[...] = xhat
        scale_o[...] = jnp.broadcast_to(scale, scale_o.shape)
        normed_o[...] = normed.astype(BF)
        acc[...] = normed + b_red[...].astype(F32)

    pre = dot(normed_o[...], w_exp[...]) + b_exp[...].astype(F32)
    cdf = 0.5 + 0.5 * lax.erf(pre * (2.0**-0.5))
    pdf = jnp.exp(-0.5 * pre * pre) * (1.0 / math.sqrt(2.0 * math.pi))
    act = (pre * cdf).astype(BF)
    act_o[...] = act
    slope_o[...] = (cdf + pre * pdf).astype(BF)
    acc[...] += dot(act, w_red[...])

    @pl.when(step == pl.num_programs(0) - 1)
    def _():
        second_o[...] = acc[...]


def second_kernel(core_at, scal, second, cot, gain, bias, out_o, grad_o, full_o, keep_o, send_o, sums_o):
    xhat, scale = normalise(second[...])
    gain_w = gain[...].astype(F32)
    out_o[...] = (xhat * gain_w + bias[...].astype(F32)).astype(BF)
    cot_w = cot[...].astype(F32)
    t = cot_w * gain_w
    grad = scale * (
        t - jnp.mean(t, axis=1, keepdims=True) - xhat * jnp.mean(t * xhat, axis=1, keepdims=True)
    )
    low = grad.astype(BF)
    grad_o[...] = grad
    full_o[...] = low
    first = scal[core_at] == 0
    half = D // 2
    left, right = grad[:, :half], grad[:, half:]
    keep_o[...] = jnp.where(first, left, right).astype(BF)
    send_o[...] = jnp.where(first, right, left).astype(BF)
    sums_o[0:1] = jnp.sum(cot_w * xhat, axis=0, keepdims=True)
    sums_o[1:2] = jnp.sum(cot_w, axis=0, keepdims=True)
    sums_o[2:3] = jnp.sum(low.astype(F32), axis=0, keepdims=True)


def back_kernel(
    core_at, scal, full, slope, w_exp, w_red, grad2, gain, xhat, scale, w_merge, att, inv, rq, tcol,
    pk_o, ps_o, first_o, mk_o, ms_o, we_o, wo_o, st_o, bexp_o, sums_o,
    acc,
):
    step = pl.program_id(0)
    steps = pl.num_programs(0)

    @pl.when(step == 0)
    def _():
        acc[...] = grad2[...]

    pre_grad = (dot_r(full[...], w_red[...]) * slope[...].astype(F32)).astype(BF)
    bexp_o[...] = jnp.sum(pre_grad.astype(F32), axis=0, keepdims=True)
    half = steps // 2
    mine = (step >= half) == (scal[core_at] == 1)
    slot = lax.rem(step, half)

    @pl.when(mine)
    def _():
        pk_o[slot] = pre_grad

    @pl.when(jnp.logical_not(mine))
    def _():
        ps_o[slot] = pre_grad

    acc[...] += dot_r(pre_grad, w_exp[...])

    @pl.when(step == steps - 1)
    def _():
        grad_normed = acc[...]
        xh = xhat[...]
        t = grad_normed * gain[...].astype(F32)
        first = scale[:, 0:1] * (
            t - jnp.mean(t, axis=1, keepdims=True) - xh * jnp.mean(t * xh, axis=1, keepdims=True)
        )
        low = first.astype(BF)
        first_o[...] = first
        sums_o[0:1] = jnp.sum(grad_normed * xh, axis=0, keepdims=True)
        sums_o[1:2] = jnp.sum(grad_normed, axis=0, keepdims=True)
        sums_o[2:3] = jnp.sum(low.astype(F32), axis=0, keepdims=True)
        is_first = scal[core_at] == 0
        left, right = first[:, : D // 2], first[:, D // 2 :]
        mk_o[...] = jnp.where(is_first, left, right).astype(BF)
        ms_o[...] = jnp.where(is_first, right, left).astype(BF)
        cos_b, sin_b = tcol[:, 3:4], tcol[:, 4:5]
        lane, even, even_b, odd_b = lane_masks()
        is_even = lane < HALF
        sq_lane, upper, diag = square_masks()
        across = jnp.where(diag, 0.0, 1.0).astype(BF)
        norms = jnp.zeros((LANES, LANES), F32)
        att_grad = dot_r(low, w_merge[...]).astype(BF)
        for pair in range(PAIRS):
            cols = slice(pair * LANES, (pair + 1) * LANES)
            w = att_grad[:, cols].astype(F32) * inv[:, cols]
            w_low = w.astype(BF).astype(F32)
            high, rest = high_low(w_low * att[:, cols])
            left = jnp.concatenate([high.astype(BF), rest.astype(BF)], axis=1)
            e = -dot(left, jnp.concatenate([across, across], axis=0))
            e_high, e_low = high_low(e)
            we = jnp.where(
                is_even, w_low, jnp.where(lane == HALF, e_high, jnp.where(lane == HALF + 1, e_low, 0.0))
            ).astype(BF)
            wo = jnp.where(
                is_even, jnp.where(lane == 0, e_high, jnp.where(lane == 1, e_low, 0.0)), w_low
            ).astype(BF)
            we_o[:, cols] = we
            wo_o[:, cols] = wo
            qp = rq[:, cols].astype(F32)
            left = jnp.concatenate([(qp * cos_b).astype(BF), (qp * sin_b).astype(BF)], axis=1)
            both = dot_t(left, jnp.concatenate([we, wo], axis=1))
            of_cos = jnp.where(upper, both[:LANES, :LANES], both[:LANES, LANES:])
            of_sin = jnp.where(upper, both[LANES:, :LANES], both[LANES:, LANES:])
            norm_cos = jnp.sum(jnp.where(diag, 0.0, of_cos), axis=1, keepdims=True)
            norm_sin = jnp.sum(jnp.where(diag, 0.0, of_sin), axis=1, keepdims=True)
            packed, norms = pack_state(of_cos, of_sin, norm_cos, norm_sin, pair, norms)
            st_o[pair] = packed
        st_o[PAIRS] = norms.astype(BF)


def attn_back_kernel(
    head_at, core_at, scal, rq, rk, v, we, wo, prior, later, tcol, trow,
    pk_o, ps_o, sums_o,
    weights, weights_t,
):
    pair = pl.program_id(0)
    rows = rq.shape[0]
    mid = rows // 2

    @pl.when(pair == 0)
    def _():
        weights[...] = weights_block(tcol, trow, False)
        weights_t[...] = weights_block(tcol, trow, True)

    lane, even, even_b, odd_b = lane_masks()
    is_even = lane < HALF
    sq_lane, upper, diag = square_masks()
    qp, kp, vp = rq[...], rk[...], v[...]
    w_of = (we[...], wo[...])
    ones_even = ((lane == HALF) | (lane == HALF + 1)).astype(F32).astype(BF)
    ones_odd = ((lane == 0) | (lane == 1)).astype(F32).astype(BF)
    v_of = (vp * even_b + ones_even, vp * odd_b + ones_odd)
    own = (even_b, odd_b)
    is_late = (scal[head_at] == 1).astype(F32)
    dq_parts, dk_parts, dv_parts = [], [], []
    for lo, hi in ((0, mid), (mid, rows)):
        outs = []
        for n in range(2):
            grads = dot_r(w_of[n][lo:hi], v_of[n][:hi]) * weights[lo:hi, :hi]
            outs.append(dot(grads.astype(BF), kp[:hi]))
        dq_parts.append(jnp.where(is_even, outs[0], outs[1]))
        outs_k, outs_v = [], []
        for n in range(2):
            grads = dot_r(v_of[n][lo:hi], w_of[n][lo:]) * weights_t[lo:hi, lo:]
            outs_k.append(dot(grads.astype(BF), qp[lo:]))
            scores = dot_r(kp[lo:hi] * own[n], qp[lo:]) * weights_t[lo:hi, lo:]
            outs_v.append(dot(scores.astype(BF), w_of[n][lo:]))
        dk_parts.append(jnp.where(is_even, outs_k[0], outs_k[1]))
        dv_parts.append(jnp.where(is_even, outs_v[0], outs_v[1]))
    dq = jnp.concatenate(dq_parts, axis=0)
    dk = jnp.concatenate(dk_parts, axis=0)
    dv = jnp.concatenate(dv_parts, axis=0)

    def by_head(of_cos, of_sin, norm_cos, norm_sin, lanes):
        ones = tuple((sum((lane == n).astype(F32) for n in run)) for run in lanes)
        def side(total, norm):
            full_e = jnp.where(upper, total + norm * ones[0], 0.0)
            full_o = jnp.where(upper, 0.0, total + norm * ones[1])
            return jnp.concatenate([full_e, full_o], axis=1)
        return jnp.concatenate([side(of_cos, norm_cos), side(of_sin, norm_sin)], axis=0).astype(BF)

    cos_b, sin_b = tcol[:, 3:4], tcol[:, 4:5]
    prior_parts = unpack_state(prior, pair)
    into = dot_r(jnp.concatenate(w_of, axis=1), by_head(*prior_parts, ((HALF, HALF + 1), (0, 1))))
    dq = dq + is_late * (cos_b * into[:, :LANES] + sin_b * into[:, LANES:])
    later_parts = unpack_state(later, pair)
    into = dot_r(jnp.concatenate(v_of, axis=1), by_head(*later_parts, ((HALF,), (0,))))
    early = 1.0 - is_late
    dk = dk + early * (cos_b * into[:, :LANES] + sin_b * into[:, LANES:])
    kw = kp.astype(F32)
    left = jnp.concatenate([(kw * (cos_b * early)).astype(BF), (kw * (sin_b * early)).astype(BF)], axis=1)
    dv = dv + dot(left, jnp.concatenate(later_parts[:2], axis=0).astype(BF))

    dq = jnp.where(qp.astype(F32) > 0, dq, 0.0).astype(BF)
    dk = jnp.where(kw > 0, dk, 0.0).astype(BF)
    dv = dv.astype(BF)
    blocks = 3 * PAIRS // 2
    for n, part in enumerate((dq, dk, dv)):
        sums_o[n] = jnp.broadcast_to(jnp.sum(part.astype(F32), axis=0, keepdims=True), sums_o.shape[1:])
        at = n * PAIRS + pair
        mine = (at >= blocks) == (scal[core_at] == 1)
        slot = lax.rem(at, blocks)

        @pl.when(mine)
        def _():
            pk_o[slot] = part

        @pl.when(jnp.logical_not(mine))
        def _():
            ps_o[slot] = part


def input_kernel(scal, first, keep, send, w_keep, w_send, out_o):
    @pl.when(pl.program_id(0) == 0)
    def _():
        out_o[...] = first[...]

    left = lambda ref: jnp.concatenate([ref[n] for n in range(ref.shape[0])], axis=1)
    out_o[...] += dot_r(left(keep), w_keep[...]) + dot_r(left(send), w_send[...])


def place(values, piece_rows, tz, tys, x, y, z, extra, outs):
    xk, xs, yk, ys = outs
    width = xk.shape[-1]
    slot_z = tz ^ z
    pieces = {}
    at = 0
    for ty in tys:
        for tc in range(2):
            for tx in range(2):
                part = values[at * piece_rows : (at + 1) * piece_rows]
                blocks = [part[:, n : n + width] for n in range(0, part.shape[1], width)]
                if extra is not None:
                    blocks.append(extra[at])
                pieces[ty, tc, tx] = jnp.concatenate(blocks, axis=0) if len(blocks) > 1 else blocks[0]
                at += 1
    for ty in tys:
        slot = ty ^ y
        a, b = pieces[ty, 0, 0], pieces[ty, 0, 1]
        xk[slot, slot_z] = jnp.where(x == 0, a, b).astype(BF)
        xs[slot, slot_z] = jnp.where(x == 0, b, a).astype(BF)
    return pieces


def place_y(pieces, tz, tys, x, y, z, outs):
    xk, xs, yk, ys = outs
    slot_z = tz ^ z
    for tx in range(2):
        slot = tx ^ x
        a, b = pieces[0, 1, tx], pieces[1, 1, tx]
        yk[slot, slot_z] = jnp.where(y == 0, a, b).astype(BF)
        ys[slot, slot_z] = jnp.where(y == 0, b, a).astype(BF)


def reduce_grad_kernel(pos_at, scal, a_own, a_oth, b_own, b_oth, *outs):
    tz = pl.program_id(0)
    x, y, z = (scal[pos_at + n] for n in range(3))
    values = dot_t(a_own[...], b_own[...]) + dot_t(a_oth[...], b_oth[...])
    piece_rows = values.shape[0] // 8
    pieces = place(values, piece_rows, tz, (0, 1), x, y, z, None, outs)
    place_y(pieces, tz, (0, 1), x, y, z, outs)


def expand_grad_kernel(pos_at, scal, a_own, a_oth, b_own, b_oth, m_own, m_oth, c_own, c_oth, *outs):
    tz = pl.program_id(0)
    x, y, z = (scal[pos_at + n] for n in range(3))
    an, ao = a_own[0], a_oth[0]
    parts = [dot(an, b_own[n]) + dot(ao, b_oth[n]) for n in range(b_own.shape[0])]
    parts.append(dot(m_own[0], c_own[...]) + dot(m_oth[0], c_oth[...]))
    values = jnp.concatenate(parts, axis=1)
    pieces = place(values, values.shape[0] // 8, tz, (0, 1), x, y, z, None, outs)
    place_y(pieces, tz, (0, 1), x, y, z, outs)


def heads_grad_kernel(pos_at, scal, a_own, a_oth, b_own, b_oth, vectors, *outs):
    tz = pl.program_id(0)
    x, y, z = (scal[pos_at + n] for n in range(3))
    join = lambda ref: jnp.concatenate([ref[n] for n in range(ref.shape[0])], axis=1)
    values = dot(a_own[0], join(b_own)) + dot(a_oth[0], join(b_oth))
    extra = [vectors[n] for n in range(8)]
    pieces = place(values, values.shape[0] // 8, tz, (0, 1), x, y, z, extra, outs)
    place_y(pieces, tz, (0, 1), x, y, z, outs)


class Ring:
    def __init__(self, n_dp):
        self.n_dp = n_dp
        self.devices = 2 * n_dp

    def swap(self, value, bits):
        return lax.ppermute(value, AXES, [(i, i ^ bits) for i in range(self.devices)])

    def core(self, value):
        return self.swap(value, 2)

    def x(self, value):
        return self.swap(value, 1)

    def y(self, value):
        return self.swap(value, 4)

    def z(self, value, step):
        return self.swap(value, 8 * step)


def scatter_group(ring, first_core, xk, xs, yk, ys):
    wide = lambda v: v.astype(F32)
    xr, yr = ring.x(xs), ring.y(ys)
    x_next, y_next = (wide(xk[1]) + wide(xr[1])).astype(BF), (wide(yk[1]) + wide(yr[1])).astype(BF)
    x_next, y_next = ring.y(x_next), ring.x(y_next)
    totals = []
    for keep, got, more in ((xk, xr, x_next), (yk, yr, y_next)):
        held = wide(keep[0]) + wide(got[0]) + wide(more)
        arrived = [ring.z(held[k].astype(BF), k) for k in (1, 2, 3)]
        totals.append(held[0] + wide(arrived[0]) + wide(arrived[1]) + wide(arrived[2]))
    keep = jnp.where(first_core, totals[0], totals[1])
    send = jnp.where(first_core, totals[1], totals[0])
    return keep, ring.core(send)


def halves(first_core, own, other):
    left = jnp.where(first_core, own, other)
    right = jnp.where(first_core, other, own)
    return jnp.concatenate([left, right], axis=1)


def columns(part, rows, blocks):
    return part.reshape(blocks, rows, part.shape[-1]).transpose(1, 0, 2).reshape(rows, -1)


def transposed_pieces(value):
    return value.T.reshape(4, D // 4, value.shape[0])


def per_device(
    tokens, w_heads, b_heads, w_merge, b_merge, gain_first, bias_first, w_expand, b_expand,
    w_reduce, b_reduce, gain_second, bias_second, seq_lengths, cotangent,
):
    rows = tokens.shape[0]
    seqs = seq_lengths.shape[1]
    n_dp = lax.axis_size("dp")
    ring = Ring(n_dp)
    head = lax.axis_index("head")
    dp = lax.axis_index("dp")
    core = dp % 2
    place_of = jnp.stack([head, core, head, (dp // 2) % 2, dp // 4]).astype(jnp.int32)
    scal = jnp.concatenate([seq_lengths[0].astype(jnp.int32), place_of])
    head_at, core_at, pos_at = seqs, seqs + 1, seqs + 2
    first_core = core == 0
    line = lambda v: v.reshape(1, -1)
    b_heads, b_merge, gain_first, bias_first, b_expand, b_reduce, gain_second, bias_second = map(
        line, (b_heads, b_merge, gain_first, bias_first, b_expand, b_reduce, gain_second, bias_second)
    )
    wide_shape = (rows, D)
    quarter = 256

    rk, v, state, tcol, trow = call(
        functools.partial(kv_kernel, seqs), "keys_values", scal, (3,),
        [
            (tokens, None, None),
            (w_heads, (D, quarter), lambda j, s: (0, 3 + j)),
            (w_heads, (D, quarter), lambda j, s: (0, 6 + j)),
            (b_heads, (1, quarter), lambda j, s: (0, 3 + j)),
            (b_heads, (1, quarter), lambda j, s: (0, 6 + j)),
        ],
        [
            (wide_shape, BF, (rows, quarter), lambda j, s: (0, j)),
            (wide_shape, BF, (rows, quarter), lambda j, s: (0, j)),
            ((PAIRS + 1, LANES, LANES), BF, None, None),
            ((rows, LANES), F32, None, None),
            ((8, rows), F32, None, None),
        ],
        [pltpu.VMEM((LANES, LANES), F32)],
        flops=4 * rows * D * D,
    )
    forward = [(i, i + 1) for i in range(0, 2 * n_dp, 2)]
    backward = [(b, a) for a, b in forward]
    prior = lax.ppermute(state, AXES, forward)

    rq, num, den = call(
        local_kernel, "local_attention", scal, (3,),
        [
            (tokens, None, None),
            (w_heads, (D, quarter), lambda j, s: (0, j)),
            (b_heads, (1, quarter), lambda j, s: (0, j)),
            (rk, (rows, quarter), lambda j, s: (0, j)),
            (v, (rows, quarter), lambda j, s: (0, j)),
            (tcol, None, None),
            (trow, None, None),
        ],
        [
            (wide_shape, BF, (rows, quarter), lambda j, s: (0, j)),
            (wide_shape, F32, (rows, quarter), lambda j, s: (0, j)),
            (wide_shape, F32, (rows, quarter), lambda j, s: (0, j)),
        ],
        [pltpu.VMEM((rows, rows), F32)],
        flops=2 * rows * D * D + 8 * rows * rows * D,
    )

    att, inv, mixed, xhat, scale, normed, act, slope, second = call(
        lambda *refs: ffn_kernel(*refs, head_at), "feed_forward", scal, (FF_STEPS,),
        [
            (rq, None, None), (num, None, None), (den, None, None), (prior, None, None),
            (tcol, None, None), (tokens, None, None), (w_merge, None, None), (b_merge, None, None),
            (gain_first, None, None), (bias_first, None, None),
            (w_expand, (D, FF_BLOCK), lambda j, s: (0, j)),
            (b_expand, (1, FF_BLOCK), lambda j, s: (0, j)),
            (w_reduce, (FF_BLOCK, D), lambda j, s: (j, 0)),
            (b_reduce, None, None),
        ],
        [
            (wide_shape, F32, None, None), (wide_shape, F32, None, None), (wide_shape, BF, None, None),
            (wide_shape, F32, None, None), ((rows, LANES), F32, None, None), (wide_shape, BF, None, None),
            ((rows, FF), BF, (rows, FF_BLOCK), lambda j, s: (0, j)),
            ((rows, FF), BF, (rows, FF_BLOCK), lambda j, s: (0, j)),
            (wide_shape, F32, None, None),
        ],
        [pltpu.VMEM(wide_shape, F32)],
        flops=2 * rows * D * (D + 2 * FF),
    )

    half_shape = (rows, D // 2)
    result, grad_second, branch, bg_keep, bg_send, sums_second = call(
        functools.partial(second_kernel, core_at), "second_norm", scal, (1,),
        [(second, None, None), (cotangent, None, None), (gain_second, None, None), (bias_second, None, None)],
        [
            (wide_shape, BF, None, None), (wide_shape, F32, None, None), (wide_shape, BF, None, None),
            (half_shape, BF, None, None), (half_shape, BF, None, None), ((8, D), F32, None, None),
        ],
        flops=20 * rows * D,
    )

    ff_half = FF_STEPS // 2
    pg_keep, pg_send, grad_first, mg_keep, mg_send, w_even, w_odd, later, sum_expand, sums_first = call(
        functools.partial(back_kernel, core_at), "feed_forward_back", scal, (FF_STEPS,),
        [
            (branch, None, None),
            (slope, (rows, FF_BLOCK), lambda j, s: (0, j)),
            (w_expand, (D, FF_BLOCK), lambda j, s: (0, j)),
            (w_reduce, (FF_BLOCK, D), lambda j, s: (j, 0)),
            (grad_second, None, None), (gain_first, None, None), (xhat, None, None), (scale, None, None),
            (w_merge, None, None), (att, None, None), (inv, None, None), (rq, None, None), (tcol, None, None),
        ],
        [
            ((ff_half, rows, FF_BLOCK), BF, None, None), ((ff_half, rows, FF_BLOCK), BF, None, None),
            (wide_shape, F32, None, None), (half_shape, BF, None, None), (half_shape, BF, None, None),
            (wide_shape, BF, None, None), (wide_shape, BF, None, None),
            ((PAIRS + 1, LANES, LANES), BF, None, None),
            ((1, FF), F32, (1, FF_BLOCK), lambda j, s: (0, j)),
            ((8, D), F32, None, None),
        ],
        [pltpu.VMEM(wide_shape, F32)],
        flops=2 * rows * D * (D + 2 * FF),
    )
    later = lax.ppermute(later, AXES, backward)

    blocks = 3 * PAIRS // 2
    pair_block = lambda a: (a, (rows, LANES), lambda j, s: (0, j))
    pj_keep, pj_send, sum_heads = call(
        functools.partial(attn_back_kernel, head_at, core_at), "attention_back", scal, (PAIRS,),
        [
            pair_block(rq), pair_block(rk), pair_block(v), pair_block(w_even), pair_block(w_odd),
            (prior, None, None), (later, None, None), (tcol, None, None), (trow, None, None),
        ],
        [
            ((blocks, rows, LANES), BF, None, None), ((blocks, rows, LANES), BF, None, None),
            ((3, 8, D), F32, (3, 8, LANES), lambda j, s: (0, 0, j)),
        ],
        [pltpu.VMEM((rows, rows), F32), pltpu.VMEM((rows, rows), F32)],
        flops=16 * rows * rows * D,
    )

    third = blocks // 3
    wide_block = third * LANES
    (input_grad,) = call(
        input_kernel, "input_grad", scal, (3,),
        [
            (grad_first, None, None),
            (pj_keep, (third, rows, LANES), lambda j, s: (j, 0, 0)),
            (pj_send, (third, rows, LANES), lambda j, s: (j, 0, 0)),
            (w_heads, (D, wide_block), lambda j, s: (0, 3 * s[core_at] + j)),
            (w_heads, (D, wide_block), lambda j, s: (0, 3 * (1 - s[core_at]) + j)),
        ],
        [(wide_shape, F32, None, None)],
        flops=6 * rows * D * D,
    )

    vectors = [
        jnp.concatenate([sum_heads[0, 0], sum_heads[1, 0]]), sum_heads[2, 0],
        sums_first[2], sums_first[0], sums_first[1],
        sum_expand[0], sums_second[2], sums_second[0], sums_second[1],
    ]
    if n_dp == 16:
        grads = exchange_fast(
            ring, first_core, scal, pos_at, vectors, tokens, mixed, normed, act,
            bg_keep, bg_send, pg_keep, pg_send, mg_keep, mg_send, pj_keep, pj_send,
        )
    else:
        by_core = lambda keep, send: jnp.concatenate(
            [jnp.where(first_core, keep, send), jnp.where(first_core, send, keep)], axis=1
        )
        flat = lambda v: v.transpose(1, 0, 2).reshape(rows, -1)
        scatter = lambda v: lax.psum_scatter(v, AXES, scatter_dimension=0, tiled=True)
        grads = (
            scatter(dot_t(tokens, by_core(flat(pj_keep), flat(pj_send)))),
            scatter(vectors[0]), scatter(vectors[1]),
            scatter(dot_t(mixed, by_core(mg_keep, mg_send))),
            scatter(vectors[2]), scatter(vectors[3]), scatter(vectors[4]),
            scatter(dot_t(normed, by_core(flat(pg_keep), flat(pg_send)))),
            scatter(vectors[5]),
            scatter(dot_t(act, branch)),
            scatter(vectors[6]), scatter(vectors[7]), scatter(vectors[8]),
        )
    return (result, input_grad) + tuple(grads)


def exchange_fast(
    ring, first_core, scal, pos_at, vectors, tokens, mixed, normed, act,
    bg_keep, bg_send, pg_keep, pg_send, mg_keep, mg_send, pj_keep, pj_send,
):
    rows = tokens.shape[0]
    devices = ring.devices
    width = D // 2
    small, large = D // devices, FF // devices
    tokens_t, normed_t, mixed_t = map(transposed_pieces, (tokens, normed, mixed))
    tokens_o, normed_o, mixed_o, act_o = map(ring.core, (tokens_t, normed_t, mixed_t, act))
    bg_o, pg_o, mg_o, pj_o = map(ring.core, (bg_send, pg_send, mg_send, pj_send))

    def group(kernel, name, ins, piece_rows, flops):
        shape = (2, 4, piece_rows, width)
        return call(
            functools.partial(kernel, pos_at), name, scal, (4,), ins, [(shape, BF, None, None)] * 4, flops=flops
        )

    by_z = lambda a: (a, (1, D // 4, rows), lambda j, s: (j, 0, 0))
    whole = lambda a: (a, None, None)
    by_col = lambda a: (a, (rows, FF // 4), lambda j, s: (0, j))
    flops = lambda n: 2 * rows * D * n
    reduce_sent = group(
        reduce_grad_kernel, "grad_reduce", [by_col(act), by_col(act_o), whole(bg_keep), whole(bg_o)],
        large, flops(FF),
    )
    reduce_own, reduce_got = scatter_group(ring, first_core, *reduce_sent)
    expand_sent = group(
        expand_grad_kernel, "grad_expand",
        [
            by_z(normed_t), by_z(normed_o), whole(pg_keep), whole(pg_o),
            by_z(mixed_t), by_z(mixed_o), whole(mg_keep), whole(mg_o),
        ],
        5 * small, flops(FF + D),
    )
    expand_own, expand_got = scatter_group(ring, first_core, *expand_sent)

    flat = jnp.concatenate([v.reshape(devices, -1) for v in vectors], axis=1)
    count = flat.shape[1]
    high = lax.optimization_barrier(flat.astype(BF)).astype(F32)
    packed = jnp.concatenate([high, flat - high], axis=1)
    packed = jnp.pad(packed, ((0, 0), (0, 8 * width - 2 * count))).reshape(devices, 8, width)
    heads_sent = group(
        heads_grad_kernel, "grad_heads",
        [
            by_z(tokens_t), by_z(tokens_o), whole(pj_keep), whole(pj_o),
            (packed, (8, 8, width), lambda j, s: (j, 0, 0)),
        ],
        3 * small + 8, flops(3 * D),
    )
    heads_own, heads_got = scatter_group(ring, first_core, *heads_sent)

    w_reduce_grad = halves(first_core, reduce_own, reduce_got)
    split = 4 * small
    w_expand_grad = halves(
        first_core, columns(expand_own[:split], small, 4), columns(expand_got[:split], small, 4)
    )
    w_merge_grad = halves(first_core, expand_own[split:], expand_got[split:])
    split = 3 * small
    w_heads_grad = halves(
        first_core, columns(heads_own[:split], small, 3), columns(heads_got[:split], small, 3)
    )
    entries = (heads_own[split:] + heads_got[split:]).reshape(-1)
    entries = entries[:count] + entries[count : 2 * count]
    shares, at = [], 0
    for v in vectors:
        n = v.shape[0] // devices
        shares.append(entries[at : at + n])
        at += n
    return (
        w_heads_grad, *shares[:2], w_merge_grad, *shares[2:5], w_expand_grad, shares[5], w_reduce_grad, *shares[6:]
    )


def solution(mesh):
    in_specs = (P(AXES, None),) + (P(),) * 12 + (P("dp", None), P(AXES, None))
    row, one = P(AXES, None), P(AXES)
    out_specs = (row, row, row, one, one, row, one, one, one, row, one, row, one, one, one)
    return jax.shard_map(
        per_device, mesh=mesh, in_specs=in_specs, out_specs=out_specs, check_vma=False
    )
```

```python
import functools
import math

import jax
import jax.numpy as jnp
from jax import lax
from jax.experimental import pallas as pl
from jax.experimental.pallas import tpu as pltpu
from jax.sharding import PartitionSpec as P

D = 768
PAIRS = 6
FF = 3072
LANES = 128
HALF = 64
BF = jnp.bfloat16
F32 = jnp.float32
AXES = ("dp", "head")
VMEM_LIMIT = 20 * 1024 * 1024
FF_BLOCK = 768
MATMUL_PER_US = 1.15e9
FF_STEPS = FF // FF_BLOCK


def dot(a, b):
    return jnp.dot(a, b, preferred_element_type=F32)


def dot_t(a, b):
    return lax.dot_general(a, b, (((0,), (0,)), ((), ())), preferred_element_type=F32)


def dot_r(a, b):
    return lax.dot_general(a, b, (((1,), (1,)), ((), ())), preferred_element_type=F32)


def call(kernel, name, scal, grid, ins, outs, scratch=(), us=1, vmem=VMEM_LIMIT):
    spec = lambda b, m: pl.BlockSpec(memory_space=pltpu.VMEM) if b is None else pl.BlockSpec(b, m)
    in_specs = [spec(b, m) for _, b, m in ins]
    out_specs = [spec(b, m) for _, _, b, m in outs]
    return pl.pallas_call(
        kernel,
        name=name,
        grid_spec=pltpu.PrefetchScalarGridSpec(
            num_scalar_prefetch=1,
            grid=grid,
            in_specs=in_specs,
            out_specs=out_specs,
            scratch_shapes=list(scratch),
        ),
        out_shape=[jax.ShapeDtypeStruct(s, d) for s, d, _, _ in outs],
        compiler_params=pltpu.CompilerParams(vmem_limit_bytes=vmem),
        cost_estimate=pl.CostEstimate(flops=int(us * MATMUL_PER_US), bytes_accessed=1, transcendentals=0),
    )(scal, *[a for a, _, _ in ins])


def lane_masks():
    lane = lax.broadcasted_iota(jnp.int32, (1, LANES), 1)
    even = (lane < HALF).astype(F32)
    return lane, even.astype(BF), (1.0 - even).astype(BF)


def both_heads(pair):
    lane, even, odd = lane_masks()
    return jnp.concatenate([pair * even, pair * odd], axis=0)


def own_lanes(stacked):
    rows = stacked.shape[0] // 2
    lane = lax.broadcasted_iota(jnp.int32, (1, LANES), 1)
    return jnp.where(lane < HALF, stacked[:rows], stacked[rows:])


def square_masks():
    row = lax.broadcasted_iota(jnp.int32, (LANES, LANES), 0)
    lane = lax.broadcasted_iota(jnp.int32, (LANES, LANES), 1)
    upper = row < HALF
    return lane, upper, upper == (lane < HALF)


def high_low(v):
    high = v.astype(BF).astype(F32)
    return high, v - high


def tables(scal, rows, seqs, tcol, trow):
    pos = lax.broadcasted_iota(jnp.int32, (1, rows), 1) + scal[seqs] * rows
    seg = jnp.zeros((1, rows), jnp.int32)
    first = jnp.zeros((1, rows), jnp.int32)
    length = jnp.ones((1, rows), jnp.int32)
    at_boundary = jnp.int32(0)
    begin = jnp.int32(0)
    for s in range(seqs):
        end = begin + scal[s]
        inside = (pos >= begin) & (pos < end)
        first = jnp.where(inside, begin, first)
        length = jnp.where(inside, jnp.maximum(scal[s], 1), length)
        seg = seg + (pos >= end).astype(jnp.int32)
        at_boundary = at_boundary + (rows - 1 >= end).astype(jnp.int32)
        begin = end
    live = (seg < seqs).astype(F32)
    angle = 0.5 * math.pi * (pos - first).astype(F32) / length.astype(F32)
    cos_w = jnp.cos(angle) * live
    sin_w = jnp.sin(angle) * live
    crossing = (seg == at_boundary).astype(F32)
    which = lax.broadcasted_iota(jnp.int32, (LANES, rows), 0)
    table = jnp.zeros((LANES, rows), F32)
    for n, entry in enumerate((cos_w, sin_w, seg.astype(F32), cos_w * crossing, sin_w * crossing)):
        table = jnp.where(which == n, entry, table)
    trow[...] = table[:8]
    tcol[...] = table.T


def pack_state(both, norm_cos, norm_sin, pair, norms):
    lane, upper, diag = square_masks()
    packed = jnp.where(diag, both[:LANES, :LANES], pltpu.roll(both[LANES:, :LANES], HALF, 1))
    cos_high, cos_low = high_low(norm_cos)
    sin_high, sin_low = high_low(norm_sin)
    for n, part in enumerate((cos_high, cos_low, sin_high, sin_low)):
        norms = jnp.where(lane == 4 * pair + n, part, norms)
    return packed.astype(BF), norms


def unpack_state(state_ref, pair):
    lane, upper, diag = square_masks()
    packed = state_ref[pair].astype(F32)
    norms = state_ref[PAIRS].astype(F32)
    of_cos = jnp.where(diag, packed, 0.0)
    of_sin = jnp.where(diag, pltpu.roll(packed, HALF, 1), 0.0)
    pick = lambda n: jnp.sum(
        jnp.where((lane == 4 * pair + n) | (lane == 4 * pair + n + 1), norms, 0.0), axis=1, keepdims=True
    )
    return of_cos, of_sin, pick(0), pick(2)


def kv_kernel(seqs, scal, tok, wk, wv, bk, bv, rk_o, v_o, st_o, tcol, trow, norms):
    step = pl.program_id(0)
    rows = tok.shape[0]

    @pl.when(step == 0)
    def _():
        tables(scal, rows, seqs, tcol, trow)
        norms[...] = jnp.zeros_like(norms)

    rk = jnp.maximum(dot(tok[...], wk[...]) + bk[...].astype(F32), 0.0).astype(BF)
    v = (dot(tok[...], wv[...]) + bv[...].astype(F32)).astype(BF)
    rk_o[...] = rk
    v_o[...] = v
    cos_b, sin_b = tcol[:, 3:4], tcol[:, 4:5]
    ones = jnp.ones((rows, LANES), BF)
    for n in range(2):
        pair = 2 * step + n
        cols = slice(n * LANES, (n + 1) * LANES)
        kp = rk[:, cols].astype(F32)
        left = jnp.concatenate([(kp * cos_b).astype(BF), (kp * sin_b).astype(BF)], axis=1)
        both = dot_t(left, jnp.concatenate([v[:, cols], ones], axis=1))
        packed, new_norms = pack_state(both, both[:LANES, LANES:], both[LANES:, LANES:], pair, norms[...])
        st_o[pair] = packed
        norms[...] = new_norms

    st_o[PAIRS] = norms[...].astype(BF)


def weights_block(tcol, trow, transposed):
    rows = tcol.shape[0]
    down = lax.broadcasted_iota(jnp.int32, (rows, rows), 0)
    along = lax.broadcasted_iota(jnp.int32, (rows, rows), 1)
    same = tcol[:, 2:3] == trow[2:3, :]
    causal = (down <= along) if transposed else (along <= down)
    value = tcol[:, 0:1] * trow[0:1, :] + tcol[:, 1:2] * trow[1:2, :]
    return jnp.where(same & causal, value, 0.0)


def weigh(stacked, weights):
    rows = weights.shape[0]
    return jnp.concatenate([stacked[:rows] * weights, stacked[rows:] * weights], axis=0).astype(BF)


def local_kernel(scal, tok, wq, bq, rk, v, tcol, trow, rq_o, num_o, den_o, weights):
    step = pl.program_id(0)
    rows = tok.shape[0]
    mid = rows // 2

    @pl.when(step == 0)
    def _():
        weights[...] = weights_block(tcol, trow, False)

    rq = jnp.maximum(dot(tok[...], wq[...]) + bq[...].astype(F32), 0.0).astype(BF)
    rq_o[...] = rq
    ones = jnp.ones((rows, LANES), BF)
    for n in range(2):
        cols = slice(n * LANES, (n + 1) * LANES)
        kp = rk[:, cols]
        values = jnp.concatenate([v[:, cols], ones], axis=1)
        first = weigh(dot_r(both_heads(rq[:, cols]), kp[:mid]), weights[:, :mid])
        second = weigh(dot_r(both_heads(rq[mid:, cols]), kp[mid:]), weights[mid:, mid:])
        sums = dot(first, values[:mid])
        late = dot(second, values[mid:])
        for own, out in ((slice(0, LANES), num_o), (slice(LANES, 2 * LANES), den_o)):
            total = own_lanes(sums[:, own])
            out[:mid, cols] = total[:mid]
            out[mid:, cols] = total[mid:] + own_lanes(late[:, own])


def normalise(entries):
    mean = jnp.mean(entries, axis=1, keepdims=True)
    centred = entries - mean
    var = jnp.mean(centred * centred, axis=1, keepdims=True)
    scale = lax.rsqrt(var + 1e-05)
    return centred * scale, scale


def merge_heads(
    head_at, scal, rq, num, den, st, tcol, tok, w_merge, b_merge, gain, bias, b_red,
    att_o, inv_o, mixed_o, xhat_o, scale_o, normed_o, acc_o,
):
    cross = (scal[head_at] == 1).astype(F32)
    cos_b, sin_b = tcol[:, 3:4] * cross, tcol[:, 4:5] * cross
    sq_lane, upper, diag = square_masks()
    for pair in range(PAIRS):
        cols = slice(pair * LANES, (pair + 1) * LANES)
        qp = rq[:, cols].astype(F32)
        of_cos, of_sin, norm_cos, norm_sin = unpack_state(st, pair)
        top = jnp.concatenate([of_cos, jnp.where(diag, norm_cos, 0.0)], axis=1)
        low = jnp.concatenate([of_sin, jnp.where(diag, norm_sin, 0.0)], axis=1)
        right = jnp.concatenate([top, low], axis=0).astype(BF)
        left = jnp.concatenate([(qp * cos_b).astype(BF), (qp * sin_b).astype(BF)], axis=1)
        prior = dot(left, right)
        inverse = 1.0 / (den[:, cols] + prior[:, LANES:] + 1.0)
        attended = (num[:, cols] + prior[:, :LANES]) * inverse
        att_o[:, cols] = attended
        inv_o[:, cols] = inverse
        mixed_o[:, cols] = attended.astype(BF)
    first_in = tok[...].astype(F32) + dot(mixed_o[...], w_merge[...]) + b_merge[...].astype(F32)
    xhat, scale = normalise(first_in)
    normed = xhat * gain[...].astype(F32) + bias[...].astype(F32)
    xhat_o[...] = xhat
    scale_o[...] = jnp.broadcast_to(scale, scale_o.shape)
    normed_o[...] = normed.astype(BF)
    acc_o[...] = normed + b_red[...].astype(F32)


def expand_reduce(normed, w_exp, b_exp, w_red, act_o, slope_o):
    pre = dot(normed[...], w_exp[...]) + b_exp[...].astype(F32)
    cdf = 0.5 + 0.5 * lax.erf(pre * (2.0**-0.5))
    pdf = jnp.exp(-0.5 * pre * pre) * (1.0 / math.sqrt(2.0 * math.pi))
    act = (pre * cdf).astype(BF)
    act_o[...] = act
    slope_o[...] = (cdf + pre * pdf).astype(BF)
    return dot(act, w_red[...])


def ffn_kernel(head_at, scal, *refs):
    w_exp, b_exp, w_red = refs[11:14]
    normed_o, acc_o, act_o, slope_o = refs[19:]

    @pl.when(pl.program_id(0) == 0)
    def _():
        merge_heads(head_at, scal, *refs[:11], *refs[14:21])

    acc_o[...] += expand_reduce(normed_o, w_exp, b_exp, w_red, act_o, slope_o)


def second_kernel(core_at, scal, second, cot, gain, bias, out_o, grad_o, full_o, keep_o, send_o, sums_o):
    xhat, scale = normalise(second[...])
    gain_w = gain[...].astype(F32)
    out_o[...] = (xhat * gain_w + bias[...].astype(F32)).astype(BF)
    cot_w = cot[...].astype(F32)
    t = cot_w * gain_w
    grad = scale * (
        t - jnp.mean(t, axis=1, keepdims=True) - xhat * jnp.mean(t * xhat, axis=1, keepdims=True)
    )
    low = grad.astype(BF)
    grad_o[...] = grad
    full_o[...] = low
    first = scal[core_at] == 0
    half = D // 2
    left, right = grad[:, :half], grad[:, half:]
    keep_o[...] = jnp.where(first, left, right).astype(BF)
    send_o[...] = jnp.where(first, right, left).astype(BF)
    sums_o[0:1] = jnp.sum(cot_w * xhat, axis=0, keepdims=True)
    sums_o[1:2] = jnp.sum(cot_w, axis=0, keepdims=True)
    sums_o[2:3] = jnp.sum(low.astype(F32), axis=0, keepdims=True)


def head_lanes(pair, lane, first):
    at = 4 * pair + jnp.where(first, 0, 2)
    return (lane == at) | (lane == at + 1)


def back_step(full, slope, w_exp, w_red, out_o, bexp_o):
    pre_grad = (dot_r(full[...], w_red[...]) * slope[...].astype(F32)).astype(BF)
    bexp_o[...] = jnp.sum(pre_grad.astype(F32), axis=0, keepdims=True)
    out_o[0] = pre_grad
    return dot_r(pre_grad, w_exp[...])


def back_sent_kernel(scal, full, slope, w_exp, w_red, grad2, sent_o, bexp_o, acc):
    @pl.when(pl.program_id(0) == 0)
    def _():
        acc[...] = grad2[...]

    acc[...] += back_step(full, slope, w_exp, w_red, sent_o, bexp_o)


def back_kernel(
    core_at, scal, full, slope, w_exp, w_red, acc_in, gain, xhat, scale, w_merge, att, inv, rq, tcol,
    kept_o, first_o, mk_o, ms_o, w_o, e_o, st_o, bexp_o, sums_o,
    acc,
):
    step = pl.program_id(0)

    @pl.when(step == 0)
    def _():
        acc[...] = acc_in[...]

    acc[...] += back_step(full, slope, w_exp, w_red, kept_o, bexp_o)

    @pl.when(step == pl.num_programs(0) - 1)
    def _():
        grad_normed = acc[...]
        xh = xhat[...]
        t = grad_normed * gain[...].astype(F32)
        first = scale[:, 0:1] * (
            t - jnp.mean(t, axis=1, keepdims=True) - xh * jnp.mean(t * xh, axis=1, keepdims=True)
        )
        low = first.astype(BF)
        first_o[...] = first
        sums_o[0:1] = jnp.sum(grad_normed * xh, axis=0, keepdims=True)
        sums_o[1:2] = jnp.sum(grad_normed, axis=0, keepdims=True)
        sums_o[2:3] = jnp.sum(low.astype(F32), axis=0, keepdims=True)
        is_first = scal[core_at] == 0
        left, right = first[:, : D // 2], first[:, D // 2 :]
        mk_o[...] = jnp.where(is_first, left, right).astype(BF)
        ms_o[...] = jnp.where(is_first, right, left).astype(BF)
        cos_b, sin_b = tcol[:, 3:4], tcol[:, 4:5]
        w = (dot_r(low, w_merge[...]).astype(BF).astype(F32) * inv[...]).astype(BF)
        w_o[...] = w
        high, rest = high_low(w.astype(F32) * att[...])
        column = lax.broadcasted_iota(jnp.int32, (D, LANES), 0)
        target = lax.broadcasted_iota(jnp.int32, (D, LANES), 1)
        picks = (target == 2 * (column // HALF)).astype(F32).astype(BF)
        e_high, e_low = high_low(-(dot(high.astype(BF), picks) + dot(rest.astype(BF), picks)))
        e = (e_high + pltpu.roll(e_low, 1, 1)).astype(BF)
        e_o[...] = e
        norms = jnp.zeros((LANES, LANES), F32)
        sq_lane, upper, diag = square_masks()
        for pair in range(PAIRS):
            cols = slice(pair * LANES, (pair + 1) * LANES)
            qp = rq[:, cols].astype(F32)
            left = jnp.concatenate([(qp * cos_b).astype(BF), (qp * sin_b).astype(BF)], axis=1)
            both = dot_t(left, jnp.concatenate([w[:, cols], e], axis=1))
            mine = head_lanes(pair, sq_lane, upper)
            norm = lambda part: jnp.sum(jnp.where(mine, part, 0.0), axis=1, keepdims=True)
            packed, norms = pack_state(both, norm(both[:LANES, LANES:]), norm(both[LANES:, LANES:]), pair, norms)
            st_o[pair] = packed
        st_o[PAIRS] = norms.astype(BF)


def attn_back_kernel(
    head_at, core_at, scal, rq, rk, v, w, e, prior, later, tcol, trow,
    pk_o, ps_o, sums_o,
    weights, weights_t,
):
    pair = pl.program_id(0)
    rows = rq.shape[0]
    mid = rows // 2

    @pl.when(pair == 0)
    def _():
        weights[...] = weights_block(tcol, trow, False)
        weights_t[...] = weights_block(tcol, trow, True)

    qp, kp, vp, wp = rq[...], rk[...], v[...], w[...]
    lane, even, odd = lane_masks()
    of_even = ((lane == 4 * pair) | (lane == 4 * pair + 1)).astype(F32).astype(BF)
    of_odd = ((lane == 4 * pair + 2) | (lane == 4 * pair + 3)).astype(F32).astype(BF)
    ones = jnp.ones((rows, LANES), BF)
    we = jnp.concatenate([wp, e[...]], axis=1)
    by_head = (jnp.concatenate([even, of_even], axis=1), jnp.concatenate([odd, of_odd], axis=1))
    ve = jnp.concatenate([vp, ones], axis=1)
    stack = lambda a, lo, hi: jnp.concatenate([a[lo:hi] * m for m in by_head], axis=0)

    grads = weigh(dot_r(stack(we, 0, rows), ve[:mid]), weights[:, :mid])
    dq = own_lanes(dot(grads, kp[:mid]))
    grads = weigh(dot_r(stack(we, mid, rows), ve[mid:]), weights[mid:, mid:])
    dq_late = own_lanes(dot(grads, kp[mid:]))

    grads = weigh(dot_r(stack(ve, 0, rows), we[mid:]), weights_t[:, mid:])
    dk = own_lanes(dot(grads, qp[mid:]))
    grads = weigh(dot_r(stack(ve, 0, mid), we[:mid]), weights_t[:mid, :mid])
    dk_early = own_lanes(dot(grads, qp[:mid]))

    scores = weigh(dot_r(both_heads(kp), qp[mid:]), weights_t[:, mid:])
    dv = own_lanes(dot(scores, wp[mid:]))
    scores = weigh(dot_r(both_heads(kp[:mid]), qp[:mid]), weights_t[:mid, :mid])
    dv_early = own_lanes(dot(scores, wp[:mid]))

    dq = jnp.concatenate([dq[:mid], dq[mid:] + dq_late], axis=0)
    dk = jnp.concatenate([dk[:mid] + dk_early, dk[mid:]], axis=0)
    dv = jnp.concatenate([dv[:mid] + dv_early, dv[mid:]], axis=0)

    sq_lane, upper, diag = square_masks()
    cos_b, sin_b = tcol[:, 3:4], tcol[:, 4:5]
    is_late = (scal[head_at] == 1).astype(F32)
    early = 1.0 - is_late

    def with_norms(parts, where):
        side = lambda total, norm: jnp.concatenate([total, jnp.where(where, norm, 0.0)], axis=1)
        of_cos, of_sin, norm_cos, norm_sin = parts
        return jnp.concatenate([side(of_cos, norm_cos), side(of_sin, norm_sin)], axis=0).astype(BF)

    prior_parts = unpack_state(prior, pair)
    into = dot_r(we, with_norms(prior_parts, head_lanes(pair, sq_lane, upper)))
    dq = dq + is_late * (cos_b * into[:, :LANES] + sin_b * into[:, LANES:])
    later_parts = unpack_state(later, pair)
    into = dot_r(ve, with_norms(later_parts, sq_lane == 0))
    dk = dk + early * (cos_b * into[:, :LANES] + sin_b * into[:, LANES:])
    kw = kp.astype(F32)
    left = jnp.concatenate([(kw * (cos_b * early)).astype(BF), (kw * (sin_b * early)).astype(BF)], axis=1)
    dv = dv + dot(left, jnp.concatenate(later_parts[:2], axis=0).astype(BF))

    dq = jnp.where(qp.astype(F32) > 0, dq, 0.0).astype(BF)
    dk = jnp.where(kw > 0, dk, 0.0).astype(BF)
    dv = dv.astype(BF)
    blocks = 3 * PAIRS // 2
    for n, part in enumerate((dq, dk, dv)):
        sums_o[n] = jnp.broadcast_to(jnp.sum(part.astype(F32), axis=0, keepdims=True), sums_o.shape[1:])
        at = n * PAIRS + pair
        mine = (at >= blocks) == (scal[core_at] == 1)
        slot = lax.rem(at, blocks)

        @pl.when(mine)
        def _():
            pk_o[slot] = part

        @pl.when(jnp.logical_not(mine))
        def _():
            ps_o[slot] = part


def input_kernel(scal, first, keep, send, w_keep, w_send, out_o):
    @pl.when(pl.program_id(0) == 0)
    def _():
        out_o[...] = first[...]

    left = lambda ref: jnp.concatenate([ref[n] for n in range(ref.shape[0])], axis=1)
    out_o[...] += dot_r(left(keep), w_keep[...]) + dot_r(left(send), w_send[...])


def place(values, piece_rows, tz, tys, x, y, z, extra, outs):
    xk, xs, yk, ys = outs
    width = xk.shape[-1]
    slot_z = tz ^ z
    pieces = {}
    at = 0
    for ty in tys:
        for tc in range(2):
            for tx in range(2):
                part = values[at * piece_rows : (at + 1) * piece_rows]
                blocks = [part[:, n : n + width] for n in range(0, part.shape[1], width)]
                if extra is not None:
                    blocks.append(extra[at])
                pieces[ty, tc, tx] = jnp.concatenate(blocks, axis=0) if len(blocks) > 1 else blocks[0]
                at += 1
    for ty in tys:
        slot = ty ^ y
        a, b = pieces[ty, 0, 0], pieces[ty, 0, 1]
        xk[slot, slot_z] = jnp.where(x == 0, a, b).astype(BF)
        xs[slot, slot_z] = jnp.where(x == 0, b, a).astype(BF)
    return pieces


def place_y(pieces, tz, tys, x, y, z, outs):
    xk, xs, yk, ys = outs
    slot_z = tz ^ z
    for tx in range(2):
        slot = tx ^ x
        a, b = pieces[0, 1, tx], pieces[1, 1, tx]
        yk[slot, slot_z] = jnp.where(y == 0, a, b).astype(BF)
        ys[slot, slot_z] = jnp.where(y == 0, b, a).astype(BF)


def reduce_grad_kernel(pos_at, scal, a_own, a_oth, b_own, b_oth, *outs):
    tz = pl.program_id(0)
    x, y, z = (scal[pos_at + n] for n in range(3))
    values = dot_t(a_own[...], b_own[...]) + dot_t(a_oth[...], b_oth[...])
    piece_rows = values.shape[0] // 8
    pieces = place(values, piece_rows, tz, (0, 1), x, y, z, None, outs)
    place_y(pieces, tz, (0, 1), x, y, z, outs)


def expand_grad_kernel(pos_at, scal, a_own, a_oth, b_own, b_oth, m_own, m_oth, c_own, c_oth, *outs):
    tz = pl.program_id(0)
    x, y, z = (scal[pos_at + n] for n in range(3))
    an, ao = a_own[0], a_oth[0]
    parts = [dot(an, b_own[n]) + dot(ao, b_oth[n]) for n in range(b_own.shape[0])]
    parts.append(dot(m_own[0], c_own[...]) + dot(m_oth[0], c_oth[...]))
    values = jnp.concatenate(parts, axis=1)
    pieces = place(values, values.shape[0] // 8, tz, (0, 1), x, y, z, None, outs)
    place_y(pieces, tz, (0, 1), x, y, z, outs)


def share_lanes(entries, devices, at, width):
    n = entries.shape[1]
    share = n // devices
    owner = lax.broadcasted_iota(jnp.int32, (devices, n), 0)
    column = lax.broadcasted_iota(jnp.int32, (devices, n), 1)
    mine = (column >= owner * share) & (column < (owner + 1) * share)
    high, low = high_low(jnp.where(mine, entries, 0.0))
    both = jnp.concatenate([high, low], axis=0).astype(BF)
    source = lax.broadcasted_iota(jnp.int32, (n, width), 0)
    target = lax.broadcasted_iota(jnp.int32, (n, width), 1)
    picks = (target >= at) & (target < at + share) & (lax.rem(source, share) == target - at)
    spread = dot(both, picks.astype(F32).astype(BF))
    return spread[:devices] + spread[devices:]


def heads_grad_kernel(
    pos_at, scal, a_own, a_oth, b_own, b_oth, sums_q, sums_k, sums_v, sums_1, sums_e, sums_2, *refs, devices
):
    outs, table = refs[:-1], refs[-1]
    tz = pl.program_id(0)
    x, y, z = (scal[pos_at + n] for n in range(3))
    width = outs[0].shape[-1]

    @pl.when(tz == 0)
    def _():
        scores = jnp.concatenate([sums_q[0, 0:1], sums_k[0, 0:1]], axis=1)
        total = jnp.zeros((devices, width), F32)
        at = 0
        for entries in (
            scores, sums_v[0, 0:1], sums_1[2:3], sums_1[0:1], sums_1[1:2],
            sums_e[...], sums_2[2:3], sums_2[0:1], sums_2[1:2],
        ):
            total = total + share_lanes(entries, devices, at, width)
            at += entries.shape[1] // devices
        table[...] = total

    join = lambda ref: jnp.concatenate([ref[n] for n in range(ref.shape[0])], axis=1)
    values = dot(a_own[0], join(b_own)) + dot(a_oth[0], join(b_oth))
    line = lax.broadcasted_iota(jnp.int32, (8, width), 0)
    rows8 = table[pl.ds(pl.multiple_of(tz * 8, 8), 8)]
    extra = []
    for n in range(8):
        high, low = high_low(rows8[n : n + 1])
        extra.append(jnp.where(line == 0, high, jnp.where(line == 1, low, 0.0)))
    pieces = place(values, values.shape[0] // 8, tz, (0, 1), x, y, z, extra, outs)
    place_y(pieces, tz, (0, 1), x, y, z, outs)


class Ring:
    def __init__(self, n_dp):
        self.n_dp = n_dp
        self.devices = 2 * n_dp

    def swap(self, value, bits):
        return lax.ppermute(value, AXES, [(i, i ^ bits) for i in range(self.devices)])

    def core(self, value):
        return self.swap(value, 2)

    def x(self, value):
        return self.swap(value, 1)

    def y(self, value):
        return self.swap(value, 4)

    def z(self, value, step):
        return self.swap(value, 8 * step)


def add_first_kernel(scal, xk, xr, yk, yr, xn, yn):
    wide = lambda ref: ref[0].astype(F32)
    xn[...] = (wide(xk) + wide(xr)).astype(BF)
    yn[...] = (wide(yk) + wide(yr)).astype(BF)


def add_second_kernel(scal, xk, xr, xm, yk, yr, ym, own, z1, z2, z3):
    for n, (keep, got, more) in enumerate(((xk, xr, xm), (yk, yr, ym))):
        total = lambda k: keep[0, k].astype(F32) + got[0, k].astype(F32) + more[k].astype(F32)
        own[n] = total(0)
        for k, out in ((1, z1), (2, z2), (3, z3)):
            out[n] = total(k).astype(BF)


def add_last_kernel(core_at, scal, own, z1, z2, z3, keep, send):
    first = scal[core_at] == 0
    total = lambda n: own[n] + z1[n].astype(F32) + z2[n].astype(F32) + z3[n].astype(F32)
    of_first, of_second = total(0), total(1)
    keep[...] = jnp.where(first, of_first, of_second)
    send[...] = jnp.where(first, of_second, of_first)


class Scatter:
    def __init__(self, ring, core_at, name, sent):
        self.ring, self.core_at, self.name = ring, core_at, name
        self.xk, self.xs, self.yk, self.ys = sent

    def send(self):
        self.xr, self.yr = self.ring.x(self.xs), self.ring.y(self.ys)

    def first(self, scal):
        shape = self.xk.shape[1:]
        part = lambda a: (a, (1,) + shape, lambda j, s: (1, 0, 0, 0))
        xn, yn = call(
            add_first_kernel, self.name + "_add1", scal, (1,), [part(a) for a in (self.xk, self.xr, self.yk, self.yr)],
            [(shape, BF, None, None)] * 2,
        )
        self.xn, self.yn = xn, yn
        return xn

    def send_first(self):
        self.xm, self.ym = self.ring.y(self.xn), self.ring.x(self.yn)

    def second(self, scal, us=1):
        shape = self.xk.shape[1:]
        piece = (2,) + shape[1:]
        part = lambda a: (a, (1,) + shape, lambda j, s: (0, 0, 0, 0))
        whole = lambda a: (a, None, None)
        self.own, *self.sends = call(
            add_second_kernel, self.name + "_add2", scal, (1,),
            [part(self.xk), part(self.xr), whole(self.xm), part(self.yk), part(self.yr), whole(self.ym)],
            [(piece, F32, None, None)] + [(piece, BF, None, None)] * 3, us=us,
        )
        return self.own

    def send_second(self):
        self.arrived = [self.ring.z(v, k + 1) for k, v in enumerate(self.sends)]

    def last(self, scal):
        piece = self.own.shape[1:]
        keep, send = call(
            functools.partial(add_last_kernel, self.core_at), self.name + "_add3", scal, (1,),
            [(a, None, None) for a in (self.own, *self.arrived)], [(piece, F32, None, None)] * 2,
        )
        return keep, self.ring.core(send)


def after(value, *others):
    return lax.optimization_barrier((value,) + others)[0]


def halves(first_core, own, other):
    left = jnp.where(first_core, own, other)
    right = jnp.where(first_core, other, own)
    return jnp.concatenate([left, right], axis=1)


def columns(part, rows, blocks):
    return part.reshape(blocks, rows, part.shape[-1]).transpose(1, 0, 2).reshape(rows, -1)


def transposed_pieces(value):
    return value.T.reshape(4, D // 4, value.shape[0])


def per_device(
    tokens, w_heads, b_heads, w_merge, b_merge, gain_first, bias_first, w_expand, b_expand,
    w_reduce, b_reduce, gain_second, bias_second, seq_lengths, cotangent,
):
    rows = tokens.shape[0]
    seqs = seq_lengths.shape[1]
    n_dp = lax.axis_size("dp")
    ring = Ring(n_dp)
    head = lax.axis_index("head")
    dp = lax.axis_index("dp")
    core = dp % 2
    place_of = jnp.stack([head, core, head, (dp // 2) % 2, dp // 4]).astype(jnp.int32)
    scal = jnp.concatenate([seq_lengths[0].astype(jnp.int32), place_of])
    head_at, core_at, pos_at = seqs, seqs + 1, seqs + 2
    first_core = core == 0
    line = lambda v: v.reshape(1, -1)
    b_heads, b_merge, gain_first, bias_first, b_expand, b_reduce, gain_second, bias_second = map(
        line, (b_heads, b_merge, gain_first, bias_first, b_expand, b_reduce, gain_second, bias_second)
    )
    wide_shape = (rows, D)
    quarter = 256

    rk, v, state, tcol, trow = call(
        functools.partial(kv_kernel, seqs), "keys_values", scal, (3,),
        [
            (tokens, None, None),
            (w_heads, (D, quarter), lambda j, s: (0, 3 + j)),
            (w_heads, (D, quarter), lambda j, s: (0, 6 + j)),
            (b_heads, (1, quarter), lambda j, s: (0, 3 + j)),
            (b_heads, (1, quarter), lambda j, s: (0, 6 + j)),
        ],
        [
            (wide_shape, BF, (rows, quarter), lambda j, s: (0, j)),
            (wide_shape, BF, (rows, quarter), lambda j, s: (0, j)),
            ((PAIRS + 1, LANES, LANES), BF, None, None),
            ((rows, LANES), F32, None, None),
            ((8, rows), F32, None, None),
        ],
        [pltpu.VMEM((LANES, LANES), F32)],
        us=4,
    )
    forward = [(i, i + 1) for i in range(0, 2 * n_dp, 2)]
    backward = [(b, a) for a, b in forward]
    prior = lax.ppermute(state, AXES, forward)

    fast = n_dp == 16
    order = scal
    if fast:
        tokens_t = transposed_pieces(tokens)
        tokens_o = ring.core(tokens_t)
    rq, num, den = call(
        local_kernel, "local_attention", scal, (3,),
        [
            (tokens, None, None),
            (w_heads, (D, quarter), lambda j, s: (0, j)),
            (b_heads, (1, quarter), lambda j, s: (0, j)),
            (rk, (rows, quarter), lambda j, s: (0, j)),
            (v, (rows, quarter), lambda j, s: (0, j)),
            (tcol, None, None),
            (trow, None, None),
        ],
        [
            (wide_shape, BF, (rows, quarter), lambda j, s: (0, j)),
            (wide_shape, F32, (rows, quarter), lambda j, s: (0, j)),
            (wide_shape, F32, (rows, quarter), lambda j, s: (0, j)),
        ],
        [pltpu.VMEM((rows, rows), F32)],
        us=6,
    )

    if fast:
        order = after(scal, tokens_o)
    att, inv, mixed, xhat, scale, normed, second, act, slope = call(
        functools.partial(ffn_kernel, head_at), "feed_forward", order, (FF_STEPS,),
        [
            (rq, None, None), (num, None, None), (den, None, None), (prior, None, None),
            (tcol, None, None), (tokens, None, None), (w_merge, None, None), (b_merge, None, None),
            (gain_first, None, None), (bias_first, None, None), (b_reduce, None, None),
            (w_expand, (D, FF_BLOCK), lambda j, s: (0, j)),
            (b_expand, (1, FF_BLOCK), lambda j, s: (0, j)),
            (w_reduce, (FF_BLOCK, D), lambda j, s: (j, 0)),
        ],
        [
            (wide_shape, F32, None, None), (wide_shape, F32, None, None), (wide_shape, BF, None, None),
            (wide_shape, F32, None, None), ((rows, LANES), F32, None, None), (wide_shape, BF, None, None),
            (wide_shape, F32, None, None),
            ((rows, FF), BF, (rows, FF_BLOCK), lambda j, s: (0, j)),
            ((rows, FF), BF, (rows, FF_BLOCK), lambda j, s: (0, j)),
        ],
        us=11,
    )

    normed_t, mixed_t = map(transposed_pieces, (normed, mixed))
    half_shape = (rows, D // 2)
    result, grad_second, branch, bg_keep, bg_send, sums_second = call(
        functools.partial(second_kernel, core_at), "second_norm", scal, (1,),
        [(second, None, None), (cotangent, None, None), (gain_second, None, None), (bias_second, None, None)],
        [
            (wide_shape, BF, None, None), (wide_shape, F32, None, None), (wide_shape, BF, None, None),
            (half_shape, BF, None, None), (half_shape, BF, None, None), ((8, D), F32, None, None),
        ],
        us=2.6,
    )

    devices = ring.devices
    small, large = D // devices, FF // devices
    whole = lambda a: (a, None, None)
    by_z = lambda a: (a, (1, D // 4, rows), lambda j, s: (j, 0, 0))
    by_col = lambda a: (a, (rows, FF // 4), lambda j, s: (0, j))

    def group(kernel, name, scal, ins, piece_rows, us, scratch=()):
        shape = (2, 4, piece_rows, D // 2)
        sent = call(
            functools.partial(kernel, pos_at), name, scal, (4,), ins, [(shape, BF, None, None)] * 4, scratch, us
        )
        return Scatter(ring, core_at, name, sent)

    ff_half = FF_STEPS // 2
    half_of = lambda core_of: [
        (slope, (rows, FF_BLOCK), lambda j, s: (0, core_of(s) * ff_half + j)),
        (w_expand, (D, FF_BLOCK), lambda j, s: (0, core_of(s) * ff_half + j)),
        (w_reduce, (FF_BLOCK, D), lambda j, s: (core_of(s) * ff_half + j, 0)),
    ]
    hidden = ((ff_half, rows, FF_BLOCK), BF, (1, rows, FF_BLOCK), lambda j, s: (j, 0, 0))
    hidden_sums = ((1, FF // 2), F32, (1, FF_BLOCK), lambda j, s: (0, j))
    pg_send, sum_sent, partial = call(
        back_sent_kernel, "feed_forward_back_sent", scal, (ff_half,),
        [(branch, None, None), *half_of(lambda s: 1 - s[core_at]), (grad_second, None, None)],
        [hidden, hidden_sums, (wide_shape, F32, None, None)],
        us=5,
    )
    order = scal
    if fast:
        pg_o = ring.core(pg_send)
        act_o, normed_o, mixed_o, bg_o = map(ring.core, (act, normed_t, mixed_t, bg_send))
        reduced = group(
            reduce_grad_kernel, "grad_reduce", after(scal, partial),
            [by_col(act), by_col(act_o), whole(bg_keep), whole(bg_o)], large, 6,
        )
        order = after(scal, reduced.xs)
        reduced.send()

    pg_keep, grad_first, mg_keep, mg_send, w_att, e_att, later, sum_kept, sums_first = call(
        functools.partial(back_kernel, core_at), "feed_forward_back", order, (ff_half,),
        [
            (branch, None, None), *half_of(lambda s: s[core_at]),
            (partial, None, None), (gain_first, None, None), (xhat, None, None), (scale, None, None),
            (w_merge, None, None), (att, None, None), (inv, None, None), (rq, None, None), (tcol, None, None),
        ],
        [
            hidden, (wide_shape, F32, None, None), (half_shape, BF, None, None), (half_shape, BF, None, None),
            (wide_shape, BF, None, None), ((rows, LANES), BF, None, None),
            ((PAIRS + 1, LANES, LANES), BF, None, None), hidden_sums, ((8, D), F32, None, None),
        ],
        [pltpu.VMEM(wide_shape, F32)],
        us=9,
    )
    sum_expand = jnp.where(
        first_core, jnp.concatenate([sum_kept, sum_sent], axis=1), jnp.concatenate([sum_sent, sum_kept], axis=1)
    )
    later = lax.ppermute(later, AXES, backward)

    if fast:
        mg_o = ring.core(mg_send)
        expanded = group(
            expand_grad_kernel, "grad_expand", scal,
            [
                by_z(normed_t), by_z(normed_o), whole(pg_keep), whole(pg_o),
                by_z(mixed_t), by_z(mixed_o), whole(mg_keep), whole(mg_o),
            ],
            5 * small, 0.5,
        )
        expanded.send()
        order = after(scal, reduced.first(after(scal, expanded.xs)))
        reduced.send_first()

    blocks = 3 * PAIRS // 2
    pair_block = lambda a: (a, (rows, LANES), lambda j, s: (0, j))
    pj_keep, pj_send, sum_heads = call(
        functools.partial(attn_back_kernel, head_at, core_at), "attention_back", order, (PAIRS,),
        [
            pair_block(rq), pair_block(rk), pair_block(v), pair_block(w_att), whole(e_att),
            (prior, None, None), (later, None, None), (tcol, None, None), (trow, None, None),
        ],
        [
            ((blocks, rows, LANES), BF, None, None), ((blocks, rows, LANES), BF, None, None),
            ((3, 8, D), F32, (3, 8, LANES), lambda j, s: (0, 0, j)),
        ],
        [pltpu.VMEM((rows, rows), F32), pltpu.VMEM((rows, rows), F32)],
        us=14,
    )

    if fast:
        pj_o = ring.core(pj_send)
        order = expanded.first(after(scal, pj_send))
        expanded.send_first()
        order = reduced.second(after(scal, order), us=12)
        reduced.send_second()
        heads = group(
            functools.partial(heads_grad_kernel, devices=devices), "grad_heads", after(scal, order),
            [
                by_z(tokens_t), by_z(tokens_o), whole(pj_keep), whole(pj_o),
                *((sum_heads, (1, 8, D), lambda j, s, n=n: (n, 0, 0)) for n in range(3)),
                whole(sums_first), whole(sum_expand), whole(sums_second),
            ],
            3 * small + 8, 5, [pltpu.VMEM((devices, D // 2), F32)],
        )
        heads.send()
        order = after(scal, heads.xs)

    third = blocks // 3
    wide_block = third * LANES
    (input_grad,) = call(
        input_kernel, "input_grad", order, (3,),
        [
            (grad_first, None, None),
            (pj_keep, (third, rows, LANES), lambda j, s: (j, 0, 0)),
            (pj_send, (third, rows, LANES), lambda j, s: (j, 0, 0)),
            (w_heads, (D, wide_block), lambda j, s: (0, 3 * s[core_at] + j)),
            (w_heads, (D, wide_block), lambda j, s: (0, 3 * (1 - s[core_at]) + j)),
        ],
        [(wide_shape, F32, None, None)],
        us=5.3,
    )

    if fast:
        order = expanded.second(after(scal, input_grad))
        expanded.send_second()
        reduce_own, reduce_got = reduced.last(after(scal, order))
        order = heads.first(after(scal, reduce_own))
        heads.send_first()
        expand_own, expand_got = expanded.last(after(scal, order))
        heads.second(after(scal, expand_own))
        heads.send_second()
        heads_own, heads_got = heads.last(scal)
        w_reduce_grad = halves(first_core, reduce_own, reduce_got)
        split = 4 * small
        w_expand_grad = halves(
            first_core, columns(expand_own[:split], small, 4), columns(expand_got[:split], small, 4)
        )
        w_merge_grad = halves(first_core, expand_own[split:], expand_got[split:])
        split = 3 * small
        w_heads_grad = halves(
            first_core, columns(heads_own[:split], small, 3), columns(heads_got[:split], small, 3)
        )
        entries = heads_own[split:] + heads_got[split:]
        entries = entries[0] + entries[1]
        shares, at = [], 0
        for n in (2 * small, small, small, small, small, large, small, small, small):
            shares.append(entries[at : at + n])
            at += n
        grads = (
            w_heads_grad, *shares[:2], w_merge_grad, *shares[2:5], w_expand_grad, shares[5], w_reduce_grad,
            *shares[6:],
        )
    else:
        by_core = lambda keep, send: jnp.concatenate(
            [jnp.where(first_core, keep, send), jnp.where(first_core, send, keep)], axis=1
        )
        flat = lambda v: v.transpose(1, 0, 2).reshape(rows, -1)
        scatter = lambda v: lax.psum_scatter(v, AXES, scatter_dimension=0, tiled=True)
        grads = (
            scatter(dot_t(tokens, by_core(flat(pj_keep), flat(pj_send)))),
            scatter(jnp.concatenate([sum_heads[0, 0], sum_heads[1, 0]])), scatter(sum_heads[2, 0]),
            scatter(dot_t(mixed, by_core(mg_keep, mg_send))),
            scatter(sums_first[2]), scatter(sums_first[0]), scatter(sums_first[1]),
            scatter(dot_t(normed, by_core(flat(pg_keep), flat(pg_send)))),
            scatter(sum_expand[0]),
            scatter(dot_t(act, branch)),
            scatter(sums_second[2]), scatter(sums_second[0]), scatter(sums_second[1]),
        )
    return (result, input_grad) + tuple(grads)


def solution(mesh):
    in_specs = (P(AXES, None),) + (P(),) * 12 + (P("dp", None), P(AXES, None))
    row, one = P(AXES, None), P(AXES)
    out_specs = (row, row, row, one, one, row, one, one, one, row, one, row, one, one, one)
    return jax.shard_map(
        per_device, mesh=mesh, in_specs=in_specs, out_specs=out_specs, check_vma=False
    )
```

```python
import functools
import math

import jax
import jax.numpy as jnp
from jax import lax
from jax.experimental import pallas as pl
from jax.experimental.pallas import tpu as pltpu
from jax.sharding import PartitionSpec as P

D = 768
PAIRS = 6
FF = 3072
LANES = 128
HALF = 64
BF = jnp.bfloat16
F32 = jnp.float32
AXES = ("dp", "head")
VMEM_LIMIT = 8 << 20
VMEM_FFN = 11 << 20
FF_BLOCK = 768
MATMUL_PER_US = 1.15e9
COST_EXPAND = 1
VMEM_BACK = 16 << 20
COST_KEPT = 5
COST_SENT = 0.5
COST_HEADS = 0.1
COST_INPUT = 0.1
FF_STEPS = FF // FF_BLOCK


def dot(a, b):
    return jnp.dot(a, b, preferred_element_type=F32)


def dot_t(a, b):
    return lax.dot_general(a, b, (((0,), (0,)), ((), ())), preferred_element_type=F32)


def dot_r(a, b):
    return lax.dot_general(a, b, (((1,), (1,)), ((), ())), preferred_element_type=F32)


def call(kernel, name, scal, grid, ins, outs, scratch=(), us=1, vmem=VMEM_LIMIT):
    def spec(b, m):
        if b is None:
            return pl.BlockSpec(memory_space=pltpu.VMEM if m is None else m)
        return pl.BlockSpec(b, m)

    in_specs = [spec(b, m) for _, b, m in ins]
    out_specs = [spec(b, m) for _, _, b, m in outs]
    return pl.pallas_call(
        kernel,
        name=name,
        grid_spec=pltpu.PrefetchScalarGridSpec(
            num_scalar_prefetch=1,
            grid=grid,
            in_specs=in_specs,
            out_specs=out_specs,
            scratch_shapes=list(scratch),
        ),
        out_shape=[jax.ShapeDtypeStruct(s, d) for s, d, _, _ in outs],
        compiler_params=pltpu.CompilerParams(vmem_limit_bytes=vmem),
        cost_estimate=pl.CostEstimate(flops=int(us * MATMUL_PER_US), bytes_accessed=1, transcendentals=0),
    )(scal, *[a for a, _, _ in ins])


def lane_masks():
    lane = lax.broadcasted_iota(jnp.int32, (1, LANES), 1)
    even = (lane < HALF).astype(F32)
    return lane, even.astype(BF), (1.0 - even).astype(BF)


def both_heads(pair):
    lane, even, odd = lane_masks()
    return jnp.concatenate([pair * even, pair * odd], axis=0)


def own_lanes(stacked):
    rows = stacked.shape[0] // 2
    lane = lax.broadcasted_iota(jnp.int32, (1, LANES), 1)
    return jnp.where(lane < HALF, stacked[:rows], stacked[rows:])


def square_masks():
    row = lax.broadcasted_iota(jnp.int32, (LANES, LANES), 0)
    lane = lax.broadcasted_iota(jnp.int32, (LANES, LANES), 1)
    upper = row < HALF
    return lane, upper, upper == (lane < HALF)


def high_low(v):
    high = v.astype(BF).astype(F32)
    return high, v - high


def tables(scal, rows, seqs, tcol, trow):
    pos = lax.broadcasted_iota(jnp.int32, (1, rows), 1) + scal[seqs] * rows
    seg = jnp.zeros((1, rows), jnp.int32)
    first = jnp.zeros((1, rows), jnp.int32)
    length = jnp.ones((1, rows), jnp.int32)
    at_boundary = jnp.int32(0)
    begin = jnp.int32(0)
    for s in range(seqs):
        end = begin + scal[s]
        inside = (pos >= begin) & (pos < end)
        first = jnp.where(inside, begin, first)
        length = jnp.where(inside, jnp.maximum(scal[s], 1), length)
        seg = seg + (pos >= end).astype(jnp.int32)
        at_boundary = at_boundary + (rows - 1 >= end).astype(jnp.int32)
        begin = end
    live = (seg < seqs).astype(F32)
    angle = 0.5 * math.pi * (pos - first).astype(F32) / length.astype(F32)
    cos_w = jnp.cos(angle) * live
    sin_w = jnp.sin(angle) * live
    crossing = (seg == at_boundary).astype(F32)
    which = lax.broadcasted_iota(jnp.int32, (LANES, rows), 0)
    table = jnp.zeros((LANES, rows), F32)
    for n, entry in enumerate((cos_w, sin_w, seg.astype(F32), cos_w * crossing, sin_w * crossing)):
        table = jnp.where(which == n, entry, table)
    trow[...] = table[:8]
    tcol[...] = table.T


def pack_state(both, norm_cos, norm_sin, pair, norms):
    lane, upper, diag = square_masks()
    packed = jnp.where(diag, both[:LANES, :LANES], pltpu.roll(both[LANES:, :LANES], HALF, 1))
    cos_high, cos_low = high_low(norm_cos)
    sin_high, sin_low = high_low(norm_sin)
    for n, part in enumerate((cos_high, cos_low, sin_high, sin_low)):
        norms = jnp.where(lane == 4 * pair + n, part, norms)
    return packed.astype(BF), norms


def unpack_state(state_ref, pair):
    lane, upper, diag = square_masks()
    packed = state_ref[pair].astype(F32)
    norms = state_ref[PAIRS].astype(F32)
    of_cos = jnp.where(diag, packed, 0.0)
    of_sin = jnp.where(diag, pltpu.roll(packed, HALF, 1), 0.0)
    pick = lambda n: jnp.sum(
        jnp.where((lane == 4 * pair + n) | (lane == 4 * pair + n + 1), norms, 0.0), axis=1, keepdims=True
    )
    return of_cos, of_sin, pick(0), pick(2)


def turn(value, out):
    turned = value.T
    share = out.shape[1]
    for n in range(out.shape[0]):
        out[n] = turned[n * share : (n + 1) * share]


def kv_kernel(seqs, scal, tok, wk, wv, bk, bv, rk_o, v_o, st_o, tcol, trow, turned_o, norms):
    step = pl.program_id(0)
    rows = tok.shape[0]

    @pl.when(step == 0)
    def _():
        tables(scal, rows, seqs, tcol, trow)
        norms[...] = jnp.zeros_like(norms)
        turn(tok[...], turned_o)

    rk = jnp.maximum(dot(tok[...], wk[...]) + bk[...].astype(F32), 0.0).astype(BF)
    v = (dot(tok[...], wv[...]) + bv[...].astype(F32)).astype(BF)
    rk_o[...] = rk
    v_o[...] = v
    cos_b, sin_b = tcol[:, 3:4], tcol[:, 4:5]
    ones = jnp.ones((rows, LANES), BF)
    for n in range(2):
        pair = 2 * step + n
        cols = slice(n * LANES, (n + 1) * LANES)
        kp = rk[:, cols].astype(F32)
        left = jnp.concatenate([(kp * cos_b).astype(BF), (kp * sin_b).astype(BF)], axis=1)
        both = dot_t(left, jnp.concatenate([v[:, cols], ones], axis=1))
        packed, new_norms = pack_state(both, both[:LANES, LANES:], both[LANES:, LANES:], pair, norms[...])
        st_o[pair] = packed
        norms[...] = new_norms

    st_o[PAIRS] = norms[...].astype(BF)


def weights_block(tcol, trow, transposed):
    rows = tcol.shape[0]
    down = lax.broadcasted_iota(jnp.int32, (rows, rows), 0)
    along = lax.broadcasted_iota(jnp.int32, (rows, rows), 1)
    same = tcol[:, 2:3] == trow[2:3, :]
    causal = (down <= along) if transposed else (along <= down)
    value = tcol[:, 0:1] * trow[0:1, :] + tcol[:, 1:2] * trow[1:2, :]
    return jnp.where(same & causal, value, 0.0)


def weigh(stacked, weights):
    rows = weights.shape[0]
    return jnp.concatenate([stacked[:rows] * weights, stacked[rows:] * weights], axis=0).astype(BF)


def local_kernel(scal, tok, wq, bq, rk, v, tcol, trow, rq_o, num_o, den_o, weights):
    step = pl.program_id(0)
    rows = tok.shape[0]
    mid = rows // 2

    @pl.when(step == 0)
    def _():
        weights[...] = weights_block(tcol, trow, False)

    rq = jnp.maximum(dot(tok[...], wq[...]) + bq[...].astype(F32), 0.0).astype(BF)
    rq_o[...] = rq
    ones = jnp.ones((rows, LANES), BF)
    for n in range(2):
        cols = slice(n * LANES, (n + 1) * LANES)
        kp = rk[:, cols]
        values = jnp.concatenate([v[:, cols], ones], axis=1)
        first = weigh(dot_r(both_heads(rq[:, cols]), kp[:mid]), weights[:, :mid])
        second = weigh(dot_r(both_heads(rq[mid:, cols]), kp[mid:]), weights[mid:, mid:])
        sums = dot(first, values[:mid])
        late = dot(second, values[mid:])
        for own, out in ((slice(0, LANES), num_o), (slice(LANES, 2 * LANES), den_o)):
            total = own_lanes(sums[:, own])
            out[:mid, cols] = total[:mid]
            out[mid:, cols] = total[mid:] + own_lanes(late[:, own])


def normalise(entries):
    mean = jnp.mean(entries, axis=1, keepdims=True)
    centred = entries - mean
    var = jnp.mean(centred * centred, axis=1, keepdims=True)
    scale = lax.rsqrt(var + 1e-05)
    return centred * scale, scale


def merge_heads(
    head_at, scal, rq, num, den, st, tcol, tok, w_merge, b_merge, gain, bias, b_red,
    att_o, inv_o, mixed_o, xhat_o, scale_o, normed_o, acc_o, turned_o,
):
    cross = (scal[head_at] == 1).astype(F32)
    cos_b, sin_b = tcol[:, 3:4] * cross, tcol[:, 4:5] * cross
    sq_lane, upper, diag = square_masks()
    for pair in range(PAIRS):
        cols = slice(pair * LANES, (pair + 1) * LANES)
        qp = rq[:, cols].astype(F32)
        of_cos, of_sin, norm_cos, norm_sin = unpack_state(st, pair)
        top = jnp.concatenate([of_cos, jnp.where(diag, norm_cos, 0.0)], axis=1)
        low = jnp.concatenate([of_sin, jnp.where(diag, norm_sin, 0.0)], axis=1)
        right = jnp.concatenate([top, low], axis=0).astype(BF)
        left = jnp.concatenate([(qp * cos_b).astype(BF), (qp * sin_b).astype(BF)], axis=1)
        prior = dot(left, right)
        inverse = 1.0 / (den[:, cols] + prior[:, LANES:] + 1.0)
        attended = (num[:, cols] + prior[:, :LANES]) * inverse
        att_o[:, cols] = attended
        inv_o[:, cols] = inverse
        mixed_o[:, cols] = attended.astype(BF)
    first_in = tok[...].astype(F32) + dot(mixed_o[...], w_merge[...]) + b_merge[...].astype(F32)
    xhat, scale = normalise(first_in)
    normed = xhat * gain[...].astype(F32) + bias[...].astype(F32)
    xhat_o[...] = xhat
    scale_o[...] = jnp.broadcast_to(scale, scale_o.shape)
    normed_o[...] = normed.astype(BF)
    acc_o[...] = normed + b_red[...].astype(F32)
    turn(mixed_o[...], turned_o.at[0])
    turn(normed_o[...], turned_o.at[1])


def expand_reduce(normed, w_exp, b_exp, w_red, act_o, slope_o):
    pre = dot(normed[...], w_exp[...]) + b_exp[...].astype(F32)
    cdf = 0.5 + 0.5 * lax.erf(pre * (2.0**-0.5))
    pdf = jnp.exp(-0.5 * pre * pre) * (1.0 / math.sqrt(2.0 * math.pi))
    act = (pre * cdf).astype(BF)
    act_o[...] = act
    slope_o[...] = (cdf + pre * pdf).astype(BF)
    return dot(act, w_red[...])


def ffn_kernel(head_at, scal, *refs):
    w_exp, b_exp, w_red = refs[11:14]
    normed_o, acc_o = refs[19:21]
    act_o, slope_o = refs[22:]

    @pl.when(pl.program_id(0) == 0)
    def _():
        merge_heads(head_at, scal, *refs[:11], *refs[14:22])

    acc_o[...] += expand_reduce(normed_o, w_exp, b_exp, w_red, act_o, slope_o)


def second_kernel(core_at, scal, second, cot, gain, bias, out_o, grad_o, full_o, keep_o, send_o, sums_o):
    xhat, scale = normalise(second[...])
    gain_w = gain[...].astype(F32)
    out_o[...] = (xhat * gain_w + bias[...].astype(F32)).astype(BF)
    cot_w = cot[...].astype(F32)
    t = cot_w * gain_w
    grad = scale * (
        t - jnp.mean(t, axis=1, keepdims=True) - xhat * jnp.mean(t * xhat, axis=1, keepdims=True)
    )
    low = grad.astype(BF)
    grad_o[...] = grad
    full_o[...] = low
    first = scal[core_at] == 0
    half = D // 2
    left, right = grad[:, :half], grad[:, half:]
    keep_o[...] = jnp.where(first, left, right).astype(BF)
    send_o[...] = jnp.where(first, right, left).astype(BF)
    sums_o[0:1] = jnp.sum(cot_w * xhat, axis=0, keepdims=True)
    sums_o[1:2] = jnp.sum(cot_w, axis=0, keepdims=True)
    sums_o[2:3] = jnp.sum(low.astype(F32), axis=0, keepdims=True)


def head_lanes(pair, lane, first):
    at = 4 * pair + jnp.where(first, 0, 2)
    return (lane == at) | (lane == at + 1)


def weight_copies(half, w_exp, w_red, exp_buf, red_buf, sems, n):
    at = pl.ds(pl.multiple_of((half * exp_buf.shape[0] + n) * FF_BLOCK, FF_BLOCK), FF_BLOCK)
    return (
        pltpu.make_async_copy(w_red.at[at, :], red_buf.at[n], sems.at[0, n]),
        pltpu.make_async_copy(w_exp.at[:, at], exp_buf.at[n], sems.at[1, n]),
    )


def back_steps(half, full, slope, w_exp, w_red, out_o, bexp_o, exp_buf, red_buf, sems):
    blocks = exp_buf.shape[0]
    copies = [weight_copies(half, w_exp, w_red, exp_buf, red_buf, sems, n) for n in range(blocks)]
    for pair in copies:
        for copy in pair:
            copy.start()
    total = None
    for n, (of_red, of_exp) in enumerate(copies):
        cols = slice(n * FF_BLOCK, (n + 1) * FF_BLOCK)
        at = pl.ds(pl.multiple_of((half * blocks + n) * FF_BLOCK, FF_BLOCK), FF_BLOCK)
        of_red.wait()
        pre_grad = (dot_r(full[...], red_buf[n]) * slope[:, at].astype(F32)).astype(BF)
        bexp_o[:, cols] = jnp.sum(pre_grad.astype(F32), axis=0, keepdims=True)
        out_o[n] = pre_grad
        of_exp.wait()
        part = dot_r(pre_grad, exp_buf[n])
        total = part if total is None else total + part
    return total


def back_sent_kernel(core_at, scal, full, slope, w_exp, w_red, grad2, sent_o, bexp_o, acc, exp_buf, red_buf, sems):
    half = 1 - scal[core_at]
    acc[...] = grad2[...] + back_steps(half, full, slope, w_exp, w_red, sent_o, bexp_o, exp_buf, red_buf, sems)


def back_kernel(
    core_at, scal, full, slope, w_exp, w_red, acc_in, gain, xhat, scale, w_merge, att, inv, rq, tcol,
    kept_o, first_o, mk_o, ms_o, w_o, e_o, st_o, bexp_o, sums_o,
    acc, exp_buf, red_buf, sems,
):
    half = scal[core_at]
    acc[...] = acc_in[...] + back_steps(half, full, slope, w_exp, w_red, kept_o, bexp_o, exp_buf, red_buf, sems)
    back_rest(
        core_at, scal, acc, gain, xhat, scale, w_merge, att, inv, rq, tcol,
        first_o, mk_o, ms_o, w_o, e_o, st_o, sums_o,
    )


def back_rest(
    core_at, scal, acc, gain, xhat, scale, w_merge, att, inv, rq, tcol,
    first_o, mk_o, ms_o, w_o, e_o, st_o, sums_o,
):
    grad_normed = acc[...]
    xh = xhat[...]
    t = grad_normed * gain[...].astype(F32)
    first = scale[:, 0:1] * (
        t - jnp.mean(t, axis=1, keepdims=True) - xh * jnp.mean(t * xh, axis=1, keepdims=True)
    )
    low = first.astype(BF)
    first_o[...] = first
    sums_o[0:1] = jnp.sum(grad_normed * xh, axis=0, keepdims=True)
    sums_o[1:2] = jnp.sum(grad_normed, axis=0, keepdims=True)
    sums_o[2:3] = jnp.sum(low.astype(F32), axis=0, keepdims=True)
    is_first = scal[core_at] == 0
    left, right = first[:, : D // 2], first[:, D // 2 :]
    mk_o[...] = jnp.where(is_first, left, right).astype(BF)
    ms_o[...] = jnp.where(is_first, right, left).astype(BF)
    cos_b, sin_b = tcol[:, 3:4], tcol[:, 4:5]
    w = (dot_r(low, w_merge[...]).astype(BF).astype(F32) * inv[...]).astype(BF)
    w_o[...] = w
    high, rest = high_low(w.astype(F32) * att[...])
    column = lax.broadcasted_iota(jnp.int32, (D, LANES), 0)
    target = lax.broadcasted_iota(jnp.int32, (D, LANES), 1)
    picks = (target == 2 * (column // HALF)).astype(F32).astype(BF)
    e_high, e_low = high_low(-(dot(high.astype(BF), picks) + dot(rest.astype(BF), picks)))
    e = (e_high + pltpu.roll(e_low, 1, 1)).astype(BF)
    e_o[...] = e
    norms = jnp.zeros((LANES, LANES), F32)
    sq_lane, upper, diag = square_masks()
    for pair in range(PAIRS):
        cols = slice(pair * LANES, (pair + 1) * LANES)
        qp = rq[:, cols].astype(F32)
        left = jnp.concatenate([(qp * cos_b).astype(BF), (qp * sin_b).astype(BF)], axis=1)
        both = dot_t(left, jnp.concatenate([w[:, cols], e], axis=1))
        mine = head_lanes(pair, sq_lane, upper)
        norm = lambda part: jnp.sum(jnp.where(mine, part, 0.0), axis=1, keepdims=True)
        packed, norms = pack_state(both, norm(both[:LANES, LANES:]), norm(both[LANES:, LANES:]), pair, norms)
        st_o[pair] = packed
    st_o[PAIRS] = norms.astype(BF)


def attn_sent_kernel(head_at, core_at, scal, rq, rk, v, w, e, prior, later, tcol, trow, out_o, sums_o, weights, weights_t):
    @pl.when(pl.program_id(0) == 0)
    def _():
        weights[...] = weights_block(tcol, trow, False)
        weights_t[...] = weights_block(tcol, trow, True)

    first = (1 - scal[core_at]) * pl.num_programs(0)
    attn_back(head_at, first, scal, rq, rk, v, w, e, prior, later, tcol, weights, weights_t, out_o, sums_o)


def attn_kept_kernel(head_at, core_at, scal, rq, rk, v, w, e, prior, later, tcol, weights, weights_t, out_o, sums_o):
    first = scal[core_at] * pl.num_programs(0)
    attn_back(head_at, first, scal, rq, rk, v, w, e, prior, later, tcol, weights, weights_t, out_o, sums_o)


def attn_back(head_at, first, scal, rq, rk, v, w, e, prior, later, tcol, weights, weights_t, out_o, sums_o):
    pair = first + pl.program_id(0)
    rows = rq.shape[0]
    mid = rows // 2

    qp, kp, vp, wp = rq[...], rk[...], v[...], w[...]
    lane, even, odd = lane_masks()
    of_even = ((lane == 4 * pair) | (lane == 4 * pair + 1)).astype(F32).astype(BF)
    of_odd = ((lane == 4 * pair + 2) | (lane == 4 * pair + 3)).astype(F32).astype(BF)
    ones = jnp.ones((rows, LANES), BF)
    we = jnp.concatenate([wp, e[...]], axis=1)
    by_head = (jnp.concatenate([even, of_even], axis=1), jnp.concatenate([odd, of_odd], axis=1))
    ve = jnp.concatenate([vp, ones], axis=1)
    stack = lambda a, lo, hi: jnp.concatenate([a[lo:hi] * m for m in by_head], axis=0)

    grads = weigh(dot_r(stack(we, 0, rows), ve[:mid]), weights[:, :mid])
    dq = own_lanes(dot(grads, kp[:mid]))
    grads = weigh(dot_r(stack(we, mid, rows), ve[mid:]), weights[mid:, mid:])
    dq_late = own_lanes(dot(grads, kp[mid:]))

    grads = weigh(dot_r(stack(ve, 0, rows), we[mid:]), weights_t[:, mid:])
    dk = own_lanes(dot(grads, qp[mid:]))
    grads = weigh(dot_r(stack(ve, 0, mid), we[:mid]), weights_t[:mid, :mid])
    dk_early = own_lanes(dot(grads, qp[:mid]))

    scores = weigh(dot_r(both_heads(kp), qp[mid:]), weights_t[:, mid:])
    dv = own_lanes(dot(scores, wp[mid:]))
    scores = weigh(dot_r(both_heads(kp[:mid]), qp[:mid]), weights_t[:mid, :mid])
    dv_early = own_lanes(dot(scores, wp[:mid]))

    dq = jnp.concatenate([dq[:mid], dq[mid:] + dq_late], axis=0)
    dk = jnp.concatenate([dk[:mid] + dk_early, dk[mid:]], axis=0)
    dv = jnp.concatenate([dv[:mid] + dv_early, dv[mid:]], axis=0)

    sq_lane, upper, diag = square_masks()
    cos_b, sin_b = tcol[:, 3:4], tcol[:, 4:5]
    is_late = (scal[head_at] == 1).astype(F32)
    early = 1.0 - is_late

    def with_norms(parts, where):
        side = lambda total, norm: jnp.concatenate([total, jnp.where(where, norm, 0.0)], axis=1)
        of_cos, of_sin, norm_cos, norm_sin = parts
        return jnp.concatenate([side(of_cos, norm_cos), side(of_sin, norm_sin)], axis=0).astype(BF)

    prior_parts = unpack_state(prior, pair)
    into = dot_r(we, with_norms(prior_parts, head_lanes(pair, sq_lane, upper)))
    dq = dq + is_late * (cos_b * into[:, :LANES] + sin_b * into[:, LANES:])
    later_parts = unpack_state(later, pair)
    into = dot_r(ve, with_norms(later_parts, sq_lane == 0))
    dk = dk + early * (cos_b * into[:, :LANES] + sin_b * into[:, LANES:])
    kw = kp.astype(F32)
    left = jnp.concatenate([(kw * (cos_b * early)).astype(BF), (kw * (sin_b * early)).astype(BF)], axis=1)
    dv = dv + dot(left, jnp.concatenate(later_parts[:2], axis=0).astype(BF))

    dq = jnp.where(qp.astype(F32) > 0, dq, 0.0).astype(BF)
    dk = jnp.where(kw > 0, dk, 0.0).astype(BF)
    dv = dv.astype(BF)
    for n, part in enumerate((dq, dk, dv)):
        sums_o[n] = jnp.broadcast_to(jnp.sum(part.astype(F32), axis=0, keepdims=True), sums_o.shape[1:])
        out_o[n] = part


def input_kernel(scal, first, keep, send, w_keep, w_send, out_o):
    @pl.when(pl.program_id(0) == 0)
    def _():
        out_o[...] = first[...]

    out_o[...] += dot_r(keep[0], w_keep[...]) + dot_r(send[0], w_send[...])


def place(values, piece_rows, tz, tys, x, y, z, extra, outs):
    xk, xs, yk, ys = outs
    width = xk.shape[-1]
    slot_z = tz ^ z
    pieces = {}
    at = 0
    for ty in tys:
        for tc in range(2):
            for tx in range(2):
                part = values[at * piece_rows : (at + 1) * piece_rows]
                blocks = [part[:, n : n + width] for n in range(0, part.shape[1], width)]
                if extra is not None:
                    blocks.append(extra[at])
                pieces[ty, tc, tx] = jnp.concatenate(blocks, axis=0) if len(blocks) > 1 else blocks[0]
                at += 1
    for ty in tys:
        slot = ty ^ y
        a, b = pieces[ty, 0, 0], pieces[ty, 0, 1]
        xk[slot, slot_z] = jnp.where(x == 0, a, b).astype(BF)
        xs[slot, slot_z] = jnp.where(x == 0, b, a).astype(BF)
    return pieces


def place_y(pieces, tz, tys, x, y, z, outs):
    xk, xs, yk, ys = outs
    slot_z = tz ^ z
    for tx in range(2):
        slot = tx ^ x
        a, b = pieces[0, 1, tx], pieces[1, 1, tx]
        yk[slot, slot_z] = jnp.where(y == 0, a, b).astype(BF)
        ys[slot, slot_z] = jnp.where(y == 0, b, a).astype(BF)


def reduce_grad_kernel(pos_at, scal, a_own, a_oth, b_own, b_oth, *outs):
    tz = pl.program_id(0)
    x, y, z = (scal[pos_at + n] for n in range(3))
    values = dot_t(a_own[...], b_own[...]) + dot_t(a_oth[...], b_oth[...])
    piece_rows = values.shape[0] // 8
    pieces = place(values, piece_rows, tz, (0, 1), x, y, z, None, outs)
    place_y(pieces, tz, (0, 1), x, y, z, outs)


def expand_grad_kernel(pos_at, scal, a_own, a_oth, b_own, b_oth, m_own, m_oth, c_own, c_oth, *outs):
    tz = pl.program_id(0)
    x, y, z = (scal[pos_at + n] for n in range(3))
    an, ao = a_own[0, 0], a_oth[0, 0]
    parts = [dot(an, b_own[n]) + dot(ao, b_oth[n]) for n in range(b_own.shape[0])]
    parts.append(dot(m_own[0, 0], c_own[...]) + dot(m_oth[0, 0], c_oth[...]))
    values = jnp.concatenate(parts, axis=1)
    pieces = place(values, values.shape[0] // 8, tz, (0, 1), x, y, z, None, outs)
    place_y(pieces, tz, (0, 1), x, y, z, outs)


def share_lanes(entries, devices, at, width):
    n = entries.shape[1]
    share = n // devices
    owner = lax.broadcasted_iota(jnp.int32, (devices, n), 0)
    column = lax.broadcasted_iota(jnp.int32, (devices, n), 1)
    mine = (column >= owner * share) & (column < (owner + 1) * share)
    high, low = high_low(jnp.where(mine, entries, 0.0))
    both = jnp.concatenate([high, low], axis=0).astype(BF)
    source = lax.broadcasted_iota(jnp.int32, (n, width), 0)
    target = lax.broadcasted_iota(jnp.int32, (n, width), 1)
    picks = (target >= at) & (target < at + share) & (lax.rem(source, share) == target - at)
    spread = dot(both, picks.astype(F32).astype(BF))
    return spread[:devices] + spread[devices:]


def heads_grad_kernel(
    pos_at, scal, a_own, a_oth, b_own, b_oth, kept_h, sent_h, sums_1, kept_e, sent_e, sums_2, *refs, devices
):
    outs, table = refs[:-1], refs[-1]
    tz = pl.program_id(0)
    x, y, z = (scal[pos_at + n] for n in range(3))
    width = outs[0].shape[-1]

    @pl.when(tz == 0)
    def _():
        first_core = scal[pos_at - 1] == 0
        ordered = lambda kept, sent: [jnp.where(first_core, kept, sent), jnp.where(first_core, sent, kept)]
        sums_e = jnp.concatenate(ordered(kept_e[...], sent_e[...]), axis=1)
        of_heads = [part for n in range(3) for part in ordered(kept_h[n, 0:1], sent_h[n, 0:1])]
        total = jnp.zeros((devices, width), F32)
        at = 0
        for entries in (
            jnp.concatenate(of_heads[:4], axis=1), jnp.concatenate(of_heads[4:], axis=1), sums_1[2:3], sums_1[0:1], sums_1[1:2],
            sums_e, sums_2[2:3], sums_2[0:1], sums_2[1:2],
        ):
            total = total + share_lanes(entries, devices, at, width)
            at += entries.shape[1] // devices
        table[...] = total

    join = lambda ref: jnp.concatenate([ref[n] for n in range(ref.shape[0])], axis=1)
    values = dot(a_own[0], join(b_own)) + dot(a_oth[0], join(b_oth))
    line = lax.broadcasted_iota(jnp.int32, (8, width), 0)
    rows8 = table[pl.ds(pl.multiple_of(tz * 8, 8), 8)]
    extra = []
    for n in range(8):
        high, low = high_low(rows8[n : n + 1])
        extra.append(jnp.where(line == 0, high, jnp.where(line == 1, low, 0.0)))
    pieces = place(values, values.shape[0] // 8, tz, (0, 1), x, y, z, extra, outs)
    place_y(pieces, tz, (0, 1), x, y, z, outs)


class Ring:
    def __init__(self, n_dp):
        self.n_dp = n_dp
        self.devices = 2 * n_dp

    def swap(self, value, bits):
        return lax.ppermute(value, AXES, [(i, i ^ bits) for i in range(self.devices)])

    def core(self, value):
        return self.swap(value, 2)

    def x(self, value):
        return self.swap(value, 1)

    def y(self, value):
        return self.swap(value, 4)

    def z(self, value, step):
        return self.swap(value, 8 * step)


def add_first_kernel(scal, xk, xr, yk, yr, xn, yn):
    wide = lambda ref: ref[0].astype(F32)
    xn[...] = (wide(xk) + wide(xr)).astype(BF)
    yn[...] = (wide(yk) + wide(yr)).astype(BF)


def add_second_kernel(scal, xk, xr, xm, yk, yr, ym, own, z1, z2, z3):
    for n, (keep, got, more) in enumerate(((xk, xr, xm), (yk, yr, ym))):
        total = lambda k: keep[0, k].astype(F32) + got[0, k].astype(F32) + more[k].astype(F32)
        own[n] = total(0)
        for k, out in ((1, z1), (2, z2), (3, z3)):
            out[n] = total(k).astype(BF)


def add_last_kernel(core_at, scal, own, z1, z2, z3, keep, send):
    first = scal[core_at] == 0
    total = lambda n: own[n] + z1[n].astype(F32) + z2[n].astype(F32) + z3[n].astype(F32)
    of_first, of_second = total(0), total(1)
    keep[...] = jnp.where(first, of_first, of_second)
    send[...] = jnp.where(first, of_second, of_first)


class Scatter:
    def __init__(self, ring, core_at, name, sent):
        self.ring, self.core_at, self.name = ring, core_at, name
        self.xk, self.xs, self.yk, self.ys = sent

    def send(self, *others):
        self.xr, self.yr = self.ring.x(after(self.xs, *others)), self.ring.y(after(self.ys, *others))

    def first(self, scal, us=1):
        shape = self.xk.shape[1:]
        part = lambda a: (a, (1,) + shape, lambda j, s: (1, 0, 0, 0))
        xn, yn = call(
            add_first_kernel, self.name + "_add1", scal, (1,), [part(a) for a in (self.xk, self.xr, self.yk, self.yr)],
            [(shape, BF, None, None)] * 2, us=us,
        )
        self.xn, self.yn = xn, yn
        return xn

    def send_first(self, *others):
        self.xm, self.ym = self.ring.y(after(self.xn, *others)), self.ring.x(after(self.yn, *others))

    def second(self, scal):
        shape = self.xk.shape[1:]
        piece = (2,) + shape[1:]
        part = lambda a: (a, (1,) + shape, lambda j, s: (0, 0, 0, 0))
        whole = lambda a: (a, None, None)
        self.own, *self.sends = call(
            add_second_kernel, self.name + "_add2", scal, (1,),
            [part(self.xk), part(self.xr), whole(self.xm), part(self.yk), part(self.yr), whole(self.ym)],
            [(piece, F32, None, None)] + [(piece, BF, None, None)] * 3,
        )
        return self.own

    def send_second(self, *others):
        self.arrived = [self.ring.z(after(v, *others), k + 1) for k, v in enumerate(self.sends)]

    def last(self, scal):
        piece = self.own.shape[1:]
        keep, send = call(
            functools.partial(add_last_kernel, self.core_at), self.name + "_add3", scal, (1,),
            [(a, None, None) for a in (self.own, *self.arrived)], [(piece, F32, None, None)] * 2,
        )
        return keep, self.ring.core(send)


def after(value, *others):
    if not others:
        return value
    return lax.optimization_barrier((value,) + others)[0]


def side_by_side(core_at, scal, own, got):
    first = scal[core_at] == 0
    return [jnp.where(first, own, got), jnp.where(first, got, own)]


def finish_first_kernel(core_at, scal, reduce_own, reduce_got, expand_own, expand_got, reduce_o, expand_o, merge_o):
    width = reduce_own.shape[1]
    for n, part in enumerate(side_by_side(core_at, scal, reduce_own[...], reduce_got[...])):
        reduce_o[:, n * width : (n + 1) * width] = part
    rows = merge_o.shape[0]
    blocks = expand_own.shape[0] // rows - 1
    for n, part in enumerate(side_by_side(core_at, scal, expand_own[...], expand_got[...])):
        for k in range(blocks):
            at = (n * blocks + k) * width
            expand_o[:, at : at + width] = part[k * rows : (k + 1) * rows]
        merge_o[:, n * width : (n + 1) * width] = part[blocks * rows :]


def finish_last_kernel(core_at, scal, own, got, heads_o, *shares_o):
    width = own.shape[1]
    rows = heads_o.shape[0]
    for n, part in enumerate(side_by_side(core_at, scal, own[...], got[...])):
        for k in range(3):
            at = (2 * k + n) * width
            heads_o[:, at : at + width] = part[k * rows : (k + 1) * rows]
    entries = own[3 * rows :] + got[3 * rows :]
    entries = entries[0:1] + entries[1:2]
    at = 0
    for share in shares_o:
        n = share.shape[1]
        moved = entries if at == 0 else pltpu.roll(entries, width - at, 1)
        share[...] = moved[:, :n]
        at += n


def per_device(
    tokens, w_heads, b_heads, w_merge, b_merge, gain_first, bias_first, w_expand, b_expand,
    w_reduce, b_reduce, gain_second, bias_second, seq_lengths, cotangent,
):
    rows = tokens.shape[0]
    seqs = seq_lengths.shape[1]
    n_dp = lax.axis_size("dp")
    ring = Ring(n_dp)
    head = lax.axis_index("head")
    dp = lax.axis_index("dp")
    core = dp % 2
    place_of = jnp.stack([head, core, head, (dp // 2) % 2, dp // 4]).astype(jnp.int32)
    scal = jnp.concatenate([seq_lengths[0].astype(jnp.int32), place_of])
    head_at, core_at, pos_at = seqs, seqs + 1, seqs + 2
    first_core = core == 0
    line = lambda v: v.reshape(1, -1)
    b_heads, b_merge, gain_first, bias_first, b_expand, b_reduce, gain_second, bias_second = map(
        line, (b_heads, b_merge, gain_first, bias_first, b_expand, b_reduce, gain_second, bias_second)
    )
    wide_shape = (rows, D)
    quarter = 256

    turned = ((4, D // 4, rows), BF, None, None)
    rk, v, state, tcol, trow, tokens_t = call(
        functools.partial(kv_kernel, seqs), "keys_values", scal, (3,),
        [
            (tokens, None, None),
            (w_heads, (D, quarter), lambda j, s: (0, 3 + j)),
            (w_heads, (D, quarter), lambda j, s: (0, 6 + j)),
            (b_heads, (1, quarter), lambda j, s: (0, 3 + j)),
            (b_heads, (1, quarter), lambda j, s: (0, 6 + j)),
        ],
        [
            (wide_shape, BF, (rows, quarter), lambda j, s: (0, j)),
            (wide_shape, BF, (rows, quarter), lambda j, s: (0, j)),
            ((PAIRS + 1, LANES, LANES), BF, None, None),
            ((rows, LANES), F32, None, None),
            ((8, rows), F32, None, None), turned,
        ],
        [pltpu.VMEM((LANES, LANES), F32)],
        us=4,
    )
    prior = ring.x(state)

    fast = n_dp == 16
    order = scal
    if fast:
        tokens_o = ring.core(tokens_t)
    rq, num, den = call(
        local_kernel, "local_attention", scal, (3,),
        [
            (tokens, None, None),
            (w_heads, (D, quarter), lambda j, s: (0, j)),
            (b_heads, (1, quarter), lambda j, s: (0, j)),
            (rk, (rows, quarter), lambda j, s: (0, j)),
            (v, (rows, quarter), lambda j, s: (0, j)),
            (tcol, None, None),
            (trow, None, None),
        ],
        [
            (wide_shape, BF, (rows, quarter), lambda j, s: (0, j)),
            (wide_shape, F32, (rows, quarter), lambda j, s: (0, j)),
            (wide_shape, F32, (rows, quarter), lambda j, s: (0, j)),
        ],
        [pltpu.VMEM((rows, rows), F32)],
        us=6,
    )

    if fast:
        order = after(scal, tokens_o)
    att, inv, mixed, xhat, scale, normed, second, turned_own, act, slope = call(
        functools.partial(ffn_kernel, head_at), "feed_forward", order, (FF_STEPS,),
        [
            (rq, None, None), (num, None, None), (den, None, None), (prior, None, None),
            (tcol, None, None), (tokens, None, None), (w_merge, None, None), (b_merge, None, None),
            (gain_first, None, None), (bias_first, None, None), (b_reduce, None, None),
            (w_expand, (D, FF_BLOCK), lambda j, s: (0, j)),
            (b_expand, (1, FF_BLOCK), lambda j, s: (0, j)),
            (w_reduce, (FF_BLOCK, D), lambda j, s: (j, 0)),
        ],
        [
            (wide_shape, F32, None, None), (wide_shape, F32, None, None), (wide_shape, BF, None, None),
            (wide_shape, F32, None, None), ((rows, LANES), F32, None, None), (wide_shape, BF, None, None),
            (wide_shape, F32, None, None), ((2, 4, D // 4, rows), BF, None, None),
            ((rows, FF), BF, (rows, FF_BLOCK), lambda j, s: (0, j)),
            ((rows, FF), BF, (rows, FF_BLOCK), lambda j, s: (0, j)),
        ],
        us=11, vmem=VMEM_FFN,
    )

    half_shape = (rows, D // 2)
    result, grad_second, branch, bg_keep, bg_send, sums_second = call(
        functools.partial(second_kernel, core_at), "second_norm", scal, (1,),
        [(second, None, None), (cotangent, None, None), (gain_second, None, None), (bias_second, None, None)],
        [
            (wide_shape, BF, None, None), (wide_shape, F32, None, None), (wide_shape, BF, None, None),
            (half_shape, BF, None, None), (half_shape, BF, None, None), ((8, D), F32, None, None),
        ],
        us=2.6,
    )

    devices = ring.devices
    small, large = D // devices, FF // devices
    whole = lambda a: (a, None, None)
    part = lambda a, n: (a, (1, 1, D // 4, rows), lambda j, s: (n, j, 0, 0))
    by_z = lambda a: (a, (1, D // 4, rows), lambda j, s: (j, 0, 0))
    by_col = lambda a: (a, (rows, FF // 4), lambda j, s: (0, j))

    def group(kernel, name, scal, ins, piece_rows, us, scratch=()):
        shape = (2, 4, piece_rows, D // 2)
        sent = call(
            functools.partial(kernel, pos_at), name, scal, (4,), ins, [(shape, BF, None, None)] * 4, scratch, us
        )
        return Scatter(ring, core_at, name, sent)

    ff_half = FF_STEPS // 2
    in_hbm = lambda a: (a, None, pltpu.HBM)
    hidden = ((ff_half, rows, FF_BLOCK), BF, None, None)
    hidden_sums = ((1, FF // 2), F32, None, None)
    buffers = [
        pltpu.VMEM((ff_half, D, FF_BLOCK), BF), pltpu.VMEM((ff_half, FF_BLOCK, D), BF),
        pltpu.SemaphoreType.DMA((2, ff_half)),
    ]
    hidden_in = [whole(branch), whole(slope), in_hbm(w_expand), in_hbm(w_reduce)]
    pg_send, sum_sent, partial = call(
        functools.partial(back_sent_kernel, core_at), "feed_forward_back_sent", scal, (),
        [*hidden_in, whole(grad_second)],
        [hidden, hidden_sums, (wide_shape, F32, None, None)], buffers,
        us=5, vmem=VMEM_BACK,
    )
    order = scal
    if fast:
        pg_o = ring.core(pg_send)
        act_o, turned_other, bg_o = map(ring.core, (act, turned_own, bg_send))
        reduced = group(
            reduce_grad_kernel, "grad_reduce", after(scal, partial, turned_other),
            [by_col(act), by_col(act_o), whole(bg_keep), whole(bg_o)], large, 6,
        )
        order = after(scal, reduced.xs)
        reduced.send()

    pg_keep, grad_first, mg_keep, mg_send, w_att, e_att, later, sum_kept, sums_first = call(
        functools.partial(back_kernel, core_at), "feed_forward_back", order, (),
        [
            *hidden_in,
            (partial, None, None), (gain_first, None, None), (xhat, None, None), (scale, None, None),
            (w_merge, None, None), (att, None, None), (inv, None, None), (rq, None, None), (tcol, None, None),
        ],
        [
            hidden, (wide_shape, F32, None, None), (half_shape, BF, None, None), (half_shape, BF, None, None),
            (wide_shape, BF, None, None), ((rows, LANES), BF, None, None),
            ((PAIRS + 1, LANES, LANES), BF, None, None), hidden_sums, ((8, D), F32, None, None),
        ],
        [pltpu.VMEM(wide_shape, F32), *buffers],
        us=9, vmem=VMEM_BACK,
    )
    later = ring.x(later)

    if fast:
        mg_o = ring.core(mg_send)
        expanded = group(
            expand_grad_kernel, "grad_expand", scal,
            [
                part(turned_own, 1), part(turned_other, 1), whole(pg_keep), whole(pg_o),
                part(turned_own, 0), part(turned_other, 0), whole(mg_keep), whole(mg_o),
            ],
            5 * small, COST_EXPAND,
        )
        order = after(scal, reduced.first(after(scal, expanded.xs, later)))
        reduced.send_first()

    half_pairs = PAIRS // 2
    pair_blocks = lambda core_of: [
        (a, (rows, LANES), lambda j, s: (0, core_of(s) * half_pairs + j)) for a in (rq, rk, v, w_att)
    ]
    both_states = [whole(e_att), whole(prior), whole(later), whole(tcol)]
    pj_out = ((3, rows, D // 2), BF, (3, rows, LANES), lambda j, s: (0, 0, j))
    pj_sums = ((3, 8, D // 2), F32, (3, 8, LANES), lambda j, s: (0, 0, j))
    table = ((rows, rows), F32, None, None)
    pj_send, sum_heads_sent, weights, weights_t = call(
        functools.partial(attn_sent_kernel, head_at, core_at), "attention_back_sent", order, (half_pairs,),
        [*pair_blocks(lambda s: 1 - s[core_at]), *both_states, whole(trow)], [pj_out, pj_sums, table, table], us=COST_SENT,
    )
    order = scal
    if fast:
        pj_o = ring.core(pj_send)
        order = after(scal, reduced.second(after(scal, pj_send)))
        expanded.send()
    pj_keep, sum_heads_kept = call(
        functools.partial(attn_kept_kernel, head_at, core_at), "attention_back_kept", order, (half_pairs,),
        [*pair_blocks(lambda s: s[core_at]), *both_states, whole(weights), whole(weights_t)], [pj_out, pj_sums], us=COST_KEPT,
    )

    if fast:
        order = after(scal, expanded.first(after(scal, pj_keep), us=20))
        expanded.send_first(pj_o)
        reduced.send_second()
        heads = group(
            functools.partial(heads_grad_kernel, devices=devices), "grad_heads", order,
            [
                by_z(tokens_t), by_z(tokens_o), whole(pj_keep), whole(pj_o),
                *map(whole, (sum_heads_kept, sum_heads_sent, sums_first, sum_kept, sum_sent, sums_second)),
            ],
            3 * small + 8, COST_HEADS, [pltpu.VMEM((devices, D // 2), F32)],
        )
        heads.send(expanded.xm, expanded.ym)
        order = after(scal, heads.xs)

    of_part = lambda a: (a, (1, rows, D // 2), lambda j, s: (j, 0, 0))
    (input_grad,) = call(
        input_kernel, "input_grad", order, (3,),
        [
            whole(grad_first), of_part(pj_keep), of_part(pj_send),
            (w_heads, (D, D // 2), lambda j, s: (0, 2 * j + s[core_at])),
            (w_heads, (D, D // 2), lambda j, s: (0, 2 * j + 1 - s[core_at])),
        ],
        [(wide_shape, F32, None, None)],
        us=COST_INPUT,
    )

    if fast:
        reduce_own, reduce_got = reduced.last(after(scal, input_grad))
        order = expanded.second(after(scal, reduce_own))
        expanded.send_second()
        order = heads.first(after(scal, order))
        heads.send_first()
        order = heads.second(after(scal, order))
        heads.send_second()
        expand_own, expand_got = expanded.last(after(scal, order))
        heads_own, heads_got = heads.last(after(scal, expand_own))
        out = lambda n, m: ((n, m), F32, None, None)
        w_reduce_grad, w_expand_grad, w_merge_grad = call(
            functools.partial(finish_first_kernel, core_at), "finish_first", after(scal, heads_own), (),
            [*map(whole, (reduce_own, reduce_got, expand_own, expand_got))],
            [out(large, D), out(small, FF), out(small, D)],
        )
        counts = (2 * small, small, small, small, small, large, small, small, small)
        w_heads_grad, *shares = call(
            functools.partial(finish_last_kernel, core_at), "finish_last", scal, (),
            [whole(heads_own), whole(heads_got)], [out(small, 3 * D), *(out(1, n) for n in counts)],
        )
        shares = [share.reshape(-1) for share in shares]
        grads = (
            w_heads_grad, *shares[:2], w_merge_grad, *shares[2:5], w_expand_grad, shares[5], w_reduce_grad,
            *shares[6:],
        )
    else:
        by_core = lambda keep, send: jnp.concatenate(
            [jnp.where(first_core, keep, send), jnp.where(first_core, send, keep)], axis=1
        )
        flat = lambda v: v.transpose(1, 0, 2).reshape(rows, -1)
        by_heads = lambda keep, send: jnp.concatenate(
            [by_core(keep[n], send[n]) for n in range(3)], axis=1
        )
        sum_heads = by_heads(sum_heads_kept, sum_heads_sent)[0]
        scatter = lambda v: lax.psum_scatter(v, AXES, scatter_dimension=0, tiled=True)
        grads = (
            scatter(dot_t(tokens, by_heads(pj_keep, pj_send))),
            scatter(sum_heads[: 2 * D]), scatter(sum_heads[2 * D :]),
            scatter(dot_t(mixed, by_core(mg_keep, mg_send))),
            scatter(sums_first[2]), scatter(sums_first[0]), scatter(sums_first[1]),
            scatter(dot_t(normed, by_core(flat(pg_keep), flat(pg_send)))),
            scatter(by_core(sum_kept, sum_sent)[0]),
            scatter(dot_t(act, branch)),
            scatter(sums_second[2]), scatter(sums_second[0]), scatter(sums_second[1]),
        )
    return (result, input_grad) + tuple(grads)


def solution(mesh):
    in_specs = (P(AXES, None),) + (P(),) * 12 + (P("dp", None), P(AXES, None))
    row, one = P(AXES, None), P(AXES)
    out_specs = (row, row, row, one, one, row, one, one, one, row, one, row, one, one, one)
    return jax.shard_map(
        per_device, mesh=mesh, in_specs=in_specs, out_specs=out_specs, check_vma=False
    )
```

```python
import functools
import math

import jax
import jax.numpy as jnp
from jax import lax
from jax.experimental import pallas as pl
from jax.experimental.pallas import tpu as pltpu
from jax.sharding import PartitionSpec as P

D = 768
PAIRS = 6
FF = 3072
LANES = 128
HALF = 64
BF = jnp.bfloat16
F32 = jnp.float32
AXES = ("dp", "head")
VMEM_LIMIT = 8 << 20
VMEM_FFN = 16 << 20
FF_BLOCK = 768
FFN_BLOCK = 1024
FFN_STEPS = FF // FFN_BLOCK
MATMUL_PER_US = 1.15e9
COST_EXPAND = 1
VMEM_BACK = 16 << 20
COST_KEPT = 0.5
COST_BACK = 3
COST_SENT = 0.5
COST_HEADS = 0.1
COST_INPUT = 0.1
FF_STEPS = FF // FF_BLOCK


def dot(a, b):
    return jnp.dot(a, b, preferred_element_type=F32)


def dot_t(a, b):
    return lax.dot_general(a, b, (((0,), (0,)), ((), ())), preferred_element_type=F32)


def dot_r(a, b):
    return lax.dot_general(a, b, (((1,), (1,)), ((), ())), preferred_element_type=F32)


def call(kernel, name, scal, grid, ins, outs, scratch=(), us=0.1, vmem=VMEM_LIMIT):
    def spec(b, m):
        if b is None:
            return pl.BlockSpec(memory_space=pltpu.VMEM if m is None else m)
        return pl.BlockSpec(b, m)

    in_specs = [spec(b, m) for _, b, m in ins]
    out_specs = [spec(b, m) for _, _, b, m in outs]
    return pl.pallas_call(
        kernel,
        name=name,
        grid_spec=pltpu.PrefetchScalarGridSpec(
            num_scalar_prefetch=1,
            grid=grid,
            in_specs=in_specs,
            out_specs=out_specs,
            scratch_shapes=list(scratch),
        ),
        out_shape=[jax.ShapeDtypeStruct(s, d) for s, d, _, _ in outs],
        compiler_params=pltpu.CompilerParams(vmem_limit_bytes=vmem),
        cost_estimate=pl.CostEstimate(flops=int(us * MATMUL_PER_US), bytes_accessed=1, transcendentals=0),
    )(scal, *[a for a, _, _ in ins])


def lane_masks():
    lane = lax.broadcasted_iota(jnp.int32, (1, LANES), 1)
    even = (lane < HALF).astype(F32)
    return lane, even.astype(BF), (1.0 - even).astype(BF)


def both_heads(pair):
    lane, even, odd = lane_masks()
    return jnp.concatenate([pair * even, pair * odd], axis=0)


def own_lanes(stacked):
    rows = stacked.shape[0] // 2
    lane = lax.broadcasted_iota(jnp.int32, (1, LANES), 1)
    return jnp.where(lane < HALF, stacked[:rows], stacked[rows:])


def square_masks():
    row = lax.broadcasted_iota(jnp.int32, (LANES, LANES), 0)
    lane = lax.broadcasted_iota(jnp.int32, (LANES, LANES), 1)
    upper = row < HALF
    return lane, upper, upper == (lane < HALF)


def high_low(v):
    high = v.astype(BF).astype(F32)
    return high, v - high


def tables(scal, rows, seqs, tcol, trow):
    pos = lax.broadcasted_iota(jnp.int32, (1, rows), 1) + scal[seqs] * rows
    seg = jnp.zeros((1, rows), jnp.int32)
    first = jnp.zeros((1, rows), jnp.int32)
    length = jnp.ones((1, rows), jnp.int32)
    at_boundary = jnp.int32(0)
    begin = jnp.int32(0)
    for s in range(seqs):
        end = begin + scal[s]
        inside = (pos >= begin) & (pos < end)
        first = jnp.where(inside, begin, first)
        length = jnp.where(inside, jnp.maximum(scal[s], 1), length)
        seg = seg + (pos >= end).astype(jnp.int32)
        at_boundary = at_boundary + (rows - 1 >= end).astype(jnp.int32)
        begin = end
    live = (seg < seqs).astype(F32)
    angle = 0.5 * math.pi * (pos - first).astype(F32) / length.astype(F32)
    cos_w = jnp.cos(angle) * live
    sin_w = jnp.sin(angle) * live
    crossing = (seg == at_boundary).astype(F32)
    which = lax.broadcasted_iota(jnp.int32, (LANES, rows), 0)
    table = jnp.zeros((LANES, rows), F32)
    for n, entry in enumerate((cos_w, sin_w, seg.astype(F32), cos_w * crossing, sin_w * crossing)):
        table = jnp.where(which == n, entry, table)
    trow[...] = table[:8]
    tcol[...] = table.T


def pack_state(both, norm_cos, norm_sin, pair, norms):
    lane, upper, diag = square_masks()
    packed = jnp.where(diag, both[:LANES, :LANES], pltpu.roll(both[LANES:, :LANES], HALF, 1))
    cos_high, cos_low = high_low(norm_cos)
    sin_high, sin_low = high_low(norm_sin)
    for n, part in enumerate((cos_high, cos_low, sin_high, sin_low)):
        norms = jnp.where(lane == 4 * pair + n, part, norms)
    return packed.astype(BF), norms


def unpack_state(state_ref, pair):
    lane, upper, diag = square_masks()
    packed = state_ref[pair].astype(F32)
    norms = state_ref[PAIRS].astype(F32)
    of_cos = jnp.where(diag, packed, 0.0)
    of_sin = jnp.where(diag, pltpu.roll(packed, HALF, 1), 0.0)
    pick = lambda n: jnp.sum(
        jnp.where((lane == 4 * pair + n) | (lane == 4 * pair + n + 1), norms, 0.0), axis=1, keepdims=True
    )
    return of_cos, of_sin, pick(0), pick(2)


def turn(value, out):
    turned = value.T
    share = out.shape[1]
    for n in range(out.shape[0]):
        out[n] = turned[n * share : (n + 1) * share]


def kv_kernel(seqs, scal, tok, wk, wv, bk, bv, rk_o, v_o, st_o, tcol, trow, turned_o, norms):
    step = pl.program_id(0)
    rows = tok.shape[0]

    @pl.when(step == 0)
    def _():
        tables(scal, rows, seqs, tcol, trow)
        norms[...] = jnp.zeros_like(norms)
        turn(tok[...], turned_o)

    rk = jnp.maximum(dot(tok[...], wk[...]) + bk[...].astype(F32), 0.0).astype(BF)
    v = (dot(tok[...], wv[...]) + bv[...].astype(F32)).astype(BF)
    rk_o[...] = rk
    v_o[...] = v
    cos_b, sin_b = tcol[:, 3:4], tcol[:, 4:5]
    ones = jnp.ones((rows, LANES), BF)
    for n in range(2):
        pair = 2 * step + n
        cols = slice(n * LANES, (n + 1) * LANES)
        kp = rk[:, cols].astype(F32)
        left = jnp.concatenate([(kp * cos_b).astype(BF), (kp * sin_b).astype(BF)], axis=1)
        both = dot_t(left, jnp.concatenate([v[:, cols], ones], axis=1))
        packed, new_norms = pack_state(both, both[:LANES, LANES:], both[LANES:, LANES:], pair, norms[...])
        st_o[pair] = packed
        norms[...] = new_norms

    st_o[PAIRS] = norms[...].astype(BF)


def weights_block(tcol, trow, transposed):
    rows = tcol.shape[0]
    down = lax.broadcasted_iota(jnp.int32, (rows, rows), 0)
    along = lax.broadcasted_iota(jnp.int32, (rows, rows), 1)
    same = tcol[:, 2:3] == trow[2:3, :]
    causal = (down <= along) if transposed else (along <= down)
    value = tcol[:, 0:1] * trow[0:1, :] + tcol[:, 1:2] * trow[1:2, :]
    return jnp.where(same & causal, value, 0.0)


def weigh(stacked, weights):
    rows = weights.shape[0]
    return jnp.concatenate([stacked[:rows] * weights, stacked[rows:] * weights], axis=0).astype(BF)


def local_kernel(scal, tok, wq, bq, rk, v, tcol, trow, rq_o, num_o, den_o, weights):
    step = pl.program_id(0)
    rows = tok.shape[0]
    mid = rows // 2

    @pl.when(step == 0)
    def _():
        weights[...] = weights_block(tcol, trow, False)

    rq = jnp.maximum(dot(tok[...], wq[...]) + bq[...].astype(F32), 0.0).astype(BF)
    rq_o[...] = rq
    ones = jnp.ones((rows, LANES), BF)
    for n in range(2):
        cols = slice(n * LANES, (n + 1) * LANES)
        kp = rk[:, cols]
        values = jnp.concatenate([v[:, cols], ones], axis=1)
        first = weigh(dot_r(both_heads(rq[:, cols]), kp[:mid]), weights[:, :mid])
        second = weigh(dot_r(both_heads(rq[mid:, cols]), kp[mid:]), weights[mid:, mid:])
        sums = dot(first, values[:mid])
        late = dot(second, values[mid:])
        for own, out in ((slice(0, LANES), num_o), (slice(LANES, 2 * LANES), den_o)):
            total = own_lanes(sums[:, own])
            out[:mid, cols] = total[:mid]
            out[mid:, cols] = total[mid:] + own_lanes(late[:, own])


def normalise(entries):
    mean = jnp.mean(entries, axis=1, keepdims=True)
    centred = entries - mean
    var = jnp.mean(centred * centred, axis=1, keepdims=True)
    scale = lax.rsqrt(var + 1e-05)
    return centred * scale, scale


def merge_heads(
    head_at, scal, rq, num, den, st, tcol, tok, w_merge, b_merge, gain, bias, b_red,
    att_o, inv_o, mixed_o, xhat_o, scale_o, normed_o, acc_o, turned_o,
):
    cross = (scal[head_at] == 1).astype(F32)
    cos_b, sin_b = tcol[:, 3:4] * cross, tcol[:, 4:5] * cross
    sq_lane, upper, diag = square_masks()
    for pair in range(PAIRS):
        cols = slice(pair * LANES, (pair + 1) * LANES)
        qp = rq[:, cols].astype(F32)
        of_cos, of_sin, norm_cos, norm_sin = unpack_state(st, pair)
        top = jnp.concatenate([of_cos, jnp.where(diag, norm_cos, 0.0)], axis=1)
        low = jnp.concatenate([of_sin, jnp.where(diag, norm_sin, 0.0)], axis=1)
        right = jnp.concatenate([top, low], axis=0).astype(BF)
        left = jnp.concatenate([(qp * cos_b).astype(BF), (qp * sin_b).astype(BF)], axis=1)
        prior = dot(left, right)
        inverse = 1.0 / (den[:, cols] + prior[:, LANES:] + 1.0)
        attended = (num[:, cols] + prior[:, :LANES]) * inverse
        att_o[:, cols] = attended
        inv_o[:, cols] = inverse
        mixed_o[:, cols] = attended.astype(BF)
    first_in = tok[...].astype(F32) + dot(mixed_o[...], w_merge[...]) + b_merge[...].astype(F32)
    xhat, scale = normalise(first_in)
    normed = xhat * gain[...].astype(F32) + bias[...].astype(F32)
    xhat_o[...] = xhat
    scale_o[...] = jnp.broadcast_to(scale, scale_o.shape)
    normed_o[...] = normed.astype(BF)
    acc_o[...] = normed + b_red[...].astype(F32)
    turn(mixed_o[...], turned_o.at[0])
    turn(normed_o[...], turned_o.at[1])


def expand_reduce(normed, w_exp, b_exp, w_red, act_o, slope_o, acc_o):
    rows = normed.shape[0]
    pre = [dot(normed[at : at + rows // 2], w_exp[...]) + b_exp[...].astype(F32) for at in (0, rows // 2)]
    for at, x in zip((0, rows // 2), pre):
        part = slice(at, at + rows // 2)
        cdf = 0.5 + 0.5 * lax.erf(x * (2.0**-0.5))
        pdf = jnp.exp(-0.5 * x * x) * (1.0 / math.sqrt(2.0 * math.pi))
        act = (x * cdf).astype(BF)
        act_o[part] = act
        slope_o[part] = (cdf + x * pdf).astype(BF)
        acc_o[part] += dot(act, w_red[...])


def ffn_kernel(head_at, scal, *refs):
    w_exp, b_exp, w_red = refs[11:14]
    normed_o, acc_o = refs[19:21]
    act_o, slope_o = refs[22:]

    @pl.when(pl.program_id(0) == 0)
    def _():
        merge_heads(head_at, scal, *refs[:11], *refs[14:22])

    expand_reduce(normed_o, w_exp, b_exp, w_red, act_o, slope_o, acc_o)


def second_kernel(core_at, scal, second, cot, gain, bias, out_o, grad_o, full_o, keep_o, send_o, sums_o):
    xhat, scale = normalise(second[...])
    gain_w = gain[...].astype(F32)
    out_o[...] = (xhat * gain_w + bias[...].astype(F32)).astype(BF)
    cot_w = cot[...].astype(F32)
    t = cot_w * gain_w
    grad = scale * (
        t - jnp.mean(t, axis=1, keepdims=True) - xhat * jnp.mean(t * xhat, axis=1, keepdims=True)
    )
    low = grad.astype(BF)
    grad_o[...] = grad
    full_o[...] = low
    first = scal[core_at] == 0
    half = D // 2
    left, right = grad[:, :half], grad[:, half:]
    keep_o[...] = jnp.where(first, left, right).astype(BF)
    send_o[...] = jnp.where(first, right, left).astype(BF)
    sums_o[0:1] = jnp.sum(cot_w * xhat, axis=0, keepdims=True)
    sums_o[1:2] = jnp.sum(cot_w, axis=0, keepdims=True)
    sums_o[2:3] = jnp.sum(low.astype(F32), axis=0, keepdims=True)


def head_lanes(pair, lane, first):
    at = 4 * pair + jnp.where(first, 0, 2)
    return (lane == at) | (lane == at + 1)


def weight_copies(half, w_exp, w_red, exp_buf, red_buf, sems, n):
    at = pl.ds(pl.multiple_of((half * exp_buf.shape[0] + n) * FF_BLOCK, FF_BLOCK), FF_BLOCK)
    return (
        pltpu.make_async_copy(w_red.at[at, :], red_buf.at[n], sems.at[0, n]),
        pltpu.make_async_copy(w_exp.at[:, at], exp_buf.at[n], sems.at[1, n]),
    )


def back_steps(half, full, slope, w_exp, w_red, out_o, bexp_o, exp_buf, red_buf, sems):
    blocks = exp_buf.shape[0]
    copies = [weight_copies(half, w_exp, w_red, exp_buf, red_buf, sems, n) for n in range(blocks)]
    for pair in copies:
        for copy in pair:
            copy.start()
    total = None
    for n, (of_red, of_exp) in enumerate(copies):
        cols = slice(n * FF_BLOCK, (n + 1) * FF_BLOCK)
        at = pl.ds(pl.multiple_of((half * blocks + n) * FF_BLOCK, FF_BLOCK), FF_BLOCK)
        of_red.wait()
        pre_grad = (dot_r(full[...], red_buf[n]) * slope[:, at].astype(F32)).astype(BF)
        bexp_o[:, cols] = jnp.sum(pre_grad.astype(F32), axis=0, keepdims=True)
        out_o[n] = pre_grad
        of_exp.wait()
        part = dot_r(pre_grad, exp_buf[n])
        total = part if total is None else total + part
    return total


def back_sent_kernel(core_at, scal, full, slope, w_exp, w_red, grad2, sent_o, bexp_o, acc, exp_buf, red_buf, sems):
    half = 1 - scal[core_at]
    acc[...] = grad2[...] + back_steps(half, full, slope, w_exp, w_red, sent_o, bexp_o, exp_buf, red_buf, sems)


def back_kernel(
    core_at, scal, full, slope, w_exp, w_red, acc_in, gain, xhat, scale, w_merge, att, inv, rq, tcol,
    kept_o, first_o, mk_o, ms_o, w_o, e_o, st_o, bexp_o, sums_o,
    acc, exp_buf, red_buf, sems,
):
    half = scal[core_at]
    acc[...] = acc_in[...] + back_steps(half, full, slope, w_exp, w_red, kept_o, bexp_o, exp_buf, red_buf, sems)
    back_rest(
        core_at, scal, acc, gain, xhat, scale, w_merge, att, inv, rq, tcol,
        first_o, mk_o, ms_o, w_o, e_o, st_o, sums_o,
    )


def back_rest(
    core_at, scal, acc, gain, xhat, scale, w_merge, att, inv, rq, tcol,
    first_o, mk_o, ms_o, w_o, e_o, st_o, sums_o,
):
    grad_normed = acc[...]
    xh = xhat[...]
    t = grad_normed * gain[...].astype(F32)
    first = scale[:, 0:1] * (
        t - jnp.mean(t, axis=1, keepdims=True) - xh * jnp.mean(t * xh, axis=1, keepdims=True)
    )
    low = first.astype(BF)
    first_o[...] = first
    sums_o[0:1] = jnp.sum(grad_normed * xh, axis=0, keepdims=True)
    sums_o[1:2] = jnp.sum(grad_normed, axis=0, keepdims=True)
    sums_o[2:3] = jnp.sum(low.astype(F32), axis=0, keepdims=True)
    is_first = scal[core_at] == 0
    left, right = first[:, : D // 2], first[:, D // 2 :]
    mk_o[...] = jnp.where(is_first, left, right).astype(BF)
    ms_o[...] = jnp.where(is_first, right, left).astype(BF)
    cos_b, sin_b = tcol[:, 3:4], tcol[:, 4:5]
    w = (dot_r(low, w_merge[...]).astype(BF).astype(F32) * inv[...]).astype(BF)
    w_o[...] = w
    high, rest = high_low(w.astype(F32) * att[...])
    column = lax.broadcasted_iota(jnp.int32, (D, LANES), 0)
    target = lax.broadcasted_iota(jnp.int32, (D, LANES), 1)
    picks = (target == 2 * (column // HALF)).astype(F32).astype(BF)
    e_high, e_low = high_low(-(dot(high.astype(BF), picks) + dot(rest.astype(BF), picks)))
    e = (e_high + pltpu.roll(e_low, 1, 1)).astype(BF)
    e_o[...] = e
    norms = jnp.zeros((LANES, LANES), F32)
    sq_lane, upper, diag = square_masks()
    for pair in range(PAIRS):
        cols = slice(pair * LANES, (pair + 1) * LANES)
        qp = rq[:, cols].astype(F32)
        left = jnp.concatenate([(qp * cos_b).astype(BF), (qp * sin_b).astype(BF)], axis=1)
        both = dot_t(left, jnp.concatenate([w[:, cols], e], axis=1))
        mine = head_lanes(pair, sq_lane, upper)
        norm = lambda part: jnp.sum(jnp.where(mine, part, 0.0), axis=1, keepdims=True)
        packed, norms = pack_state(both, norm(both[:LANES, LANES:]), norm(both[LANES:, LANES:]), pair, norms)
        st_o[pair] = packed
    st_o[PAIRS] = norms.astype(BF)


def attn_sent_kernel(head_at, core_at, scal, rq, rk, v, w, e, prior, later, tcol, trow, early_o, late_o, sums_o, weights, weights_t):
    @pl.when(pl.program_id(0) == 0)
    def _():
        weights[...] = weights_block(tcol, trow, False)
        weights_t[...] = weights_block(tcol, trow, True)

    first = (1 - scal[core_at]) * pl.num_programs(0)
    attn_back(head_at, first, scal, rq, rk, v, w, e, prior, later, tcol, weights, weights_t, early_o, late_o, sums_o)


def attn_kept_kernel(head_at, core_at, scal, rq, rk, v, w, e, prior, later, tcol, weights, weights_t, early_o, late_o, sums_o):
    first = scal[core_at] * pl.num_programs(0)
    attn_back(head_at, first, scal, rq, rk, v, w, e, prior, later, tcol, weights, weights_t, early_o, late_o, sums_o)


def attn_back(head_at, first, scal, rq, rk, v, w, e, prior, later, tcol, weights, weights_t, early_o, late_o, sums_o):
    pair = first + pl.program_id(0)
    rows = rq.shape[0]
    mid = rows // 2

    qp, kp, vp, wp = rq[...], rk[...], v[...], w[...]
    lane, even, odd = lane_masks()
    of_even = ((lane == 4 * pair) | (lane == 4 * pair + 1)).astype(F32).astype(BF)
    of_odd = ((lane == 4 * pair + 2) | (lane == 4 * pair + 3)).astype(F32).astype(BF)
    ones = jnp.ones((rows, LANES), BF)
    we = jnp.concatenate([wp, e[...]], axis=1)
    by_head = (jnp.concatenate([even, of_even], axis=1), jnp.concatenate([odd, of_odd], axis=1))
    ve = jnp.concatenate([vp, ones], axis=1)
    stack = lambda a, lo, hi: jnp.concatenate([a[lo:hi] * m for m in by_head], axis=0)

    grads = weigh(dot_r(stack(we, 0, rows), ve[:mid]), weights[:, :mid])
    dq = own_lanes(dot(grads, kp[:mid]))
    grads = weigh(dot_r(stack(we, mid, rows), ve[mid:]), weights[mid:, mid:])
    dq_late = own_lanes(dot(grads, kp[mid:]))

    grads = weigh(dot_r(stack(ve, 0, rows), we[mid:]), weights_t[:, mid:])
    dk = own_lanes(dot(grads, qp[mid:]))
    grads = weigh(dot_r(stack(ve, 0, mid), we[:mid]), weights_t[:mid, :mid])
    dk_early = own_lanes(dot(grads, qp[:mid]))

    scores = weigh(dot_r(both_heads(kp), qp[mid:]), weights_t[:, mid:])
    dv = own_lanes(dot(scores, wp[mid:]))
    scores = weigh(dot_r(both_heads(kp[:mid]), qp[:mid]), weights_t[:mid, :mid])
    dv_early = own_lanes(dot(scores, wp[:mid]))

    dq = jnp.concatenate([dq[:mid], dq[mid:] + dq_late], axis=0)
    dk = jnp.concatenate([dk[:mid] + dk_early, dk[mid:]], axis=0)
    dv = jnp.concatenate([dv[:mid] + dv_early, dv[mid:]], axis=0)

    sq_lane, upper, diag = square_masks()
    cos_b, sin_b = tcol[:, 3:4], tcol[:, 4:5]
    is_late = (scal[head_at] == 1).astype(F32)
    early = 1.0 - is_late

    def with_norms(parts, where):
        side = lambda total, norm: jnp.concatenate([total, jnp.where(where, norm, 0.0)], axis=1)
        of_cos, of_sin, norm_cos, norm_sin = parts
        return jnp.concatenate([side(of_cos, norm_cos), side(of_sin, norm_sin)], axis=0).astype(BF)

    prior_parts = unpack_state(prior, pair)
    into = dot_r(we, with_norms(prior_parts, head_lanes(pair, sq_lane, upper)))
    dq = dq + is_late * (cos_b * into[:, :LANES] + sin_b * into[:, LANES:])
    later_parts = unpack_state(later, pair)
    into = dot_r(ve, with_norms(later_parts, sq_lane == 0))
    dk = dk + early * (cos_b * into[:, :LANES] + sin_b * into[:, LANES:])
    kw = kp.astype(F32)
    left = jnp.concatenate([(kw * (cos_b * early)).astype(BF), (kw * (sin_b * early)).astype(BF)], axis=1)
    dv = dv + dot(left, jnp.concatenate(later_parts[:2], axis=0).astype(BF))

    dq = jnp.where(qp.astype(F32) > 0, dq, 0.0).astype(BF)
    dk = jnp.where(kw > 0, dk, 0.0).astype(BF)
    dv = dv.astype(BF)
    for n, part in enumerate((dq, dk, dv)):
        sums_o[n] = jnp.broadcast_to(jnp.sum(part.astype(F32), axis=0, keepdims=True), sums_o.shape[1:])
        early_o[n] = part[:mid]
        late_o[n] = part[mid:]


def input_kernel(scal, first, keep_early, keep_late, send_early, send_late, w_keep, w_send, out_o):
    @pl.when(pl.program_id(0) == 0)
    def _():
        out_o[...] = first[...]

    rows = lambda early, late: jnp.concatenate([early[0], late[0]], axis=0)
    out_o[...] += dot_r(rows(keep_early, keep_late), w_keep[...]) + dot_r(rows(send_early, send_late), w_send[...])


def place(values, piece_rows, tz, tys, x, y, z, extra, outs):
    xk, xs, yk, ys = outs
    width = xk.shape[-1]
    slot_z = tz ^ z
    pieces = {}
    at = 0
    for ty in tys:
        for tc in range(2):
            for tx in range(2):
                part = values[at * piece_rows : (at + 1) * piece_rows]
                blocks = [part[:, n : n + width] for n in range(0, part.shape[1], width)]
                if extra is not None:
                    blocks.append(extra[at])
                pieces[ty, tc, tx] = jnp.concatenate(blocks, axis=0) if len(blocks) > 1 else blocks[0]
                at += 1
    for ty in tys:
        slot = ty ^ y
        a, b = pieces[ty, 0, 0], pieces[ty, 0, 1]
        xk[slot, slot_z] = jnp.where(x == 0, a, b).astype(BF)
        xs[slot, slot_z] = jnp.where(x == 0, b, a).astype(BF)
    return pieces


def place_y(pieces, tz, tys, x, y, z, outs):
    xk, xs, yk, ys = outs
    slot_z = tz ^ z
    for tx in range(2):
        slot = tx ^ x
        a, b = pieces[0, 1, tx], pieces[1, 1, tx]
        yk[slot, slot_z] = jnp.where(y == 0, a, b).astype(BF)
        ys[slot, slot_z] = jnp.where(y == 0, b, a).astype(BF)


def reduce_grad_kernel(pos_at, scal, a_own, a_oth, b_own, b_oth, kept, near):
    tz = pl.program_id(0)
    x, y, z = (scal[pos_at + n] for n in range(3))
    values = dot_t(a_own[...], b_own[...]) + dot_t(a_oth[...], b_oth[...])
    rows = values.shape[0] // 8
    slot = tz ^ z

    def put(out):
        for n in range(8):
            ty, tc, tx = n // 4, n // 2 % 2, n % 2
            out[slot // 2, tc, tx ^ x, ty ^ y] = values[n * rows : (n + 1) * rows].astype(BF)

    @pl.when(slot % 2 == 0)
    def _():
        put(kept)

    @pl.when(slot % 2 == 1)
    def _():
        put(near)


def expand_grad_kernel(pos_at, scal, a_own, a_oth, b_own, b_oth, m_own, m_oth, c_own, c_oth, *outs):
    tz = pl.program_id(0)
    x, y, z = (scal[pos_at + n] for n in range(3))
    an, ao = a_own[0, 0], a_oth[0, 0]
    parts = [dot(an, b_own[n]) + dot(ao, b_oth[n]) for n in range(b_own.shape[0])]
    parts.append(dot(m_own[0, 0], c_own[...]) + dot(m_oth[0, 0], c_oth[...]))
    values = jnp.concatenate(parts, axis=1)
    pieces = place(values, values.shape[0] // 8, tz, (0, 1), x, y, z, None, outs)
    place_y(pieces, tz, (0, 1), x, y, z, outs)


def share_lanes(entries, devices, at, width):
    n = entries.shape[1]
    share = n // devices
    owner = lax.broadcasted_iota(jnp.int32, (devices, n), 0)
    column = lax.broadcasted_iota(jnp.int32, (devices, n), 1)
    mine = (column >= owner * share) & (column < (owner + 1) * share)
    high, low = high_low(jnp.where(mine, entries, 0.0))
    both = jnp.concatenate([high, low], axis=0).astype(BF)
    source = lax.broadcasted_iota(jnp.int32, (n, width), 0)
    target = lax.broadcasted_iota(jnp.int32, (n, width), 1)
    picks = (target >= at) & (target < at + share) & (lax.rem(source, share) == target - at)
    spread = dot(both, picks.astype(F32).astype(BF))
    return spread[:devices] + spread[devices:]


def heads_grad_kernel(
    pos_at, scal, a_own, a_oth, own_early, own_late, oth_early, oth_late, kept_h, sent_h, sums_1, kept_e, sent_e, sums_2, *refs, devices
):
    outs, table = refs[:-1], refs[-1]
    tz = pl.program_id(0)
    x, y, z = (scal[pos_at + n] for n in range(3))
    width = outs[0].shape[-1]

    @pl.when(tz == 0)
    def _():
        first_core = scal[pos_at - 1] == 0
        ordered = lambda kept, sent: [jnp.where(first_core, kept, sent), jnp.where(first_core, sent, kept)]
        sums_e = jnp.concatenate(ordered(kept_e[...], sent_e[...]), axis=1)
        of_heads = [part for n in range(3) for part in ordered(kept_h[n, 0:1], sent_h[n, 0:1])]
        total = jnp.zeros((devices, width), F32)
        at = 0
        for entries in (
            jnp.concatenate(of_heads[:4], axis=1), jnp.concatenate(of_heads[4:], axis=1), sums_1[2:3], sums_1[0:1], sums_1[1:2],
            sums_e, sums_2[2:3], sums_2[0:1], sums_2[1:2],
        ):
            total = total + share_lanes(entries, devices, at, width)
            at += entries.shape[1] // devices
        table[...] = total

    join = lambda early, late: jnp.concatenate(
        [jnp.concatenate([early[n], late[n]], axis=0) for n in range(early.shape[0])], axis=1
    )
    values = dot(a_own[0], join(own_early, own_late)) + dot(a_oth[0], join(oth_early, oth_late))
    line = lax.broadcasted_iota(jnp.int32, (8, width), 0)
    rows8 = table[pl.ds(pl.multiple_of(tz * 8, 8), 8)]
    extra = []
    for n in range(8):
        high, low = high_low(rows8[n : n + 1])
        extra.append(jnp.where(line == 0, high, jnp.where(line == 1, low, 0.0)))
    pieces = place(values, values.shape[0] // 8, tz, (0, 1), x, y, z, extra, outs)
    place_y(pieces, tz, (0, 1), x, y, z, outs)


class Ring:
    def __init__(self, n_dp):
        self.n_dp = n_dp
        self.devices = 2 * n_dp

    def swap(self, value, bits):
        return lax.ppermute(value, AXES, [(i, i ^ bits) for i in range(self.devices)])

    def core(self, value):
        return self.swap(value, 2)

    def x(self, value):
        return self.swap(value, 1)

    def y(self, value):
        return self.swap(value, 4)

    def z(self, value, step):
        return self.swap(value, 8 * step)


def add_first_kernel(scal, xk, xr, yk, yr, xn, yn):
    wide = lambda ref: ref[0].astype(F32)
    xn[...] = (wide(xk) + wide(xr)).astype(BF)
    yn[...] = (wide(yk) + wide(yr)).astype(BF)


def add_second_kernel(scal, xk, xr, xm, yk, yr, ym, own, z1, z2, z3):
    for n, (keep, got, more) in enumerate(((xk, xr, xm), (yk, yr, ym))):
        total = lambda k: keep[0, k].astype(F32) + got[0, k].astype(F32) + more[k].astype(F32)
        own[n] = total(0)
        for k, out in ((1, z1), (2, z2), (3, z3)):
            out[n] = total(k).astype(BF)


def add_last_kernel(core_at, scal, own, z1, z2, z3, keep, send):
    first = scal[core_at] == 0
    total = lambda n: own[n] + z1[n].astype(F32) + z2[n].astype(F32) + z3[n].astype(F32)
    of_first, of_second = total(0), total(1)
    keep[...] = jnp.where(first, of_first, of_second)
    send[...] = jnp.where(first, of_second, of_first)


def add_second_half_kernel(scal, xk, xr, xm, yk, yr, ym, kept, sent):
    for n, (keep, got, more) in enumerate(((xk, xr, xm), (yk, yr, ym))):
        total = lambda k: keep[0, k].astype(F32) + got[0, k].astype(F32) + more[k].astype(F32)
        for k in range(2):
            kept[k, n] = total(2 * k)
            sent[k, n] = total(2 * k + 1).astype(BF)


def add_third_half_kernel(scal, kept, got, own, sent):
    own[...] = kept[0] + got[0].astype(F32)
    sent[...] = (kept[1] + got[1].astype(F32)).astype(BF)


def add_last_half_kernel(core_at, scal, own, got, keep, send):
    first = scal[core_at] == 0
    of_first, of_second = (own[n] + got[n].astype(F32) for n in range(2))
    keep[...] = jnp.where(first, of_first, of_second)
    send[...] = jnp.where(first, of_second, of_first)


def add_near_kernel(scal, kept, got, own, far):
    own[...] = kept[0].astype(F32) + got[0].astype(F32)
    far[...] = (kept[1].astype(F32) + got[1].astype(F32)).astype(BF)


def add_far_kernel(scal, own, got, xk, xs, yk, ys):
    total = lambda *at: own[at] + got[at].astype(F32)
    for n in range(2):
        xk[n] = total(0, 0, n)
        xs[n] = total(0, 1, n).astype(BF)
        yk[n] = total(1, n, 0)
        ys[n] = total(1, n, 1).astype(BF)


def add_side_kernel(scal, xk, xr, yk, yr, own, xn, yn):
    own[0] = xk[0] + xr[0].astype(F32)
    own[1] = yk[0] + yr[0].astype(F32)
    xn[...] = (xk[1] + xr[1].astype(F32)).astype(BF)
    yn[...] = (yk[1] + yr[1].astype(F32)).astype(BF)


def add_end_kernel(core_at, scal, own, xm, ym, keep, send):
    first = scal[core_at] == 0
    of_first, of_second = own[0] + xm[...].astype(F32), own[1] + ym[...].astype(F32)
    keep[...] = jnp.where(first, of_first, of_second)
    send[...] = jnp.where(first, of_second, of_first)


class Scatter:
    def __init__(self, ring, core_at, name, sent):
        self.ring, self.core_at, self.name = ring, core_at, name
        self.xk, self.xs, self.yk, self.ys = sent

    def send(self, *others):
        self.xr, self.yr = self.ring.x(after(self.xs, *others)), self.ring.y(after(self.ys, *others))

    def first(self, scal, us=0.1):
        shape = self.xk.shape[1:]
        part = lambda a: (a, (1,) + shape, lambda j, s: (1, 0, 0, 0))
        xn, yn = call(
            add_first_kernel, self.name + "_add1", scal, (1,), [part(a) for a in (self.xk, self.xr, self.yk, self.yr)],
            [(shape, BF, None, None)] * 2, us=us,
        )
        self.xn, self.yn = xn, yn
        return xn

    def send_first(self, *others):
        self.xm, self.ym = self.ring.y(after(self.xn, *others)), self.ring.x(after(self.yn, *others))

    def second(self, scal):
        shape = self.xk.shape[1:]
        piece = (2,) + shape[1:]
        part = lambda a: (a, (1,) + shape, lambda j, s: (0, 0, 0, 0))
        whole = lambda a: (a, None, None)
        self.own, *self.sends = call(
            add_second_kernel, self.name + "_add2", scal, (1,),
            [part(self.xk), part(self.xr), whole(self.xm), part(self.yk), part(self.yr), whole(self.ym)],
            [(piece, F32, None, None)] + [(piece, BF, None, None)] * 3,
        )
        return self.own

    def send_second(self, *others):
        self.arrived = [self.ring.z(after(v, *others), k + 1) for k, v in enumerate(self.sends)]

    def last(self, scal):
        piece = self.own.shape[1:]
        keep, send = call(
            functools.partial(add_last_kernel, self.core_at), self.name + "_add3", scal, (1,),
            [(a, None, None) for a in (self.own, *self.arrived)], [(piece, F32, None, None)] * 2,
        )
        return keep, self.ring.core(send)


class HalvingScatter(Scatter):
    def second(self, scal):
        shape = self.xk.shape[1:]
        piece = (2, 2) + shape[1:]
        part = lambda a: (a, (1,) + shape, lambda j, s: (0, 0, 0, 0))
        whole = lambda a: (a, None, None)
        self.kept, self.near = call(
            add_second_half_kernel, self.name + "_add2", scal, (1,),
            [part(self.xk), part(self.xr), whole(self.xm), part(self.yk), part(self.yr), whole(self.ym)],
            [(piece, F32, None, None), (piece, BF, None, None)],
        )
        return self.kept

    def send_second(self):
        self.got = self.ring.z(self.near, 1)

    def third(self, scal):
        piece = self.kept.shape[1:]
        self.own, self.far = call(
            add_third_half_kernel, self.name + "_add3", scal, (1,),
            [(a, None, None) for a in (self.kept, self.got)], [(piece, F32, None, None), (piece, BF, None, None)],
        )
        return self.own

    def send_third(self):
        self.arrived = self.ring.z(self.far, 2)

    def last(self, scal):
        piece = self.own.shape[1:]
        keep, send = call(
            functools.partial(add_last_half_kernel, self.core_at), self.name + "_add4", scal, (1,),
            [(a, None, None) for a in (self.own, self.arrived)], [(piece, F32, None, None)] * 2,
        )
        return keep, self.ring.core(send)


class DepthScatter:
    def __init__(self, ring, core_at, name, sent):
        self.ring, self.core_at, self.name = ring, core_at, name
        self.kept, self.near = sent

    def call(self, kernel, step, scal, ins, outs):
        whole = lambda a: (a, None, None)
        return call(kernel, self.name + step, scal, (), [*map(whole, ins)], [(s, d, None, None) for s, d in outs])

    def send_near(self):
        self.got = self.ring.z(self.near, 1)

    def add_near(self, scal):
        shape = self.kept.shape[1:]
        self.own, self.far = self.call(add_near_kernel, "_add1", scal, (self.kept, self.got), [(shape, F32), (shape, BF)])
        return self.own

    def send_far(self):
        self.got = self.ring.z(self.far, 2)

    def add_far(self, scal):
        shape = self.own.shape[2:]
        self.xk, self.xs, self.yk, self.ys = self.call(
            add_far_kernel, "_add2", scal, (self.own, self.got), [(shape, F32), (shape, BF)] * 2
        )
        return self.xk

    def send_side(self):
        self.xr, self.yr = self.ring.x(self.xs), self.ring.y(self.ys)

    def add_side(self, scal):
        shape = self.xk.shape
        self.own, xn, yn = self.call(
            add_side_kernel, "_add3", scal, (self.xk, self.xr, self.yk, self.yr),
            [(shape, F32), (shape[1:], BF), (shape[1:], BF)],
        )
        self.xm, self.ym = self.ring.y(xn), self.ring.x(yn)
        return self.own

    def last(self, scal):
        shape = self.own.shape[1:]
        keep, send = self.call(
            functools.partial(add_end_kernel, self.core_at), "_add4", scal, (self.own, self.xm, self.ym),
            [(shape, F32)] * 2,
        )
        return keep, self.ring.core(send)


def after(value, *others):
    if not others:
        return value
    return lax.optimization_barrier((value,) + others)[0]


def side_by_side(core_at, scal, own, got):
    first = scal[core_at] == 0
    return [jnp.where(first, own, got), jnp.where(first, got, own)]


def finish_kernel(
    core_at, scal, own, got, reduce_own, reduce_got, expand_own, expand_got,
    heads_o, reduce_o, expand_o, merge_o, *shares_o,
):
    width = own.shape[1]
    rows = heads_o.shape[0]
    for n, part in enumerate(side_by_side(core_at, scal, reduce_own[...], reduce_got[...])):
        reduce_o[:, n * width : (n + 1) * width] = part
    blocks = expand_own.shape[0] // rows - 1
    for n, part in enumerate(side_by_side(core_at, scal, expand_own[...], expand_got[...])):
        for k in range(blocks):
            at = (n * blocks + k) * width
            expand_o[:, at : at + width] = part[k * rows : (k + 1) * rows]
        merge_o[:, n * width : (n + 1) * width] = part[blocks * rows :]
    for n, part in enumerate(side_by_side(core_at, scal, own[...], got[...])):
        for k in range(3):
            at = (2 * k + n) * width
            heads_o[:, at : at + width] = part[k * rows : (k + 1) * rows]
    entries = own[3 * rows :] + got[3 * rows :]
    entries = entries[0:1] + entries[1:2]
    at = 0
    for share in shares_o:
        n = share.shape[1]
        moved = entries if at == 0 else pltpu.roll(entries, width - at, 1)
        share[...] = moved[:, :n]
        at += n


def per_device(
    tokens, w_heads, b_heads, w_merge, b_merge, gain_first, bias_first, w_expand, b_expand,
    w_reduce, b_reduce, gain_second, bias_second, seq_lengths, cotangent,
):
    rows = tokens.shape[0]
    seqs = seq_lengths.shape[1]
    n_dp = lax.axis_size("dp")
    ring = Ring(n_dp)
    head = lax.axis_index("head")
    dp = lax.axis_index("dp")
    core = dp % 2
    place_of = jnp.stack([head, core, head, (dp // 2) % 2, dp // 4]).astype(jnp.int32)
    scal = jnp.concatenate([seq_lengths[0].astype(jnp.int32), place_of])
    head_at, core_at, pos_at = seqs, seqs + 1, seqs + 2
    first_core = core == 0
    line = lambda v: v.reshape(1, -1)
    b_heads, b_merge, gain_first, bias_first, b_expand, b_reduce, gain_second, bias_second = map(
        line, (b_heads, b_merge, gain_first, bias_first, b_expand, b_reduce, gain_second, bias_second)
    )
    wide_shape = (rows, D)
    quarter = 256

    turned = ((4, D // 4, rows), BF, None, None)
    rk, v, state, tcol, trow, tokens_t = call(
        functools.partial(kv_kernel, seqs), "keys_values", scal, (3,),
        [
            (tokens, None, None),
            (w_heads, (D, quarter), lambda j, s: (0, 3 + j)),
            (w_heads, (D, quarter), lambda j, s: (0, 6 + j)),
            (b_heads, (1, quarter), lambda j, s: (0, 3 + j)),
            (b_heads, (1, quarter), lambda j, s: (0, 6 + j)),
        ],
        [
            (wide_shape, BF, (rows, quarter), lambda j, s: (0, j)),
            (wide_shape, BF, (rows, quarter), lambda j, s: (0, j)),
            ((PAIRS + 1, LANES, LANES), BF, None, None),
            ((rows, LANES), F32, None, None),
            ((8, rows), F32, None, None), turned,
        ],
        [pltpu.VMEM((LANES, LANES), F32)],
        us=4,
    )
    prior = ring.x(state)

    fast = n_dp == 16
    order = scal
    if fast:
        tokens_o = ring.core(tokens_t)
    rq, num, den = call(
        local_kernel, "local_attention", scal, (3,),
        [
            (tokens, None, None),
            (w_heads, (D, quarter), lambda j, s: (0, j)),
            (b_heads, (1, quarter), lambda j, s: (0, j)),
            (rk, (rows, quarter), lambda j, s: (0, j)),
            (v, (rows, quarter), lambda j, s: (0, j)),
            (tcol, None, None),
            (trow, None, None),
        ],
        [
            (wide_shape, BF, (rows, quarter), lambda j, s: (0, j)),
            (wide_shape, F32, (rows, quarter), lambda j, s: (0, j)),
            (wide_shape, F32, (rows, quarter), lambda j, s: (0, j)),
        ],
        [pltpu.VMEM((rows, rows), F32)],
        us=6,
    )

    if fast:
        order = after(scal, tokens_o)
    att, inv, mixed, xhat, scale, normed, second, turned_own, act, slope = call(
        functools.partial(ffn_kernel, head_at), "feed_forward", order, (FFN_STEPS,),
        [
            (rq, None, None), (num, None, None), (den, None, None), (prior, None, None),
            (tcol, None, None), (tokens, None, None), (w_merge, None, None), (b_merge, None, None),
            (gain_first, None, None), (bias_first, None, None), (b_reduce, None, None),
            (w_expand, (D, FFN_BLOCK), lambda j, s: (0, j)),
            (b_expand, (1, FFN_BLOCK), lambda j, s: (0, j)),
            (w_reduce, (FFN_BLOCK, D), lambda j, s: (j, 0)),
        ],
        [
            (wide_shape, F32, None, None), (wide_shape, F32, None, None), (wide_shape, BF, None, None),
            (wide_shape, F32, None, None), ((rows, LANES), F32, None, None), (wide_shape, BF, None, None),
            (wide_shape, F32, None, None), ((2, 4, D // 4, rows), BF, None, None),
            ((rows, FF), BF, (rows, FFN_BLOCK), lambda j, s: (0, j)),
            ((rows, FF), BF, (rows, FFN_BLOCK), lambda j, s: (0, j)),
        ],
        us=11, vmem=VMEM_FFN,
    )

    half_shape = (rows, D // 2)
    result, grad_second, branch, bg_keep, bg_send, sums_second = call(
        functools.partial(second_kernel, core_at), "second_norm", scal, (1,),
        [(second, None, None), (cotangent, None, None), (gain_second, None, None), (bias_second, None, None)],
        [
            (wide_shape, BF, None, None), (wide_shape, F32, None, None), (wide_shape, BF, None, None),
            (half_shape, BF, None, None), (half_shape, BF, None, None), ((8, D), F32, None, None),
        ],
        us=2.6,
    )

    devices = ring.devices
    small, large = D // devices, FF // devices
    whole = lambda a: (a, None, None)
    part = lambda a, n: (a, (1, 1, D // 4, rows), lambda j, s: (n, j, 0, 0))
    by_z = lambda a: (a, (1, D // 4, rows), lambda j, s: (j, 0, 0))
    by_col = lambda a: (a, (rows, FF // 4), lambda j, s: (0, j))

    def group(kernel, name, scal, ins, piece_rows, us, scratch=(), kind=Scatter):
        shape = (2, 4, piece_rows, D // 2)
        sent = call(
            functools.partial(kernel, pos_at), name, scal, (4,), ins, [(shape, BF, None, None)] * 4, scratch, us
        )
        return kind(ring, core_at, name, sent)

    ff_half = FF_STEPS // 2
    in_hbm = lambda a: (a, None, pltpu.HBM)
    hidden = ((ff_half, rows, FF_BLOCK), BF, None, None)
    hidden_sums = ((1, FF // 2), F32, None, None)
    buffers = [
        pltpu.VMEM((ff_half, D, FF_BLOCK), BF), pltpu.VMEM((ff_half, FF_BLOCK, D), BF),
        pltpu.SemaphoreType.DMA((2, ff_half)),
    ]
    hidden_in = [whole(branch), whole(slope), in_hbm(w_expand), in_hbm(w_reduce)]
    pg_send, sum_sent, partial = call(
        functools.partial(back_sent_kernel, core_at), "feed_forward_back_sent", scal, (),
        [*hidden_in, whole(grad_second)],
        [hidden, hidden_sums, (wide_shape, F32, None, None)], buffers,
        us=5, vmem=VMEM_BACK,
    )
    order = scal
    if fast:
        pg_o = ring.core(pg_send)
        act_o, turned_other, bg_o = map(ring.core, (act, turned_own, bg_send))
        pieces = ((2, 2, 2, 2, large, D // 2), BF, None, None)
        sent = call(
            functools.partial(reduce_grad_kernel, pos_at), "grad_reduce", after(scal, partial, turned_other), (4,),
            [by_col(act), by_col(act_o), whole(bg_keep), whole(bg_o)], [pieces, pieces], us=6,
        )
        reduced = DepthScatter(ring, core_at, "grad_reduce", sent)
        reduced.send_near()
        order = after(scal, reduced.near)

    pg_keep, grad_first, mg_keep, mg_send, w_att, e_att, later, sum_kept, sums_first = call(
        functools.partial(back_kernel, core_at), "feed_forward_back", order, (),
        [
            *hidden_in,
            (partial, None, None), (gain_first, None, None), (xhat, None, None), (scale, None, None),
            (w_merge, None, None), (att, None, None), (inv, None, None), (rq, None, None), (tcol, None, None),
        ],
        [
            hidden, (wide_shape, F32, None, None), (half_shape, BF, None, None), (half_shape, BF, None, None),
            (wide_shape, BF, None, None), ((rows, LANES), BF, None, None),
            ((PAIRS + 1, LANES, LANES), BF, None, None), hidden_sums, ((8, D), F32, None, None),
        ],
        [pltpu.VMEM(wide_shape, F32), *buffers],
        us=COST_BACK, vmem=VMEM_BACK,
    )
    later = ring.x(later)

    if fast:
        mg_o = ring.core(mg_send)
        expanded = group(
            expand_grad_kernel, "grad_expand", scal,
            [
                part(turned_own, 1), part(turned_other, 1), whole(pg_keep), whole(pg_o),
                part(turned_own, 0), part(turned_other, 0), whole(mg_keep), whole(mg_o),
            ],
            5 * small, COST_EXPAND, kind=HalvingScatter,
        )
        expanded.send(later)
        order = after(scal, expanded.xs, later)

    half_pairs = PAIRS // 2
    pair_blocks = lambda core_of: [
        (a, (rows, LANES), lambda j, s: (0, core_of(s) * half_pairs + j)) for a in (rq, rk, v, w_att)
    ]
    both_states = [whole(e_att), whole(prior), whole(later), whole(tcol)]
    pj_out = [((3, rows // 2, D // 2), BF, (3, rows // 2, LANES), lambda j, s: (0, 0, j))] * 2
    pj_sums = ((3, 8, D // 2), F32, (3, 8, LANES), lambda j, s: (0, 0, j))
    table = ((rows, rows), F32, None, None)
    *pj_send, sum_heads_sent, weights, weights_t = call(
        functools.partial(attn_sent_kernel, head_at, core_at), "attention_back_sent", order, (half_pairs,),
        [*pair_blocks(lambda s: 1 - s[core_at]), *both_states, whole(trow)], [*pj_out, pj_sums, table, table], us=COST_SENT,
    )
    order = scal
    if fast:
        pj_o = [ring.core(v) for v in pj_send]
        order = after(scal, reduced.add_near(after(scal, pj_send[0])))
        reduced.send_far()
    *pj_keep, sum_heads_kept = call(
        functools.partial(attn_kept_kernel, head_at, core_at), "attention_back_kept", order, (half_pairs,),
        [*pair_blocks(lambda s: s[core_at]), *both_states, whole(weights), whole(weights_t)], [*pj_out, pj_sums], us=COST_KEPT,
    )

    if fast:
        order = after(scal, expanded.first(after(scal, pj_keep[0])))
        expanded.send_first()
        heads = group(
            functools.partial(heads_grad_kernel, devices=devices), "grad_heads", order,
            [
                by_z(tokens_t), by_z(tokens_o), *map(whole, (*pj_keep, *pj_o)),
                *map(whole, (sum_heads_kept, sum_heads_sent, sums_first, sum_kept, sum_sent, sums_second)),
            ],
            3 * small + 8, COST_HEADS, [pltpu.VMEM((devices, D // 2), F32)],
        )
        heads.send()
        order = after(scal, heads.xs)

    of_part = lambda a: (a, (1, rows // 2, D // 2), lambda j, s: (j, 0, 0))
    (input_grad,) = call(
        input_kernel, "input_grad", order, (3,),
        [
            whole(grad_first), *map(of_part, (*pj_keep, *pj_send)),
            (w_heads, (D, D // 2), lambda j, s: (0, 2 * j + s[core_at])),
            (w_heads, (D, D // 2), lambda j, s: (0, 2 * j + 1 - s[core_at])),
        ],
        [(wide_shape, F32, None, None)],
        us=COST_INPUT,
    )

    if fast:
        order = reduced.add_far(after(scal, input_grad))
        order = expanded.second(after(scal, order))
        expanded.send_second()
        reduced.send_side()
        order = heads.first(after(scal, order))
        heads.send_first()
        order = expanded.third(after(scal, order))
        expanded.send_third()
        order = heads.second(after(scal, order))
        heads.send_second()
        order = reduced.add_side(after(scal, order))
        expand_own, expand_got = expanded.last(after(scal, order))
        reduce_own, reduce_got = reduced.last(after(scal, expand_own))
        heads_own, heads_got = heads.last(after(scal, reduce_own))
        out = lambda n, m: ((n, m), F32, None, None)
        counts = (2 * small, small, small, small, small, large, small, small, small)
        w_heads_grad, w_reduce_grad, w_expand_grad, w_merge_grad, *shares = call(
            functools.partial(finish_kernel, core_at), "finish", scal, (),
            [*map(whole, (heads_own, heads_got, reduce_own, reduce_got, expand_own, expand_got))],
            [out(small, 3 * D), out(large, D), out(small, FF), out(small, D), *(out(1, n) for n in counts)],
        )
        shares = [share.reshape(-1) for share in shares]
        grads = (
            w_heads_grad, *shares[:2], w_merge_grad, *shares[2:5], w_expand_grad, shares[5], w_reduce_grad,
            *shares[6:],
        )
    else:
        by_core = lambda keep, send: jnp.concatenate(
            [jnp.where(first_core, keep, send), jnp.where(first_core, send, keep)], axis=1
        )
        flat = lambda v: v.transpose(1, 0, 2).reshape(rows, -1)
        by_heads = lambda keep, send: jnp.concatenate(
            [by_core(keep[n], send[n]) for n in range(3)], axis=1
        )
        pj_keep, pj_send = (jnp.concatenate(v, axis=1) for v in (pj_keep, pj_send))
        sum_heads = by_heads(sum_heads_kept, sum_heads_sent)[0]
        scatter = lambda v: lax.psum_scatter(v, AXES, scatter_dimension=0, tiled=True)
        grads = (
            scatter(dot_t(tokens, by_heads(pj_keep, pj_send))),
            scatter(sum_heads[: 2 * D]), scatter(sum_heads[2 * D :]),
            scatter(dot_t(mixed, by_core(mg_keep, mg_send))),
            scatter(sums_first[2]), scatter(sums_first[0]), scatter(sums_first[1]),
            scatter(dot_t(normed, by_core(flat(pg_keep), flat(pg_send)))),
            scatter(by_core(sum_kept, sum_sent)[0]),
            scatter(dot_t(act, branch)),
            scatter(sums_second[2]), scatter(sums_second[0]), scatter(sums_second[1]),
        )
    return (result, input_grad) + tuple(grads)


def solution(mesh):
    in_specs = (P(AXES, None),) + (P(),) * 12 + (P("dp", None), P(AXES, None))
    row, one = P(AXES, None), P(AXES)
    out_specs = (row, row, row, one, one, row, one, one, one, row, one, row, one, one, one)
    return jax.shard_map(
        per_device, mesh=mesh, in_specs=in_specs, out_specs=out_specs, check_vma=False
    )
```

```python
import functools
import math

import jax
import jax.numpy as jnp
from jax import lax
from jax.experimental import pallas as pl
from jax.experimental.pallas import tpu as pltpu
from jax.sharding import PartitionSpec as P

D = 768
PAIRS = 6
FF = 3072
LANES = 128
HALF = 64
BF = jnp.bfloat16
F32 = jnp.float32
AXES = ("dp", "head")
VMEM_LIMIT = 8 << 20
VMEM_FFN = 16 << 20
VMEM_ATTN = 10 << 20
FF_BLOCK = 768
FFN_BLOCK = 1024
FFN_STEPS = FF // FFN_BLOCK
MATMUL_PER_US = 1.15e9
COST_EXPAND = 1
VMEM_BACK = 16 << 20
COST_KEPT = 0.5
COST_BACK = 3
COST_SENT = 0.5
COST_HEADS = 0.1
COST_INPUT = 0.1
FF_STEPS = FF // FF_BLOCK


def dot(a, b):
    return jnp.dot(a, b, preferred_element_type=F32)


def dot_t(a, b):
    return lax.dot_general(a, b, (((0,), (0,)), ((), ())), preferred_element_type=F32)


def dot_r(a, b):
    return lax.dot_general(a, b, (((1,), (1,)), ((), ())), preferred_element_type=F32)


def call(kernel, name, scal, grid, ins, outs, scratch=(), us=0.1, vmem=VMEM_LIMIT):
    def spec(b, m):
        if b is None:
            return pl.BlockSpec(memory_space=pltpu.VMEM if m is None else m)
        return pl.BlockSpec(b, m)

    in_specs = [spec(b, m) for _, b, m in ins]
    out_specs = [spec(b, m) for _, _, b, m in outs]
    return pl.pallas_call(
        kernel,
        name=name,
        grid_spec=pltpu.PrefetchScalarGridSpec(
            num_scalar_prefetch=1,
            grid=grid,
            in_specs=in_specs,
            out_specs=out_specs,
            scratch_shapes=list(scratch),
        ),
        out_shape=[jax.ShapeDtypeStruct(s, d) for s, d, _, _ in outs],
        compiler_params=pltpu.CompilerParams(vmem_limit_bytes=vmem),
        cost_estimate=pl.CostEstimate(flops=int(us * MATMUL_PER_US), bytes_accessed=1, transcendentals=0),
    )(scal, *[a for a, _, _ in ins])


def lane_masks():
    lane = lax.broadcasted_iota(jnp.int32, (1, LANES), 1)
    even = (lane < HALF).astype(F32)
    return lane, even.astype(BF), (1.0 - even).astype(BF)


def both_heads(pair):
    lane, even, odd = lane_masks()
    return jnp.concatenate([pair * even, pair * odd], axis=0)


def own_lanes(stacked):
    rows = stacked.shape[0] // 2
    lane = lax.broadcasted_iota(jnp.int32, (1, LANES), 1)
    return jnp.where(lane < HALF, stacked[:rows], stacked[rows:])


def square_masks():
    row = lax.broadcasted_iota(jnp.int32, (LANES, LANES), 0)
    lane = lax.broadcasted_iota(jnp.int32, (LANES, LANES), 1)
    upper = row < HALF
    return lane, upper, upper == (lane < HALF)


def high_low(v):
    high = v.astype(BF).astype(F32)
    return high, v - high


def tables(scal, rows, seqs, tcol, trow):
    pos = lax.broadcasted_iota(jnp.int32, (1, rows), 1) + scal[seqs] * rows
    seg = jnp.zeros((1, rows), jnp.int32)
    first = jnp.zeros((1, rows), jnp.int32)
    length = jnp.ones((1, rows), jnp.int32)
    at_boundary = jnp.int32(0)
    begin = jnp.int32(0)
    for s in range(seqs):
        end = begin + scal[s]
        inside = (pos >= begin) & (pos < end)
        first = jnp.where(inside, begin, first)
        length = jnp.where(inside, jnp.maximum(scal[s], 1), length)
        seg = seg + (pos >= end).astype(jnp.int32)
        at_boundary = at_boundary + (rows - 1 >= end).astype(jnp.int32)
        begin = end
    live = (seg < seqs).astype(F32)
    angle = 0.5 * math.pi * (pos - first).astype(F32) / length.astype(F32)
    cos_w = jnp.cos(angle) * live
    sin_w = jnp.sin(angle) * live
    crossing = (seg == at_boundary).astype(F32)
    which = lax.broadcasted_iota(jnp.int32, (LANES, rows), 0)
    table = jnp.zeros((LANES, rows), F32)
    for n, entry in enumerate((cos_w, sin_w, seg.astype(F32), cos_w * crossing, sin_w * crossing)):
        table = jnp.where(which == n, entry, table)
    trow[...] = table[:8]
    tcol[...] = table.T


def pack_state(both, norm_cos, norm_sin, pair, norms):
    lane, upper, diag = square_masks()
    packed = jnp.where(diag, both[:LANES, :LANES], pltpu.roll(both[LANES:, :LANES], HALF, 1))
    cos_high, cos_low = high_low(norm_cos)
    sin_high, sin_low = high_low(norm_sin)
    for n, part in enumerate((cos_high, cos_low, sin_high, sin_low)):
        norms = jnp.where(lane == 4 * pair + n, part, norms)
    return packed.astype(BF), norms


def unpack_state(state_ref, pair):
    lane, upper, diag = square_masks()
    packed = state_ref[pair].astype(F32)
    norms = state_ref[PAIRS].astype(F32)
    of_cos = jnp.where(diag, packed, 0.0)
    of_sin = jnp.where(diag, pltpu.roll(packed, HALF, 1), 0.0)
    pick = lambda n: jnp.sum(
        jnp.where((lane == 4 * pair + n) | (lane == 4 * pair + n + 1), norms, 0.0), axis=1, keepdims=True
    )
    return of_cos, of_sin, pick(0), pick(2)


def turn(value, out):
    turned = value.T
    share = out.shape[1]
    for n in range(out.shape[0]):
        out[n] = turned[n * share : (n + 1) * share]


def kv_kernel(seqs, scal, tok, wk, wv, bk, bv, rk_o, v_o, st_o, tcol, trow, turned_o, norms):
    step = pl.program_id(0)
    rows = tok.shape[0]

    @pl.when(step == 0)
    def _():
        tables(scal, rows, seqs, tcol, trow)
        norms[...] = jnp.zeros_like(norms)
        turn(tok[...], turned_o)

    rk = jnp.maximum(dot(tok[...], wk[...]) + bk[...].astype(F32), 0.0).astype(BF)
    v = (dot(tok[...], wv[...]) + bv[...].astype(F32)).astype(BF)
    rk_o[...] = rk
    v_o[...] = v
    cos_b, sin_b = tcol[:, 3:4], tcol[:, 4:5]
    ones = jnp.ones((rows, LANES), BF)
    for n in range(2):
        pair = 2 * step + n
        cols = slice(n * LANES, (n + 1) * LANES)
        kp = rk[:, cols].astype(F32)
        left = jnp.concatenate([(kp * cos_b).astype(BF), (kp * sin_b).astype(BF)], axis=1)
        both = dot_t(left, jnp.concatenate([v[:, cols], ones], axis=1))
        packed, new_norms = pack_state(both, both[:LANES, LANES:], both[LANES:, LANES:], pair, norms[...])
        st_o[pair] = packed
        norms[...] = new_norms

    st_o[PAIRS] = norms[...].astype(BF)


def weights_block(tcol, trow, transposed):
    rows = tcol.shape[0]
    down = lax.broadcasted_iota(jnp.int32, (rows, rows), 0)
    along = lax.broadcasted_iota(jnp.int32, (rows, rows), 1)
    same = tcol[:, 2:3] == trow[2:3, :]
    causal = (down <= along) if transposed else (along <= down)
    value = tcol[:, 0:1] * trow[0:1, :] + tcol[:, 1:2] * trow[1:2, :]
    return jnp.where(same & causal, value, 0.0)


def weigh(stacked, weights):
    rows = weights.shape[0]
    return jnp.concatenate([stacked[:rows] * weights, stacked[rows:] * weights], axis=0).astype(BF)


def local_kernel(scal, tok, wq, bq, rk, v, tcol, trow, rq_o, num_o, den_o, weights):
    step = pl.program_id(0)
    rows = tok.shape[0]
    mid = rows // 2

    @pl.when(step == 0)
    def _():
        weights[...] = weights_block(tcol, trow, False)

    rq = jnp.maximum(dot(tok[...], wq[...]) + bq[...].astype(F32), 0.0).astype(BF)
    rq_o[...] = rq
    ones = jnp.ones((rows, LANES), BF)
    for n in range(2):
        cols = slice(n * LANES, (n + 1) * LANES)
        kp = rk[:, cols]
        values = jnp.concatenate([v[:, cols], ones], axis=1)
        first = weigh(dot_r(both_heads(rq[:, cols]), kp[:mid]), weights[:, :mid])
        second = weigh(dot_r(both_heads(rq[mid:, cols]), kp[mid:]), weights[mid:, mid:])
        sums = dot(first, values[:mid])
        late = dot(second, values[mid:])
        for own, out in ((slice(0, LANES), num_o), (slice(LANES, 2 * LANES), den_o)):
            total = own_lanes(sums[:, own])
            out[:mid, cols] = total[:mid]
            out[mid:, cols] = total[mid:] + own_lanes(late[:, own])


def normalise(entries):
    mean = jnp.mean(entries, axis=1, keepdims=True)
    centred = entries - mean
    var = jnp.mean(centred * centred, axis=1, keepdims=True)
    scale = lax.rsqrt(var + 1e-05)
    return centred * scale, scale


def merge_heads(
    head_at, scal, rq, num, den, st, tcol, tok, w_merge, b_merge, gain, bias, b_red,
    att_o, inv_o, mixed_o, xhat_o, scale_o, normed_o, acc_o, turned_o,
):
    cross = (scal[head_at] == 1).astype(F32)
    cos_b, sin_b = tcol[:, 3:4] * cross, tcol[:, 4:5] * cross
    sq_lane, upper, diag = square_masks()
    for pair in range(PAIRS):
        cols = slice(pair * LANES, (pair + 1) * LANES)
        qp = rq[:, cols].astype(F32)
        of_cos, of_sin, norm_cos, norm_sin = unpack_state(st, pair)
        top = jnp.concatenate([of_cos, jnp.where(diag, norm_cos, 0.0)], axis=1)
        low = jnp.concatenate([of_sin, jnp.where(diag, norm_sin, 0.0)], axis=1)
        right = jnp.concatenate([top, low], axis=0).astype(BF)
        left = jnp.concatenate([(qp * cos_b).astype(BF), (qp * sin_b).astype(BF)], axis=1)
        prior = dot(left, right)
        inverse = 1.0 / (den[:, cols] + prior[:, LANES:] + 1.0)
        attended = (num[:, cols] + prior[:, :LANES]) * inverse
        att_o[:, cols] = attended
        inv_o[:, cols] = inverse
        mixed_o[:, cols] = attended.astype(BF)
    first_in = tok[...].astype(F32) + dot(mixed_o[...], w_merge[...]) + b_merge[...].astype(F32)
    xhat, scale = normalise(first_in)
    normed = xhat * gain[...].astype(F32) + bias[...].astype(F32)
    xhat_o[...] = xhat
    scale_o[...] = jnp.broadcast_to(scale, scale_o.shape)
    normed_o[...] = normed.astype(BF)
    acc_o[...] = normed + b_red[...].astype(F32)
    turn(mixed_o[...], turned_o.at[0])
    turn(normed_o[...], turned_o.at[1])


def expand_reduce(normed, w_exp, b_exp, w_red, act_o, slope_o, acc_o):
    rows = normed.shape[0]
    pre = [dot(normed[at : at + rows // 2], w_exp[...]) + b_exp[...].astype(F32) for at in (0, rows // 2)]
    for at, x in zip((0, rows // 2), pre):
        part = slice(at, at + rows // 2)
        cdf = 0.5 + 0.5 * lax.erf(x * (2.0**-0.5))
        pdf = jnp.exp(-0.5 * x * x) * (1.0 / math.sqrt(2.0 * math.pi))
        act = (x * cdf).astype(BF)
        act_o[part] = act
        slope_o[part] = (cdf + x * pdf).astype(BF)
        acc_o[part] += dot(act, w_red[...])


def ffn_kernel(head_at, scal, *refs):
    w_exp, b_exp, w_red = refs[11:14]
    normed_o, acc_o = refs[19:21]
    act_o, slope_o = refs[22:]

    @pl.when(pl.program_id(0) == 0)
    def _():
        merge_heads(head_at, scal, *refs[:11], *refs[14:22])

    expand_reduce(normed_o, w_exp, b_exp, w_red, act_o, slope_o, acc_o)


def second_kernel(core_at, scal, second, cot, gain, bias, out_o, grad_o, full_o, keep_o, send_o, sums_o):
    xhat, scale = normalise(second[...])
    gain_w = gain[...].astype(F32)
    out_o[...] = (xhat * gain_w + bias[...].astype(F32)).astype(BF)
    cot_w = cot[...].astype(F32)
    t = cot_w * gain_w
    grad = scale * (
        t - jnp.mean(t, axis=1, keepdims=True) - xhat * jnp.mean(t * xhat, axis=1, keepdims=True)
    )
    low = grad.astype(BF)
    grad_o[...] = grad
    full_o[...] = low
    first = scal[core_at] == 0
    half = D // 2
    left, right = grad[:, :half], grad[:, half:]
    keep_o[...] = jnp.where(first, left, right).astype(BF)
    send_o[...] = jnp.where(first, right, left).astype(BF)
    sums_o[0:1] = jnp.sum(cot_w * xhat, axis=0, keepdims=True)
    sums_o[1:2] = jnp.sum(cot_w, axis=0, keepdims=True)
    sums_o[2:3] = jnp.sum(low.astype(F32), axis=0, keepdims=True)


def head_lanes(pair, lane, first):
    at = 4 * pair + jnp.where(first, 0, 2)
    return (lane == at) | (lane == at + 1)


def weight_copies(half, w_exp, w_red, exp_buf, red_buf, sems, n):
    at = pl.ds(pl.multiple_of((half * exp_buf.shape[0] + n) * FF_BLOCK, FF_BLOCK), FF_BLOCK)
    return (
        pltpu.make_async_copy(w_red.at[at, :], red_buf.at[n], sems.at[0, n]),
        pltpu.make_async_copy(w_exp.at[:, at], exp_buf.at[n], sems.at[1, n]),
    )


def back_steps(half, full, slope, w_exp, w_red, out_o, bexp_o, exp_buf, red_buf, sems):
    blocks = exp_buf.shape[0]
    copies = [weight_copies(half, w_exp, w_red, exp_buf, red_buf, sems, n) for n in range(blocks)]
    for pair in copies:
        for copy in pair:
            copy.start()
    total = None
    for n, (of_red, of_exp) in enumerate(copies):
        cols = slice(n * FF_BLOCK, (n + 1) * FF_BLOCK)
        at = pl.ds(pl.multiple_of((half * blocks + n) * FF_BLOCK, FF_BLOCK), FF_BLOCK)
        of_red.wait()
        pre_grad = (dot_r(full[...], red_buf[n]) * slope[:, at].astype(F32)).astype(BF)
        bexp_o[:, cols] = jnp.sum(pre_grad.astype(F32), axis=0, keepdims=True)
        out_o[n] = pre_grad
        of_exp.wait()
        part = dot_r(pre_grad, exp_buf[n])
        total = part if total is None else total + part
    return total


def back_sent_kernel(core_at, scal, full, slope, w_exp, w_red, grad2, sent_o, bexp_o, acc, exp_buf, red_buf, sems):
    half = 1 - scal[core_at]
    acc[...] = grad2[...] + back_steps(half, full, slope, w_exp, w_red, sent_o, bexp_o, exp_buf, red_buf, sems)


def back_kernel(
    core_at, scal, full, slope, w_exp, w_red, acc_in, gain, xhat, scale, w_merge, att, inv, rq, tcol,
    kept_o, first_o, mk_o, ms_o, w_o, e_o, st_o, bexp_o, sums_o,
    acc, exp_buf, red_buf, sems,
):
    half = scal[core_at]
    acc[...] = acc_in[...] + back_steps(half, full, slope, w_exp, w_red, kept_o, bexp_o, exp_buf, red_buf, sems)
    back_rest(
        core_at, scal, acc, gain, xhat, scale, w_merge, att, inv, rq, tcol,
        first_o, mk_o, ms_o, w_o, e_o, st_o, sums_o,
    )


def back_rest(
    core_at, scal, acc, gain, xhat, scale, w_merge, att, inv, rq, tcol,
    first_o, mk_o, ms_o, w_o, e_o, st_o, sums_o,
):
    grad_normed = acc[...]
    xh = xhat[...]
    t = grad_normed * gain[...].astype(F32)
    first = scale[:, 0:1] * (
        t - jnp.mean(t, axis=1, keepdims=True) - xh * jnp.mean(t * xh, axis=1, keepdims=True)
    )
    low = first.astype(BF)
    first_o[...] = first
    sums_o[0:1] = jnp.sum(grad_normed * xh, axis=0, keepdims=True)
    sums_o[1:2] = jnp.sum(grad_normed, axis=0, keepdims=True)
    sums_o[2:3] = jnp.sum(low.astype(F32), axis=0, keepdims=True)
    is_first = scal[core_at] == 0
    left, right = first[:, : D // 2], first[:, D // 2 :]
    mk_o[...] = jnp.where(is_first, left, right).astype(BF)
    ms_o[...] = jnp.where(is_first, right, left).astype(BF)
    cos_b, sin_b = tcol[:, 3:4], tcol[:, 4:5]
    w = (dot_r(low, w_merge[...]).astype(BF).astype(F32) * inv[...]).astype(BF)
    w_o[...] = w
    high, rest = high_low(w.astype(F32) * att[...])
    column = lax.broadcasted_iota(jnp.int32, (D, LANES), 0)
    target = lax.broadcasted_iota(jnp.int32, (D, LANES), 1)
    picks = (target == 2 * (column // HALF)).astype(F32).astype(BF)
    e_high, e_low = high_low(-(dot(high.astype(BF), picks) + dot(rest.astype(BF), picks)))
    e = (e_high + pltpu.roll(e_low, 1, 1)).astype(BF)
    e_o[...] = e
    norms = jnp.zeros((LANES, LANES), F32)
    sq_lane, upper, diag = square_masks()
    for pair in range(PAIRS):
        cols = slice(pair * LANES, (pair + 1) * LANES)
        qp = rq[:, cols].astype(F32)
        left = jnp.concatenate([(qp * cos_b).astype(BF), (qp * sin_b).astype(BF)], axis=1)
        both = dot_t(left, jnp.concatenate([w[:, cols], e], axis=1))
        mine = head_lanes(pair, sq_lane, upper)
        norm = lambda part: jnp.sum(jnp.where(mine, part, 0.0), axis=1, keepdims=True)
        packed, norms = pack_state(both, norm(both[:LANES, LANES:]), norm(both[LANES:, LANES:]), pair, norms)
        st_o[pair] = packed
    st_o[PAIRS] = norms.astype(BF)


def attn_sent_kernel(head_at, core_at, scal, rq, rk, v, w, e, prior, later, tcol, trow, early_o, late_o, sums_o, weights, weights_t):
    weights[...] = weights_block(tcol, trow, False)
    weights_t[...] = weights_block(tcol, trow, True)
    first = (1 - scal[core_at]) * (PAIRS // 2)
    attn_back(head_at, first, scal, rq, rk, v, w, e, prior, later, tcol, weights, weights_t, early_o, late_o, sums_o)


def attn_kept_kernel(head_at, core_at, scal, rq, rk, v, w, e, prior, later, tcol, weights, weights_t, early_o, late_o, sums_o):
    first = scal[core_at] * (PAIRS // 2)
    attn_back(head_at, first, scal, rq, rk, v, w, e, prior, later, tcol, weights, weights_t, early_o, late_o, sums_o)


def attn_back(head_at, first, scal, rq, rk, v, w, e, prior, later, tcol, weights, weights_t, early_o, late_o, sums_o):
    for n in range(PAIRS // 2):
        attn_back_pair(
            head_at, first + n, n, scal, rq, rk, v, w, e, prior, later, tcol, weights, weights_t, early_o, late_o, sums_o
        )


def attn_back_pair(
    head_at, pair, slot, scal, rq, rk, v, w, e, prior, later, tcol, weights, weights_t, early_o, late_o, sums_o
):
    rows = rq.shape[0]
    mid = rows // 2
    cols = pl.ds(pl.multiple_of(pair * LANES, LANES), LANES)
    out = slice(slot * LANES, (slot + 1) * LANES)

    qp, kp, vp, wp = rq[:, cols], rk[:, cols], v[:, cols], w[:, cols]
    lane, even, odd = lane_masks()
    of_even = ((lane == 4 * pair) | (lane == 4 * pair + 1)).astype(F32).astype(BF)
    of_odd = ((lane == 4 * pair + 2) | (lane == 4 * pair + 3)).astype(F32).astype(BF)
    ones = jnp.ones((rows, LANES), BF)
    we = jnp.concatenate([wp, e[...]], axis=1)
    by_head = (jnp.concatenate([even, of_even], axis=1), jnp.concatenate([odd, of_odd], axis=1))
    ve = jnp.concatenate([vp, ones], axis=1)
    stack = lambda a, lo, hi: jnp.concatenate([a[lo:hi] * m for m in by_head], axis=0)

    grads = weigh(dot_r(stack(we, 0, rows), ve[:mid]), weights[:, :mid])
    dq = own_lanes(dot(grads, kp[:mid]))
    grads = weigh(dot_r(stack(we, mid, rows), ve[mid:]), weights[mid:, mid:])
    dq_late = own_lanes(dot(grads, kp[mid:]))

    grads = weigh(dot_r(stack(ve, 0, rows), we[mid:]), weights_t[:, mid:])
    dk = own_lanes(dot(grads, qp[mid:]))
    grads = weigh(dot_r(stack(ve, 0, mid), we[:mid]), weights_t[:mid, :mid])
    dk_early = own_lanes(dot(grads, qp[:mid]))

    scores = weigh(dot_r(both_heads(kp), qp[mid:]), weights_t[:, mid:])
    dv = own_lanes(dot(scores, wp[mid:]))
    scores = weigh(dot_r(both_heads(kp[:mid]), qp[:mid]), weights_t[:mid, :mid])
    dv_early = own_lanes(dot(scores, wp[:mid]))

    dq = jnp.concatenate([dq[:mid], dq[mid:] + dq_late], axis=0)
    dk = jnp.concatenate([dk[:mid] + dk_early, dk[mid:]], axis=0)
    dv = jnp.concatenate([dv[:mid] + dv_early, dv[mid:]], axis=0)

    sq_lane, upper, diag = square_masks()
    cos_b, sin_b = tcol[:, 3:4], tcol[:, 4:5]
    is_late = (scal[head_at] == 1).astype(F32)
    early = 1.0 - is_late

    def with_norms(parts, where):
        side = lambda total, norm: jnp.concatenate([total, jnp.where(where, norm, 0.0)], axis=1)
        of_cos, of_sin, norm_cos, norm_sin = parts
        return jnp.concatenate([side(of_cos, norm_cos), side(of_sin, norm_sin)], axis=0).astype(BF)

    prior_parts = unpack_state(prior, pair)
    into = dot_r(we, with_norms(prior_parts, head_lanes(pair, sq_lane, upper)))
    dq = dq + is_late * (cos_b * into[:, :LANES] + sin_b * into[:, LANES:])
    later_parts = unpack_state(later, pair)
    into = dot_r(ve, with_norms(later_parts, sq_lane == 0))
    dk = dk + early * (cos_b * into[:, :LANES] + sin_b * into[:, LANES:])
    kw = kp.astype(F32)
    left = jnp.concatenate([(kw * (cos_b * early)).astype(BF), (kw * (sin_b * early)).astype(BF)], axis=1)
    dv = dv + dot(left, jnp.concatenate(later_parts[:2], axis=0).astype(BF))

    dq = jnp.where(qp.astype(F32) > 0, dq, 0.0).astype(BF)
    dk = jnp.where(kw > 0, dk, 0.0).astype(BF)
    dv = dv.astype(BF)
    for n, part in enumerate((dq, dk, dv)):
        total = jnp.sum(part.astype(F32), axis=0, keepdims=True)
        sums_o[n, :, out] = jnp.broadcast_to(total, (sums_o.shape[1], LANES))
        early_o[n, :, out] = part[:mid]
        late_o[n, :, out] = part[mid:]


def input_kernel(scal, first, keep_early, keep_late, send_early, send_late, w_keep, w_send, out_o):
    @pl.when(pl.program_id(0) == 0)
    def _():
        out_o[...] = first[...]

    rows = lambda early, late: jnp.concatenate([early[0], late[0]], axis=0)
    out_o[...] += dot_r(rows(keep_early, keep_late), w_keep[...]) + dot_r(rows(send_early, send_late), w_send[...])


def place(values, piece_rows, tz, tys, x, y, z, extra, outs):
    xk, xs, yk, ys = outs
    width = xk.shape[-1]
    slot_z = tz ^ z
    pieces = {}
    at = 0
    for ty in tys:
        for tc in range(2):
            for tx in range(2):
                part = values[at * piece_rows : (at + 1) * piece_rows]
                blocks = [part[:, n : n + width] for n in range(0, part.shape[1], width)]
                if extra is not None:
                    blocks.append(extra[at])
                pieces[ty, tc, tx] = jnp.concatenate(blocks, axis=0) if len(blocks) > 1 else blocks[0]
                at += 1
    for ty in tys:
        slot = ty ^ y
        a, b = pieces[ty, 0, 0], pieces[ty, 0, 1]
        xk[slot, slot_z] = jnp.where(x == 0, a, b).astype(BF)
        xs[slot, slot_z] = jnp.where(x == 0, b, a).astype(BF)
    return pieces


def place_y(pieces, tz, tys, x, y, z, outs):
    xk, xs, yk, ys = outs
    slot_z = tz ^ z
    for tx in range(2):
        slot = tx ^ x
        a, b = pieces[0, 1, tx], pieces[1, 1, tx]
        yk[slot, slot_z] = jnp.where(y == 0, a, b).astype(BF)
        ys[slot, slot_z] = jnp.where(y == 0, b, a).astype(BF)


def reduce_grad_kernel(pos_at, scal, a_own, a_oth, b_own, b_oth, kept, near):
    tz = pl.program_id(0)
    x, y, z = (scal[pos_at + n] for n in range(3))
    values = dot_t(a_own[...], b_own[...]) + dot_t(a_oth[...], b_oth[...])
    rows = values.shape[0] // 8
    slot = tz ^ z

    def put(out):
        for n in range(8):
            ty, tc, tx = n // 4, n // 2 % 2, n % 2
            out[slot // 2, tc, tx ^ x, ty ^ y] = values[n * rows : (n + 1) * rows].astype(BF)

    @pl.when(slot % 2 == 0)
    def _():
        put(kept)

    @pl.when(slot % 2 == 1)
    def _():
        put(near)


def expand_grad_kernel(pos_at, scal, a_own, a_oth, b_own, b_oth, m_own, m_oth, c_own, c_oth, *outs):
    tz = pl.program_id(0)
    x, y, z = (scal[pos_at + n] for n in range(3))
    an, ao = a_own[0, 0], a_oth[0, 0]
    parts = [dot(an, b_own[n]) + dot(ao, b_oth[n]) for n in range(b_own.shape[0])]
    parts.append(dot(m_own[0, 0], c_own[...]) + dot(m_oth[0, 0], c_oth[...]))
    values = jnp.concatenate(parts, axis=1)
    pieces = place(values, values.shape[0] // 8, tz, (0, 1), x, y, z, None, outs)
    place_y(pieces, tz, (0, 1), x, y, z, outs)


def share_lanes(entries, devices, at, width):
    n = entries.shape[1]
    share = n // devices
    owner = lax.broadcasted_iota(jnp.int32, (devices, n), 0)
    column = lax.broadcasted_iota(jnp.int32, (devices, n), 1)
    mine = (column >= owner * share) & (column < (owner + 1) * share)
    high, low = high_low(jnp.where(mine, entries, 0.0))
    both = jnp.concatenate([high, low], axis=0).astype(BF)
    source = lax.broadcasted_iota(jnp.int32, (n, width), 0)
    target = lax.broadcasted_iota(jnp.int32, (n, width), 1)
    picks = (target >= at) & (target < at + share) & (lax.rem(source, share) == target - at)
    spread = dot(both, picks.astype(F32).astype(BF))
    return spread[:devices] + spread[devices:]


def heads_grad_kernel(
    pos_at, scal, a_own, a_oth, own_early, own_late, oth_early, oth_late, kept_h, sent_h, sums_1, kept_e, sent_e, sums_2, *refs, devices
):
    outs, table = refs[:-1], refs[-1]
    x, y, z = (scal[pos_at + n] for n in range(3))
    width = outs[0].shape[-1]

    def fill():
        first_core = scal[pos_at - 1] == 0
        ordered = lambda kept, sent: [jnp.where(first_core, kept, sent), jnp.where(first_core, sent, kept)]
        sums_e = jnp.concatenate(ordered(kept_e[...], sent_e[...]), axis=1)
        of_heads = [part for n in range(3) for part in ordered(kept_h[n, 0:1], sent_h[n, 0:1])]
        total = jnp.zeros((devices, width), F32)
        at = 0
        for entries in (
            jnp.concatenate(of_heads[:4], axis=1), jnp.concatenate(of_heads[4:], axis=1), sums_1[2:3], sums_1[0:1], sums_1[1:2],
            sums_e, sums_2[2:3], sums_2[0:1], sums_2[1:2],
        ):
            total = total + share_lanes(entries, devices, at, width)
            at += entries.shape[1] // devices
        table[...] = total

    fill()

    join = lambda early, late: jnp.concatenate(
        [jnp.concatenate([early[n], late[n]], axis=0) for n in range(early.shape[0])], axis=1
    )
    own, other = join(own_early, own_late), join(oth_early, oth_late)
    line = lax.broadcasted_iota(jnp.int32, (8, width), 0)
    for tz in range(a_own.shape[0]):
        values = dot(a_own[tz], own) + dot(a_oth[tz], other)
        extra = []
        for n in range(8):
            high, low = high_low(table[tz * 8 + n : tz * 8 + n + 1])
            extra.append(jnp.where(line == 0, high, jnp.where(line == 1, low, 0.0)))
        pieces = place(values, values.shape[0] // 8, tz, (0, 1), x, y, z, extra, outs)
        place_y(pieces, tz, (0, 1), x, y, z, outs)


class Ring:
    def __init__(self, n_dp):
        self.n_dp = n_dp
        self.devices = 2 * n_dp

    def swap(self, value, bits):
        return lax.ppermute(value, AXES, [(i, i ^ bits) for i in range(self.devices)])

    def core(self, value):
        return self.swap(value, 2)

    def x(self, value):
        return self.swap(value, 1)

    def y(self, value):
        return self.swap(value, 4)

    def z(self, value, step):
        return self.swap(value, 8 * step)


def add_first_kernel(scal, xk, xr, yk, yr, xn, yn):
    wide = lambda ref: ref[0].astype(F32)
    xn[...] = (wide(xk) + wide(xr)).astype(BF)
    yn[...] = (wide(yk) + wide(yr)).astype(BF)


def add_second_kernel(scal, xk, xr, xm, yk, yr, ym, own, z1, z2, z3):
    for n, (keep, got, more) in enumerate(((xk, xr, xm), (yk, yr, ym))):
        total = lambda k: keep[0, k].astype(F32) + got[0, k].astype(F32) + more[k].astype(F32)
        own[n] = total(0)
        for k, out in ((1, z1), (2, z2), (3, z3)):
            out[n] = total(k).astype(BF)


def add_last_kernel(core_at, scal, own, z1, z2, z3, keep, send):
    first = scal[core_at] == 0
    total = lambda n: own[n] + z1[n].astype(F32) + z2[n].astype(F32) + z3[n].astype(F32)
    of_first, of_second = total(0), total(1)
    keep[...] = jnp.where(first, of_first, of_second)
    send[...] = jnp.where(first, of_second, of_first)


def add_second_half_kernel(scal, xk, xr, xm, yk, yr, ym, kept, sent):
    for n, (keep, got, more) in enumerate(((xk, xr, xm), (yk, yr, ym))):
        total = lambda k: keep[0, k].astype(F32) + got[0, k].astype(F32) + more[k].astype(F32)
        for k in range(2):
            kept[k, n] = total(2 * k)
            sent[k, n] = total(2 * k + 1).astype(BF)


def add_third_half_kernel(scal, kept, got, own, sent):
    own[...] = kept[0] + got[0].astype(F32)
    sent[...] = (kept[1] + got[1].astype(F32)).astype(BF)


def add_last_half_kernel(core_at, scal, own, got, keep, send):
    first = scal[core_at] == 0
    of_first, of_second = (own[n] + got[n].astype(F32) for n in range(2))
    keep[...] = jnp.where(first, of_first, of_second)
    send[...] = jnp.where(first, of_second, of_first)


def add_near_kernel(scal, kept, got, own, far):
    own[...] = kept[0].astype(F32) + got[0].astype(F32)
    far[...] = (kept[1].astype(F32) + got[1].astype(F32)).astype(BF)


def add_far_kernel(scal, own, got, xk, xs, yk, ys):
    total = lambda *at: own[at] + got[at].astype(F32)
    for n in range(2):
        xk[n] = total(0, 0, n)
        xs[n] = total(0, 1, n).astype(BF)
        yk[n] = total(1, n, 0)
        ys[n] = total(1, n, 1).astype(BF)


def add_side_kernel(scal, xk, xr, yk, yr, own, xn, yn):
    own[0] = xk[0] + xr[0].astype(F32)
    own[1] = yk[0] + yr[0].astype(F32)
    xn[...] = (xk[1] + xr[1].astype(F32)).astype(BF)
    yn[...] = (yk[1] + yr[1].astype(F32)).astype(BF)


def add_end_kernel(core_at, scal, own, xm, ym, keep, send):
    first = scal[core_at] == 0
    of_first, of_second = own[0] + xm[...].astype(F32), own[1] + ym[...].astype(F32)
    keep[...] = jnp.where(first, of_first, of_second)
    send[...] = jnp.where(first, of_second, of_first)


class Scatter:
    def __init__(self, ring, core_at, name, sent):
        self.ring, self.core_at, self.name = ring, core_at, name
        self.xk, self.xs, self.yk, self.ys = sent

    def send(self, *others):
        self.xr, self.yr = self.ring.x(after(self.xs, *others)), self.ring.y(after(self.ys, *others))

    def first(self, scal, us=0.1):
        shape = self.xk.shape[1:]
        part = lambda a: (a, (1,) + shape, lambda j, s: (1, 0, 0, 0))
        xn, yn = call(
            add_first_kernel, self.name + "_add1", scal, (1,), [part(a) for a in (self.xk, self.xr, self.yk, self.yr)],
            [(shape, BF, None, None)] * 2, us=us,
        )
        self.xn, self.yn = xn, yn
        return xn

    def send_first(self, *others):
        self.xm, self.ym = self.ring.y(after(self.xn, *others)), self.ring.x(after(self.yn, *others))

    def second(self, scal):
        shape = self.xk.shape[1:]
        piece = (2,) + shape[1:]
        part = lambda a: (a, (1,) + shape, lambda j, s: (0, 0, 0, 0))
        whole = lambda a: (a, None, None)
        self.own, *self.sends = call(
            add_second_kernel, self.name + "_add2", scal, (1,),
            [part(self.xk), part(self.xr), whole(self.xm), part(self.yk), part(self.yr), whole(self.ym)],
            [(piece, F32, None, None)] + [(piece, BF, None, None)] * 3,
        )
        return self.own

    def send_second(self, *others):
        self.arrived = [self.ring.z(after(v, *others), k + 1) for k, v in enumerate(self.sends)]

    def last(self, scal):
        piece = self.own.shape[1:]
        keep, send = call(
            functools.partial(add_last_kernel, self.core_at), self.name + "_add3", scal, (1,),
            [(a, None, None) for a in (self.own, *self.arrived)], [(piece, F32, None, None)] * 2,
        )
        return keep, self.ring.core(send)


class HalvingScatter(Scatter):
    def second(self, scal):
        shape = self.xk.shape[1:]
        piece = (2, 2) + shape[1:]
        part = lambda a: (a, (1,) + shape, lambda j, s: (0, 0, 0, 0))
        whole = lambda a: (a, None, None)
        self.kept, self.near = call(
            add_second_half_kernel, self.name + "_add2", scal, (1,),
            [part(self.xk), part(self.xr), whole(self.xm), part(self.yk), part(self.yr), whole(self.ym)],
            [(piece, F32, None, None), (piece, BF, None, None)],
        )
        return self.kept

    def send_second(self):
        self.got = self.ring.z(self.near, 1)

    def third(self, scal):
        piece = self.kept.shape[1:]
        self.own, self.far = call(
            add_third_half_kernel, self.name + "_add3", scal, (1,),
            [(a, None, None) for a in (self.kept, self.got)], [(piece, F32, None, None), (piece, BF, None, None)],
        )
        return self.own

    def send_third(self):
        self.arrived = self.ring.z(self.far, 2)

    def last(self, scal):
        piece = self.own.shape[1:]
        keep, send = call(
            functools.partial(add_last_half_kernel, self.core_at), self.name + "_add4", scal, (1,),
            [(a, None, None) for a in (self.own, self.arrived)], [(piece, F32, None, None)] * 2,
        )
        return keep, self.ring.core(send)


class DepthScatter:
    def __init__(self, ring, core_at, name, sent):
        self.ring, self.core_at, self.name = ring, core_at, name
        self.kept, self.near = sent

    def call(self, kernel, step, scal, ins, outs):
        whole = lambda a: (a, None, None)
        return call(kernel, self.name + step, scal, (), [*map(whole, ins)], [(s, d, None, None) for s, d in outs])

    def send_near(self):
        self.got = self.ring.z(self.near, 1)

    def add_near(self, scal):
        shape = self.kept.shape[1:]
        self.own, self.far = self.call(add_near_kernel, "_add1", scal, (self.kept, self.got), [(shape, F32), (shape, BF)])
        return self.own

    def send_far(self):
        self.got = self.ring.z(self.far, 2)

    def add_far(self, scal):
        shape = self.own.shape[2:]
        self.xk, self.xs, self.yk, self.ys = self.call(
            add_far_kernel, "_add2", scal, (self.own, self.got), [(shape, F32), (shape, BF)] * 2
        )
        return self.xk

    def send_side(self):
        self.xr, self.yr = self.ring.x(self.xs), self.ring.y(self.ys)

    def add_side(self, scal):
        shape = self.xk.shape
        self.own, xn, yn = self.call(
            add_side_kernel, "_add3", scal, (self.xk, self.xr, self.yk, self.yr),
            [(shape, F32), (shape[1:], BF), (shape[1:], BF)],
        )
        self.xm, self.ym = self.ring.y(xn), self.ring.x(yn)
        return self.own

    def last(self, scal):
        shape = self.own.shape[1:]
        keep, send = self.call(
            functools.partial(add_end_kernel, self.core_at), "_add4", scal, (self.own, self.xm, self.ym),
            [(shape, F32)] * 2,
        )
        return keep, self.ring.core(send)


def after(value, *others):
    if not others:
        return value
    return lax.optimization_barrier((value,) + others)[0]


def side_by_side(core_at, scal, own, got):
    first = scal[core_at] == 0
    return [jnp.where(first, own, got), jnp.where(first, got, own)]


def finish_kernel(
    core_at, scal, own, got, reduce_own, reduce_got, expand_own, expand_got,
    heads_o, reduce_o, expand_o, merge_o, *shares_o,
):
    width = own.shape[1]
    rows = heads_o.shape[0]
    for n, part in enumerate(side_by_side(core_at, scal, reduce_own[...], reduce_got[...])):
        reduce_o[:, n * width : (n + 1) * width] = part
    blocks = expand_own.shape[0] // rows - 1
    for n, part in enumerate(side_by_side(core_at, scal, expand_own[...], expand_got[...])):
        for k in range(blocks):
            at = (n * blocks + k) * width
            expand_o[:, at : at + width] = part[k * rows : (k + 1) * rows]
        merge_o[:, n * width : (n + 1) * width] = part[blocks * rows :]
    for n, part in enumerate(side_by_side(core_at, scal, own[...], got[...])):
        for k in range(3):
            at = (2 * k + n) * width
            heads_o[:, at : at + width] = part[k * rows : (k + 1) * rows]
    entries = own[3 * rows :] + got[3 * rows :]
    entries = entries[0:1] + entries[1:2]
    at = 0
    for share in shares_o:
        n = share.shape[1]
        moved = entries if at == 0 else pltpu.roll(entries, width - at, 1)
        share[...] = moved[:, :n]
        at += n


def per_device(
    tokens, w_heads, b_heads, w_merge, b_merge, gain_first, bias_first, w_expand, b_expand,
    w_reduce, b_reduce, gain_second, bias_second, seq_lengths, cotangent,
):
    rows = tokens.shape[0]
    seqs = seq_lengths.shape[1]
    n_dp = lax.axis_size("dp")
    ring = Ring(n_dp)
    head = lax.axis_index("head")
    dp = lax.axis_index("dp")
    core = dp % 2
    place_of = jnp.stack([head, core, head, (dp // 2) % 2, dp // 4]).astype(jnp.int32)
    scal = jnp.concatenate([seq_lengths[0].astype(jnp.int32), place_of])
    head_at, core_at, pos_at = seqs, seqs + 1, seqs + 2
    first_core = core == 0
    line = lambda v: v.reshape(1, -1)
    b_heads, b_merge, gain_first, bias_first, b_expand, b_reduce, gain_second, bias_second = map(
        line, (b_heads, b_merge, gain_first, bias_first, b_expand, b_reduce, gain_second, bias_second)
    )
    wide_shape = (rows, D)
    quarter = 256

    turned = ((4, D // 4, rows), BF, None, None)
    rk, v, state, tcol, trow, tokens_t = call(
        functools.partial(kv_kernel, seqs), "keys_values", scal, (3,),
        [
            (tokens, None, None),
            (w_heads, (D, quarter), lambda j, s: (0, 3 + j)),
            (w_heads, (D, quarter), lambda j, s: (0, 6 + j)),
            (b_heads, (1, quarter), lambda j, s: (0, 3 + j)),
            (b_heads, (1, quarter), lambda j, s: (0, 6 + j)),
        ],
        [
            (wide_shape, BF, (rows, quarter), lambda j, s: (0, j)),
            (wide_shape, BF, (rows, quarter), lambda j, s: (0, j)),
            ((PAIRS + 1, LANES, LANES), BF, None, None),
            ((rows, LANES), F32, None, None),
            ((8, rows), F32, None, None), turned,
        ],
        [pltpu.VMEM((LANES, LANES), F32)],
        us=4,
    )
    prior = ring.x(state)

    fast = n_dp == 16
    order = scal
    if fast:
        tokens_o = ring.core(tokens_t)
    rq, num, den = call(
        local_kernel, "local_attention", scal, (3,),
        [
            (tokens, None, None),
            (w_heads, (D, quarter), lambda j, s: (0, j)),
            (b_heads, (1, quarter), lambda j, s: (0, j)),
            (rk, (rows, quarter), lambda j, s: (0, j)),
            (v, (rows, quarter), lambda j, s: (0, j)),
            (tcol, None, None),
            (trow, None, None),
        ],
        [
            (wide_shape, BF, (rows, quarter), lambda j, s: (0, j)),
            (wide_shape, F32, (rows, quarter), lambda j, s: (0, j)),
            (wide_shape, F32, (rows, quarter), lambda j, s: (0, j)),
        ],
        [pltpu.VMEM((rows, rows), F32)],
        us=6,
    )

    if fast:
        order = after(scal, tokens_o)
    att, inv, mixed, xhat, scale, normed, second, turned_own, act, slope = call(
        functools.partial(ffn_kernel, head_at), "feed_forward", order, (FFN_STEPS,),
        [
            (rq, None, None), (num, None, None), (den, None, None), (prior, None, None),
            (tcol, None, None), (tokens, None, None), (w_merge, None, None), (b_merge, None, None),
            (gain_first, None, None), (bias_first, None, None), (b_reduce, None, None),
            (w_expand, (D, FFN_BLOCK), lambda j, s: (0, j)),
            (b_expand, (1, FFN_BLOCK), lambda j, s: (0, j)),
            (w_reduce, (FFN_BLOCK, D), lambda j, s: (j, 0)),
        ],
        [
            (wide_shape, F32, None, None), (wide_shape, F32, None, None), (wide_shape, BF, None, None),
            (wide_shape, F32, None, None), ((rows, LANES), F32, None, None), (wide_shape, BF, None, None),
            (wide_shape, F32, None, None), ((2, 4, D // 4, rows), BF, None, None),
            ((rows, FF), BF, (rows, FFN_BLOCK), lambda j, s: (0, j)),
            ((rows, FF), BF, (rows, FFN_BLOCK), lambda j, s: (0, j)),
        ],
        us=11, vmem=VMEM_FFN,
    )

    half_shape = (rows, D // 2)
    result, grad_second, branch, bg_keep, bg_send, sums_second = call(
        functools.partial(second_kernel, core_at), "second_norm", scal, (1,),
        [(second, None, None), (cotangent, None, None), (gain_second, None, None), (bias_second, None, None)],
        [
            (wide_shape, BF, None, None), (wide_shape, F32, None, None), (wide_shape, BF, None, None),
            (half_shape, BF, None, None), (half_shape, BF, None, None), ((8, D), F32, None, None),
        ],
        us=2.6,
    )

    devices = ring.devices
    small, large = D // devices, FF // devices
    whole = lambda a: (a, None, None)
    part = lambda a, n: (a, (1, 1, D // 4, rows), lambda j, s: (n, j, 0, 0))
    by_z = lambda a: (a, (1, D // 4, rows), lambda j, s: (j, 0, 0))
    by_col = lambda a: (a, (rows, FF // 4), lambda j, s: (0, j))

    def group(kernel, name, scal, grid, ins, piece_rows, us, scratch=(), kind=Scatter):
        shape = (2, 4, piece_rows, D // 2)
        sent = call(
            functools.partial(kernel, pos_at), name, scal, grid, ins, [(shape, BF, None, None)] * 4, scratch, us
        )
        return kind(ring, core_at, name, sent)

    ff_half = FF_STEPS // 2
    in_hbm = lambda a: (a, None, pltpu.HBM)
    hidden = ((ff_half, rows, FF_BLOCK), BF, None, None)
    hidden_sums = ((1, FF // 2), F32, None, None)
    buffers = [
        pltpu.VMEM((ff_half, D, FF_BLOCK), BF), pltpu.VMEM((ff_half, FF_BLOCK, D), BF),
        pltpu.SemaphoreType.DMA((2, ff_half)),
    ]
    hidden_in = [whole(branch), whole(slope), in_hbm(w_expand), in_hbm(w_reduce)]
    pg_send, sum_sent, partial = call(
        functools.partial(back_sent_kernel, core_at), "feed_forward_back_sent", scal, (),
        [*hidden_in, whole(grad_second)],
        [hidden, hidden_sums, (wide_shape, F32, None, None)], buffers,
        us=5, vmem=VMEM_BACK,
    )
    order = scal
    if fast:
        pg_o = ring.core(pg_send)
        act_o, turned_other, bg_o = map(ring.core, (act, turned_own, bg_send))
        pieces = ((2, 2, 2, 2, large, D // 2), BF, None, None)
        sent = call(
            functools.partial(reduce_grad_kernel, pos_at), "grad_reduce", after(scal, partial, turned_other), (4,),
            [by_col(act), by_col(act_o), whole(bg_keep), whole(bg_o)], [pieces, pieces], us=6,
        )
        reduced = DepthScatter(ring, core_at, "grad_reduce", sent)
        reduced.send_near()
        order = after(scal, reduced.near)

    pg_keep, grad_first, mg_keep, mg_send, w_att, e_att, later, sum_kept, sums_first = call(
        functools.partial(back_kernel, core_at), "feed_forward_back", order, (),
        [
            *hidden_in,
            (partial, None, None), (gain_first, None, None), (xhat, None, None), (scale, None, None),
            (w_merge, None, None), (att, None, None), (inv, None, None), (rq, None, None), (tcol, None, None),
        ],
        [
            hidden, (wide_shape, F32, None, None), (half_shape, BF, None, None), (half_shape, BF, None, None),
            (wide_shape, BF, None, None), ((rows, LANES), BF, None, None),
            ((PAIRS + 1, LANES, LANES), BF, None, None), hidden_sums, ((8, D), F32, None, None),
        ],
        [pltpu.VMEM(wide_shape, F32), *buffers],
        us=COST_BACK, vmem=VMEM_BACK,
    )
    later = ring.x(later)

    if fast:
        mg_o = ring.core(mg_send)
        expanded = group(
            expand_grad_kernel, "grad_expand", scal, (4,),
            [
                part(turned_own, 1), part(turned_other, 1), whole(pg_keep), whole(pg_o),
                part(turned_own, 0), part(turned_other, 0), whole(mg_keep), whole(mg_o),
            ],
            5 * small, COST_EXPAND, kind=HalvingScatter,
        )
        expanded.send(later)
        order = after(scal, expanded.xs, later)

    by_pair = [*map(whole, (rq, rk, v, w_att))]
    both_states = [whole(e_att), whole(prior), whole(later), whole(tcol)]
    pj_out = [((3, rows // 2, D // 2), BF, None, None)] * 2
    pj_sums = ((3, 8, D // 2), F32, None, None)
    table = ((rows, rows), F32, None, None)
    *pj_send, sum_heads_sent, weights, weights_t = call(
        functools.partial(attn_sent_kernel, head_at, core_at), "attention_back_sent", order, (),
        [*by_pair, *both_states, whole(trow)], [*pj_out, pj_sums, table, table], us=COST_SENT, vmem=VMEM_ATTN,
    )
    order = scal
    if fast:
        pj_o = [ring.core(v) for v in pj_send]
        order = after(scal, reduced.add_near(after(scal, pj_send[0])))
        reduced.send_far()
    *pj_keep, sum_heads_kept = call(
        functools.partial(attn_kept_kernel, head_at, core_at), "attention_back_kept", order, (),
        [*by_pair, *both_states, whole(weights), whole(weights_t)], [*pj_out, pj_sums], us=COST_KEPT, vmem=VMEM_ATTN,
    )

    if fast:
        order = after(scal, expanded.first(after(scal, pj_keep[0])))
        expanded.send_first()
        heads = group(
            functools.partial(heads_grad_kernel, devices=devices), "grad_heads", order, (),
            [
                *map(whole, (tokens_t, tokens_o, *pj_keep, *pj_o)),
                *map(whole, (sum_heads_kept, sum_heads_sent, sums_first, sum_kept, sum_sent, sums_second)),
            ],
            3 * small + 8, COST_HEADS, [pltpu.VMEM((devices, D // 2), F32)],
        )
        heads.send()
        order = after(scal, heads.xs)

    of_part = lambda a: (a, (1, rows // 2, D // 2), lambda j, s: (j, 0, 0))
    (input_grad,) = call(
        input_kernel, "input_grad", order, (3,),
        [
            whole(grad_first), *map(of_part, (*pj_keep, *pj_send)),
            (w_heads, (D, D // 2), lambda j, s: (0, 2 * j + s[core_at])),
            (w_heads, (D, D // 2), lambda j, s: (0, 2 * j + 1 - s[core_at])),
        ],
        [(wide_shape, F32, None, None)],
        us=COST_INPUT,
    )

    if fast:
        order = reduced.add_far(after(scal, input_grad))
        order = expanded.second(after(scal, order))
        expanded.send_second()
        reduced.send_side()
        order = heads.first(after(scal, order))
        heads.send_first()
        order = expanded.third(after(scal, order))
        expanded.send_third()
        order = heads.second(after(scal, order))
        heads.send_second()
        order = reduced.add_side(after(scal, order))
        expand_own, expand_got = expanded.last(after(scal, order))
        reduce_own, reduce_got = reduced.last(after(scal, expand_own))
        heads_own, heads_got = heads.last(after(scal, reduce_own))
        out = lambda n, m: ((n, m), F32, None, None)
        counts = (2 * small, small, small, small, small, large, small, small, small)
        w_heads_grad, w_reduce_grad, w_expand_grad, w_merge_grad, *shares = call(
            functools.partial(finish_kernel, core_at), "finish", scal, (),
            [*map(whole, (heads_own, heads_got, reduce_own, reduce_got, expand_own, expand_got))],
            [out(small, 3 * D), out(large, D), out(small, FF), out(small, D), *(out(1, n) for n in counts)],
        )
        shares = [share.reshape(-1) for share in shares]
        grads = (
            w_heads_grad, *shares[:2], w_merge_grad, *shares[2:5], w_expand_grad, shares[5], w_reduce_grad,
            *shares[6:],
        )
    else:
        by_core = lambda keep, send: jnp.concatenate(
            [jnp.where(first_core, keep, send), jnp.where(first_core, send, keep)], axis=1
        )
        flat = lambda v: v.transpose(1, 0, 2).reshape(rows, -1)
        by_heads = lambda keep, send: jnp.concatenate(
            [by_core(keep[n], send[n]) for n in range(3)], axis=1
        )
        pj_keep, pj_send = (jnp.concatenate(v, axis=1) for v in (pj_keep, pj_send))
        sum_heads = by_heads(sum_heads_kept, sum_heads_sent)[0]
        scatter = lambda v: lax.psum_scatter(v, AXES, scatter_dimension=0, tiled=True)
        grads = (
            scatter(dot_t(tokens, by_heads(pj_keep, pj_send))),
            scatter(sum_heads[: 2 * D]), scatter(sum_heads[2 * D :]),
            scatter(dot_t(mixed, by_core(mg_keep, mg_send))),
            scatter(sums_first[2]), scatter(sums_first[0]), scatter(sums_first[1]),
            scatter(dot_t(normed, by_core(flat(pg_keep), flat(pg_send)))),
            scatter(by_core(sum_kept, sum_sent)[0]),
            scatter(dot_t(act, branch)),
            scatter(sums_second[2]), scatter(sums_second[0]), scatter(sums_second[1]),
        )
    return (result, input_grad) + tuple(grads)


def solution(mesh):
    in_specs = (P(AXES, None),) + (P(),) * 12 + (P("dp", None), P(AXES, None))
    row, one = P(AXES, None), P(AXES)
    out_specs = (row, row, row, one, one, row, one, one, one, row, one, row, one, one, one)
    return jax.shard_map(
        per_device, mesh=mesh, in_specs=in_specs, out_specs=out_specs, check_vma=False
    )
```

```python
import functools
import math

import jax
import jax.numpy as jnp
from jax import lax
from jax.experimental import pallas as pl
from jax.experimental.pallas import tpu as pltpu
from jax.sharding import PartitionSpec as P

D = 768
PAIRS = 6
FF = 3072
LANES = 128
HALF = 64
BF = jnp.bfloat16
F32 = jnp.float32
AXES = ("dp", "head")
VMEM_LIMIT = 8 << 20
VMEM_FFN = 16 << 20
VMEM_ATTN = 10 << 20
FF_BLOCK = 768
FFN_BLOCK = 1024
FFN_STEPS = FF // FFN_BLOCK
MATMUL_PER_US = 1.15e9
COST_EXPAND = 1
VMEM_BACK = 16 << 20
COST_KEPT = 0.5
COST_BACK = 3
COST_SENT = 0.5
COST_HEADS = 0.1
COST_INPUT = 0.1
FF_STEPS = FF // FF_BLOCK


def dot(a, b):
    return jnp.dot(a, b, preferred_element_type=F32)


def dot_t(a, b):
    return lax.dot_general(a, b, (((0,), (0,)), ((), ())), preferred_element_type=F32)


def dot_r(a, b):
    return lax.dot_general(a, b, (((1,), (1,)), ((), ())), preferred_element_type=F32)


def call(kernel, name, scal, grid, ins, outs, scratch=(), us=0.1, vmem=VMEM_LIMIT):
    def spec(b, m):
        if b is None:
            return pl.BlockSpec(memory_space=pltpu.VMEM if m is None else m)
        return pl.BlockSpec(b, m)

    in_specs = [spec(b, m) for _, b, m in ins]
    out_specs = [spec(b, m) for _, _, b, m in outs]
    return pl.pallas_call(
        kernel,
        name=name,
        grid_spec=pltpu.PrefetchScalarGridSpec(
            num_scalar_prefetch=1,
            grid=grid,
            in_specs=in_specs,
            out_specs=out_specs,
            scratch_shapes=list(scratch),
        ),
        out_shape=[jax.ShapeDtypeStruct(s, d) for s, d, _, _ in outs],
        compiler_params=pltpu.CompilerParams(vmem_limit_bytes=vmem),
        cost_estimate=pl.CostEstimate(flops=int(us * MATMUL_PER_US), bytes_accessed=1, transcendentals=0),
    )(scal, *[a for a, _, _ in ins])


def lane_masks():
    lane = lax.broadcasted_iota(jnp.int32, (1, LANES), 1)
    even = (lane < HALF).astype(F32)
    return lane, even.astype(BF), (1.0 - even).astype(BF)


def both_heads(pair):
    lane, even, odd = lane_masks()
    return jnp.concatenate([pair * even, pair * odd], axis=0)


def own_lanes(stacked):
    rows = stacked.shape[0] // 2
    lane = lax.broadcasted_iota(jnp.int32, (1, LANES), 1)
    return jnp.where(lane < HALF, stacked[:rows], stacked[rows:])


def square_masks():
    row = lax.broadcasted_iota(jnp.int32, (LANES, LANES), 0)
    lane = lax.broadcasted_iota(jnp.int32, (LANES, LANES), 1)
    upper = row < HALF
    return lane, upper, upper == (lane < HALF)


def high_low(v):
    high = v.astype(BF).astype(F32)
    return high, v - high


def tables(scal, rows, seqs, tcol, trow):
    pos = lax.broadcasted_iota(jnp.int32, (1, rows), 1) + scal[seqs] * rows
    seg = jnp.zeros((1, rows), jnp.int32)
    first = jnp.zeros((1, rows), jnp.int32)
    length = jnp.ones((1, rows), jnp.int32)
    at_boundary = jnp.int32(0)
    begin = jnp.int32(0)
    for s in range(seqs):
        end = begin + scal[s]
        inside = (pos >= begin) & (pos < end)
        first = jnp.where(inside, begin, first)
        length = jnp.where(inside, jnp.maximum(scal[s], 1), length)
        seg = seg + (pos >= end).astype(jnp.int32)
        at_boundary = at_boundary + (rows - 1 >= end).astype(jnp.int32)
        begin = end
    live = (seg < seqs).astype(F32)
    angle = 0.5 * math.pi * (pos - first).astype(F32) / length.astype(F32)
    cos_w = jnp.cos(angle) * live
    sin_w = jnp.sin(angle) * live
    crossing = (seg == at_boundary).astype(F32)
    which = lax.broadcasted_iota(jnp.int32, (LANES, rows), 0)
    table = jnp.zeros((LANES, rows), F32)
    for n, entry in enumerate((cos_w, sin_w, seg.astype(F32), cos_w * crossing, sin_w * crossing)):
        table = jnp.where(which == n, entry, table)
    trow[...] = table[:8]
    tcol[...] = table.T


def pack_state(both, norm_cos, norm_sin, pair, norms):
    lane, upper, diag = square_masks()
    packed = jnp.where(diag, both[:LANES, :LANES], pltpu.roll(both[LANES:, :LANES], HALF, 1))
    cos_high, cos_low = high_low(norm_cos)
    sin_high, sin_low = high_low(norm_sin)
    for n, part in enumerate((cos_high, cos_low, sin_high, sin_low)):
        norms = jnp.where(lane == 4 * pair + n, part, norms)
    return packed.astype(BF), norms


def unpack_state(state_ref, pair):
    lane, upper, diag = square_masks()
    packed = state_ref[pair].astype(F32)
    norms = state_ref[PAIRS].astype(F32)
    of_cos = jnp.where(diag, packed, 0.0)
    of_sin = jnp.where(diag, pltpu.roll(packed, HALF, 1), 0.0)
    pick = lambda n: jnp.sum(
        jnp.where((lane == 4 * pair + n) | (lane == 4 * pair + n + 1), norms, 0.0), axis=1, keepdims=True
    )
    return of_cos, of_sin, pick(0), pick(2)


def turn(value, out):
    turned = value.T
    share = out.shape[1]
    for n in range(out.shape[0]):
        out[n] = turned[n * share : (n + 1) * share]


def kv_kernel(seqs, scal, tok, wk, wv, bk, bv, rk_o, v_o, st_o, tcol, trow, turned_o, norms):
    step = pl.program_id(0)
    rows = tok.shape[0]

    @pl.when(step == 0)
    def _():
        tables(scal, rows, seqs, tcol, trow)
        norms[...] = jnp.zeros_like(norms)
        turn(tok[...], turned_o)

    rk = jnp.maximum(dot(tok[...], wk[...]) + bk[...].astype(F32), 0.0).astype(BF)
    v = (dot(tok[...], wv[...]) + bv[...].astype(F32)).astype(BF)
    rk_o[...] = rk
    v_o[...] = v
    cos_b, sin_b = tcol[:, 3:4], tcol[:, 4:5]
    ones = jnp.ones((rows, LANES), BF)
    for n in range(2):
        pair = 2 * step + n
        cols = slice(n * LANES, (n + 1) * LANES)
        kp = rk[:, cols].astype(F32)
        left = jnp.concatenate([(kp * cos_b).astype(BF), (kp * sin_b).astype(BF)], axis=1)
        both = dot_t(left, jnp.concatenate([v[:, cols], ones], axis=1))
        packed, new_norms = pack_state(both, both[:LANES, LANES:], both[LANES:, LANES:], pair, norms[...])
        st_o[pair] = packed
        norms[...] = new_norms

    st_o[PAIRS] = norms[...].astype(BF)


def weights_block(tcol, trow, transposed):
    rows = tcol.shape[0]
    down = lax.broadcasted_iota(jnp.int32, (rows, rows), 0)
    along = lax.broadcasted_iota(jnp.int32, (rows, rows), 1)
    same = tcol[:, 2:3] == trow[2:3, :]
    causal = (down <= along) if transposed else (along <= down)
    value = tcol[:, 0:1] * trow[0:1, :] + tcol[:, 1:2] * trow[1:2, :]
    return jnp.where(same & causal, value, 0.0)


def weigh(stacked, weights):
    rows = weights.shape[0]
    return jnp.concatenate([stacked[:rows] * weights, stacked[rows:] * weights], axis=0).astype(BF)


def local_kernel(scal, tok, wq, bq, rk, v, tcol, trow, rq_o, num_o, den_o, weights):
    step = pl.program_id(0)
    rows = tok.shape[0]
    mid = rows // 2

    @pl.when(step == 0)
    def _():
        weights[...] = weights_block(tcol, trow, False)

    rq = jnp.maximum(dot(tok[...], wq[...]) + bq[...].astype(F32), 0.0).astype(BF)
    rq_o[...] = rq
    ones = jnp.ones((rows, LANES), BF)
    for n in range(2):
        cols = slice(n * LANES, (n + 1) * LANES)
        kp = rk[:, cols]
        values = jnp.concatenate([v[:, cols], ones], axis=1)
        first = weigh(dot_r(both_heads(rq[:, cols]), kp[:mid]), weights[:, :mid])
        second = weigh(dot_r(both_heads(rq[mid:, cols]), kp[mid:]), weights[mid:, mid:])
        sums = dot(first, values[:mid])
        late = dot(second, values[mid:])
        for own, out in ((slice(0, LANES), num_o), (slice(LANES, 2 * LANES), den_o)):
            total = own_lanes(sums[:, own])
            out[:mid, cols] = total[:mid]
            out[mid:, cols] = total[mid:] + own_lanes(late[:, own])


def normalise(entries):
    mean = jnp.mean(entries, axis=1, keepdims=True)
    centred = entries - mean
    var = jnp.mean(centred * centred, axis=1, keepdims=True)
    scale = lax.rsqrt(var + 1e-05)
    return centred * scale, scale


def merge_heads(
    head_at, scal, rq, num, den, st, tcol, tok, w_merge, b_merge, gain, bias, b_red,
    att_o, inv_o, mixed_o, xhat_o, scale_o, normed_o, acc_o, turned_o,
):
    cross = (scal[head_at] == 1).astype(F32)
    cos_b, sin_b = tcol[:, 3:4] * cross, tcol[:, 4:5] * cross
    sq_lane, upper, diag = square_masks()
    for pair in range(PAIRS):
        cols = slice(pair * LANES, (pair + 1) * LANES)
        qp = rq[:, cols].astype(F32)
        of_cos, of_sin, norm_cos, norm_sin = unpack_state(st, pair)
        top = jnp.concatenate([of_cos, jnp.where(diag, norm_cos, 0.0)], axis=1)
        low = jnp.concatenate([of_sin, jnp.where(diag, norm_sin, 0.0)], axis=1)
        right = jnp.concatenate([top, low], axis=0).astype(BF)
        left = jnp.concatenate([(qp * cos_b).astype(BF), (qp * sin_b).astype(BF)], axis=1)
        prior = dot(left, right)
        inverse = 1.0 / (den[:, cols] + prior[:, LANES:] + 1.0)
        attended = (num[:, cols] + prior[:, :LANES]) * inverse
        att_o[:, cols] = attended
        inv_o[:, cols] = inverse
        mixed_o[:, cols] = attended.astype(BF)
    first_in = tok[...].astype(F32) + dot(mixed_o[...], w_merge[...]) + b_merge[...].astype(F32)
    xhat, scale = normalise(first_in)
    normed = xhat * gain[...].astype(F32) + bias[...].astype(F32)
    xhat_o[...] = xhat
    scale_o[...] = jnp.broadcast_to(scale, scale_o.shape)
    normed_o[...] = normed.astype(BF)
    acc_o[...] = normed + b_red[...].astype(F32)
    turn(mixed_o[...], turned_o.at[0])
    turn(normed_o[...], turned_o.at[1])


def expand_reduce(normed, w_exp, b_exp, w_red, act_o, slope_o, acc_o):
    rows = normed.shape[0]
    pre = [dot(normed[at : at + rows // 2], w_exp[...]) + b_exp[...].astype(F32) for at in (0, rows // 2)]
    for at, x in zip((0, rows // 2), pre):
        part = slice(at, at + rows // 2)
        cdf = 0.5 + 0.5 * lax.erf(x * (2.0**-0.5))
        pdf = jnp.exp(-0.5 * x * x) * (1.0 / math.sqrt(2.0 * math.pi))
        act = (x * cdf).astype(BF)
        act_o[part] = act
        slope_o[part] = (cdf + x * pdf).astype(BF)
        acc_o[part] += dot(act, w_red[...])


def ffn_kernel(head_at, scal, *refs):
    w_exp, b_exp, w_red = refs[11:14]
    normed_o, acc_o = refs[19:21]
    act_o, slope_o = refs[22:]

    @pl.when(pl.program_id(0) == 0)
    def _():
        merge_heads(head_at, scal, *refs[:11], *refs[14:22])

    expand_reduce(normed_o, w_exp, b_exp, w_red, act_o, slope_o, acc_o)


def second_kernel(core_at, scal, second, cot, gain, bias, out_o, grad_o, full_o, keep_o, send_o, sums_o):
    xhat, scale = normalise(second[...])
    gain_w = gain[...].astype(F32)
    out_o[...] = (xhat * gain_w + bias[...].astype(F32)).astype(BF)
    cot_w = cot[...].astype(F32)
    t = cot_w * gain_w
    grad = scale * (
        t - jnp.mean(t, axis=1, keepdims=True) - xhat * jnp.mean(t * xhat, axis=1, keepdims=True)
    )
    low = grad.astype(BF)
    grad_o[...] = grad
    full_o[...] = low
    first = scal[core_at] == 0
    half = D // 2
    left, right = grad[:, :half], grad[:, half:]
    keep_o[...] = jnp.where(first, left, right).astype(BF)
    send_o[...] = jnp.where(first, right, left).astype(BF)
    sums_o[0:1] = jnp.sum(cot_w * xhat, axis=0, keepdims=True)
    sums_o[1:2] = jnp.sum(cot_w, axis=0, keepdims=True)
    sums_o[2:3] = jnp.sum(low.astype(F32), axis=0, keepdims=True)


def head_lanes(pair, lane, first):
    at = 4 * pair + jnp.where(first, 0, 2)
    return (lane == at) | (lane == at + 1)


def weight_copies(half, w_exp, w_red, exp_buf, red_buf, sems, n):
    at = pl.ds(pl.multiple_of((half * exp_buf.shape[0] + n) * FF_BLOCK, FF_BLOCK), FF_BLOCK)
    return (
        pltpu.make_async_copy(w_red.at[at, :], red_buf.at[n], sems.at[0, n]),
        pltpu.make_async_copy(w_exp.at[:, at], exp_buf.at[n], sems.at[1, n]),
    )


def back_steps(half, full, slope, w_exp, w_red, out_o, bexp_o, exp_buf, red_buf, sems):
    blocks = exp_buf.shape[0]
    copies = [weight_copies(half, w_exp, w_red, exp_buf, red_buf, sems, n) for n in range(blocks)]
    for pair in copies:
        for copy in pair:
            copy.start()
    total = None
    for n, (of_red, of_exp) in enumerate(copies):
        cols = slice(n * FF_BLOCK, (n + 1) * FF_BLOCK)
        at = pl.ds(pl.multiple_of((half * blocks + n) * FF_BLOCK, FF_BLOCK), FF_BLOCK)
        of_red.wait()
        pre_grad = (dot_r(full[...], red_buf[n]) * slope[:, at].astype(F32)).astype(BF)
        bexp_o[:, cols] = jnp.sum(pre_grad.astype(F32), axis=0, keepdims=True)
        out_o[n] = pre_grad
        of_exp.wait()
        part = dot_r(pre_grad, exp_buf[n])
        total = part if total is None else total + part
    return total


def back_sent_kernel(core_at, scal, full, slope, w_exp, w_red, grad2, sent_o, bexp_o, acc, exp_buf, red_buf, sems):
    half = 1 - scal[core_at]
    acc[...] = grad2[...] + back_steps(half, full, slope, w_exp, w_red, sent_o, bexp_o, exp_buf, red_buf, sems)


def back_kernel(
    core_at, scal, full, slope, w_exp, w_red, acc_in, gain, xhat, scale, w_merge, att, inv, rq, tcol,
    kept_o, first_o, mk_o, ms_o, w_o, e_o, st_o, bexp_o, sums_o,
    acc, exp_buf, red_buf, sems,
):
    half = scal[core_at]
    acc[...] = acc_in[...] + back_steps(half, full, slope, w_exp, w_red, kept_o, bexp_o, exp_buf, red_buf, sems)
    back_rest(
        core_at, scal, acc, gain, xhat, scale, w_merge, att, inv, rq, tcol,
        first_o, mk_o, ms_o, w_o, e_o, st_o, sums_o,
    )


def back_rest(
    core_at, scal, acc, gain, xhat, scale, w_merge, att, inv, rq, tcol,
    first_o, mk_o, ms_o, w_o, e_o, st_o, sums_o,
):
    grad_normed = acc[...]
    xh = xhat[...]
    t = grad_normed * gain[...].astype(F32)
    first = scale[:, 0:1] * (
        t - jnp.mean(t, axis=1, keepdims=True) - xh * jnp.mean(t * xh, axis=1, keepdims=True)
    )
    low = first.astype(BF)
    first_o[...] = first
    sums_o[0:1] = jnp.sum(grad_normed * xh, axis=0, keepdims=True)
    sums_o[1:2] = jnp.sum(grad_normed, axis=0, keepdims=True)
    sums_o[2:3] = jnp.sum(low.astype(F32), axis=0, keepdims=True)
    is_first = scal[core_at] == 0
    left, right = first[:, : D // 2], first[:, D // 2 :]
    mk_o[...] = jnp.where(is_first, left, right).astype(BF)
    ms_o[...] = jnp.where(is_first, right, left).astype(BF)
    cos_b, sin_b = tcol[:, 3:4], tcol[:, 4:5]
    w = (dot_r(low, w_merge[...]).astype(BF).astype(F32) * inv[...]).astype(BF)
    w_o[...] = w
    high, rest = high_low(w.astype(F32) * att[...])
    column = lax.broadcasted_iota(jnp.int32, (D, LANES), 0)
    target = lax.broadcasted_iota(jnp.int32, (D, LANES), 1)
    picks = (target == 2 * (column // HALF)).astype(F32).astype(BF)
    e_high, e_low = high_low(-(dot(high.astype(BF), picks) + dot(rest.astype(BF), picks)))
    e = (e_high + pltpu.roll(e_low, 1, 1)).astype(BF)
    e_o[...] = e
    norms = jnp.zeros((LANES, LANES), F32)
    sq_lane, upper, diag = square_masks()
    for pair in range(PAIRS):
        cols = slice(pair * LANES, (pair + 1) * LANES)
        qp = rq[:, cols].astype(F32)
        left = jnp.concatenate([(qp * cos_b).astype(BF), (qp * sin_b).astype(BF)], axis=1)
        both = dot_t(left, jnp.concatenate([w[:, cols], e], axis=1))
        mine = head_lanes(pair, sq_lane, upper)
        norm = lambda part: jnp.sum(jnp.where(mine, part, 0.0), axis=1, keepdims=True)
        packed, norms = pack_state(both, norm(both[:LANES, LANES:]), norm(both[LANES:, LANES:]), pair, norms)
        st_o[pair] = packed
    st_o[PAIRS] = norms.astype(BF)


def attn_sent_kernel(head_at, core_at, scal, rq, rk, v, w, e, prior, later, tcol, trow, early_o, late_o, sums_o, weights, weights_t):
    weights[...] = weights_block(tcol, trow, False)
    weights_t[...] = weights_block(tcol, trow, True)
    first = (1 - scal[core_at]) * (PAIRS // 2)
    attn_back(head_at, first, scal, rq, rk, v, w, e, prior, later, tcol, weights, weights_t, early_o, late_o, sums_o)


def attn_kept_kernel(head_at, core_at, scal, rq, rk, v, w, e, prior, later, tcol, weights, weights_t, early_o, late_o, sums_o):
    first = scal[core_at] * (PAIRS // 2)
    attn_back(head_at, first, scal, rq, rk, v, w, e, prior, later, tcol, weights, weights_t, early_o, late_o, sums_o)


def attn_back(head_at, first, scal, rq, rk, v, w, e, prior, later, tcol, weights, weights_t, early_o, late_o, sums_o):
    for n in range(PAIRS // 2):
        attn_back_pair(
            head_at, first + n, n, scal, rq, rk, v, w, e, prior, later, tcol, weights, weights_t, early_o, late_o, sums_o
        )


def attn_back_pair(
    head_at, pair, slot, scal, rq, rk, v, w, e, prior, later, tcol, weights, weights_t, early_o, late_o, sums_o
):
    rows = rq.shape[0]
    mid = rows // 2
    cols = pl.ds(pl.multiple_of(pair * LANES, LANES), LANES)
    out = slice(slot * LANES, (slot + 1) * LANES)

    qp, kp, vp, wp = rq[:, cols], rk[:, cols], v[:, cols], w[:, cols]
    lane, even, odd = lane_masks()
    of_even = ((lane == 4 * pair) | (lane == 4 * pair + 1)).astype(F32).astype(BF)
    of_odd = ((lane == 4 * pair + 2) | (lane == 4 * pair + 3)).astype(F32).astype(BF)
    ones = jnp.ones((rows, LANES), BF)
    we = jnp.concatenate([wp, e[...]], axis=1)
    by_head = (jnp.concatenate([even, of_even], axis=1), jnp.concatenate([odd, of_odd], axis=1))
    ve = jnp.concatenate([vp, ones], axis=1)
    stack = lambda a, lo, hi: jnp.concatenate([a[lo:hi] * m for m in by_head], axis=0)

    grads = weigh(dot_r(stack(we, 0, rows), ve[:mid]), weights[:, :mid])
    dq = own_lanes(dot(grads, kp[:mid]))
    grads = weigh(dot_r(stack(we, mid, rows), ve[mid:]), weights[mid:, mid:])
    dq_late = own_lanes(dot(grads, kp[mid:]))

    grads = weigh(dot_r(stack(ve, 0, rows), we[mid:]), weights_t[:, mid:])
    dk = own_lanes(dot(grads, qp[mid:]))
    grads = weigh(dot_r(stack(ve, 0, mid), we[:mid]), weights_t[:mid, :mid])
    dk_early = own_lanes(dot(grads, qp[:mid]))

    scores = weigh(dot_r(both_heads(kp), qp[mid:]), weights_t[:, mid:])
    dv = own_lanes(dot(scores, wp[mid:]))
    scores = weigh(dot_r(both_heads(kp[:mid]), qp[:mid]), weights_t[:mid, :mid])
    dv_early = own_lanes(dot(scores, wp[:mid]))

    dq = jnp.concatenate([dq[:mid], dq[mid:] + dq_late], axis=0)
    dk = jnp.concatenate([dk[:mid] + dk_early, dk[mid:]], axis=0)
    dv = jnp.concatenate([dv[:mid] + dv_early, dv[mid:]], axis=0)

    sq_lane, upper, diag = square_masks()
    cos_b, sin_b = tcol[:, 3:4], tcol[:, 4:5]
    is_late = (scal[head_at] == 1).astype(F32)
    early = 1.0 - is_late

    def with_norms(parts, where):
        side = lambda total, norm: jnp.concatenate([total, jnp.where(where, norm, 0.0)], axis=1)
        of_cos, of_sin, norm_cos, norm_sin = parts
        return jnp.concatenate([side(of_cos, norm_cos), side(of_sin, norm_sin)], axis=0).astype(BF)

    prior_parts = unpack_state(prior, pair)
    into = dot_r(we, with_norms(prior_parts, head_lanes(pair, sq_lane, upper)))
    dq = dq + is_late * (cos_b * into[:, :LANES] + sin_b * into[:, LANES:])
    later_parts = unpack_state(later, pair)
    into = dot_r(ve, with_norms(later_parts, sq_lane == 0))
    dk = dk + early * (cos_b * into[:, :LANES] + sin_b * into[:, LANES:])
    kw = kp.astype(F32)
    left = jnp.concatenate([(kw * (cos_b * early)).astype(BF), (kw * (sin_b * early)).astype(BF)], axis=1)
    dv = dv + dot(left, jnp.concatenate(later_parts[:2], axis=0).astype(BF))

    dq = jnp.where(qp.astype(F32) > 0, dq, 0.0).astype(BF)
    dk = jnp.where(kw > 0, dk, 0.0).astype(BF)
    dv = dv.astype(BF)
    for n, part in enumerate((dq, dk, dv)):
        total = jnp.sum(part.astype(F32), axis=0, keepdims=True)
        sums_o[n, :, out] = jnp.broadcast_to(total, (sums_o.shape[1], LANES))
        early_o[n, :, out] = part[:mid]
        late_o[n, :, out] = part[mid:]


def input_kernel(scal, first, keep_early, keep_late, send_early, send_late, w_keep, w_send, out_o):
    @pl.when(pl.program_id(0) == 0)
    def _():
        out_o[...] = first[...]

    rows = lambda early, late: jnp.concatenate([early[0], late[0]], axis=0)
    out_o[...] += dot_r(rows(keep_early, keep_late), w_keep[...]) + dot_r(rows(send_early, send_late), w_send[...])


def place(values, piece_rows, tz, tys, x, y, z, extra, outs):
    xk, xs, yk, ys = outs
    width = xk.shape[-1]
    slot_z = tz ^ z
    pieces = {}
    at = 0
    for ty in tys:
        for tc in range(2):
            for tx in range(2):
                part = values[at * piece_rows : (at + 1) * piece_rows]
                blocks = [part[:, n : n + width] for n in range(0, part.shape[1], width)]
                if extra is not None:
                    blocks.append(extra[at])
                pieces[ty, tc, tx] = jnp.concatenate(blocks, axis=0) if len(blocks) > 1 else blocks[0]
                at += 1
    for ty in tys:
        slot = ty ^ y
        a, b = pieces[ty, 0, 0], pieces[ty, 0, 1]
        xk[slot, slot_z] = jnp.where(x == 0, a, b).astype(BF)
        xs[slot, slot_z] = jnp.where(x == 0, b, a).astype(BF)
    return pieces


def place_y(pieces, tz, tys, x, y, z, outs):
    xk, xs, yk, ys = outs
    slot_z = tz ^ z
    for tx in range(2):
        slot = tx ^ x
        a, b = pieces[0, 1, tx], pieces[1, 1, tx]
        yk[slot, slot_z] = jnp.where(y == 0, a, b).astype(BF)
        ys[slot, slot_z] = jnp.where(y == 0, b, a).astype(BF)


def reduce_grad_kernel(pos_at, scal, a_own, a_oth, b_own, b_oth, kept, near):
    tz = pl.program_id(0)
    x, y, z = (scal[pos_at + n] for n in range(3))
    values = dot_t(a_own[...], b_own[...]) + dot_t(a_oth[...], b_oth[...])
    rows = values.shape[0] // 8
    slot = tz ^ z

    def put(out):
        for n in range(8):
            ty, tc, tx = n // 4, n // 2 % 2, n % 2
            out[slot // 2, tc, tx ^ x, ty ^ y] = values[n * rows : (n + 1) * rows].astype(BF)

    @pl.when(slot % 2 == 0)
    def _():
        put(kept)

    @pl.when(slot % 2 == 1)
    def _():
        put(near)


def expand_grad_kernel(pos_at, scal, a_own, a_oth, b_own, b_oth, m_own, m_oth, c_own, c_oth, *outs):
    tz = pl.program_id(0)
    x, y, z = (scal[pos_at + n] for n in range(3))
    an, ao = a_own[0, 0], a_oth[0, 0]
    parts = [dot(an, b_own[n]) + dot(ao, b_oth[n]) for n in range(b_own.shape[0])]
    parts.append(dot(m_own[0, 0], c_own[...]) + dot(m_oth[0, 0], c_oth[...]))
    values = jnp.concatenate(parts, axis=1)
    pieces = place(values, values.shape[0] // 8, tz, (0, 1), x, y, z, None, outs)
    place_y(pieces, tz, (0, 1), x, y, z, outs)


def share_lanes(entries, devices, at, width):
    n = entries.shape[1]
    share = n // devices
    owner = lax.broadcasted_iota(jnp.int32, (devices, n), 0)
    column = lax.broadcasted_iota(jnp.int32, (devices, n), 1)
    mine = (column >= owner * share) & (column < (owner + 1) * share)
    high, low = high_low(jnp.where(mine, entries, 0.0))
    both = jnp.concatenate([high, low], axis=0).astype(BF)
    source = lax.broadcasted_iota(jnp.int32, (n, width), 0)
    target = lax.broadcasted_iota(jnp.int32, (n, width), 1)
    picks = (target >= at) & (target < at + share) & (lax.rem(source, share) == target - at)
    spread = dot(both, picks.astype(F32).astype(BF))
    return spread[:devices] + spread[devices:]


def heads_grad_kernel(
    pos_at, scal, a_own, a_oth, own_early, own_late, oth_early, oth_late, kept_h, sent_h, sums_1, kept_e, sent_e, sums_2, *refs, devices
):
    outs, table = refs[:-1], refs[-1]
    x, y, z = (scal[pos_at + n] for n in range(3))
    width = outs[0].shape[-1]

    def fill():
        first_core = scal[pos_at - 1] == 0
        ordered = lambda kept, sent: [jnp.where(first_core, kept, sent), jnp.where(first_core, sent, kept)]
        sums_e = jnp.concatenate(ordered(kept_e[...], sent_e[...]), axis=1)
        of_heads = [part for n in range(3) for part in ordered(kept_h[n, 0:1], sent_h[n, 0:1])]
        total = jnp.zeros((devices, width), F32)
        at = 0
        for entries in (
            jnp.concatenate(of_heads[:4], axis=1), jnp.concatenate(of_heads[4:], axis=1), sums_1[2:3], sums_1[0:1], sums_1[1:2],
            sums_e, sums_2[2:3], sums_2[0:1], sums_2[1:2],
        ):
            total = total + share_lanes(entries, devices, at, width)
            at += entries.shape[1] // devices
        table[...] = total

    fill()

    join = lambda early, late: jnp.concatenate(
        [jnp.concatenate([early[n], late[n]], axis=0) for n in range(early.shape[0])], axis=1
    )
    own, other = join(own_early, own_late), join(oth_early, oth_late)
    line = lax.broadcasted_iota(jnp.int32, (8, width), 0)
    for tz in range(a_own.shape[0]):
        values = dot(a_own[tz], own) + dot(a_oth[tz], other)
        extra = []
        for n in range(8):
            high, low = high_low(table[tz * 8 + n : tz * 8 + n + 1])
            extra.append(jnp.where(line == 0, high, jnp.where(line == 1, low, 0.0)))
        pieces = place(values, values.shape[0] // 8, tz, (0, 1), x, y, z, extra, outs)
        place_y(pieces, tz, (0, 1), x, y, z, outs)


class Ring:
    def __init__(self, n_dp):
        self.n_dp = n_dp
        self.devices = 2 * n_dp

    def swap(self, value, bits):
        return lax.ppermute(value, AXES, [(i, i ^ bits) for i in range(self.devices)])

    def core(self, value):
        return self.swap(value, 2)

    def x(self, value):
        return self.swap(value, 1)

    def y(self, value):
        return self.swap(value, 4)

    def z(self, value, step):
        return self.swap(value, 8 * step)


def add_first_kernel(scal, xk, xr, yk, yr, xn, yn):
    wide = lambda ref: ref[0].astype(F32)
    xn[...] = (wide(xk) + wide(xr)).astype(BF)
    yn[...] = (wide(yk) + wide(yr)).astype(BF)


def add_second_kernel(scal, xk, xr, xm, yk, yr, ym, own, z1, z2, z3):
    for n, (keep, got, more) in enumerate(((xk, xr, xm), (yk, yr, ym))):
        total = lambda k: keep[0, k].astype(F32) + got[0, k].astype(F32) + more[k].astype(F32)
        own[n] = total(0)
        for k, out in ((1, z1), (2, z2), (3, z3)):
            out[n] = total(k).astype(BF)


def add_last_kernel(core_at, scal, own, z1, z2, z3, keep, send):
    first = scal[core_at] == 0
    total = lambda n: own[n] + z1[n].astype(F32) + z2[n].astype(F32) + z3[n].astype(F32)
    of_first, of_second = total(0), total(1)
    keep[...] = jnp.where(first, of_first, of_second)
    send[...] = jnp.where(first, of_second, of_first)


def add_second_half_kernel(scal, xk, xr, xm, yk, yr, ym, kept, sent):
    for n, (keep, got, more) in enumerate(((xk, xr, xm), (yk, yr, ym))):
        total = lambda k: keep[0, k].astype(F32) + got[0, k].astype(F32) + more[k].astype(F32)
        for k in range(2):
            kept[k, n] = total(2 * k)
            sent[k, n] = total(2 * k + 1).astype(BF)


def add_third_half_kernel(scal, kept, got, own, sent):
    own[...] = kept[0] + got[0].astype(F32)
    sent[...] = (kept[1] + got[1].astype(F32)).astype(BF)


def add_last_half_kernel(core_at, scal, own, got, keep, send):
    first = scal[core_at] == 0
    of_first, of_second = (own[n] + got[n].astype(F32) for n in range(2))
    keep[...] = jnp.where(first, of_first, of_second)
    send[...] = jnp.where(first, of_second, of_first)


def add_near_kernel(scal, kept, got, own, far):
    own[...] = kept[0].astype(F32) + got[0].astype(F32)
    far[...] = (kept[1].astype(F32) + got[1].astype(F32)).astype(BF)


def add_far_kernel(scal, own, got, kept, sent):
    for n in range(2):
        kept[n] = own[n, 0] + got[n, 0].astype(F32)
        sent[n] = (own[n, 1] + got[n, 1].astype(F32)).astype(BF)


def add_side_kernel(scal, kept, got, own, sent):
    for n in range(2):
        own[n] = kept[n, 0] + got[n, 0].astype(F32)
        sent[n] = (kept[n, 1] + got[n, 1].astype(F32)).astype(BF)


def add_end_kernel(core_at, scal, own, got, keep, send):
    first = scal[core_at] == 0
    of_first, of_second = (own[n] + got[n].astype(F32) for n in range(2))
    keep[...] = jnp.where(first, of_first, of_second)
    send[...] = jnp.where(first, of_second, of_first)


class Scatter:
    def __init__(self, ring, core_at, name, sent):
        self.ring, self.core_at, self.name = ring, core_at, name
        self.xk, self.xs, self.yk, self.ys = sent

    def send(self, *others):
        self.xr, self.yr = self.ring.x(after(self.xs, *others)), self.ring.y(after(self.ys, *others))

    def first(self, scal, us=0.1):
        shape = self.xk.shape[1:]
        part = lambda a: (a, (1,) + shape, lambda j, s: (1, 0, 0, 0))
        xn, yn = call(
            add_first_kernel, self.name + "_add1", scal, (1,), [part(a) for a in (self.xk, self.xr, self.yk, self.yr)],
            [(shape, BF, None, None)] * 2, us=us,
        )
        self.xn, self.yn = xn, yn
        return xn

    def send_first(self, *others):
        self.xm, self.ym = self.ring.y(after(self.xn, *others)), self.ring.x(after(self.yn, *others))

    def second(self, scal):
        shape = self.xk.shape[1:]
        piece = (2,) + shape[1:]
        part = lambda a: (a, (1,) + shape, lambda j, s: (0, 0, 0, 0))
        whole = lambda a: (a, None, None)
        self.own, *self.sends = call(
            add_second_kernel, self.name + "_add2", scal, (1,),
            [part(self.xk), part(self.xr), whole(self.xm), part(self.yk), part(self.yr), whole(self.ym)],
            [(piece, F32, None, None)] + [(piece, BF, None, None)] * 3,
        )
        return self.own

    def send_second(self, *others):
        self.arrived = [self.ring.z(after(v, *others), k + 1) for k, v in enumerate(self.sends)]

    def last(self, scal):
        piece = self.own.shape[1:]
        keep, send = call(
            functools.partial(add_last_kernel, self.core_at), self.name + "_add3", scal, (1,),
            [(a, None, None) for a in (self.own, *self.arrived)], [(piece, F32, None, None)] * 2,
        )
        return keep, self.ring.core(send)


class HalvingScatter(Scatter):
    def second(self, scal):
        shape = self.xk.shape[1:]
        piece = (2, 2) + shape[1:]
        part = lambda a: (a, (1,) + shape, lambda j, s: (0, 0, 0, 0))
        whole = lambda a: (a, None, None)
        self.kept, self.near = call(
            add_second_half_kernel, self.name + "_add2", scal, (1,),
            [part(self.xk), part(self.xr), whole(self.xm), part(self.yk), part(self.yr), whole(self.ym)],
            [(piece, F32, None, None), (piece, BF, None, None)],
        )
        return self.kept

    def send_second(self):
        self.got = self.ring.z(self.near, 1)

    def third(self, scal):
        piece = self.kept.shape[1:]
        self.own, self.far = call(
            add_third_half_kernel, self.name + "_add3", scal, (1,),
            [(a, None, None) for a in (self.kept, self.got)], [(piece, F32, None, None), (piece, BF, None, None)],
        )
        return self.own

    def send_third(self):
        self.arrived = self.ring.z(self.far, 2)

    def last(self, scal):
        piece = self.own.shape[1:]
        keep, send = call(
            functools.partial(add_last_half_kernel, self.core_at), self.name + "_add4", scal, (1,),
            [(a, None, None) for a in (self.own, self.arrived)], [(piece, F32, None, None)] * 2,
        )
        return keep, self.ring.core(send)


class DepthScatter:
    def __init__(self, ring, core_at, name, sent):
        self.ring, self.core_at, self.name = ring, core_at, name
        self.kept, self.near = sent

    def call(self, kernel, step, scal, ins, outs):
        whole = lambda a: (a, None, None)
        return call(kernel, self.name + step, scal, (), [*map(whole, ins)], [(s, d, None, None) for s, d in outs])

    def send_near(self):
        self.got = self.ring.z(self.near, 1)

    def add_near(self, scal):
        shape = self.kept.shape[1:]
        self.own, self.far = self.call(add_near_kernel, "_add1", scal, (self.kept, self.got), [(shape, F32), (shape, BF)])
        return self.own

    def send_far(self):
        self.got = self.ring.z(self.far, 2)

    def add_far(self, scal):
        shape = self.own.shape[:1] + self.own.shape[2:]
        self.kept, self.side = self.call(add_far_kernel, "_add2", scal, (self.own, self.got), [(shape, F32), (shape, BF)])
        return self.kept

    def send_side(self):
        self.got = self.ring.x(self.side)

    def add_side(self, scal):
        shape = self.kept.shape[:1] + self.kept.shape[2:]
        self.own, sent = self.call(add_side_kernel, "_add3", scal, (self.kept, self.got), [(shape, F32), (shape, BF)])
        self.got = self.ring.y(sent)
        return self.own

    def last(self, scal):
        shape = self.own.shape[1:]
        keep, send = self.call(
            functools.partial(add_end_kernel, self.core_at), "_add4", scal, (self.own, self.got), [(shape, F32)] * 2
        )
        return keep, self.ring.core(send)


def after(value, *others):
    if not others:
        return value
    return lax.optimization_barrier((value,) + others)[0]


def side_by_side(core_at, scal, own, got):
    first = scal[core_at] == 0
    return [jnp.where(first, own, got), jnp.where(first, got, own)]


def finish_kernel(
    core_at, scal, own, got, reduce_own, reduce_got, expand_own, expand_got,
    heads_o, reduce_o, expand_o, merge_o, *shares_o,
):
    width = own.shape[1]
    rows = heads_o.shape[0]
    for n, part in enumerate(side_by_side(core_at, scal, reduce_own[...], reduce_got[...])):
        reduce_o[:, n * width : (n + 1) * width] = part
    blocks = expand_own.shape[0] // rows - 1
    for n, part in enumerate(side_by_side(core_at, scal, expand_own[...], expand_got[...])):
        for k in range(blocks):
            at = (n * blocks + k) * width
            expand_o[:, at : at + width] = part[k * rows : (k + 1) * rows]
        merge_o[:, n * width : (n + 1) * width] = part[blocks * rows :]
    for n, part in enumerate(side_by_side(core_at, scal, own[...], got[...])):
        for k in range(3):
            at = (2 * k + n) * width
            heads_o[:, at : at + width] = part[k * rows : (k + 1) * rows]
    entries = own[3 * rows :] + got[3 * rows :]
    entries = entries[0:1] + entries[1:2]
    at = 0
    for share in shares_o:
        n = share.shape[1]
        moved = entries if at == 0 else pltpu.roll(entries, width - at, 1)
        share[...] = moved[:, :n]
        at += n


def per_device(
    tokens, w_heads, b_heads, w_merge, b_merge, gain_first, bias_first, w_expand, b_expand,
    w_reduce, b_reduce, gain_second, bias_second, seq_lengths, cotangent,
):
    rows = tokens.shape[0]
    seqs = seq_lengths.shape[1]
    n_dp = lax.axis_size("dp")
    ring = Ring(n_dp)
    head = lax.axis_index("head")
    dp = lax.axis_index("dp")
    core = dp % 2
    place_of = jnp.stack([head, core, head, (dp // 2) % 2, dp // 4]).astype(jnp.int32)
    scal = jnp.concatenate([seq_lengths[0].astype(jnp.int32), place_of])
    head_at, core_at, pos_at = seqs, seqs + 1, seqs + 2
    first_core = core == 0
    line = lambda v: v.reshape(1, -1)
    b_heads, b_merge, gain_first, bias_first, b_expand, b_reduce, gain_second, bias_second = map(
        line, (b_heads, b_merge, gain_first, bias_first, b_expand, b_reduce, gain_second, bias_second)
    )
    wide_shape = (rows, D)
    quarter = 256

    turned = ((4, D // 4, rows), BF, None, None)
    rk, v, state, tcol, trow, tokens_t = call(
        functools.partial(kv_kernel, seqs), "keys_values", scal, (3,),
        [
            (tokens, None, None),
            (w_heads, (D, quarter), lambda j, s: (0, 3 + j)),
            (w_heads, (D, quarter), lambda j, s: (0, 6 + j)),
            (b_heads, (1, quarter), lambda j, s: (0, 3 + j)),
            (b_heads, (1, quarter), lambda j, s: (0, 6 + j)),
        ],
        [
            (wide_shape, BF, (rows, quarter), lambda j, s: (0, j)),
            (wide_shape, BF, (rows, quarter), lambda j, s: (0, j)),
            ((PAIRS + 1, LANES, LANES), BF, None, None),
            ((rows, LANES), F32, None, None),
            ((8, rows), F32, None, None), turned,
        ],
        [pltpu.VMEM((LANES, LANES), F32)],
        us=4,
    )
    prior = ring.x(state)

    fast = n_dp == 16
    order = scal
    if fast:
        tokens_o = ring.core(tokens_t)
    rq, num, den = call(
        local_kernel, "local_attention", scal, (3,),
        [
            (tokens, None, None),
            (w_heads, (D, quarter), lambda j, s: (0, j)),
            (b_heads, (1, quarter), lambda j, s: (0, j)),
            (rk, (rows, quarter), lambda j, s: (0, j)),
            (v, (rows, quarter), lambda j, s: (0, j)),
            (tcol, None, None),
            (trow, None, None),
        ],
        [
            (wide_shape, BF, (rows, quarter), lambda j, s: (0, j)),
            (wide_shape, F32, (rows, quarter), lambda j, s: (0, j)),
            (wide_shape, F32, (rows, quarter), lambda j, s: (0, j)),
        ],
        [pltpu.VMEM((rows, rows), F32)],
        us=6,
    )

    if fast:
        order = after(scal, tokens_o)
    att, inv, mixed, xhat, scale, normed, second, turned_own, act, slope = call(
        functools.partial(ffn_kernel, head_at), "feed_forward", order, (FFN_STEPS,),
        [
            (rq, None, None), (num, None, None), (den, None, None), (prior, None, None),
            (tcol, None, None), (tokens, None, None), (w_merge, None, None), (b_merge, None, None),
            (gain_first, None, None), (bias_first, None, None), (b_reduce, None, None),
            (w_expand, (D, FFN_BLOCK), lambda j, s: (0, j)),
            (b_expand, (1, FFN_BLOCK), lambda j, s: (0, j)),
            (w_reduce, (FFN_BLOCK, D), lambda j, s: (j, 0)),
        ],
        [
            (wide_shape, F32, None, None), (wide_shape, F32, None, None), (wide_shape, BF, None, None),
            (wide_shape, F32, None, None), ((rows, LANES), F32, None, None), (wide_shape, BF, None, None),
            (wide_shape, F32, None, None), ((2, 4, D // 4, rows), BF, None, None),
            ((rows, FF), BF, (rows, FFN_BLOCK), lambda j, s: (0, j)),
            ((rows, FF), BF, (rows, FFN_BLOCK), lambda j, s: (0, j)),
        ],
        us=11, vmem=VMEM_FFN,
    )

    half_shape = (rows, D // 2)
    result, grad_second, branch, bg_keep, bg_send, sums_second = call(
        functools.partial(second_kernel, core_at), "second_norm", scal, (1,),
        [(second, None, None), (cotangent, None, None), (gain_second, None, None), (bias_second, None, None)],
        [
            (wide_shape, BF, None, None), (wide_shape, F32, None, None), (wide_shape, BF, None, None),
            (half_shape, BF, None, None), (half_shape, BF, None, None), ((8, D), F32, None, None),
        ],
        us=2.6,
    )

    devices = ring.devices
    small, large = D // devices, FF // devices
    whole = lambda a: (a, None, None)
    part = lambda a, n: (a, (1, 1, D // 4, rows), lambda j, s: (n, j, 0, 0))
    by_z = lambda a: (a, (1, D // 4, rows), lambda j, s: (j, 0, 0))
    by_col = lambda a: (a, (rows, FF // 4), lambda j, s: (0, j))

    def group(kernel, name, scal, grid, ins, piece_rows, us, scratch=(), kind=Scatter):
        shape = (2, 4, piece_rows, D // 2)
        sent = call(
            functools.partial(kernel, pos_at), name, scal, grid, ins, [(shape, BF, None, None)] * 4, scratch, us
        )
        return kind(ring, core_at, name, sent)

    ff_half = FF_STEPS // 2
    in_hbm = lambda a: (a, None, pltpu.HBM)
    hidden = ((ff_half, rows, FF_BLOCK), BF, None, None)
    hidden_sums = ((1, FF // 2), F32, None, None)
    buffers = [
        pltpu.VMEM((ff_half, D, FF_BLOCK), BF), pltpu.VMEM((ff_half, FF_BLOCK, D), BF),
        pltpu.SemaphoreType.DMA((2, ff_half)),
    ]
    hidden_in = [whole(branch), whole(slope), in_hbm(w_expand), in_hbm(w_reduce)]
    pg_send, sum_sent, partial = call(
        functools.partial(back_sent_kernel, core_at), "feed_forward_back_sent", scal, (),
        [*hidden_in, whole(grad_second)],
        [hidden, hidden_sums, (wide_shape, F32, None, None)], buffers,
        us=5, vmem=VMEM_BACK,
    )
    order = scal
    if fast:
        pg_o = ring.core(pg_send)
        act_o, turned_other, bg_o = map(ring.core, (act, turned_own, bg_send))
        pieces = ((2, 2, 2, 2, large, D // 2), BF, None, None)
        sent = call(
            functools.partial(reduce_grad_kernel, pos_at), "grad_reduce", after(scal, partial, turned_other), (4,),
            [by_col(act), by_col(act_o), whole(bg_keep), whole(bg_o)], [pieces, pieces], us=6,
        )
        reduced = DepthScatter(ring, core_at, "grad_reduce", sent)
        reduced.send_near()
        order = after(scal, reduced.near)

    pg_keep, grad_first, mg_keep, mg_send, w_att, e_att, later, sum_kept, sums_first = call(
        functools.partial(back_kernel, core_at), "feed_forward_back", order, (),
        [
            *hidden_in,
            (partial, None, None), (gain_first, None, None), (xhat, None, None), (scale, None, None),
            (w_merge, None, None), (att, None, None), (inv, None, None), (rq, None, None), (tcol, None, None),
        ],
        [
            hidden, (wide_shape, F32, None, None), (half_shape, BF, None, None), (half_shape, BF, None, None),
            (wide_shape, BF, None, None), ((rows, LANES), BF, None, None),
            ((PAIRS + 1, LANES, LANES), BF, None, None), hidden_sums, ((8, D), F32, None, None),
        ],
        [pltpu.VMEM(wide_shape, F32), *buffers],
        us=COST_BACK, vmem=VMEM_BACK,
    )
    later = ring.x(later)

    if fast:
        mg_o = ring.core(mg_send)
        expanded = group(
            expand_grad_kernel, "grad_expand", scal, (4,),
            [
                part(turned_own, 1), part(turned_other, 1), whole(pg_keep), whole(pg_o),
                part(turned_own, 0), part(turned_other, 0), whole(mg_keep), whole(mg_o),
            ],
            5 * small, COST_EXPAND, kind=HalvingScatter,
        )
        expanded.send(later)
        order = after(scal, expanded.xs, later)

    by_pair = [*map(whole, (rq, rk, v, w_att))]
    both_states = [whole(e_att), whole(prior), whole(later), whole(tcol)]
    pj_out = [((3, rows // 2, D // 2), BF, None, None)] * 2
    pj_sums = ((3, 8, D // 2), F32, None, None)
    table = ((rows, rows), F32, None, None)
    *pj_send, sum_heads_sent, weights, weights_t = call(
        functools.partial(attn_sent_kernel, head_at, core_at), "attention_back_sent", order, (),
        [*by_pair, *both_states, whole(trow)], [*pj_out, pj_sums, table, table], us=COST_SENT, vmem=VMEM_ATTN,
    )
    order = scal
    if fast:
        pj_o = [ring.core(v) for v in pj_send]
        order = after(scal, reduced.add_near(after(scal, pj_send[0])))
        reduced.send_far()
    *pj_keep, sum_heads_kept = call(
        functools.partial(attn_kept_kernel, head_at, core_at), "attention_back_kept", order, (),
        [*by_pair, *both_states, whole(weights), whole(weights_t)], [*pj_out, pj_sums], us=COST_KEPT, vmem=VMEM_ATTN,
    )

    if fast:
        order = after(scal, expanded.first(after(scal, pj_keep[0])))
        expanded.send_first()
        heads = group(
            functools.partial(heads_grad_kernel, devices=devices), "grad_heads", order, (),
            [
                *map(whole, (tokens_t, tokens_o, *pj_keep, *pj_o)),
                *map(whole, (sum_heads_kept, sum_heads_sent, sums_first, sum_kept, sum_sent, sums_second)),
            ],
            3 * small + 8, COST_HEADS, [pltpu.VMEM((devices, D // 2), F32)],
        )
        heads.send()
        order = after(scal, heads.xs)

    of_part = lambda a: (a, (1, rows // 2, D // 2), lambda j, s: (j, 0, 0))
    (input_grad,) = call(
        input_kernel, "input_grad", order, (3,),
        [
            whole(grad_first), *map(of_part, (*pj_keep, *pj_send)),
            (w_heads, (D, D // 2), lambda j, s: (0, 2 * j + s[core_at])),
            (w_heads, (D, D // 2), lambda j, s: (0, 2 * j + 1 - s[core_at])),
        ],
        [(wide_shape, F32, None, None)],
        us=COST_INPUT,
    )

    if fast:
        order = reduced.add_far(after(scal, input_grad))
        order = expanded.second(after(scal, order))
        expanded.send_second()
        reduced.send_side()
        order = heads.first(after(scal, order))
        heads.send_first()
        order = expanded.third(after(scal, order))
        expanded.send_third()
        order = heads.second(after(scal, order))
        heads.send_second()
        order = reduced.add_side(after(scal, order))
        expand_own, expand_got = expanded.last(after(scal, order))
        reduce_own, reduce_got = reduced.last(after(scal, expand_own))
        heads_own, heads_got = heads.last(after(scal, reduce_own))
        out = lambda n, m: ((n, m), F32, None, None)
        counts = (2 * small, small, small, small, small, large, small, small, small)
        w_heads_grad, w_reduce_grad, w_expand_grad, w_merge_grad, *shares = call(
            functools.partial(finish_kernel, core_at), "finish", scal, (),
            [*map(whole, (heads_own, heads_got, reduce_own, reduce_got, expand_own, expand_got))],
            [out(small, 3 * D), out(large, D), out(small, FF), out(small, D), *(out(1, n) for n in counts)],
        )
        shares = [share.reshape(-1) for share in shares]
        grads = (
            w_heads_grad, *shares[:2], w_merge_grad, *shares[2:5], w_expand_grad, shares[5], w_reduce_grad,
            *shares[6:],
        )
    else:
        by_core = lambda keep, send: jnp.concatenate(
            [jnp.where(first_core, keep, send), jnp.where(first_core, send, keep)], axis=1
        )
        flat = lambda v: v.transpose(1, 0, 2).reshape(rows, -1)
        by_heads = lambda keep, send: jnp.concatenate(
            [by_core(keep[n], send[n]) for n in range(3)], axis=1
        )
        pj_keep, pj_send = (jnp.concatenate(v, axis=1) for v in (pj_keep, pj_send))
        sum_heads = by_heads(sum_heads_kept, sum_heads_sent)[0]
        scatter = lambda v: lax.psum_scatter(v, AXES, scatter_dimension=0, tiled=True)
        grads = (
            scatter(dot_t(tokens, by_heads(pj_keep, pj_send))),
            scatter(sum_heads[: 2 * D]), scatter(sum_heads[2 * D :]),
            scatter(dot_t(mixed, by_core(mg_keep, mg_send))),
            scatter(sums_first[2]), scatter(sums_first[0]), scatter(sums_first[1]),
            scatter(dot_t(normed, by_core(flat(pg_keep), flat(pg_send)))),
            scatter(by_core(sum_kept, sum_sent)[0]),
            scatter(dot_t(act, branch)),
            scatter(sums_second[2]), scatter(sums_second[0]), scatter(sums_second[1]),
        )
    return (result, input_grad) + tuple(grads)


def solution(mesh):
    in_specs = (P(AXES, None),) + (P(),) * 12 + (P("dp", None), P(AXES, None))
    row, one = P(AXES, None), P(AXES)
    out_specs = (row, row, row, one, one, row, one, one, one, row, one, row, one, one, one)
    return jax.shard_map(
        per_device, mesh=mesh, in_specs=in_specs, out_specs=out_specs, check_vma=False
    )
```

```python
import functools
import math

import jax
import jax.numpy as jnp
from jax import lax
from jax.experimental import pallas as pl
from jax.experimental.pallas import tpu as pltpu
from jax.sharding import PartitionSpec as P

D = 768
PAIRS = 6
FF = 3072
LANES = 128
HALF = 64
BF = jnp.bfloat16
F32 = jnp.float32
AXES = ("dp", "head")
VMEM_LIMIT = 8 << 20
VMEM_FFN = 16 << 20
VMEM_ATTN = 10 << 20
FF_BLOCK = 768
FFN_BLOCK = 1024
FFN_STEPS = FF // FFN_BLOCK
MATMUL_PER_US = 1.15e9
COST_EXPAND = 1
VMEM_BACK = 16 << 20
COST_KEPT = 0.5
COST_BACK = 3
COST_SENT = 0.5
COST_HEADS = 0.1
COST_INPUT = 0.1
FF_STEPS = FF // FF_BLOCK


def dot(a, b):
    return jnp.dot(a, b, preferred_element_type=F32)


def dot_t(a, b):
    return lax.dot_general(a, b, (((0,), (0,)), ((), ())), preferred_element_type=F32)


def dot_r(a, b):
    return lax.dot_general(a, b, (((1,), (1,)), ((), ())), preferred_element_type=F32)


def call(kernel, name, scal, grid, ins, outs, scratch=(), us=0.1, vmem=VMEM_LIMIT):
    def spec(b, m):
        if b is None:
            return pl.BlockSpec(memory_space=pltpu.VMEM if m is None else m)
        return pl.BlockSpec(b, m)

    in_specs = [spec(b, m) for _, b, m in ins]
    out_specs = [spec(b, m) for _, _, b, m in outs]
    return pl.pallas_call(
        kernel,
        name=name,
        grid_spec=pltpu.PrefetchScalarGridSpec(
            num_scalar_prefetch=1,
            grid=grid,
            in_specs=in_specs,
            out_specs=out_specs,
            scratch_shapes=list(scratch),
        ),
        out_shape=[jax.ShapeDtypeStruct(s, d) for s, d, _, _ in outs],
        compiler_params=pltpu.CompilerParams(vmem_limit_bytes=vmem),
        cost_estimate=pl.CostEstimate(flops=int(us * MATMUL_PER_US), bytes_accessed=1, transcendentals=0),
    )(scal, *[a for a, _, _ in ins])


def lane_masks():
    lane = lax.broadcasted_iota(jnp.int32, (1, LANES), 1)
    even = (lane < HALF).astype(F32)
    return lane, even.astype(BF), (1.0 - even).astype(BF)


def both_heads(pair):
    lane, even, odd = lane_masks()
    return jnp.concatenate([pair * even, pair * odd], axis=0)


def own_lanes(stacked):
    rows = stacked.shape[0] // 2
    lane = lax.broadcasted_iota(jnp.int32, (1, LANES), 1)
    return jnp.where(lane < HALF, stacked[:rows], stacked[rows:])


def square_masks():
    row = lax.broadcasted_iota(jnp.int32, (LANES, LANES), 0)
    lane = lax.broadcasted_iota(jnp.int32, (LANES, LANES), 1)
    upper = row < HALF
    return lane, upper, upper == (lane < HALF)


def high_low(v):
    high = v.astype(BF).astype(F32)
    return high, v - high


def tables(scal, rows, seqs, tcol, trow):
    pos = lax.broadcasted_iota(jnp.int32, (1, rows), 1) + scal[seqs] * rows
    seg = jnp.zeros((1, rows), jnp.int32)
    first = jnp.zeros((1, rows), jnp.int32)
    length = jnp.ones((1, rows), jnp.int32)
    at_boundary = jnp.int32(0)
    begin = jnp.int32(0)
    for s in range(seqs):
        end = begin + scal[s]
        inside = (pos >= begin) & (pos < end)
        first = jnp.where(inside, begin, first)
        length = jnp.where(inside, jnp.maximum(scal[s], 1), length)
        seg = seg + (pos >= end).astype(jnp.int32)
        at_boundary = at_boundary + (rows - 1 >= end).astype(jnp.int32)
        begin = end
    live = (seg < seqs).astype(F32)
    angle = 0.5 * math.pi * (pos - first).astype(F32) / length.astype(F32)
    cos_w = jnp.cos(angle) * live
    sin_w = jnp.sin(angle) * live
    crossing = (seg == at_boundary).astype(F32)
    which = lax.broadcasted_iota(jnp.int32, (LANES, rows), 0)
    table = jnp.zeros((LANES, rows), F32)
    for n, entry in enumerate((cos_w, sin_w, seg.astype(F32), cos_w * crossing, sin_w * crossing)):
        table = jnp.where(which == n, entry, table)
    trow[...] = table[:8]
    tcol[...] = table.T


def pack_state(both, norm_cos, norm_sin, pair, norms):
    lane, upper, diag = square_masks()
    packed = jnp.where(diag, both[:LANES, :LANES], pltpu.roll(both[LANES:, :LANES], HALF, 1))
    cos_high, cos_low = high_low(norm_cos)
    sin_high, sin_low = high_low(norm_sin)
    for n, part in enumerate((cos_high, cos_low, sin_high, sin_low)):
        norms = jnp.where(lane == 4 * pair + n, part, norms)
    return packed.astype(BF), norms


def unpack_state(state_ref, pair):
    lane, upper, diag = square_masks()
    packed = state_ref[pair].astype(F32)
    norms = state_ref[PAIRS].astype(F32)
    of_cos = jnp.where(diag, packed, 0.0)
    of_sin = jnp.where(diag, pltpu.roll(packed, HALF, 1), 0.0)
    pick = lambda n: jnp.sum(
        jnp.where((lane == 4 * pair + n) | (lane == 4 * pair + n + 1), norms, 0.0), axis=1, keepdims=True
    )
    return of_cos, of_sin, pick(0), pick(2)


def turn(value, out):
    turned = value.T
    share = out.shape[1]
    for n in range(out.shape[0]):
        out[n] = turned[n * share : (n + 1) * share]


def kv_kernel(seqs, scal, tok, wk, wv, bk, bv, rk_o, v_o, st_o, tcol, trow, turned_o, norms):
    step = pl.program_id(0)
    rows = tok.shape[0]

    @pl.when(step == 0)
    def _():
        tables(scal, rows, seqs, tcol, trow)
        norms[...] = jnp.zeros_like(norms)
        turn(tok[...], turned_o)

    rk = jnp.maximum(dot(tok[...], wk[...]) + bk[...].astype(F32), 0.0).astype(BF)
    v = (dot(tok[...], wv[...]) + bv[...].astype(F32)).astype(BF)
    rk_o[...] = rk
    v_o[...] = v
    cos_b, sin_b = tcol[:, 3:4], tcol[:, 4:5]
    ones = jnp.ones((rows, LANES), BF)
    for n in range(2):
        pair = 2 * step + n
        cols = slice(n * LANES, (n + 1) * LANES)
        kp = rk[:, cols].astype(F32)
        left = jnp.concatenate([(kp * cos_b).astype(BF), (kp * sin_b).astype(BF)], axis=1)
        both = dot_t(left, jnp.concatenate([v[:, cols], ones], axis=1))
        packed, new_norms = pack_state(both, both[:LANES, LANES:], both[LANES:, LANES:], pair, norms[...])
        st_o[pair] = packed
        norms[...] = new_norms

    st_o[PAIRS] = norms[...].astype(BF)


def weights_block(tcol, trow, transposed):
    rows = tcol.shape[0]
    down = lax.broadcasted_iota(jnp.int32, (rows, rows), 0)
    along = lax.broadcasted_iota(jnp.int32, (rows, rows), 1)
    same = tcol[:, 2:3] == trow[2:3, :]
    causal = (down <= along) if transposed else (along <= down)
    value = tcol[:, 0:1] * trow[0:1, :] + tcol[:, 1:2] * trow[1:2, :]
    return jnp.where(same & causal, value, 0.0)


def weigh(stacked, weights):
    rows = weights.shape[0]
    return jnp.concatenate([stacked[:rows] * weights, stacked[rows:] * weights], axis=0).astype(BF)


def local_kernel(scal, tok, wq, bq, rk, v, tcol, trow, rq_o, num_o, den_o, weights):
    step = pl.program_id(0)
    rows = tok.shape[0]
    mid = rows // 2

    @pl.when(step == 0)
    def _():
        weights[...] = weights_block(tcol, trow, False)

    rq = jnp.maximum(dot(tok[...], wq[...]) + bq[...].astype(F32), 0.0).astype(BF)
    rq_o[...] = rq
    ones = jnp.ones((rows, LANES), BF)
    for n in range(2):
        cols = slice(n * LANES, (n + 1) * LANES)
        kp = rk[:, cols]
        values = jnp.concatenate([v[:, cols], ones], axis=1)
        first = weigh(dot_r(both_heads(rq[:, cols]), kp[:mid]), weights[:, :mid])
        second = weigh(dot_r(both_heads(rq[mid:, cols]), kp[mid:]), weights[mid:, mid:])
        sums = dot(first, values[:mid])
        late = dot(second, values[mid:])
        for own, out in ((slice(0, LANES), num_o), (slice(LANES, 2 * LANES), den_o)):
            total = own_lanes(sums[:, own])
            out[:mid, cols] = total[:mid]
            out[mid:, cols] = total[mid:] + own_lanes(late[:, own])


def normalise(entries):
    mean = jnp.mean(entries, axis=1, keepdims=True)
    centred = entries - mean
    var = jnp.mean(centred * centred, axis=1, keepdims=True)
    scale = lax.rsqrt(var + 1e-05)
    return centred * scale, scale


def merge_heads(
    head_at, scal, rq, num, den, st, tcol, tok, w_merge, b_merge, gain, bias, b_red,
    att_o, inv_o, mixed_o, xhat_o, scale_o, normed_o, acc_o, turned_o,
):
    cross = (scal[head_at] == 1).astype(F32)
    cos_b, sin_b = tcol[:, 3:4] * cross, tcol[:, 4:5] * cross
    sq_lane, upper, diag = square_masks()
    for pair in range(PAIRS):
        cols = slice(pair * LANES, (pair + 1) * LANES)
        qp = rq[:, cols].astype(F32)
        of_cos, of_sin, norm_cos, norm_sin = unpack_state(st, pair)
        top = jnp.concatenate([of_cos, jnp.where(diag, norm_cos, 0.0)], axis=1)
        low = jnp.concatenate([of_sin, jnp.where(diag, norm_sin, 0.0)], axis=1)
        right = jnp.concatenate([top, low], axis=0).astype(BF)
        left = jnp.concatenate([(qp * cos_b).astype(BF), (qp * sin_b).astype(BF)], axis=1)
        prior = dot(left, right)
        inverse = 1.0 / (den[:, cols] + prior[:, LANES:] + 1.0)
        attended = (num[:, cols] + prior[:, :LANES]) * inverse
        att_o[:, cols] = attended
        inv_o[:, cols] = inverse
        mixed_o[:, cols] = attended.astype(BF)
    first_in = tok[...].astype(F32) + dot(mixed_o[...], w_merge[...]) + b_merge[...].astype(F32)
    xhat, scale = normalise(first_in)
    normed = xhat * gain[...].astype(F32) + bias[...].astype(F32)
    xhat_o[...] = xhat
    scale_o[...] = jnp.broadcast_to(scale, scale_o.shape)
    normed_o[...] = normed.astype(BF)
    acc_o[...] = normed + b_red[...].astype(F32)
    turn(mixed_o[...], turned_o.at[0])
    turn(normed_o[...], turned_o.at[1])


def expand_reduce(normed, w_exp, b_exp, w_red, act_o, slope_o, acc_o):
    rows = normed.shape[0]
    pre = [dot(normed[at : at + rows // 2], w_exp[...]) + b_exp[...].astype(F32) for at in (0, rows // 2)]
    for at, x in zip((0, rows // 2), pre):
        part = slice(at, at + rows // 2)
        cdf = 0.5 + 0.5 * lax.erf(x * (2.0**-0.5))
        pdf = jnp.exp(-0.5 * x * x) * (1.0 / math.sqrt(2.0 * math.pi))
        act = (x * cdf).astype(BF)
        act_o[part] = act
        slope_o[part] = (cdf + x * pdf).astype(BF)
        acc_o[part] += dot(act, w_red[...])


def ffn_kernel(head_at, scal, *refs):
    w_exp, b_exp, w_red = refs[11:14]
    normed_o, acc_o = refs[19:21]
    act_o, slope_o = refs[22:]

    @pl.when(pl.program_id(0) == 0)
    def _():
        merge_heads(head_at, scal, *refs[:11], *refs[14:22])

    expand_reduce(normed_o, w_exp, b_exp, w_red, act_o, slope_o, acc_o)


def second_kernel(core_at, scal, second, cot, gain, bias, out_o, grad_o, full_o, keep_o, send_o, sums_o):
    xhat, scale = normalise(second[...])
    gain_w = gain[...].astype(F32)
    out_o[...] = (xhat * gain_w + bias[...].astype(F32)).astype(BF)
    cot_w = cot[...].astype(F32)
    t = cot_w * gain_w
    grad = scale * (
        t - jnp.mean(t, axis=1, keepdims=True) - xhat * jnp.mean(t * xhat, axis=1, keepdims=True)
    )
    low = grad.astype(BF)
    grad_o[...] = grad
    full_o[...] = low
    first = scal[core_at] == 0
    half = D // 2
    left, right = grad[:, :half], grad[:, half:]
    keep_o[...] = jnp.where(first, left, right).astype(BF)
    send_o[...] = jnp.where(first, right, left).astype(BF)
    sums_o[0:1] = jnp.sum(cot_w * xhat, axis=0, keepdims=True)
    sums_o[1:2] = jnp.sum(cot_w, axis=0, keepdims=True)
    sums_o[2:3] = jnp.sum(low.astype(F32), axis=0, keepdims=True)


def head_lanes(pair, lane, first):
    at = 4 * pair + jnp.where(first, 0, 2)
    return (lane == at) | (lane == at + 1)


def weight_copies(half, w_exp, w_red, exp_buf, red_buf, sems, n):
    at = pl.ds(pl.multiple_of((half * exp_buf.shape[0] + n) * FF_BLOCK, FF_BLOCK), FF_BLOCK)
    return (
        pltpu.make_async_copy(w_red.at[at, :], red_buf.at[n], sems.at[0, n]),
        pltpu.make_async_copy(w_exp.at[:, at], exp_buf.at[n], sems.at[1, n]),
    )


def back_steps(half, full, slope, w_exp, w_red, out_o, bexp_o, exp_buf, red_buf, sems):
    blocks = exp_buf.shape[0]
    copies = [weight_copies(half, w_exp, w_red, exp_buf, red_buf, sems, n) for n in range(blocks)]
    for pair in copies:
        for copy in pair:
            copy.start()
    total = None
    for n, (of_red, of_exp) in enumerate(copies):
        cols = slice(n * FF_BLOCK, (n + 1) * FF_BLOCK)
        at = pl.ds(pl.multiple_of((half * blocks + n) * FF_BLOCK, FF_BLOCK), FF_BLOCK)
        of_red.wait()
        pre_grad = (dot_r(full[...], red_buf[n]) * slope[:, at].astype(F32)).astype(BF)
        bexp_o[:, cols] = jnp.sum(pre_grad.astype(F32), axis=0, keepdims=True)
        out_o[n] = pre_grad
        of_exp.wait()
        part = dot_r(pre_grad, exp_buf[n])
        total = part if total is None else total + part
    return total


def back_sent_kernel(core_at, scal, full, slope, w_exp, w_red, grad2, sent_o, bexp_o, acc, exp_buf, red_buf, sems):
    half = 1 - scal[core_at]
    acc[...] = grad2[...] + back_steps(half, full, slope, w_exp, w_red, sent_o, bexp_o, exp_buf, red_buf, sems)


def back_kernel(
    core_at, scal, full, slope, w_exp, w_red, acc_in, gain, xhat, scale, w_merge, att, inv, rq, tcol,
    kept_o, first_o, mk_o, ms_o, w_o, e_o, st_o, bexp_o, sums_o,
    acc, exp_buf, red_buf, sems,
):
    half = scal[core_at]
    acc[...] = acc_in[...] + back_steps(half, full, slope, w_exp, w_red, kept_o, bexp_o, exp_buf, red_buf, sems)
    back_rest(
        core_at, scal, acc, gain, xhat, scale, w_merge, att, inv, rq, tcol,
        first_o, mk_o, ms_o, w_o, e_o, st_o, sums_o,
    )


def back_rest(
    core_at, scal, acc, gain, xhat, scale, w_merge, att, inv, rq, tcol,
    first_o, mk_o, ms_o, w_o, e_o, st_o, sums_o,
):
    grad_normed = acc[...]
    xh = xhat[...]
    t = grad_normed * gain[...].astype(F32)
    first = scale[:, 0:1] * (
        t - jnp.mean(t, axis=1, keepdims=True) - xh * jnp.mean(t * xh, axis=1, keepdims=True)
    )
    low = first.astype(BF)
    first_o[...] = first
    sums_o[0:1] = jnp.sum(grad_normed * xh, axis=0, keepdims=True)
    sums_o[1:2] = jnp.sum(grad_normed, axis=0, keepdims=True)
    sums_o[2:3] = jnp.sum(low.astype(F32), axis=0, keepdims=True)
    is_first = scal[core_at] == 0
    left, right = first[:, : D // 2], first[:, D // 2 :]
    mk_o[...] = jnp.where(is_first, left, right).astype(BF)
    ms_o[...] = jnp.where(is_first, right, left).astype(BF)
    cos_b, sin_b = tcol[:, 3:4], tcol[:, 4:5]
    w = (dot_r(low, w_merge[...]).astype(BF).astype(F32) * inv[...]).astype(BF)
    w_o[...] = w
    high, rest = high_low(w.astype(F32) * att[...])
    column = lax.broadcasted_iota(jnp.int32, (D, LANES), 0)
    target = lax.broadcasted_iota(jnp.int32, (D, LANES), 1)
    picks = (target == 2 * (column // HALF)).astype(F32).astype(BF)
    e_high, e_low = high_low(-(dot(high.astype(BF), picks) + dot(rest.astype(BF), picks)))
    e = (e_high + pltpu.roll(e_low, 1, 1)).astype(BF)
    e_o[...] = e
    norms = jnp.zeros((LANES, LANES), F32)
    sq_lane, upper, diag = square_masks()
    for pair in range(PAIRS):
        cols = slice(pair * LANES, (pair + 1) * LANES)
        qp = rq[:, cols].astype(F32)
        left = jnp.concatenate([(qp * cos_b).astype(BF), (qp * sin_b).astype(BF)], axis=1)
        both = dot_t(left, jnp.concatenate([w[:, cols], e], axis=1))
        mine = head_lanes(pair, sq_lane, upper)
        norm = lambda part: jnp.sum(jnp.where(mine, part, 0.0), axis=1, keepdims=True)
        packed, norms = pack_state(both, norm(both[:LANES, LANES:]), norm(both[LANES:, LANES:]), pair, norms)
        st_o[pair] = packed
    st_o[PAIRS] = norms.astype(BF)


def attn_sent_kernel(head_at, core_at, scal, rq, rk, v, w, e, prior, later, tcol, trow, early_o, late_o, sums_o, weights, weights_t):
    weights[...] = weights_block(tcol, trow, False)
    weights_t[...] = weights_block(tcol, trow, True)
    first = (1 - scal[core_at]) * (PAIRS // 2)
    attn_back(head_at, first, scal, rq, rk, v, w, e, prior, later, tcol, weights, weights_t, early_o, late_o, sums_o)


def attn_kept_kernel(head_at, core_at, scal, rq, rk, v, w, e, prior, later, tcol, weights, weights_t, early_o, late_o, sums_o):
    step = pl.program_id(0)
    attn_back_pair(
        head_at, scal[core_at] * (PAIRS // 2) + step, step,
        scal, rq, rk, v, w, e, prior, later, tcol, weights, weights_t, early_o, late_o, sums_o,
    )


def attn_back(head_at, first, scal, rq, rk, v, w, e, prior, later, tcol, weights, weights_t, early_o, late_o, sums_o):
    for n in range(PAIRS // 2):
        attn_back_pair(
            head_at, first + n, n, scal, rq, rk, v, w, e, prior, later, tcol, weights, weights_t, early_o, late_o, sums_o
        )


def attn_back_pair(
    head_at, pair, slot, scal, rq, rk, v, w, e, prior, later, tcol, weights, weights_t, early_o, late_o, sums_o
):
    rows = rq.shape[0]
    mid = rows // 2
    cols = pl.ds(pl.multiple_of(pair * LANES, LANES), LANES)
    out = pl.ds(pl.multiple_of(slot * LANES, LANES), LANES)

    qp, kp, vp, wp = rq[:, cols], rk[:, cols], v[:, cols], w[:, cols]
    lane, even, odd = lane_masks()
    of_even = ((lane == 4 * pair) | (lane == 4 * pair + 1)).astype(F32).astype(BF)
    of_odd = ((lane == 4 * pair + 2) | (lane == 4 * pair + 3)).astype(F32).astype(BF)
    ones = jnp.ones((rows, LANES), BF)
    we = jnp.concatenate([wp, e[...]], axis=1)
    by_head = (jnp.concatenate([even, of_even], axis=1), jnp.concatenate([odd, of_odd], axis=1))
    ve = jnp.concatenate([vp, ones], axis=1)
    stack = lambda a, lo, hi: jnp.concatenate([a[lo:hi] * m for m in by_head], axis=0)

    grads = weigh(dot_r(stack(we, 0, rows), ve[:mid]), weights[:, :mid])
    dq = own_lanes(dot(grads, kp[:mid]))
    grads = weigh(dot_r(stack(we, mid, rows), ve[mid:]), weights[mid:, mid:])
    dq_late = own_lanes(dot(grads, kp[mid:]))

    grads = weigh(dot_r(stack(ve, 0, rows), we[mid:]), weights_t[:, mid:])
    dk = own_lanes(dot(grads, qp[mid:]))
    grads = weigh(dot_r(stack(ve, 0, mid), we[:mid]), weights_t[:mid, :mid])
    dk_early = own_lanes(dot(grads, qp[:mid]))

    scores = weigh(dot_r(both_heads(kp), qp[mid:]), weights_t[:, mid:])
    dv = own_lanes(dot(scores, wp[mid:]))
    scores = weigh(dot_r(both_heads(kp[:mid]), qp[:mid]), weights_t[:mid, :mid])
    dv_early = own_lanes(dot(scores, wp[:mid]))

    dq = jnp.concatenate([dq[:mid], dq[mid:] + dq_late], axis=0)
    dk = jnp.concatenate([dk[:mid] + dk_early, dk[mid:]], axis=0)
    dv = jnp.concatenate([dv[:mid] + dv_early, dv[mid:]], axis=0)

    sq_lane, upper, diag = square_masks()
    cos_b, sin_b = tcol[:, 3:4], tcol[:, 4:5]
    is_late = (scal[head_at] == 1).astype(F32)
    early = 1.0 - is_late

    def with_norms(parts, where):
        side = lambda total, norm: jnp.concatenate([total, jnp.where(where, norm, 0.0)], axis=1)
        of_cos, of_sin, norm_cos, norm_sin = parts
        return jnp.concatenate([side(of_cos, norm_cos), side(of_sin, norm_sin)], axis=0).astype(BF)

    prior_parts = unpack_state(prior, pair)
    into = dot_r(we, with_norms(prior_parts, head_lanes(pair, sq_lane, upper)))
    dq = dq + is_late * (cos_b * into[:, :LANES] + sin_b * into[:, LANES:])
    later_parts = unpack_state(later, pair)
    into = dot_r(ve, with_norms(later_parts, sq_lane == 0))
    dk = dk + early * (cos_b * into[:, :LANES] + sin_b * into[:, LANES:])
    kw = kp.astype(F32)
    left = jnp.concatenate([(kw * (cos_b * early)).astype(BF), (kw * (sin_b * early)).astype(BF)], axis=1)
    dv = dv + dot(left, jnp.concatenate(later_parts[:2], axis=0).astype(BF))

    dq = jnp.where(qp.astype(F32) > 0, dq, 0.0).astype(BF)
    dk = jnp.where(kw > 0, dk, 0.0).astype(BF)
    dv = dv.astype(BF)
    for n, part in enumerate((dq, dk, dv)):
        total = jnp.sum(part.astype(F32), axis=0, keepdims=True)
        sums_o[n, :, out] = jnp.broadcast_to(total, (sums_o.shape[1], LANES))
        early_o[n, :, out] = part[:mid]
        late_o[n, :, out] = part[mid:]


def input_kernel(scal, first, keep_early, keep_late, send_early, send_late, w_keep, w_send, out_o):
    @pl.when(pl.program_id(0) == 0)
    def _():
        out_o[...] = first[...]

    rows = lambda early, late: jnp.concatenate([early[0], late[0]], axis=0)
    out_o[...] += dot_r(rows(keep_early, keep_late), w_keep[...]) + dot_r(rows(send_early, send_late), w_send[...])


def place(values, piece_rows, tz, tys, x, y, z, extra, outs):
    xk, xs, yk, ys = outs
    width = xk.shape[-1]
    slot_z = tz ^ z
    pieces = {}
    at = 0
    for ty in tys:
        for tc in range(2):
            for tx in range(2):
                part = values[at * piece_rows : (at + 1) * piece_rows]
                blocks = [part[:, n : n + width] for n in range(0, part.shape[1], width)]
                if extra is not None:
                    blocks.append(extra[at])
                pieces[ty, tc, tx] = jnp.concatenate(blocks, axis=0) if len(blocks) > 1 else blocks[0]
                at += 1
    for ty in tys:
        slot = ty ^ y
        a, b = pieces[ty, 0, 0], pieces[ty, 0, 1]
        xk[slot, slot_z] = jnp.where(x == 0, a, b).astype(BF)
        xs[slot, slot_z] = jnp.where(x == 0, b, a).astype(BF)
    return pieces


def place_y(pieces, tz, tys, x, y, z, outs):
    xk, xs, yk, ys = outs
    slot_z = tz ^ z
    for tx in range(2):
        slot = tx ^ x
        a, b = pieces[0, 1, tx], pieces[1, 1, tx]
        yk[slot, slot_z] = jnp.where(y == 0, a, b).astype(BF)
        ys[slot, slot_z] = jnp.where(y == 0, b, a).astype(BF)


def reduce_grad_kernel(pos_at, scal, a_own, a_oth, b_own, b_oth, kept, near):
    tz = pl.program_id(0)
    x, y, z = (scal[pos_at + n] for n in range(3))
    values = dot_t(a_own[...], b_own[...]) + dot_t(a_oth[...], b_oth[...])
    rows = values.shape[0] // 8
    slot = tz ^ z

    def put(out):
        for n in range(8):
            ty, tc, tx = n // 4, n // 2 % 2, n % 2
            out[slot // 2, tc, tx ^ x, ty ^ y] = values[n * rows : (n + 1) * rows].astype(BF)

    @pl.when(slot % 2 == 0)
    def _():
        put(kept)

    @pl.when(slot % 2 == 1)
    def _():
        put(near)


def expand_grad_kernel(pos_at, scal, a_own, a_oth, b_own, b_oth, m_own, m_oth, c_own, c_oth, *outs):
    tz = pl.program_id(0)
    x, y, z = (scal[pos_at + n] for n in range(3))
    an, ao = a_own[0, 0], a_oth[0, 0]
    parts = [dot(an, b_own[n]) + dot(ao, b_oth[n]) for n in range(b_own.shape[0])]
    parts.append(dot(m_own[0, 0], c_own[...]) + dot(m_oth[0, 0], c_oth[...]))
    values = jnp.concatenate(parts, axis=1)
    pieces = place(values, values.shape[0] // 8, tz, (0, 1), x, y, z, None, outs)
    place_y(pieces, tz, (0, 1), x, y, z, outs)


def share_lanes(entries, devices, at, width):
    n = entries.shape[1]
    share = n // devices
    owner = lax.broadcasted_iota(jnp.int32, (devices, n), 0)
    column = lax.broadcasted_iota(jnp.int32, (devices, n), 1)
    mine = (column >= owner * share) & (column < (owner + 1) * share)
    high, low = high_low(jnp.where(mine, entries, 0.0))
    both = jnp.concatenate([high, low], axis=0).astype(BF)
    source = lax.broadcasted_iota(jnp.int32, (n, width), 0)
    target = lax.broadcasted_iota(jnp.int32, (n, width), 1)
    picks = (target >= at) & (target < at + share) & (lax.rem(source, share) == target - at)
    spread = dot(both, picks.astype(F32).astype(BF))
    return spread[:devices] + spread[devices:]


def heads_grad_kernel(
    pos_at, scal, a_own, a_oth, own_early, own_late, oth_early, oth_late, kept_h, sent_h, sums_1, kept_e, sent_e, sums_2, *refs, devices
):
    outs, table = refs[:-1], refs[-1]
    tz = pl.program_id(0)
    x, y, z = (scal[pos_at + n] for n in range(3))
    width = outs[0].shape[-1]

    @pl.when(tz == 0)
    def _():
        first_core = scal[pos_at - 1] == 0
        ordered = lambda kept, sent: [jnp.where(first_core, kept, sent), jnp.where(first_core, sent, kept)]
        sums_e = jnp.concatenate(ordered(kept_e[...], sent_e[...]), axis=1)
        of_heads = [part for n in range(3) for part in ordered(kept_h[n, 0:1], sent_h[n, 0:1])]
        total = jnp.zeros((devices, width), F32)
        at = 0
        for entries in (
            jnp.concatenate(of_heads[:4], axis=1), jnp.concatenate(of_heads[4:], axis=1), sums_1[2:3], sums_1[0:1], sums_1[1:2],
            sums_e, sums_2[2:3], sums_2[0:1], sums_2[1:2],
        ):
            total = total + share_lanes(entries, devices, at, width)
            at += entries.shape[1] // devices
        table[...] = total

    join = lambda early, late: jnp.concatenate(
        [jnp.concatenate([early[n], late[n]], axis=0) for n in range(early.shape[0])], axis=1
    )
    values = dot(a_own[0], join(own_early, own_late)) + dot(a_oth[0], join(oth_early, oth_late))
    line = lax.broadcasted_iota(jnp.int32, (8, width), 0)
    rows8 = table[pl.ds(pl.multiple_of(tz * 8, 8), 8)]
    extra = []
    for n in range(8):
        high, low = high_low(rows8[n : n + 1])
        extra.append(jnp.where(line == 0, high, jnp.where(line == 1, low, 0.0)))
    pieces = place(values, values.shape[0] // 8, tz, (0, 1), x, y, z, extra, outs)
    place_y(pieces, tz, (0, 1), x, y, z, outs)


class Ring:
    def __init__(self, n_dp):
        self.n_dp = n_dp
        self.devices = 2 * n_dp

    def swap(self, value, bits):
        return lax.ppermute(value, AXES, [(i, i ^ bits) for i in range(self.devices)])

    def core(self, value):
        return self.swap(value, 2)

    def x(self, value):
        return self.swap(value, 1)

    def y(self, value):
        return self.swap(value, 4)

    def z(self, value, step):
        return self.swap(value, 8 * step)


def add_first_kernel(scal, xk, xr, yk, yr, xn, yn):
    wide = lambda ref: ref[0].astype(F32)
    xn[...] = (wide(xk) + wide(xr)).astype(BF)
    yn[...] = (wide(yk) + wide(yr)).astype(BF)


def add_second_kernel(scal, xk, xr, xm, yk, yr, ym, own, z1, z2, z3):
    for n, (keep, got, more) in enumerate(((xk, xr, xm), (yk, yr, ym))):
        total = lambda k: keep[0, k].astype(F32) + got[0, k].astype(F32) + more[k].astype(F32)
        own[n] = total(0)
        for k, out in ((1, z1), (2, z2), (3, z3)):
            out[n] = total(k).astype(BF)


def add_last_kernel(core_at, scal, own, z1, z2, z3, keep, send):
    first = scal[core_at] == 0
    total = lambda n: own[n] + z1[n].astype(F32) + z2[n].astype(F32) + z3[n].astype(F32)
    of_first, of_second = total(0), total(1)
    keep[...] = jnp.where(first, of_first, of_second)
    send[...] = jnp.where(first, of_second, of_first)


def add_second_half_kernel(scal, xk, xr, xm, yk, yr, ym, kept, sent):
    for n, (keep, got, more) in enumerate(((xk, xr, xm), (yk, yr, ym))):
        total = lambda k: keep[0, k].astype(F32) + got[0, k].astype(F32) + more[k].astype(F32)
        for k in range(2):
            kept[k, n] = total(2 * k)
            sent[k, n] = total(2 * k + 1).astype(BF)


def add_third_half_kernel(scal, kept, got, own, sent):
    own[...] = kept[0] + got[0].astype(F32)
    sent[...] = (kept[1] + got[1].astype(F32)).astype(BF)


def add_last_half_kernel(core_at, scal, own, got, keep, send):
    first = scal[core_at] == 0
    of_first, of_second = (own[n] + got[n].astype(F32) for n in range(2))
    keep[...] = jnp.where(first, of_first, of_second)
    send[...] = jnp.where(first, of_second, of_first)


def add_near_kernel(scal, kept, got, own, far):
    own[...] = kept[0].astype(F32) + got[0].astype(F32)
    far[...] = (kept[1].astype(F32) + got[1].astype(F32)).astype(BF)


def add_far_kernel(scal, own, got, kept, sent):
    for n in range(2):
        kept[n] = own[n, 0] + got[n, 0].astype(F32)
        sent[n] = (own[n, 1] + got[n, 1].astype(F32)).astype(BF)


def add_side_kernel(scal, kept, got, own, sent):
    for n in range(2):
        own[n] = kept[n, 0] + got[n, 0].astype(F32)
        sent[n] = (kept[n, 1] + got[n, 1].astype(F32)).astype(BF)


def add_end_kernel(core_at, scal, own, got, keep, send):
    first = scal[core_at] == 0
    of_first, of_second = (own[n] + got[n].astype(F32) for n in range(2))
    keep[...] = jnp.where(first, of_first, of_second)
    send[...] = jnp.where(first, of_second, of_first)


class Scatter:
    def __init__(self, ring, core_at, name, sent):
        self.ring, self.core_at, self.name = ring, core_at, name
        self.xk, self.xs, self.yk, self.ys = sent

    def send(self, *others):
        self.xr, self.yr = self.ring.x(after(self.xs, *others)), self.ring.y(after(self.ys, *others))

    def first(self, scal, us=0.1):
        shape = self.xk.shape[1:]
        part = lambda a: (a, (1,) + shape, lambda j, s: (1, 0, 0, 0))
        xn, yn = call(
            add_first_kernel, self.name + "_add1", scal, (1,), [part(a) for a in (self.xk, self.xr, self.yk, self.yr)],
            [(shape, BF, None, None)] * 2, us=us,
        )
        self.xn, self.yn = xn, yn
        return xn

    def send_first(self, *others):
        self.xm, self.ym = self.ring.y(after(self.xn, *others)), self.ring.x(after(self.yn, *others))

    def second(self, scal):
        shape = self.xk.shape[1:]
        piece = (2,) + shape[1:]
        part = lambda a: (a, (1,) + shape, lambda j, s: (0, 0, 0, 0))
        whole = lambda a: (a, None, None)
        self.own, *self.sends = call(
            add_second_kernel, self.name + "_add2", scal, (1,),
            [part(self.xk), part(self.xr), whole(self.xm), part(self.yk), part(self.yr), whole(self.ym)],
            [(piece, F32, None, None)] + [(piece, BF, None, None)] * 3,
        )
        return self.own

    def send_second(self, *others):
        self.arrived = [self.ring.z(after(v, *others), k + 1) for k, v in enumerate(self.sends)]

    def last(self, scal):
        piece = self.own.shape[1:]
        keep, send = call(
            functools.partial(add_last_kernel, self.core_at), self.name + "_add3", scal, (1,),
            [(a, None, None) for a in (self.own, *self.arrived)], [(piece, F32, None, None)] * 2,
        )
        return keep, self.ring.core(send)


class HalvingScatter(Scatter):
    def second(self, scal):
        shape = self.xk.shape[1:]
        piece = (2, 2) + shape[1:]
        part = lambda a: (a, (1,) + shape, lambda j, s: (0, 0, 0, 0))
        whole = lambda a: (a, None, None)
        self.kept, self.near = call(
            add_second_half_kernel, self.name + "_add2", scal, (1,),
            [part(self.xk), part(self.xr), whole(self.xm), part(self.yk), part(self.yr), whole(self.ym)],
            [(piece, F32, None, None), (piece, BF, None, None)],
        )
        return self.kept

    def send_second(self):
        self.got = self.ring.z(self.near, 1)

    def third(self, scal):
        piece = self.kept.shape[1:]
        self.own, self.far = call(
            add_third_half_kernel, self.name + "_add3", scal, (1,),
            [(a, None, None) for a in (self.kept, self.got)], [(piece, F32, None, None), (piece, BF, None, None)],
        )
        return self.own

    def send_third(self):
        self.arrived = self.ring.z(self.far, 2)

    def last(self, scal):
        piece = self.own.shape[1:]
        keep, send = call(
            functools.partial(add_last_half_kernel, self.core_at), self.name + "_add4", scal, (1,),
            [(a, None, None) for a in (self.own, self.arrived)], [(piece, F32, None, None)] * 2,
        )
        return keep, self.ring.core(send)


class DepthScatter:
    def __init__(self, ring, core_at, name, sent):
        self.ring, self.core_at, self.name = ring, core_at, name
        self.kept, self.near = sent

    def call(self, kernel, step, scal, ins, outs):
        whole = lambda a: (a, None, None)
        return call(kernel, self.name + step, scal, (), [*map(whole, ins)], [(s, d, None, None) for s, d in outs])

    def send_near(self):
        self.got = self.ring.z(self.near, 1)

    def add_near(self, scal):
        shape = self.kept.shape[1:]
        self.own, self.far = self.call(add_near_kernel, "_add1", scal, (self.kept, self.got), [(shape, F32), (shape, BF)])
        return self.own

    def send_far(self):
        self.got = self.ring.z(self.far, 2)

    def add_far(self, scal):
        shape = self.own.shape[:1] + self.own.shape[2:]
        self.kept, self.side = self.call(add_far_kernel, "_add2", scal, (self.own, self.got), [(shape, F32), (shape, BF)])
        return self.kept

    def send_side(self):
        self.got = self.ring.x(self.side)

    def add_side(self, scal):
        shape = self.kept.shape[:1] + self.kept.shape[2:]
        self.own, sent = self.call(add_side_kernel, "_add3", scal, (self.kept, self.got), [(shape, F32), (shape, BF)])
        self.got = self.ring.y(sent)
        return self.own

    def last(self, scal):
        shape = self.own.shape[1:]
        keep, send = self.call(
            functools.partial(add_end_kernel, self.core_at), "_add4", scal, (self.own, self.got), [(shape, F32)] * 2
        )
        return keep, self.ring.core(send)


def after(value, *others):
    if not others:
        return value
    return lax.optimization_barrier((value,) + others)[0]


def side_by_side(core_at, scal, own, got):
    first = scal[core_at] == 0
    return [jnp.where(first, own, got), jnp.where(first, got, own)]


def finish_kernel(
    core_at, scal, own, got, reduce_own, reduce_got, expand_own, expand_got,
    heads_o, reduce_o, expand_o, merge_o, *shares_o,
):
    width = own.shape[1]
    rows = heads_o.shape[0]
    for n, part in enumerate(side_by_side(core_at, scal, reduce_own[...], reduce_got[...])):
        reduce_o[:, n * width : (n + 1) * width] = part
    blocks = expand_own.shape[0] // rows - 1
    for n, part in enumerate(side_by_side(core_at, scal, expand_own[...], expand_got[...])):
        for k in range(blocks):
            at = (n * blocks + k) * width
            expand_o[:, at : at + width] = part[k * rows : (k + 1) * rows]
        merge_o[:, n * width : (n + 1) * width] = part[blocks * rows :]
    for n, part in enumerate(side_by_side(core_at, scal, own[...], got[...])):
        for k in range(3):
            at = (2 * k + n) * width
            heads_o[:, at : at + width] = part[k * rows : (k + 1) * rows]
    entries = own[3 * rows :] + got[3 * rows :]
    entries = entries[0:1] + entries[1:2]
    at = 0
    for share in shares_o:
        n = share.shape[1]
        moved = entries if at == 0 else pltpu.roll(entries, width - at, 1)
        share[...] = moved[:, :n]
        at += n


def per_device(
    tokens, w_heads, b_heads, w_merge, b_merge, gain_first, bias_first, w_expand, b_expand,
    w_reduce, b_reduce, gain_second, bias_second, seq_lengths, cotangent,
):
    rows = tokens.shape[0]
    seqs = seq_lengths.shape[1]
    n_dp = lax.axis_size("dp")
    ring = Ring(n_dp)
    head = lax.axis_index("head")
    dp = lax.axis_index("dp")
    core = dp % 2
    place_of = jnp.stack([head, core, head, (dp // 2) % 2, dp // 4]).astype(jnp.int32)
    scal = jnp.concatenate([seq_lengths[0].astype(jnp.int32), place_of])
    head_at, core_at, pos_at = seqs, seqs + 1, seqs + 2
    first_core = core == 0
    line = lambda v: v.reshape(1, -1)
    b_heads, b_merge, gain_first, bias_first, b_expand, b_reduce, gain_second, bias_second = map(
        line, (b_heads, b_merge, gain_first, bias_first, b_expand, b_reduce, gain_second, bias_second)
    )
    wide_shape = (rows, D)
    quarter = 256

    turned = ((4, D // 4, rows), BF, None, None)
    rk, v, state, tcol, trow, tokens_t = call(
        functools.partial(kv_kernel, seqs), "keys_values", scal, (3,),
        [
            (tokens, None, None),
            (w_heads, (D, quarter), lambda j, s: (0, 3 + j)),
            (w_heads, (D, quarter), lambda j, s: (0, 6 + j)),
            (b_heads, (1, quarter), lambda j, s: (0, 3 + j)),
            (b_heads, (1, quarter), lambda j, s: (0, 6 + j)),
        ],
        [
            (wide_shape, BF, (rows, quarter), lambda j, s: (0, j)),
            (wide_shape, BF, (rows, quarter), lambda j, s: (0, j)),
            ((PAIRS + 1, LANES, LANES), BF, None, None),
            ((rows, LANES), F32, None, None),
            ((8, rows), F32, None, None), turned,
        ],
        [pltpu.VMEM((LANES, LANES), F32)],
        us=4,
    )
    prior = ring.x(state)

    fast = n_dp == 16
    order = scal
    if fast:
        tokens_o = ring.core(tokens_t)
    rq, num, den = call(
        local_kernel, "local_attention", scal, (3,),
        [
            (tokens, None, None),
            (w_heads, (D, quarter), lambda j, s: (0, j)),
            (b_heads, (1, quarter), lambda j, s: (0, j)),
            (rk, (rows, quarter), lambda j, s: (0, j)),
            (v, (rows, quarter), lambda j, s: (0, j)),
            (tcol, None, None),
            (trow, None, None),
        ],
        [
            (wide_shape, BF, (rows, quarter), lambda j, s: (0, j)),
            (wide_shape, F32, (rows, quarter), lambda j, s: (0, j)),
            (wide_shape, F32, (rows, quarter), lambda j, s: (0, j)),
        ],
        [pltpu.VMEM((rows, rows), F32)],
        us=6,
    )

    if fast:
        order = after(scal, tokens_o)
    att, inv, mixed, xhat, scale, normed, second, turned_own, act, slope = call(
        functools.partial(ffn_kernel, head_at), "feed_forward", order, (FFN_STEPS,),
        [
            (rq, None, None), (num, None, None), (den, None, None), (prior, None, None),
            (tcol, None, None), (tokens, None, None), (w_merge, None, None), (b_merge, None, None),
            (gain_first, None, None), (bias_first, None, None), (b_reduce, None, None),
            (w_expand, (D, FFN_BLOCK), lambda j, s: (0, j)),
            (b_expand, (1, FFN_BLOCK), lambda j, s: (0, j)),
            (w_reduce, (FFN_BLOCK, D), lambda j, s: (j, 0)),
        ],
        [
            (wide_shape, F32, None, None), (wide_shape, F32, None, None), (wide_shape, BF, None, None),
            (wide_shape, F32, None, None), ((rows, LANES), F32, None, None), (wide_shape, BF, None, None),
            (wide_shape, F32, None, None), ((2, 4, D // 4, rows), BF, None, None),
            ((rows, FF), BF, (rows, FFN_BLOCK), lambda j, s: (0, j)),
            ((rows, FF), BF, (rows, FFN_BLOCK), lambda j, s: (0, j)),
        ],
        us=11, vmem=VMEM_FFN,
    )

    half_shape = (rows, D // 2)
    result, grad_second, branch, bg_keep, bg_send, sums_second = call(
        functools.partial(second_kernel, core_at), "second_norm", scal, (1,),
        [(second, None, None), (cotangent, None, None), (gain_second, None, None), (bias_second, None, None)],
        [
            (wide_shape, BF, None, None), (wide_shape, F32, None, None), (wide_shape, BF, None, None),
            (half_shape, BF, None, None), (half_shape, BF, None, None), ((8, D), F32, None, None),
        ],
        us=2.6,
    )

    devices = ring.devices
    small, large = D // devices, FF // devices
    whole = lambda a: (a, None, None)
    part = lambda a, n: (a, (1, 1, D // 4, rows), lambda j, s: (n, j, 0, 0))
    by_z = lambda a: (a, (1, D // 4, rows), lambda j, s: (j, 0, 0))
    by_col = lambda a: (a, (rows, FF // 4), lambda j, s: (0, j))

    def group(kernel, name, scal, grid, ins, piece_rows, us, scratch=(), kind=Scatter):
        shape = (2, 4, piece_rows, D // 2)
        sent = call(
            functools.partial(kernel, pos_at), name, scal, grid, ins, [(shape, BF, None, None)] * 4, scratch, us
        )
        return kind(ring, core_at, name, sent)

    ff_half = FF_STEPS // 2
    in_hbm = lambda a: (a, None, pltpu.HBM)
    hidden = ((ff_half, rows, FF_BLOCK), BF, None, None)
    hidden_sums = ((1, FF // 2), F32, None, None)
    buffers = [
        pltpu.VMEM((ff_half, D, FF_BLOCK), BF), pltpu.VMEM((ff_half, FF_BLOCK, D), BF),
        pltpu.SemaphoreType.DMA((2, ff_half)),
    ]
    hidden_in = [whole(branch), whole(slope), in_hbm(w_expand), in_hbm(w_reduce)]
    pg_send, sum_sent, partial = call(
        functools.partial(back_sent_kernel, core_at), "feed_forward_back_sent", scal, (),
        [*hidden_in, whole(grad_second)],
        [hidden, hidden_sums, (wide_shape, F32, None, None)], buffers,
        us=5, vmem=VMEM_BACK,
    )
    order = scal
    if fast:
        pg_o = ring.core(pg_send)
        act_o, turned_other, bg_o = map(ring.core, (act, turned_own, bg_send))
        pieces = ((2, 2, 2, 2, large, D // 2), BF, None, None)
        sent = call(
            functools.partial(reduce_grad_kernel, pos_at), "grad_reduce", after(scal, partial, turned_other), (4,),
            [by_col(act), by_col(act_o), whole(bg_keep), whole(bg_o)], [pieces, pieces], us=6,
        )
        reduced = DepthScatter(ring, core_at, "grad_reduce", sent)
        reduced.send_near()
        order = after(scal, reduced.near)

    pg_keep, grad_first, mg_keep, mg_send, w_att, e_att, later, sum_kept, sums_first = call(
        functools.partial(back_kernel, core_at), "feed_forward_back", order, (),
        [
            *hidden_in,
            (partial, None, None), (gain_first, None, None), (xhat, None, None), (scale, None, None),
            (w_merge, None, None), (att, None, None), (inv, None, None), (rq, None, None), (tcol, None, None),
        ],
        [
            hidden, (wide_shape, F32, None, None), (half_shape, BF, None, None), (half_shape, BF, None, None),
            (wide_shape, BF, None, None), ((rows, LANES), BF, None, None),
            ((PAIRS + 1, LANES, LANES), BF, None, None), hidden_sums, ((8, D), F32, None, None),
        ],
        [pltpu.VMEM(wide_shape, F32), *buffers],
        us=COST_BACK, vmem=VMEM_BACK,
    )
    later = ring.x(later)

    if fast:
        mg_o = ring.core(mg_send)
        expanded = group(
            expand_grad_kernel, "grad_expand", scal, (4,),
            [
                part(turned_own, 1), part(turned_other, 1), whole(pg_keep), whole(pg_o),
                part(turned_own, 0), part(turned_other, 0), whole(mg_keep), whole(mg_o),
            ],
            5 * small, COST_EXPAND, kind=HalvingScatter,
        )
        expanded.send(later)
        order = after(scal, expanded.xs, later)

    by_pair = [*map(whole, (rq, rk, v, w_att))]
    both_states = [whole(e_att), whole(prior), whole(later), whole(tcol)]
    pj_out = [((3, rows // 2, D // 2), BF, None, None)] * 2
    pj_sums = ((3, 8, D // 2), F32, None, None)
    table = ((rows, rows), F32, None, None)
    *pj_send, sum_heads_sent, weights, weights_t = call(
        functools.partial(attn_sent_kernel, head_at, core_at), "attention_back_sent", order, (),
        [*by_pair, *both_states, whole(trow)], [*pj_out, pj_sums, table, table], us=COST_SENT, vmem=VMEM_ATTN,
    )
    order = scal
    if fast:
        pj_o = [ring.core(v) for v in pj_send]
        order = after(scal, reduced.add_near(after(scal, pj_send[0])))
        reduced.send_far()
    *pj_keep, sum_heads_kept = call(
        functools.partial(attn_kept_kernel, head_at, core_at), "attention_back_kept", order, (PAIRS // 2,),
        [*by_pair, *both_states, whole(weights), whole(weights_t)], [*pj_out, pj_sums], us=COST_KEPT, vmem=VMEM_ATTN,
    )

    if fast:
        order = after(scal, expanded.first(after(scal, pj_keep[0])))
        expanded.send_first()
        heads = group(
            functools.partial(heads_grad_kernel, devices=devices), "grad_heads", order, (4,),
            [
                by_z(tokens_t), by_z(tokens_o), *map(whole, (*pj_keep, *pj_o)),
                *map(whole, (sum_heads_kept, sum_heads_sent, sums_first, sum_kept, sum_sent, sums_second)),
            ],
            3 * small + 8, COST_HEADS, [pltpu.VMEM((devices, D // 2), F32)],
        )
        heads.send()
        order = after(scal, heads.xs)

    of_part = lambda a: (a, (1, rows // 2, D // 2), lambda j, s: (j, 0, 0))
    (input_grad,) = call(
        input_kernel, "input_grad", order, (3,),
        [
            whole(grad_first), *map(of_part, (*pj_keep, *pj_send)),
            (w_heads, (D, D // 2), lambda j, s: (0, 2 * j + s[core_at])),
            (w_heads, (D, D // 2), lambda j, s: (0, 2 * j + 1 - s[core_at])),
        ],
        [(wide_shape, F32, None, None)],
        us=COST_INPUT,
    )

    if fast:
        order = reduced.add_far(after(scal, input_grad))
        order = expanded.second(after(scal, order))
        expanded.send_second()
        reduced.send_side()
        order = heads.first(after(scal, order))
        heads.send_first()
        order = expanded.third(after(scal, order))
        expanded.send_third()
        order = heads.second(after(scal, order))
        heads.send_second()
        order = reduced.add_side(after(scal, order))
        expand_own, expand_got = expanded.last(after(scal, order))
        reduce_own, reduce_got = reduced.last(after(scal, expand_own))
        heads_own, heads_got = heads.last(after(scal, reduce_own))
        out = lambda n, m: ((n, m), F32, None, None)
        counts = (2 * small, small, small, small, small, large, small, small, small)
        w_heads_grad, w_reduce_grad, w_expand_grad, w_merge_grad, *shares = call(
            functools.partial(finish_kernel, core_at), "finish", scal, (),
            [*map(whole, (heads_own, heads_got, reduce_own, reduce_got, expand_own, expand_got))],
            [out(small, 3 * D), out(large, D), out(small, FF), out(small, D), *(out(1, n) for n in counts)],
        )
        shares = [share.reshape(-1) for share in shares]
        grads = (
            w_heads_grad, *shares[:2], w_merge_grad, *shares[2:5], w_expand_grad, shares[5], w_reduce_grad,
            *shares[6:],
        )
    else:
        by_core = lambda keep, send: jnp.concatenate(
            [jnp.where(first_core, keep, send), jnp.where(first_core, send, keep)], axis=1
        )
        flat = lambda v: v.transpose(1, 0, 2).reshape(rows, -1)
        by_heads = lambda keep, send: jnp.concatenate(
            [by_core(keep[n], send[n]) for n in range(3)], axis=1
        )
        pj_keep, pj_send = (jnp.concatenate(v, axis=1) for v in (pj_keep, pj_send))
        sum_heads = by_heads(sum_heads_kept, sum_heads_sent)[0]
        scatter = lambda v: lax.psum_scatter(v, AXES, scatter_dimension=0, tiled=True)
        grads = (
            scatter(dot_t(tokens, by_heads(pj_keep, pj_send))),
            scatter(sum_heads[: 2 * D]), scatter(sum_heads[2 * D :]),
            scatter(dot_t(mixed, by_core(mg_keep, mg_send))),
            scatter(sums_first[2]), scatter(sums_first[0]), scatter(sums_first[1]),
            scatter(dot_t(normed, by_core(flat(pg_keep), flat(pg_send)))),
            scatter(by_core(sum_kept, sum_sent)[0]),
            scatter(dot_t(act, branch)),
            scatter(sums_second[2]), scatter(sums_second[0]), scatter(sums_second[1]),
        )
    return (result, input_grad) + tuple(grads)


def solution(mesh):
    in_specs = (P(AXES, None),) + (P(),) * 12 + (P("dp", None), P(AXES, None))
    row, one = P(AXES, None), P(AXES)
    out_specs = (row, row, row, one, one, row, one, one, one, row, one, row, one, one, one)
    return jax.shard_map(
        per_device, mesh=mesh, in_specs=in_specs, out_specs=out_specs, check_vma=False
    )
```

```python
import functools
import math

import jax
import jax.numpy as jnp
from jax import lax
from jax.experimental import pallas as pl
from jax.experimental.pallas import tpu as pltpu
from jax.sharding import PartitionSpec as P

D = 768
PAIRS = 6
FF = 3072
LANES = 128
HALF = 64
BF = jnp.bfloat16
F32 = jnp.float32
AXES = ("dp", "head")
VMEM_LIMIT = 8 << 20
VMEM_FFN = 16 << 20
VMEM_ATTN = 10 << 20
FF_BLOCK = 768
FFN_BLOCK = 1024
FFN_STEPS = FF // FFN_BLOCK
MATMUL_PER_US = 1.15e9
COST_EXPAND = 1
VMEM_BACK = 16 << 20
COST_KEPT = 0.5
COST_BACK = 3
COST_SENT = 0.5
COST_HEADS = 0.1
COST_INPUT = 0.1
FF_STEPS = FF // FF_BLOCK


def dot(a, b):
    return jnp.dot(a, b, preferred_element_type=F32)


def dot_t(a, b):
    return lax.dot_general(a, b, (((0,), (0,)), ((), ())), preferred_element_type=F32)


def dot_r(a, b):
    return lax.dot_general(a, b, (((1,), (1,)), ((), ())), preferred_element_type=F32)


def call(kernel, name, scal, grid, ins, outs, scratch=(), us=0.1, vmem=VMEM_LIMIT):
    def spec(b, m):
        if b is None:
            return pl.BlockSpec(memory_space=pltpu.VMEM if m is None else m)
        return pl.BlockSpec(b, m)

    in_specs = [spec(b, m) for _, b, m in ins]
    out_specs = [spec(b, m) for _, _, b, m in outs]
    return pl.pallas_call(
        kernel,
        name=name,
        grid_spec=pltpu.PrefetchScalarGridSpec(
            num_scalar_prefetch=1,
            grid=grid,
            in_specs=in_specs,
            out_specs=out_specs,
            scratch_shapes=list(scratch),
        ),
        out_shape=[jax.ShapeDtypeStruct(s, d) for s, d, _, _ in outs],
        compiler_params=pltpu.CompilerParams(vmem_limit_bytes=vmem),
        cost_estimate=pl.CostEstimate(flops=int(us * MATMUL_PER_US), bytes_accessed=1, transcendentals=0),
    )(scal, *[a for a, _, _ in ins])


def lane_masks():
    lane = lax.broadcasted_iota(jnp.int32, (1, LANES), 1)
    even = (lane < HALF).astype(F32)
    return lane, even.astype(BF), (1.0 - even).astype(BF)


def both_heads(pair):
    lane, even, odd = lane_masks()
    return jnp.concatenate([pair * even, pair * odd], axis=0)


def own_lanes(stacked):
    rows = stacked.shape[0] // 2
    lane = lax.broadcasted_iota(jnp.int32, (1, LANES), 1)
    return jnp.where(lane < HALF, stacked[:rows], stacked[rows:])


def square_masks():
    row = lax.broadcasted_iota(jnp.int32, (LANES, LANES), 0)
    lane = lax.broadcasted_iota(jnp.int32, (LANES, LANES), 1)
    upper = row < HALF
    return lane, upper, upper == (lane < HALF)


def high_low(v):
    high = v.astype(BF).astype(F32)
    return high, v - high


def tables(scal, rows, seqs, tcol, trow):
    pos = lax.broadcasted_iota(jnp.int32, (1, rows), 1) + scal[seqs] * rows
    seg = jnp.zeros((1, rows), jnp.int32)
    first = jnp.zeros((1, rows), jnp.int32)
    length = jnp.ones((1, rows), jnp.int32)
    at_boundary = jnp.int32(0)
    begin = jnp.int32(0)
    for s in range(seqs):
        end = begin + scal[s]
        inside = (pos >= begin) & (pos < end)
        first = jnp.where(inside, begin, first)
        length = jnp.where(inside, jnp.maximum(scal[s], 1), length)
        seg = seg + (pos >= end).astype(jnp.int32)
        at_boundary = at_boundary + (rows - 1 >= end).astype(jnp.int32)
        begin = end
    live = (seg < seqs).astype(F32)
    angle = 0.5 * math.pi * (pos - first).astype(F32) / length.astype(F32)
    cos_w = jnp.cos(angle) * live
    sin_w = jnp.sin(angle) * live
    crossing = (seg == at_boundary).astype(F32)
    which = lax.broadcasted_iota(jnp.int32, (LANES, rows), 0)
    table = jnp.zeros((LANES, rows), F32)
    for n, entry in enumerate((cos_w, sin_w, seg.astype(F32), cos_w * crossing, sin_w * crossing)):
        table = jnp.where(which == n, entry, table)
    trow[...] = table[:8]
    tcol[...] = table.T


def pack_state(both, norm_cos, norm_sin, pair, norms):
    lane, upper, diag = square_masks()
    packed = jnp.where(diag, both[:LANES, :LANES], pltpu.roll(both[LANES:, :LANES], HALF, 1))
    cos_high, cos_low = high_low(norm_cos)
    sin_high, sin_low = high_low(norm_sin)
    for n, part in enumerate((cos_high, cos_low, sin_high, sin_low)):
        norms = jnp.where(lane == 4 * pair + n, part, norms)
    return packed.astype(BF), norms


def unpack_state(state_ref, pair):
    lane, upper, diag = square_masks()
    packed = state_ref[pair].astype(F32)
    norms = state_ref[PAIRS].astype(F32)
    of_cos = jnp.where(diag, packed, 0.0)
    of_sin = jnp.where(diag, pltpu.roll(packed, HALF, 1), 0.0)
    pick = lambda n: jnp.sum(
        jnp.where((lane == 4 * pair + n) | (lane == 4 * pair + n + 1), norms, 0.0), axis=1, keepdims=True
    )
    return of_cos, of_sin, pick(0), pick(2)


def turn(value, out):
    turned = value.T
    share = out.shape[1]
    for n in range(out.shape[0]):
        out[n] = turned[n * share : (n + 1) * share]


def kv_kernel(seqs, scal, tok, wk, wv, bk, bv, rk_o, v_o, st_o, tcol, trow, turned_o, norms):
    step = pl.program_id(0)
    rows = tok.shape[0]

    @pl.when(step == 0)
    def _():
        tables(scal, rows, seqs, tcol, trow)
        norms[...] = jnp.zeros_like(norms)
        turn(tok[...], turned_o)

    rk = jnp.maximum(dot(tok[...], wk[...]) + bk[...].astype(F32), 0.0).astype(BF)
    v = (dot(tok[...], wv[...]) + bv[...].astype(F32)).astype(BF)
    rk_o[...] = rk
    v_o[...] = v
    cos_b, sin_b = tcol[:, 3:4], tcol[:, 4:5]
    ones = jnp.ones((rows, LANES), BF)
    for n in range(2):
        pair = 2 * step + n
        cols = slice(n * LANES, (n + 1) * LANES)
        kp = rk[:, cols].astype(F32)
        left = jnp.concatenate([(kp * cos_b).astype(BF), (kp * sin_b).astype(BF)], axis=1)
        both = dot_t(left, jnp.concatenate([v[:, cols], ones], axis=1))
        packed, new_norms = pack_state(both, both[:LANES, LANES:], both[LANES:, LANES:], pair, norms[...])
        st_o[pair] = packed
        norms[...] = new_norms

    st_o[PAIRS] = norms[...].astype(BF)


def weights_block(tcol, trow, transposed):
    rows = tcol.shape[0]
    down = lax.broadcasted_iota(jnp.int32, (rows, rows), 0)
    along = lax.broadcasted_iota(jnp.int32, (rows, rows), 1)
    same = tcol[:, 2:3] == trow[2:3, :]
    causal = (down <= along) if transposed else (along <= down)
    value = tcol[:, 0:1] * trow[0:1, :] + tcol[:, 1:2] * trow[1:2, :]
    return jnp.where(same & causal, value, 0.0)


def weigh(stacked, weights):
    rows = weights.shape[0]
    return jnp.concatenate([stacked[:rows] * weights, stacked[rows:] * weights], axis=0).astype(BF)


def local_kernel(scal, tok, wq, bq, rk, v, tcol, trow, rq_o, num_o, den_o, weights):
    step = pl.program_id(0)
    rows = tok.shape[0]
    mid = rows // 2

    @pl.when(step == 0)
    def _():
        weights[...] = weights_block(tcol, trow, False)

    rq = jnp.maximum(dot(tok[...], wq[...]) + bq[...].astype(F32), 0.0).astype(BF)
    rq_o[...] = rq
    ones = jnp.ones((rows, LANES), BF)
    for n in range(2):
        cols = slice(n * LANES, (n + 1) * LANES)
        kp = rk[:, cols]
        values = jnp.concatenate([v[:, cols], ones], axis=1)
        first = weigh(dot_r(both_heads(rq[:, cols]), kp[:mid]), weights[:, :mid])
        second = weigh(dot_r(both_heads(rq[mid:, cols]), kp[mid:]), weights[mid:, mid:])
        sums = dot(first, values[:mid])
        late = dot(second, values[mid:])
        for own, out in ((slice(0, LANES), num_o), (slice(LANES, 2 * LANES), den_o)):
            total = own_lanes(sums[:, own])
            out[:mid, cols] = total[:mid]
            out[mid:, cols] = total[mid:] + own_lanes(late[:, own])


def normalise(entries):
    mean = jnp.mean(entries, axis=1, keepdims=True)
    centred = entries - mean
    var = jnp.mean(centred * centred, axis=1, keepdims=True)
    scale = lax.rsqrt(var + 1e-05)
    return centred * scale, scale


def merge_heads(
    head_at, scal, rq, num, den, st, tcol, tok, w_merge, b_merge, gain, bias, b_red,
    att_o, inv_o, mixed_o, xhat_o, scale_o, normed_o, acc_o, turned_o,
):
    cross = (scal[head_at] == 1).astype(F32)
    cos_b, sin_b = tcol[:, 3:4] * cross, tcol[:, 4:5] * cross
    sq_lane, upper, diag = square_masks()
    for pair in range(PAIRS):
        cols = slice(pair * LANES, (pair + 1) * LANES)
        qp = rq[:, cols].astype(F32)
        of_cos, of_sin, norm_cos, norm_sin = unpack_state(st, pair)
        top = jnp.concatenate([of_cos, jnp.where(diag, norm_cos, 0.0)], axis=1)
        low = jnp.concatenate([of_sin, jnp.where(diag, norm_sin, 0.0)], axis=1)
        right = jnp.concatenate([top, low], axis=0).astype(BF)
        left = jnp.concatenate([(qp * cos_b).astype(BF), (qp * sin_b).astype(BF)], axis=1)
        prior = dot(left, right)
        inverse = 1.0 / (den[:, cols] + prior[:, LANES:] + 1.0)
        attended = (num[:, cols] + prior[:, :LANES]) * inverse
        att_o[:, cols] = attended
        inv_o[:, cols] = inverse
        mixed_o[:, cols] = attended.astype(BF)
    first_in = tok[...].astype(F32) + dot(mixed_o[...], w_merge[...]) + b_merge[...].astype(F32)
    xhat, scale = normalise(first_in)
    normed = xhat * gain[...].astype(F32) + bias[...].astype(F32)
    xhat_o[...] = xhat
    scale_o[...] = jnp.broadcast_to(scale, scale_o.shape)
    normed_o[...] = normed.astype(BF)
    acc_o[...] = normed + b_red[...].astype(F32)
    turn(mixed_o[...], turned_o.at[0])
    turn(normed_o[...], turned_o.at[1])


def expand_reduce(normed, w_exp, b_exp, w_red, act_o, slope_o, acc_o):
    rows = normed.shape[0]
    pre = [dot(normed[at : at + rows // 2], w_exp[...]) + b_exp[...].astype(F32) for at in (0, rows // 2)]
    for at, x in zip((0, rows // 2), pre):
        part = slice(at, at + rows // 2)
        cdf = 0.5 + 0.5 * lax.erf(x * (2.0**-0.5))
        pdf = jnp.exp(-0.5 * x * x) * (1.0 / math.sqrt(2.0 * math.pi))
        act = (x * cdf).astype(BF)
        act_o[part] = act
        slope_o[part] = (cdf + x * pdf).astype(BF)
        acc_o[part] += dot(act, w_red[...])


def ffn_kernel(head_at, scal, *refs):
    w_exp, b_exp, w_red = refs[11:14]
    normed_o, acc_o = refs[19:21]
    act_o, slope_o = refs[22:]

    @pl.when(pl.program_id(0) == 0)
    def _():
        merge_heads(head_at, scal, *refs[:11], *refs[14:22])

    expand_reduce(normed_o, w_exp, b_exp, w_red, act_o, slope_o, acc_o)


def second_kernel(core_at, scal, second, cot, gain, bias, out_o, grad_o, full_o, keep_o, send_o, sums_o):
    xhat, scale = normalise(second[...])
    gain_w = gain[...].astype(F32)
    out_o[...] = (xhat * gain_w + bias[...].astype(F32)).astype(BF)
    cot_w = cot[...].astype(F32)
    t = cot_w * gain_w
    grad = scale * (
        t - jnp.mean(t, axis=1, keepdims=True) - xhat * jnp.mean(t * xhat, axis=1, keepdims=True)
    )
    low = grad.astype(BF)
    grad_o[...] = grad
    full_o[...] = low
    first = scal[core_at] == 0
    half = D // 2
    left, right = grad[:, :half], grad[:, half:]
    keep_o[...] = jnp.where(first, left, right).astype(BF)
    send_o[...] = jnp.where(first, right, left).astype(BF)
    sums_o[0:1] = jnp.sum(cot_w * xhat, axis=0, keepdims=True)
    sums_o[1:2] = jnp.sum(cot_w, axis=0, keepdims=True)
    sums_o[2:3] = jnp.sum(low.astype(F32), axis=0, keepdims=True)


def head_lanes(pair, lane, first):
    at = 4 * pair + jnp.where(first, 0, 2)
    return (lane == at) | (lane == at + 1)


def weight_copies(half, w_exp, w_red, exp_buf, red_buf, sems, n):
    at = pl.ds(pl.multiple_of((half * exp_buf.shape[0] + n) * FF_BLOCK, FF_BLOCK), FF_BLOCK)
    return (
        pltpu.make_async_copy(w_red.at[at, :], red_buf.at[n], sems.at[0, n]),
        pltpu.make_async_copy(w_exp.at[:, at], exp_buf.at[n], sems.at[1, n]),
    )


def back_steps(half, full, slope, w_exp, w_red, out_o, bexp_o, exp_buf, red_buf, sems):
    blocks = exp_buf.shape[0]
    copies = [weight_copies(half, w_exp, w_red, exp_buf, red_buf, sems, n) for n in range(blocks)]
    for pair in copies:
        for copy in pair:
            copy.start()
    total = None
    for n, (of_red, of_exp) in enumerate(copies):
        cols = slice(n * FF_BLOCK, (n + 1) * FF_BLOCK)
        at = pl.ds(pl.multiple_of((half * blocks + n) * FF_BLOCK, FF_BLOCK), FF_BLOCK)
        of_red.wait()
        pre_grad = (dot_r(full[...], red_buf[n]) * slope[:, at].astype(F32)).astype(BF)
        bexp_o[:, cols] = jnp.sum(pre_grad.astype(F32), axis=0, keepdims=True)
        out_o[n] = pre_grad
        of_exp.wait()
        part = dot_r(pre_grad, exp_buf[n])
        total = part if total is None else total + part
    return total


def back_sent_kernel(core_at, scal, full, slope, w_exp, w_red, grad2, sent_o, bexp_o, acc, exp_buf, red_buf, sems):
    half = 1 - scal[core_at]
    acc[...] = grad2[...] + back_steps(half, full, slope, w_exp, w_red, sent_o, bexp_o, exp_buf, red_buf, sems)


def back_kernel(
    core_at, scal, full, slope, w_exp, w_red, acc_in, gain, xhat, scale, w_merge, att, inv, rq, tcol,
    kept_o, first_o, mk_o, ms_o, w_o, e_o, st_o, bexp_o, sums_o,
    acc, exp_buf, red_buf, sems,
):
    half = scal[core_at]
    acc[...] = acc_in[...] + back_steps(half, full, slope, w_exp, w_red, kept_o, bexp_o, exp_buf, red_buf, sems)
    back_rest(
        core_at, scal, acc, gain, xhat, scale, w_merge, att, inv, rq, tcol,
        first_o, mk_o, ms_o, w_o, e_o, st_o, sums_o,
    )


def back_rest(
    core_at, scal, acc, gain, xhat, scale, w_merge, att, inv, rq, tcol,
    first_o, mk_o, ms_o, w_o, e_o, st_o, sums_o,
):
    grad_normed = acc[...]
    xh = xhat[...]
    t = grad_normed * gain[...].astype(F32)
    first = scale[:, 0:1] * (
        t - jnp.mean(t, axis=1, keepdims=True) - xh * jnp.mean(t * xh, axis=1, keepdims=True)
    )
    low = first.astype(BF)
    first_o[...] = first
    sums_o[0:1] = jnp.sum(grad_normed * xh, axis=0, keepdims=True)
    sums_o[1:2] = jnp.sum(grad_normed, axis=0, keepdims=True)
    sums_o[2:3] = jnp.sum(low.astype(F32), axis=0, keepdims=True)
    is_first = scal[core_at] == 0
    left, right = first[:, : D // 2], first[:, D // 2 :]
    mk_o[...] = jnp.where(is_first, left, right).astype(BF)
    ms_o[...] = jnp.where(is_first, right, left).astype(BF)
    cos_b, sin_b = tcol[:, 3:4], tcol[:, 4:5]
    w = (dot_r(low, w_merge[...]).astype(BF).astype(F32) * inv[...]).astype(BF)
    w_o[...] = w
    high, rest = high_low(w.astype(F32) * att[...])
    column = lax.broadcasted_iota(jnp.int32, (D, LANES), 0)
    target = lax.broadcasted_iota(jnp.int32, (D, LANES), 1)
    picks = (target == 2 * (column // HALF)).astype(F32).astype(BF)
    e_high, e_low = high_low(-(dot(high.astype(BF), picks) + dot(rest.astype(BF), picks)))
    e = (e_high + pltpu.roll(e_low, 1, 1)).astype(BF)
    e_o[...] = e
    norms = jnp.zeros((LANES, LANES), F32)
    sq_lane, upper, diag = square_masks()
    for pair in range(PAIRS):
        cols = slice(pair * LANES, (pair + 1) * LANES)
        qp = rq[:, cols].astype(F32)
        left = jnp.concatenate([(qp * cos_b).astype(BF), (qp * sin_b).astype(BF)], axis=1)
        both = dot_t(left, jnp.concatenate([w[:, cols], e], axis=1))
        mine = head_lanes(pair, sq_lane, upper)
        norm = lambda part: jnp.sum(jnp.where(mine, part, 0.0), axis=1, keepdims=True)
        packed, norms = pack_state(both, norm(both[:LANES, LANES:]), norm(both[LANES:, LANES:]), pair, norms)
        st_o[pair] = packed
    st_o[PAIRS] = norms.astype(BF)


def attn_sent_kernel(head_at, core_at, scal, rq, rk, v, w, e, prior, later, tcol, trow, early_o, late_o, sums_o, weights, weights_t):
    weights[...] = weights_block(tcol, trow, False)
    weights_t[...] = weights_block(tcol, trow, True)
    first = (1 - scal[core_at]) * (PAIRS // 2)
    attn_back(head_at, first, scal, rq, rk, v, w, e, prior, later, tcol, weights, weights_t, early_o, late_o, sums_o)


def attn_kept_kernel(head_at, core_at, scal, rq, rk, v, w, e, prior, later, tcol, weights, weights_t, early_o, late_o, sums_o):
    step = pl.program_id(0)
    attn_back_pair(
        head_at, scal[core_at] * (PAIRS // 2) + step, step,
        scal, rq, rk, v, w, e, prior, later, tcol, weights, weights_t, early_o, late_o, sums_o,
    )


def attn_back(head_at, first, scal, rq, rk, v, w, e, prior, later, tcol, weights, weights_t, early_o, late_o, sums_o):
    for n in range(PAIRS // 2):
        attn_back_pair(
            head_at, first + n, n, scal, rq, rk, v, w, e, prior, later, tcol, weights, weights_t, early_o, late_o, sums_o
        )


def attn_back_pair(
    head_at, pair, slot, scal, rq, rk, v, w, e, prior, later, tcol, weights, weights_t, early_o, late_o, sums_o
):
    rows = rq.shape[0]
    mid = rows // 2
    cols = pl.ds(pl.multiple_of(pair * LANES, LANES), LANES)
    out = pl.ds(pl.multiple_of(slot * LANES, LANES), LANES)

    qp, kp, vp, wp = rq[:, cols], rk[:, cols], v[:, cols], w[:, cols]
    lane, even, odd = lane_masks()
    of_even = ((lane == 4 * pair) | (lane == 4 * pair + 1)).astype(F32).astype(BF)
    of_odd = ((lane == 4 * pair + 2) | (lane == 4 * pair + 3)).astype(F32).astype(BF)
    ones = jnp.ones((rows, LANES), BF)
    we = jnp.concatenate([wp, e[...]], axis=1)
    by_head = (jnp.concatenate([even, of_even], axis=1), jnp.concatenate([odd, of_odd], axis=1))
    ve = jnp.concatenate([vp, ones], axis=1)
    stack = lambda a, lo, hi: jnp.concatenate([a[lo:hi] * m for m in by_head], axis=0)

    grads = weigh(dot_r(stack(we, 0, rows), ve[:mid]), weights[:, :mid])
    dq = own_lanes(dot(grads, kp[:mid]))
    grads = weigh(dot_r(stack(we, mid, rows), ve[mid:]), weights[mid:, mid:])
    dq_late = own_lanes(dot(grads, kp[mid:]))

    grads = weigh(dot_r(stack(ve, 0, rows), we[mid:]), weights_t[:, mid:])
    dk = own_lanes(dot(grads, qp[mid:]))
    grads = weigh(dot_r(stack(ve, 0, mid), we[:mid]), weights_t[:mid, :mid])
    dk_early = own_lanes(dot(grads, qp[:mid]))

    scores = weigh(dot_r(both_heads(kp), qp[mid:]), weights_t[:, mid:])
    dv = own_lanes(dot(scores, wp[mid:]))
    scores = weigh(dot_r(both_heads(kp[:mid]), qp[:mid]), weights_t[:mid, :mid])
    dv_early = own_lanes(dot(scores, wp[:mid]))

    dq = jnp.concatenate([dq[:mid], dq[mid:] + dq_late], axis=0)
    dk = jnp.concatenate([dk[:mid] + dk_early, dk[mid:]], axis=0)
    dv = jnp.concatenate([dv[:mid] + dv_early, dv[mid:]], axis=0)

    sq_lane, upper, diag = square_masks()
    cos_b, sin_b = tcol[:, 3:4], tcol[:, 4:5]
    is_late = (scal[head_at] == 1).astype(F32)
    early = 1.0 - is_late

    def with_norms(parts, where):
        side = lambda total, norm: jnp.concatenate([total, jnp.where(where, norm, 0.0)], axis=1)
        of_cos, of_sin, norm_cos, norm_sin = parts
        return jnp.concatenate([side(of_cos, norm_cos), side(of_sin, norm_sin)], axis=0).astype(BF)

    prior_parts = unpack_state(prior, pair)
    into = dot_r(we, with_norms(prior_parts, head_lanes(pair, sq_lane, upper)))
    dq = dq + is_late * (cos_b * into[:, :LANES] + sin_b * into[:, LANES:])
    later_parts = unpack_state(later, pair)
    into = dot_r(ve, with_norms(later_parts, sq_lane == 0))
    dk = dk + early * (cos_b * into[:, :LANES] + sin_b * into[:, LANES:])
    kw = kp.astype(F32)
    left = jnp.concatenate([(kw * (cos_b * early)).astype(BF), (kw * (sin_b * early)).astype(BF)], axis=1)
    dv = dv + dot(left, jnp.concatenate(later_parts[:2], axis=0).astype(BF))

    dq = jnp.where(qp.astype(F32) > 0, dq, 0.0).astype(BF)
    dk = jnp.where(kw > 0, dk, 0.0).astype(BF)
    dv = dv.astype(BF)
    for n, part in enumerate((dq, dk, dv)):
        total = jnp.sum(part.astype(F32), axis=0, keepdims=True)
        sums_o[n, :, out] = jnp.broadcast_to(total, (sums_o.shape[1], LANES))
        early_o[n, :, out] = part[:mid]
        late_o[n, :, out] = part[mid:]


def input_kernel(scal, first, keep_early, keep_late, send_early, send_late, w_keep, w_send, out_o):
    @pl.when(pl.program_id(0) == 0)
    def _():
        out_o[...] = first[...]

    rows = lambda early, late: jnp.concatenate([early[0], late[0]], axis=0)
    out_o[...] += dot_r(rows(keep_early, keep_late), w_keep[...]) + dot_r(rows(send_early, send_late), w_send[...])


def place(values, piece_rows, tz, tys, x, y, z, extra, outs):
    xk, xs, yk, ys = outs
    width = xk.shape[-1]
    slot_z = tz ^ z
    pieces = {}
    at = 0
    for ty in tys:
        for tc in range(2):
            for tx in range(2):
                part = values[at * piece_rows : (at + 1) * piece_rows]
                blocks = [part[:, n : n + width] for n in range(0, part.shape[1], width)]
                if extra is not None:
                    blocks.append(extra[at])
                pieces[ty, tc, tx] = jnp.concatenate(blocks, axis=0) if len(blocks) > 1 else blocks[0]
                at += 1
    for ty in tys:
        slot = ty ^ y
        a, b = pieces[ty, 0, 0], pieces[ty, 0, 1]
        xk[slot, slot_z] = jnp.where(x == 0, a, b).astype(BF)
        xs[slot, slot_z] = jnp.where(x == 0, b, a).astype(BF)
    return pieces


def place_y(pieces, tz, tys, x, y, z, outs):
    xk, xs, yk, ys = outs
    slot_z = tz ^ z
    for tx in range(2):
        slot = tx ^ x
        a, b = pieces[0, 1, tx], pieces[1, 1, tx]
        yk[slot, slot_z] = jnp.where(y == 0, a, b).astype(BF)
        ys[slot, slot_z] = jnp.where(y == 0, b, a).astype(BF)


def reduce_grad_kernel(pos_at, scal, a_own, a_oth, b_own, b_oth, kept, near):
    tz = pl.program_id(0)
    x, y, z = (scal[pos_at + n] for n in range(3))
    values = dot_t(a_own[...], b_own[...]) + dot_t(a_oth[...], b_oth[...])
    rows = values.shape[0] // 8
    slot = tz ^ z

    def put(out):
        for n in range(8):
            ty, tc, tx = n // 4, n // 2 % 2, n % 2
            out[slot // 2, tc, tx ^ x, ty ^ y] = values[n * rows : (n + 1) * rows].astype(BF)

    @pl.when(slot % 2 == 0)
    def _():
        put(kept)

    @pl.when(slot % 2 == 1)
    def _():
        put(near)


def expand_grad_kernel(pos_at, scal, a_own, a_oth, b_own, b_oth, m_own, m_oth, c_own, c_oth, *outs):
    x, y, z = (scal[pos_at + n] for n in range(3))
    for half in range(2):
        tz = 2 * pl.program_id(0) + half
        an, ao = a_own[0, half], a_oth[0, half]
        parts = [dot(an, b_own[n]) + dot(ao, b_oth[n]) for n in range(b_own.shape[0])]
        parts.append(dot(m_own[0, half], c_own[...]) + dot(m_oth[0, half], c_oth[...]))
        values = jnp.concatenate(parts, axis=1)
        pieces = place(values, values.shape[0] // 8, tz, (0, 1), x, y, z, None, outs)
        place_y(pieces, tz, (0, 1), x, y, z, outs)


def share_lanes(entries, devices, at, width):
    n = entries.shape[1]
    share = n // devices
    owner = lax.broadcasted_iota(jnp.int32, (devices, n), 0)
    column = lax.broadcasted_iota(jnp.int32, (devices, n), 1)
    mine = (column >= owner * share) & (column < (owner + 1) * share)
    high, low = high_low(jnp.where(mine, entries, 0.0))
    both = jnp.concatenate([high, low], axis=0).astype(BF)
    source = lax.broadcasted_iota(jnp.int32, (n, width), 0)
    target = lax.broadcasted_iota(jnp.int32, (n, width), 1)
    picks = (target >= at) & (target < at + share) & (lax.rem(source, share) == target - at)
    spread = dot(both, picks.astype(F32).astype(BF))
    return spread[:devices] + spread[devices:]


def heads_grad_kernel(
    pos_at, scal, a_own, a_oth, own_early, own_late, oth_early, oth_late, kept_h, sent_h, sums_1, kept_e, sent_e, sums_2, *refs, devices
):
    outs, table = refs[:-1], refs[-1]
    tz = pl.program_id(0)
    x, y, z = (scal[pos_at + n] for n in range(3))
    width = outs[0].shape[-1]

    @pl.when(tz == 0)
    def _():
        first_core = scal[pos_at - 1] == 0
        ordered = lambda kept, sent: [jnp.where(first_core, kept, sent), jnp.where(first_core, sent, kept)]
        sums_e = jnp.concatenate(ordered(kept_e[...], sent_e[...]), axis=1)
        of_heads = [part for n in range(3) for part in ordered(kept_h[n, 0:1], sent_h[n, 0:1])]
        total = jnp.zeros((devices, width), F32)
        at = 0
        for entries in (
            jnp.concatenate(of_heads[:4], axis=1), jnp.concatenate(of_heads[4:], axis=1), sums_1[2:3], sums_1[0:1], sums_1[1:2],
            sums_e, sums_2[2:3], sums_2[0:1], sums_2[1:2],
        ):
            total = total + share_lanes(entries, devices, at, width)
            at += entries.shape[1] // devices
        table[...] = total

    join = lambda early, late: jnp.concatenate(
        [jnp.concatenate([early[n], late[n]], axis=0) for n in range(early.shape[0])], axis=1
    )
    values = dot(a_own[0], join(own_early, own_late)) + dot(a_oth[0], join(oth_early, oth_late))
    line = lax.broadcasted_iota(jnp.int32, (8, width), 0)
    rows8 = table[pl.ds(pl.multiple_of(tz * 8, 8), 8)]
    extra = []
    for n in range(8):
        high, low = high_low(rows8[n : n + 1])
        extra.append(jnp.where(line == 0, high, jnp.where(line == 1, low, 0.0)))
    pieces = place(values, values.shape[0] // 8, tz, (0, 1), x, y, z, extra, outs)
    place_y(pieces, tz, (0, 1), x, y, z, outs)


class Ring:
    def __init__(self, n_dp):
        self.n_dp = n_dp
        self.devices = 2 * n_dp

    def swap(self, value, bits):
        return lax.ppermute(value, AXES, [(i, i ^ bits) for i in range(self.devices)])

    def core(self, value):
        return self.swap(value, 2)

    def x(self, value):
        return self.swap(value, 1)

    def y(self, value):
        return self.swap(value, 4)

    def z(self, value, step):
        return self.swap(value, 8 * step)


def add_first_kernel(scal, xk, xr, yk, yr, xn, yn):
    wide = lambda ref: ref[0].astype(F32)
    xn[...] = (wide(xk) + wide(xr)).astype(BF)
    yn[...] = (wide(yk) + wide(yr)).astype(BF)


def add_second_kernel(scal, xk, xr, xm, yk, yr, ym, own, z1, z2, z3):
    for n, (keep, got, more) in enumerate(((xk, xr, xm), (yk, yr, ym))):
        total = lambda k: keep[0, k].astype(F32) + got[0, k].astype(F32) + more[k].astype(F32)
        own[n] = total(0)
        for k, out in ((1, z1), (2, z2), (3, z3)):
            out[n] = total(k).astype(BF)


def add_last_kernel(core_at, scal, own, z1, z2, z3, keep, send):
    first = scal[core_at] == 0
    total = lambda n: own[n] + z1[n].astype(F32) + z2[n].astype(F32) + z3[n].astype(F32)
    of_first, of_second = total(0), total(1)
    keep[...] = jnp.where(first, of_first, of_second)
    send[...] = jnp.where(first, of_second, of_first)


def add_second_half_kernel(scal, xk, xr, xm, yk, yr, ym, kept, sent):
    for n, (keep, got, more) in enumerate(((xk, xr, xm), (yk, yr, ym))):
        total = lambda k: keep[0, k].astype(F32) + got[0, k].astype(F32) + more[k].astype(F32)
        for k in range(2):
            kept[k, n] = total(2 * k)
            sent[k, n] = total(2 * k + 1).astype(BF)


def add_third_half_kernel(scal, kept, got, own, sent):
    own[...] = kept[0] + got[0].astype(F32)
    sent[...] = (kept[1] + got[1].astype(F32)).astype(BF)


def add_last_half_kernel(core_at, scal, own, got, keep, send):
    first = scal[core_at] == 0
    of_first, of_second = (own[n] + got[n].astype(F32) for n in range(2))
    keep[...] = jnp.where(first, of_first, of_second)
    send[...] = jnp.where(first, of_second, of_first)


def add_near_kernel(scal, kept, got, own, far):
    own[...] = kept[0].astype(F32) + got[0].astype(F32)
    far[...] = (kept[1].astype(F32) + got[1].astype(F32)).astype(BF)


def add_far_kernel(scal, own, got, kept, sent):
    for n in range(2):
        kept[n] = own[n, 0] + got[n, 0].astype(F32)
        sent[n] = (own[n, 1] + got[n, 1].astype(F32)).astype(BF)


def add_side_kernel(scal, kept, got, own, sent):
    for n in range(2):
        own[n] = kept[n, 0] + got[n, 0].astype(F32)
        sent[n] = (kept[n, 1] + got[n, 1].astype(F32)).astype(BF)


def add_end_kernel(core_at, scal, own, got, keep, send):
    first = scal[core_at] == 0
    of_first, of_second = (own[n] + got[n].astype(F32) for n in range(2))
    keep[...] = jnp.where(first, of_first, of_second)
    send[...] = jnp.where(first, of_second, of_first)


class Scatter:
    def __init__(self, ring, core_at, name, sent):
        self.ring, self.core_at, self.name = ring, core_at, name
        self.xk, self.xs, self.yk, self.ys = sent

    def send(self, *others):
        self.xr, self.yr = self.ring.x(after(self.xs, *others)), self.ring.y(after(self.ys, *others))

    def first(self, scal, us=0.1):
        shape = self.xk.shape[1:]
        part = lambda a: (a, (1,) + shape, lambda j, s: (1, 0, 0, 0))
        xn, yn = call(
            add_first_kernel, self.name + "_add1", scal, (1,), [part(a) for a in (self.xk, self.xr, self.yk, self.yr)],
            [(shape, BF, None, None)] * 2, us=us,
        )
        self.xn, self.yn = xn, yn
        return xn

    def send_first(self, *others):
        self.xm, self.ym = self.ring.y(after(self.xn, *others)), self.ring.x(after(self.yn, *others))

    def second(self, scal):
        shape = self.xk.shape[1:]
        piece = (2,) + shape[1:]
        part = lambda a: (a, (1,) + shape, lambda j, s: (0, 0, 0, 0))
        whole = lambda a: (a, None, None)
        self.own, *self.sends = call(
            add_second_kernel, self.name + "_add2", scal, (1,),
            [part(self.xk), part(self.xr), whole(self.xm), part(self.yk), part(self.yr), whole(self.ym)],
            [(piece, F32, None, None)] + [(piece, BF, None, None)] * 3,
        )
        return self.own

    def send_second(self, *others):
        self.arrived = [self.ring.z(after(v, *others), k + 1) for k, v in enumerate(self.sends)]

    def last(self, scal):
        piece = self.own.shape[1:]
        keep, send = call(
            functools.partial(add_last_kernel, self.core_at), self.name + "_add3", scal, (1,),
            [(a, None, None) for a in (self.own, *self.arrived)], [(piece, F32, None, None)] * 2,
        )
        return keep, self.ring.core(send)


class HalvingScatter(Scatter):
    def second(self, scal):
        shape = self.xk.shape[1:]
        piece = (2, 2) + shape[1:]
        part = lambda a: (a, (1,) + shape, lambda j, s: (0, 0, 0, 0))
        whole = lambda a: (a, None, None)
        self.kept, self.near = call(
            add_second_half_kernel, self.name + "_add2", scal, (1,),
            [part(self.xk), part(self.xr), whole(self.xm), part(self.yk), part(self.yr), whole(self.ym)],
            [(piece, F32, None, None), (piece, BF, None, None)],
        )
        return self.kept

    def send_second(self):
        self.got = self.ring.z(self.near, 1)

    def third(self, scal):
        piece = self.kept.shape[1:]
        self.own, self.far = call(
            add_third_half_kernel, self.name + "_add3", scal, (1,),
            [(a, None, None) for a in (self.kept, self.got)], [(piece, F32, None, None), (piece, BF, None, None)],
        )
        return self.own

    def send_third(self):
        self.arrived = self.ring.z(self.far, 2)

    def last(self, scal):
        piece = self.own.shape[1:]
        keep, send = call(
            functools.partial(add_last_half_kernel, self.core_at), self.name + "_add4", scal, (1,),
            [(a, None, None) for a in (self.own, self.arrived)], [(piece, F32, None, None)] * 2,
        )
        return keep, self.ring.core(send)


class DepthScatter:
    def __init__(self, ring, core_at, name, sent):
        self.ring, self.core_at, self.name = ring, core_at, name
        self.kept, self.near = sent

    def call(self, kernel, step, scal, ins, outs):
        whole = lambda a: (a, None, None)
        return call(kernel, self.name + step, scal, (), [*map(whole, ins)], [(s, d, None, None) for s, d in outs])

    def send_near(self):
        self.got = self.ring.z(self.near, 1)

    def add_near(self, scal):
        shape = self.kept.shape[1:]
        self.own, self.far = self.call(add_near_kernel, "_add1", scal, (self.kept, self.got), [(shape, F32), (shape, BF)])
        return self.own

    def send_far(self):
        self.got = self.ring.z(self.far, 2)

    def add_far(self, scal):
        shape = self.own.shape[:1] + self.own.shape[2:]
        self.kept, self.side = self.call(add_far_kernel, "_add2", scal, (self.own, self.got), [(shape, F32), (shape, BF)])
        return self.kept

    def send_side(self):
        self.got = self.ring.x(self.side)

    def add_side(self, scal):
        shape = self.kept.shape[:1] + self.kept.shape[2:]
        self.own, sent = self.call(add_side_kernel, "_add3", scal, (self.kept, self.got), [(shape, F32), (shape, BF)])
        self.got = self.ring.y(sent)
        return self.own

    def last(self, scal):
        shape = self.own.shape[1:]
        keep, send = self.call(
            functools.partial(add_end_kernel, self.core_at), "_add4", scal, (self.own, self.got), [(shape, F32)] * 2
        )
        return keep, self.ring.core(send)


def after(value, *others):
    if not others:
        return value
    return lax.optimization_barrier((value,) + others)[0]


def side_by_side(core_at, scal, own, got):
    first = scal[core_at] == 0
    return [jnp.where(first, own, got), jnp.where(first, got, own)]


def finish_kernel(
    core_at, scal, own, got, reduce_own, reduce_got, expand_own, expand_got,
    heads_o, reduce_o, expand_o, merge_o, *shares_o,
):
    width = own.shape[1]
    rows = heads_o.shape[0]
    for n, part in enumerate(side_by_side(core_at, scal, reduce_own[...], reduce_got[...])):
        reduce_o[:, n * width : (n + 1) * width] = part
    blocks = expand_own.shape[0] // rows - 1
    for n, part in enumerate(side_by_side(core_at, scal, expand_own[...], expand_got[...])):
        for k in range(blocks):
            at = (n * blocks + k) * width
            expand_o[:, at : at + width] = part[k * rows : (k + 1) * rows]
        merge_o[:, n * width : (n + 1) * width] = part[blocks * rows :]
    for n, part in enumerate(side_by_side(core_at, scal, own[...], got[...])):
        for k in range(3):
            at = (2 * k + n) * width
            heads_o[:, at : at + width] = part[k * rows : (k + 1) * rows]
    entries = own[3 * rows :] + got[3 * rows :]
    entries = entries[0:1] + entries[1:2]
    at = 0
    for share in shares_o:
        n = share.shape[1]
        moved = entries if at == 0 else pltpu.roll(entries, width - at, 1)
        share[...] = moved[:, :n]
        at += n


def per_device(
    tokens, w_heads, b_heads, w_merge, b_merge, gain_first, bias_first, w_expand, b_expand,
    w_reduce, b_reduce, gain_second, bias_second, seq_lengths, cotangent,
):
    rows = tokens.shape[0]
    seqs = seq_lengths.shape[1]
    n_dp = lax.axis_size("dp")
    ring = Ring(n_dp)
    head = lax.axis_index("head")
    dp = lax.axis_index("dp")
    core = dp % 2
    place_of = jnp.stack([head, core, head, (dp // 2) % 2, dp // 4]).astype(jnp.int32)
    scal = jnp.concatenate([seq_lengths[0].astype(jnp.int32), place_of])
    head_at, core_at, pos_at = seqs, seqs + 1, seqs + 2
    first_core = core == 0
    line = lambda v: v.reshape(1, -1)
    b_heads, b_merge, gain_first, bias_first, b_expand, b_reduce, gain_second, bias_second = map(
        line, (b_heads, b_merge, gain_first, bias_first, b_expand, b_reduce, gain_second, bias_second)
    )
    wide_shape = (rows, D)
    quarter = 256

    turned = ((4, D // 4, rows), BF, None, None)
    rk, v, state, tcol, trow, tokens_t = call(
        functools.partial(kv_kernel, seqs), "keys_values", scal, (3,),
        [
            (tokens, None, None),
            (w_heads, (D, quarter), lambda j, s: (0, 3 + j)),
            (w_heads, (D, quarter), lambda j, s: (0, 6 + j)),
            (b_heads, (1, quarter), lambda j, s: (0, 3 + j)),
            (b_heads, (1, quarter), lambda j, s: (0, 6 + j)),
        ],
        [
            (wide_shape, BF, (rows, quarter), lambda j, s: (0, j)),
            (wide_shape, BF, (rows, quarter), lambda j, s: (0, j)),
            ((PAIRS + 1, LANES, LANES), BF, None, None),
            ((rows, LANES), F32, None, None),
            ((8, rows), F32, None, None), turned,
        ],
        [pltpu.VMEM((LANES, LANES), F32)],
        us=4,
    )
    prior = ring.x(state)

    fast = n_dp == 16
    order = scal
    if fast:
        tokens_o = ring.core(tokens_t)
    rq, num, den = call(
        local_kernel, "local_attention", scal, (3,),
        [
            (tokens, None, None),
            (w_heads, (D, quarter), lambda j, s: (0, j)),
            (b_heads, (1, quarter), lambda j, s: (0, j)),
            (rk, (rows, quarter), lambda j, s: (0, j)),
            (v, (rows, quarter), lambda j, s: (0, j)),
            (tcol, None, None),
            (trow, None, None),
        ],
        [
            (wide_shape, BF, (rows, quarter), lambda j, s: (0, j)),
            (wide_shape, F32, (rows, quarter), lambda j, s: (0, j)),
            (wide_shape, F32, (rows, quarter), lambda j, s: (0, j)),
        ],
        [pltpu.VMEM((rows, rows), F32)],
        us=6,
    )

    if fast:
        order = after(scal, tokens_o)
    att, inv, mixed, xhat, scale, normed, second, turned_own, act, slope = call(
        functools.partial(ffn_kernel, head_at), "feed_forward", order, (FFN_STEPS,),
        [
            (rq, None, None), (num, None, None), (den, None, None), (prior, None, None),
            (tcol, None, None), (tokens, None, None), (w_merge, None, None), (b_merge, None, None),
            (gain_first, None, None), (bias_first, None, None), (b_reduce, None, None),
            (w_expand, (D, FFN_BLOCK), lambda j, s: (0, j)),
            (b_expand, (1, FFN_BLOCK), lambda j, s: (0, j)),
            (w_reduce, (FFN_BLOCK, D), lambda j, s: (j, 0)),
        ],
        [
            (wide_shape, F32, None, None), (wide_shape, F32, None, None), (wide_shape, BF, None, None),
            (wide_shape, F32, None, None), ((rows, LANES), F32, None, None), (wide_shape, BF, None, None),
            (wide_shape, F32, None, None), ((2, 4, D // 4, rows), BF, None, None),
            ((rows, FF), BF, (rows, FFN_BLOCK), lambda j, s: (0, j)),
            ((rows, FF), BF, (rows, FFN_BLOCK), lambda j, s: (0, j)),
        ],
        us=11, vmem=VMEM_FFN,
    )

    half_shape = (rows, D // 2)
    result, grad_second, branch, bg_keep, bg_send, sums_second = call(
        functools.partial(second_kernel, core_at), "second_norm", scal, (1,),
        [(second, None, None), (cotangent, None, None), (gain_second, None, None), (bias_second, None, None)],
        [
            (wide_shape, BF, None, None), (wide_shape, F32, None, None), (wide_shape, BF, None, None),
            (half_shape, BF, None, None), (half_shape, BF, None, None), ((8, D), F32, None, None),
        ],
        us=2.6,
    )

    devices = ring.devices
    small, large = D // devices, FF // devices
    whole = lambda a: (a, None, None)
    part = lambda a, n: (a, (1, 2, D // 4, rows), lambda j, s: (n, j, 0, 0))
    by_z = lambda a: (a, (1, D // 4, rows), lambda j, s: (j, 0, 0))
    by_col = lambda a: (a, (rows, FF // 4), lambda j, s: (0, j))

    def group(kernel, name, scal, grid, ins, piece_rows, us, scratch=(), kind=Scatter):
        shape = (2, 4, piece_rows, D // 2)
        sent = call(
            functools.partial(kernel, pos_at), name, scal, grid, ins, [(shape, BF, None, None)] * 4, scratch, us
        )
        return kind(ring, core_at, name, sent)

    ff_half = FF_STEPS // 2
    in_hbm = lambda a: (a, None, pltpu.HBM)
    hidden = ((ff_half, rows, FF_BLOCK), BF, None, None)
    hidden_sums = ((1, FF // 2), F32, None, None)
    buffers = [
        pltpu.VMEM((ff_half, D, FF_BLOCK), BF), pltpu.VMEM((ff_half, FF_BLOCK, D), BF),
        pltpu.SemaphoreType.DMA((2, ff_half)),
    ]
    hidden_in = [whole(branch), whole(slope), in_hbm(w_expand), in_hbm(w_reduce)]
    pg_send, sum_sent, partial = call(
        functools.partial(back_sent_kernel, core_at), "feed_forward_back_sent", scal, (),
        [*hidden_in, whole(grad_second)],
        [hidden, hidden_sums, (wide_shape, F32, None, None)], buffers,
        us=5, vmem=VMEM_BACK,
    )
    order = scal
    if fast:
        pg_o = ring.core(pg_send)
        act_o, turned_other, bg_o = map(ring.core, (act, turned_own, bg_send))
        pieces = ((2, 2, 2, 2, large, D // 2), BF, None, None)
        sent = call(
            functools.partial(reduce_grad_kernel, pos_at), "grad_reduce", after(scal, partial, turned_other), (4,),
            [by_col(act), by_col(act_o), whole(bg_keep), whole(bg_o)], [pieces, pieces], us=6,
        )
        reduced = DepthScatter(ring, core_at, "grad_reduce", sent)
        reduced.send_near()
        order = after(scal, reduced.near)

    pg_keep, grad_first, mg_keep, mg_send, w_att, e_att, later, sum_kept, sums_first = call(
        functools.partial(back_kernel, core_at), "feed_forward_back", order, (),
        [
            *hidden_in,
            (partial, None, None), (gain_first, None, None), (xhat, None, None), (scale, None, None),
            (w_merge, None, None), (att, None, None), (inv, None, None), (rq, None, None), (tcol, None, None),
        ],
        [
            hidden, (wide_shape, F32, None, None), (half_shape, BF, None, None), (half_shape, BF, None, None),
            (wide_shape, BF, None, None), ((rows, LANES), BF, None, None),
            ((PAIRS + 1, LANES, LANES), BF, None, None), hidden_sums, ((8, D), F32, None, None),
        ],
        [pltpu.VMEM(wide_shape, F32), *buffers],
        us=COST_BACK, vmem=VMEM_BACK,
    )
    later = ring.x(later)

    if fast:
        mg_o = ring.core(mg_send)
        expanded = group(
            expand_grad_kernel, "grad_expand", scal, (2,),
            [
                part(turned_own, 1), part(turned_other, 1), whole(pg_keep), whole(pg_o),
                part(turned_own, 0), part(turned_other, 0), whole(mg_keep), whole(mg_o),
            ],
            5 * small, COST_EXPAND, kind=HalvingScatter,
        )
        expanded.send(later)
        order = after(scal, expanded.xs, later)

    by_pair = [*map(whole, (rq, rk, v, w_att))]
    both_states = [whole(e_att), whole(prior), whole(later), whole(tcol)]
    pj_out = [((3, rows // 2, D // 2), BF, None, None)] * 2
    pj_sums = ((3, 8, D // 2), F32, None, None)
    table = ((rows, rows), F32, None, None)
    *pj_send, sum_heads_sent, weights, weights_t = call(
        functools.partial(attn_sent_kernel, head_at, core_at), "attention_back_sent", order, (),
        [*by_pair, *both_states, whole(trow)], [*pj_out, pj_sums, table, table], us=COST_SENT, vmem=VMEM_ATTN,
    )
    order = scal
    if fast:
        pj_o = [ring.core(v) for v in pj_send]
        order = after(scal, reduced.add_near(after(scal, pj_send[0])))
        reduced.send_far()
    *pj_keep, sum_heads_kept = call(
        functools.partial(attn_kept_kernel, head_at, core_at), "attention_back_kept", order, (PAIRS // 2,),
        [*by_pair, *both_states, whole(weights), whole(weights_t)], [*pj_out, pj_sums], us=COST_KEPT, vmem=VMEM_ATTN,
    )

    if fast:
        order = after(scal, expanded.first(after(scal, pj_keep[0])))
        expanded.send_first()
        heads = group(
            functools.partial(heads_grad_kernel, devices=devices), "grad_heads", order, (4,),
            [
                by_z(tokens_t), by_z(tokens_o), *map(whole, (*pj_keep, *pj_o)),
                *map(whole, (sum_heads_kept, sum_heads_sent, sums_first, sum_kept, sum_sent, sums_second)),
            ],
            3 * small + 8, COST_HEADS, [pltpu.VMEM((devices, D // 2), F32)],
        )
        heads.send()
        order = after(scal, heads.xs)

    of_part = lambda a: (a, (1, rows // 2, D // 2), lambda j, s: (j, 0, 0))
    (input_grad,) = call(
        input_kernel, "input_grad", order, (3,),
        [
            whole(grad_first), *map(of_part, (*pj_keep, *pj_send)),
            (w_heads, (D, D // 2), lambda j, s: (0, 2 * j + s[core_at])),
            (w_heads, (D, D // 2), lambda j, s: (0, 2 * j + 1 - s[core_at])),
        ],
        [(wide_shape, F32, None, None)],
        us=COST_INPUT,
    )

    if fast:
        order = reduced.add_far(after(scal, input_grad))
        order = expanded.second(after(scal, order))
        expanded.send_second()
        reduced.send_side()
        order = heads.first(after(scal, order))
        heads.send_first()
        order = expanded.third(after(scal, order))
        expanded.send_third()
        order = heads.second(after(scal, order))
        heads.send_second()
        order = reduced.add_side(after(scal, order))
        expand_own, expand_got = expanded.last(after(scal, order))
        reduce_own, reduce_got = reduced.last(after(scal, expand_own))
        heads_own, heads_got = heads.last(after(scal, reduce_own))
        out = lambda n, m: ((n, m), F32, None, None)
        counts = (2 * small, small, small, small, small, large, small, small, small)
        w_heads_grad, w_reduce_grad, w_expand_grad, w_merge_grad, *shares = call(
            functools.partial(finish_kernel, core_at), "finish", scal, (),
            [*map(whole, (heads_own, heads_got, reduce_own, reduce_got, expand_own, expand_got))],
            [out(small, 3 * D), out(large, D), out(small, FF), out(small, D), *(out(1, n) for n in counts)],
        )
        shares = [share.reshape(-1) for share in shares]
        grads = (
            w_heads_grad, *shares[:2], w_merge_grad, *shares[2:5], w_expand_grad, shares[5], w_reduce_grad,
            *shares[6:],
        )
    else:
        by_core = lambda keep, send: jnp.concatenate(
            [jnp.where(first_core, keep, send), jnp.where(first_core, send, keep)], axis=1
        )
        flat = lambda v: v.transpose(1, 0, 2).reshape(rows, -1)
        by_heads = lambda keep, send: jnp.concatenate(
            [by_core(keep[n], send[n]) for n in range(3)], axis=1
        )
        pj_keep, pj_send = (jnp.concatenate(v, axis=1) for v in (pj_keep, pj_send))
        sum_heads = by_heads(sum_heads_kept, sum_heads_sent)[0]
        scatter = lambda v: lax.psum_scatter(v, AXES, scatter_dimension=0, tiled=True)
        grads = (
            scatter(dot_t(tokens, by_heads(pj_keep, pj_send))),
            scatter(sum_heads[: 2 * D]), scatter(sum_heads[2 * D :]),
            scatter(dot_t(mixed, by_core(mg_keep, mg_send))),
            scatter(sums_first[2]), scatter(sums_first[0]), scatter(sums_first[1]),
            scatter(dot_t(normed, by_core(flat(pg_keep), flat(pg_send)))),
            scatter(by_core(sum_kept, sum_sent)[0]),
            scatter(dot_t(act, branch)),
            scatter(sums_second[2]), scatter(sums_second[0]), scatter(sums_second[1]),
        )
    return (result, input_grad) + tuple(grads)


def solution(mesh):
    in_specs = (P(AXES, None),) + (P(),) * 12 + (P("dp", None), P(AXES, None))
    row, one = P(AXES, None), P(AXES)
    out_specs = (row, row, row, one, one, row, one, one, one, row, one, row, one, one, one)
    return jax.shard_map(
        per_device, mesh=mesh, in_specs=in_specs, out_specs=out_specs, check_vma=False
    )
```

```python
import functools
import math

import jax
import jax.numpy as jnp
from jax import lax
from jax.experimental import pallas as pl
from jax.experimental.pallas import tpu as pltpu
from jax.sharding import PartitionSpec as P

D = 768
PAIRS = 6
FF = 3072
LANES = 128
HALF = 64
BF = jnp.bfloat16
F32 = jnp.float32
AXES = ("dp", "head")
VMEM_LIMIT = 8 << 20
VMEM_FFN = 16 << 20
VMEM_ATTN = 10 << 20
FF_BLOCK = 768
FFN_BLOCK = 1024
FFN_STEPS = FF // FFN_BLOCK
MATMUL_PER_US = 1.15e9
COST_EXPAND = 1
VMEM_BACK = 16 << 20
COST_KEPT = 0.5
COST_BACK = 3
COST_SENT = 0.5
COST_HEADS = 0.1
COST_INPUT = 0.1
FF_STEPS = FF // FF_BLOCK


def dot(a, b):
    return jnp.dot(a, b, preferred_element_type=F32)


def dot_t(a, b):
    return lax.dot_general(a, b, (((0,), (0,)), ((), ())), preferred_element_type=F32)


def dot_r(a, b):
    return lax.dot_general(a, b, (((1,), (1,)), ((), ())), preferred_element_type=F32)


def call(kernel, name, scal, grid, ins, outs, scratch=(), us=0.1, vmem=VMEM_LIMIT):
    def spec(b, m):
        if b is None:
            return pl.BlockSpec(memory_space=pltpu.VMEM if m is None else m)
        return pl.BlockSpec(b, m)

    in_specs = [spec(b, m) for _, b, m in ins]
    out_specs = [spec(b, m) for _, _, b, m in outs]
    return pl.pallas_call(
        kernel,
        name=name,
        grid_spec=pltpu.PrefetchScalarGridSpec(
            num_scalar_prefetch=1,
            grid=grid,
            in_specs=in_specs,
            out_specs=out_specs,
            scratch_shapes=list(scratch),
        ),
        out_shape=[jax.ShapeDtypeStruct(s, d) for s, d, _, _ in outs],
        compiler_params=pltpu.CompilerParams(vmem_limit_bytes=vmem),
        cost_estimate=pl.CostEstimate(flops=int(us * MATMUL_PER_US), bytes_accessed=1, transcendentals=0),
    )(scal, *[a for a, _, _ in ins])


def lane_masks():
    lane = lax.broadcasted_iota(jnp.int32, (1, LANES), 1)
    even = (lane < HALF).astype(F32)
    return lane, even.astype(BF), (1.0 - even).astype(BF)


def both_heads(pair):
    lane, even, odd = lane_masks()
    return jnp.concatenate([pair * even, pair * odd], axis=0)


def own_lanes(stacked):
    rows = stacked.shape[0] // 2
    lane = lax.broadcasted_iota(jnp.int32, (1, LANES), 1)
    return jnp.where(lane < HALF, stacked[:rows], stacked[rows:])


def square_masks():
    row = lax.broadcasted_iota(jnp.int32, (LANES, LANES), 0)
    lane = lax.broadcasted_iota(jnp.int32, (LANES, LANES), 1)
    upper = row < HALF
    return lane, upper, upper == (lane < HALF)


def high_low(v):
    high = v.astype(BF).astype(F32)
    return high, v - high


def tables(scal, rows, seqs, tcol, trow):
    pos = lax.broadcasted_iota(jnp.int32, (1, rows), 1) + scal[seqs] * rows
    seg = jnp.zeros((1, rows), jnp.int32)
    first = jnp.zeros((1, rows), jnp.int32)
    length = jnp.ones((1, rows), jnp.int32)
    at_boundary = jnp.int32(0)
    begin = jnp.int32(0)
    for s in range(seqs):
        end = begin + scal[s]
        inside = (pos >= begin) & (pos < end)
        first = jnp.where(inside, begin, first)
        length = jnp.where(inside, jnp.maximum(scal[s], 1), length)
        seg = seg + (pos >= end).astype(jnp.int32)
        at_boundary = at_boundary + (rows - 1 >= end).astype(jnp.int32)
        begin = end
    live = (seg < seqs).astype(F32)
    angle = 0.5 * math.pi * (pos - first).astype(F32) / length.astype(F32)
    cos_w = jnp.cos(angle) * live
    sin_w = jnp.sin(angle) * live
    crossing = (seg == at_boundary).astype(F32)
    which = lax.broadcasted_iota(jnp.int32, (LANES, rows), 0)
    table = jnp.zeros((LANES, rows), F32)
    for n, entry in enumerate((cos_w, sin_w, seg.astype(F32), cos_w * crossing, sin_w * crossing)):
        table = jnp.where(which == n, entry, table)
    trow[...] = table[:8]
    tcol[...] = table.T


def pack_state(both, norm_cos, norm_sin, pair, norms):
    lane, upper, diag = square_masks()
    packed = jnp.where(diag, both[:LANES, :LANES], pltpu.roll(both[LANES:, :LANES], HALF, 1))
    cos_high, cos_low = high_low(norm_cos)
    sin_high, sin_low = high_low(norm_sin)
    for n, part in enumerate((cos_high, cos_low, sin_high, sin_low)):
        norms = jnp.where(lane == 4 * pair + n, part, norms)
    return packed.astype(BF), norms


def unpack_state(state_ref, pair):
    lane, upper, diag = square_masks()
    packed = state_ref[pair].astype(F32)
    norms = state_ref[PAIRS].astype(F32)
    of_cos = jnp.where(diag, packed, 0.0)
    of_sin = jnp.where(diag, pltpu.roll(packed, HALF, 1), 0.0)
    pick = lambda n: jnp.sum(
        jnp.where((lane == 4 * pair + n) | (lane == 4 * pair + n + 1), norms, 0.0), axis=1, keepdims=True
    )
    return of_cos, of_sin, pick(0), pick(2)


def turn(value, out):
    turned = value.T
    share = out.shape[1]
    for n in range(out.shape[0]):
        out[n] = turned[n * share : (n + 1) * share]


def kv_kernel(seqs, scal, tok, wk, wv, bk, bv, rk_o, v_o, st_o, tcol, trow, turned_o, norms):
    step = pl.program_id(0)
    rows = tok.shape[0]

    @pl.when(step == 0)
    def _():
        tables(scal, rows, seqs, tcol, trow)
        norms[...] = jnp.zeros_like(norms)
        turn(tok[...], turned_o)

    rk = jnp.maximum(dot(tok[...], wk[...]) + bk[...].astype(F32), 0.0).astype(BF)
    v = (dot(tok[...], wv[...]) + bv[...].astype(F32)).astype(BF)
    rk_o[...] = rk
    v_o[...] = v
    cos_b, sin_b = tcol[:, 3:4], tcol[:, 4:5]
    ones = jnp.ones((rows, LANES), BF)
    for n in range(2):
        pair = 2 * step + n
        cols = slice(n * LANES, (n + 1) * LANES)
        kp = rk[:, cols].astype(F32)
        left = jnp.concatenate([(kp * cos_b).astype(BF), (kp * sin_b).astype(BF)], axis=1)
        both = dot_t(left, jnp.concatenate([v[:, cols], ones], axis=1))
        packed, new_norms = pack_state(both, both[:LANES, LANES:], both[LANES:, LANES:], pair, norms[...])
        st_o[pair] = packed
        norms[...] = new_norms

    st_o[PAIRS] = norms[...].astype(BF)


def weights_block(tcol, trow, transposed):
    rows = tcol.shape[0]
    down = lax.broadcasted_iota(jnp.int32, (rows, rows), 0)
    along = lax.broadcasted_iota(jnp.int32, (rows, rows), 1)
    same = tcol[:, 2:3] == trow[2:3, :]
    causal = (down <= along) if transposed else (along <= down)
    value = tcol[:, 0:1] * trow[0:1, :] + tcol[:, 1:2] * trow[1:2, :]
    return jnp.where(same & causal, value, 0.0)


def weigh(stacked, weights):
    rows = weights.shape[0]
    return jnp.concatenate([stacked[:rows] * weights, stacked[rows:] * weights], axis=0).astype(BF)


def local_kernel(scal, tok, wq, bq, rk, v, tcol, trow, rq_o, num_o, den_o, weights):
    step = pl.program_id(0)
    rows = tok.shape[0]
    mid = rows // 2

    @pl.when(step == 0)
    def _():
        weights[...] = weights_block(tcol, trow, False)

    rq = jnp.maximum(dot(tok[...], wq[...]) + bq[...].astype(F32), 0.0).astype(BF)
    rq_o[...] = rq
    ones = jnp.ones((rows, LANES), BF)
    for n in range(2):
        cols = slice(n * LANES, (n + 1) * LANES)
        kp = rk[:, cols]
        values = jnp.concatenate([v[:, cols], ones], axis=1)
        first = weigh(dot_r(both_heads(rq[:, cols]), kp[:mid]), weights[:, :mid])
        second = weigh(dot_r(both_heads(rq[mid:, cols]), kp[mid:]), weights[mid:, mid:])
        sums = dot(first, values[:mid])
        late = dot(second, values[mid:])
        for own, out in ((slice(0, LANES), num_o), (slice(LANES, 2 * LANES), den_o)):
            total = own_lanes(sums[:, own])
            out[:mid, cols] = total[:mid]
            out[mid:, cols] = total[mid:] + own_lanes(late[:, own])


def normalise(entries):
    mean = jnp.mean(entries, axis=1, keepdims=True)
    centred = entries - mean
    var = jnp.mean(centred * centred, axis=1, keepdims=True)
    scale = lax.rsqrt(var + 1e-05)
    return centred * scale, scale


def merge_heads(
    head_at, scal, rq, num, den, st, tcol, tok, w_merge, b_merge, gain, bias, b_red,
    att_o, inv_o, mixed_o, xhat_o, scale_o, normed_o, acc_o, turned_o,
):
    cross = (scal[head_at] == 1).astype(F32)
    cos_b, sin_b = tcol[:, 3:4] * cross, tcol[:, 4:5] * cross
    sq_lane, upper, diag = square_masks()
    for pair in range(PAIRS):
        cols = slice(pair * LANES, (pair + 1) * LANES)
        qp = rq[:, cols].astype(F32)
        of_cos, of_sin, norm_cos, norm_sin = unpack_state(st, pair)
        top = jnp.concatenate([of_cos, jnp.where(diag, norm_cos, 0.0)], axis=1)
        low = jnp.concatenate([of_sin, jnp.where(diag, norm_sin, 0.0)], axis=1)
        right = jnp.concatenate([top, low], axis=0).astype(BF)
        left = jnp.concatenate([(qp * cos_b).astype(BF), (qp * sin_b).astype(BF)], axis=1)
        prior = dot(left, right)
        inverse = 1.0 / (den[:, cols] + prior[:, LANES:] + 1.0)
        attended = (num[:, cols] + prior[:, :LANES]) * inverse
        att_o[:, cols] = attended
        inv_o[:, cols] = inverse
        mixed_o[:, cols] = attended.astype(BF)
    first_in = tok[...].astype(F32) + dot(mixed_o[...], w_merge[...]) + b_merge[...].astype(F32)
    xhat, scale = normalise(first_in)
    normed = xhat * gain[...].astype(F32) + bias[...].astype(F32)
    xhat_o[...] = xhat
    scale_o[...] = jnp.broadcast_to(scale, scale_o.shape)
    normed_o[...] = normed.astype(BF)
    acc_o[...] = normed + b_red[...].astype(F32)
    turn(mixed_o[...], turned_o.at[0])
    turn(normed_o[...], turned_o.at[1])


def expand_reduce(normed, w_exp, b_exp, w_red, act_o, slope_o, acc_o):
    rows = normed.shape[0]
    pre = [dot(normed[at : at + rows // 2], w_exp[...]) + b_exp[...].astype(F32) for at in (0, rows // 2)]
    for at, x in zip((0, rows // 2), pre):
        part = slice(at, at + rows // 2)
        cdf = 0.5 + 0.5 * lax.erf(x * (2.0**-0.5))
        pdf = jnp.exp(-0.5 * x * x) * (1.0 / math.sqrt(2.0 * math.pi))
        act = (x * cdf).astype(BF)
        act_o[part] = act
        slope_o[part] = (cdf + x * pdf).astype(BF)
        acc_o[part] += dot(act, w_red[...])


def ffn_kernel(head_at, scal, *refs):
    w_exp, b_exp, w_red = refs[11:14]
    normed_o, acc_o = refs[19:21]
    act_o, slope_o = refs[22:]

    @pl.when(pl.program_id(0) == 0)
    def _():
        merge_heads(head_at, scal, *refs[:11], *refs[14:22])

    expand_reduce(normed_o, w_exp, b_exp, w_red, act_o, slope_o, acc_o)


def second_kernel(core_at, scal, second, cot, gain, bias, out_o, grad_o, full_o, keep_o, send_o, sums_o):
    xhat, scale = normalise(second[...])
    gain_w = gain[...].astype(F32)
    out_o[...] = (xhat * gain_w + bias[...].astype(F32)).astype(BF)
    cot_w = cot[...].astype(F32)
    t = cot_w * gain_w
    grad = scale * (
        t - jnp.mean(t, axis=1, keepdims=True) - xhat * jnp.mean(t * xhat, axis=1, keepdims=True)
    )
    low = grad.astype(BF)
    grad_o[...] = grad
    full_o[...] = low
    first = scal[core_at] == 0
    half = D // 2
    left, right = grad[:, :half], grad[:, half:]
    keep_o[...] = jnp.where(first, left, right).astype(BF)
    send_o[...] = jnp.where(first, right, left).astype(BF)
    sums_o[0:1] = jnp.sum(cot_w * xhat, axis=0, keepdims=True)
    sums_o[1:2] = jnp.sum(cot_w, axis=0, keepdims=True)
    sums_o[2:3] = jnp.sum(low.astype(F32), axis=0, keepdims=True)


def head_lanes(pair, lane, first):
    at = 4 * pair + jnp.where(first, 0, 2)
    return (lane == at) | (lane == at + 1)


def weight_copies(half, w_exp, w_red, exp_buf, red_buf, sems, n):
    at = pl.ds(pl.multiple_of((half * exp_buf.shape[0] + n) * FF_BLOCK, FF_BLOCK), FF_BLOCK)
    return (
        pltpu.make_async_copy(w_red.at[at, :], red_buf.at[n], sems.at[0, n]),
        pltpu.make_async_copy(w_exp.at[:, at], exp_buf.at[n], sems.at[1, n]),
    )


def back_steps(half, full, slope, w_exp, w_red, out_o, bexp_o, exp_buf, red_buf, sems):
    blocks = exp_buf.shape[0]
    copies = [weight_copies(half, w_exp, w_red, exp_buf, red_buf, sems, n) for n in range(blocks)]
    for pair in copies:
        for copy in pair:
            copy.start()
    total = None
    for n, (of_red, of_exp) in enumerate(copies):
        cols = slice(n * FF_BLOCK, (n + 1) * FF_BLOCK)
        at = pl.ds(pl.multiple_of((half * blocks + n) * FF_BLOCK, FF_BLOCK), FF_BLOCK)
        of_red.wait()
        pre_grad = (dot_r(full[...], red_buf[n]) * slope[:, at].astype(F32)).astype(BF)
        bexp_o[:, cols] = jnp.sum(pre_grad.astype(F32), axis=0, keepdims=True)
        out_o[n] = pre_grad
        of_exp.wait()
        part = dot_r(pre_grad, exp_buf[n])
        total = part if total is None else total + part
    return total


def back_sent_kernel(core_at, scal, full, slope, w_exp, w_red, grad2, sent_o, bexp_o, acc, exp_buf, red_buf, sems):
    half = 1 - scal[core_at]
    acc[...] = grad2[...] + back_steps(half, full, slope, w_exp, w_red, sent_o, bexp_o, exp_buf, red_buf, sems)


def back_kernel(
    core_at, scal, full, slope, w_exp, w_red, acc_in, gain, xhat, scale, w_merge, att, inv, rq, tcol,
    kept_o, first_o, mk_o, ms_o, w_o, e_o, st_o, bexp_o, sums_o,
    acc, exp_buf, red_buf, sems,
):
    half = scal[core_at]
    acc[...] = acc_in[...] + back_steps(half, full, slope, w_exp, w_red, kept_o, bexp_o, exp_buf, red_buf, sems)
    back_rest(
        core_at, scal, acc, gain, xhat, scale, w_merge, att, inv, rq, tcol,
        first_o, mk_o, ms_o, w_o, e_o, st_o, sums_o,
    )


def back_rest(
    core_at, scal, acc, gain, xhat, scale, w_merge, att, inv, rq, tcol,
    first_o, mk_o, ms_o, w_o, e_o, st_o, sums_o,
):
    grad_normed = acc[...]
    xh = xhat[...]
    t = grad_normed * gain[...].astype(F32)
    first = scale[:, 0:1] * (
        t - jnp.mean(t, axis=1, keepdims=True) - xh * jnp.mean(t * xh, axis=1, keepdims=True)
    )
    low = first.astype(BF)
    first_o[...] = first
    sums_o[0:1] = jnp.sum(grad_normed * xh, axis=0, keepdims=True)
    sums_o[1:2] = jnp.sum(grad_normed, axis=0, keepdims=True)
    sums_o[2:3] = jnp.sum(low.astype(F32), axis=0, keepdims=True)
    is_first = scal[core_at] == 0
    left, right = first[:, : D // 2], first[:, D // 2 :]
    mk_o[...] = jnp.where(is_first, left, right).astype(BF)
    ms_o[...] = jnp.where(is_first, right, left).astype(BF)
    cos_b, sin_b = tcol[:, 3:4], tcol[:, 4:5]
    w = (dot_r(low, w_merge[...]).astype(BF).astype(F32) * inv[...]).astype(BF)
    w_o[...] = w
    high, rest = high_low(w.astype(F32) * att[...])
    column = lax.broadcasted_iota(jnp.int32, (D, LANES), 0)
    target = lax.broadcasted_iota(jnp.int32, (D, LANES), 1)
    picks = (target == 2 * (column // HALF)).astype(F32).astype(BF)
    e_high, e_low = high_low(-(dot(high.astype(BF), picks) + dot(rest.astype(BF), picks)))
    e = (e_high + pltpu.roll(e_low, 1, 1)).astype(BF)
    e_o[...] = e
    norms = jnp.zeros((LANES, LANES), F32)
    sq_lane, upper, diag = square_masks()
    for pair in range(PAIRS):
        cols = slice(pair * LANES, (pair + 1) * LANES)
        qp = rq[:, cols].astype(F32)
        left = jnp.concatenate([(qp * cos_b).astype(BF), (qp * sin_b).astype(BF)], axis=1)
        both = dot_t(left, jnp.concatenate([w[:, cols], e], axis=1))
        mine = head_lanes(pair, sq_lane, upper)
        norm = lambda part: jnp.sum(jnp.where(mine, part, 0.0), axis=1, keepdims=True)
        packed, norms = pack_state(both, norm(both[:LANES, LANES:]), norm(both[LANES:, LANES:]), pair, norms)
        st_o[pair] = packed
    st_o[PAIRS] = norms.astype(BF)


def attn_sent_kernel(head_at, core_at, scal, rq, rk, v, w, e, prior, later, tcol, trow, early_o, late_o, sums_o, weights, weights_t):
    weights[...] = weights_block(tcol, trow, False)
    weights_t[...] = weights_block(tcol, trow, True)
    first = (1 - scal[core_at]) * (PAIRS // 2)
    attn_back(head_at, first, scal, rq, rk, v, w, e, prior, later, tcol, weights, weights_t, early_o, late_o, sums_o)


def attn_kept_kernel(head_at, core_at, scal, rq, rk, v, w, e, prior, later, tcol, weights, weights_t, early_o, late_o, sums_o):
    step = pl.program_id(0)
    attn_back_pair(
        head_at, scal[core_at] * (PAIRS // 2) + step, step,
        scal, rq, rk, v, w, e, prior, later, tcol, weights, weights_t, early_o, late_o, sums_o,
    )


def attn_back(head_at, first, scal, rq, rk, v, w, e, prior, later, tcol, weights, weights_t, early_o, late_o, sums_o):
    for n in range(PAIRS // 2):
        attn_back_pair(
            head_at, first + n, n, scal, rq, rk, v, w, e, prior, later, tcol, weights, weights_t, early_o, late_o, sums_o
        )


def attn_back_pair(
    head_at, pair, slot, scal, rq, rk, v, w, e, prior, later, tcol, weights, weights_t, early_o, late_o, sums_o
):
    rows = rq.shape[0]
    mid = rows // 2
    cols = pl.ds(pl.multiple_of(pair * LANES, LANES), LANES)
    out = pl.ds(pl.multiple_of(slot * LANES, LANES), LANES)

    qp, kp, vp, wp = rq[:, cols], rk[:, cols], v[:, cols], w[:, cols]
    lane, even, odd = lane_masks()
    of_even = ((lane == 4 * pair) | (lane == 4 * pair + 1)).astype(F32).astype(BF)
    of_odd = ((lane == 4 * pair + 2) | (lane == 4 * pair + 3)).astype(F32).astype(BF)
    ones = jnp.ones((rows, LANES), BF)
    we = jnp.concatenate([wp, e[...]], axis=1)
    by_head = (jnp.concatenate([even, of_even], axis=1), jnp.concatenate([odd, of_odd], axis=1))
    ve = jnp.concatenate([vp, ones], axis=1)
    stack = lambda a, lo, hi: jnp.concatenate([a[lo:hi] * m for m in by_head], axis=0)

    grads = weigh(dot_r(stack(we, 0, rows), ve[:mid]), weights[:, :mid])
    dq = own_lanes(dot(grads, kp[:mid]))
    grads = weigh(dot_r(stack(we, mid, rows), ve[mid:]), weights[mid:, mid:])
    dq_late = own_lanes(dot(grads, kp[mid:]))

    grads = weigh(dot_r(stack(ve, 0, rows), we[mid:]), weights_t[:, mid:])
    dk = own_lanes(dot(grads, qp[mid:]))
    grads = weigh(dot_r(stack(ve, 0, mid), we[:mid]), weights_t[:mid, :mid])
    dk_early = own_lanes(dot(grads, qp[:mid]))

    scores = weigh(dot_r(both_heads(kp), qp[mid:]), weights_t[:, mid:])
    dv = own_lanes(dot(scores, wp[mid:]))
    scores = weigh(dot_r(both_heads(kp[:mid]), qp[:mid]), weights_t[:mid, :mid])
    dv_early = own_lanes(dot(scores, wp[:mid]))

    dq = jnp.concatenate([dq[:mid], dq[mid:] + dq_late], axis=0)
    dk = jnp.concatenate([dk[:mid] + dk_early, dk[mid:]], axis=0)
    dv = jnp.concatenate([dv[:mid] + dv_early, dv[mid:]], axis=0)

    sq_lane, upper, diag = square_masks()
    cos_b, sin_b = tcol[:, 3:4], tcol[:, 4:5]
    is_late = (scal[head_at] == 1).astype(F32)
    early = 1.0 - is_late

    def with_norms(parts, where):
        side = lambda total, norm: jnp.concatenate([total, jnp.where(where, norm, 0.0)], axis=1)
        of_cos, of_sin, norm_cos, norm_sin = parts
        return jnp.concatenate([side(of_cos, norm_cos), side(of_sin, norm_sin)], axis=0).astype(BF)

    prior_parts = unpack_state(prior, pair)
    into = dot_r(we, with_norms(prior_parts, head_lanes(pair, sq_lane, upper)))
    dq = dq + is_late * (cos_b * into[:, :LANES] + sin_b * into[:, LANES:])
    later_parts = unpack_state(later, pair)
    into = dot_r(ve, with_norms(later_parts, sq_lane == 0))
    dk = dk + early * (cos_b * into[:, :LANES] + sin_b * into[:, LANES:])
    kw = kp.astype(F32)
    left = jnp.concatenate([(kw * (cos_b * early)).astype(BF), (kw * (sin_b * early)).astype(BF)], axis=1)
    dv = dv + dot(left, jnp.concatenate(later_parts[:2], axis=0).astype(BF))

    dq = jnp.where(qp.astype(F32) > 0, dq, 0.0).astype(BF)
    dk = jnp.where(kw > 0, dk, 0.0).astype(BF)
    dv = dv.astype(BF)
    for n, part in enumerate((dq, dk, dv)):
        total = jnp.sum(part.astype(F32), axis=0, keepdims=True)
        sums_o[n, :, out] = jnp.broadcast_to(total, (sums_o.shape[1], LANES))
        early_o[n, :, out] = part[:mid]
        late_o[n, :, out] = part[mid:]


def input_kernel(scal, first, keep_early, keep_late, send_early, send_late, w_keep, w_send, out_o):
    @pl.when(pl.program_id(0) == 0)
    def _():
        out_o[...] = first[...]

    rows = lambda early, late: jnp.concatenate([early[0], late[0]], axis=0)
    out_o[...] += dot_r(rows(keep_early, keep_late), w_keep[...]) + dot_r(rows(send_early, send_late), w_send[...])


def place(values, piece_rows, tz, tys, x, y, z, extra, outs):
    xk, xs, yk, ys = outs
    width = xk.shape[-1]
    slot_z = tz ^ z
    pieces = {}
    at = 0
    for ty in tys:
        for tc in range(2):
            for tx in range(2):
                part = values[at * piece_rows : (at + 1) * piece_rows]
                blocks = [part[:, n : n + width] for n in range(0, part.shape[1], width)]
                if extra is not None:
                    blocks.append(extra[at])
                pieces[ty, tc, tx] = jnp.concatenate(blocks, axis=0) if len(blocks) > 1 else blocks[0]
                at += 1
    for ty in tys:
        slot = ty ^ y
        a, b = pieces[ty, 0, 0], pieces[ty, 0, 1]
        xk[slot, slot_z] = jnp.where(x == 0, a, b).astype(BF)
        xs[slot, slot_z] = jnp.where(x == 0, b, a).astype(BF)
    return pieces


def place_y(pieces, tz, tys, x, y, z, outs):
    xk, xs, yk, ys = outs
    slot_z = tz ^ z
    for tx in range(2):
        slot = tx ^ x
        a, b = pieces[0, 1, tx], pieces[1, 1, tx]
        yk[slot, slot_z] = jnp.where(y == 0, a, b).astype(BF)
        ys[slot, slot_z] = jnp.where(y == 0, b, a).astype(BF)


def reduce_grad_kernel(pos_at, scal, a_own, a_oth, b_own, b_oth, kept, near):
    tz = pl.program_id(0)
    x, y, z = (scal[pos_at + n] for n in range(3))
    values = dot_t(a_own[...], b_own[...]) + dot_t(a_oth[...], b_oth[...])
    rows = values.shape[0] // 8
    slot = tz ^ z

    def put(out):
        for n in range(8):
            ty, tc, tx = n // 4, n // 2 % 2, n % 2
            out[slot // 2, tc, tx ^ x, ty ^ y] = values[n * rows : (n + 1) * rows].astype(BF)

    @pl.when(slot % 2 == 0)
    def _():
        put(kept)

    @pl.when(slot % 2 == 1)
    def _():
        put(near)


def expand_grad_kernel(pos_at, scal, a_own, a_oth, b_own, b_oth, m_own, m_oth, c_own, c_oth, *outs):
    x, y, z = (scal[pos_at + n] for n in range(3))
    for half in range(2):
        tz = 2 * pl.program_id(0) + half
        an, ao = a_own[0, half], a_oth[0, half]
        parts = [dot(an, b_own[n]) + dot(ao, b_oth[n]) for n in range(b_own.shape[0])]
        parts.append(dot(m_own[0, half], c_own[...]) + dot(m_oth[0, half], c_oth[...]))
        values = jnp.concatenate(parts, axis=1)
        pieces = place(values, values.shape[0] // 8, tz, (0, 1), x, y, z, None, outs)
        place_y(pieces, tz, (0, 1), x, y, z, outs)


def share_lanes(entries, devices, at, width):
    n = entries.shape[1]
    share = n // devices
    owner = lax.broadcasted_iota(jnp.int32, (devices, n), 0)
    column = lax.broadcasted_iota(jnp.int32, (devices, n), 1)
    mine = (column >= owner * share) & (column < (owner + 1) * share)
    high, low = high_low(jnp.where(mine, entries, 0.0))
    both = jnp.concatenate([high, low], axis=0).astype(BF)
    source = lax.broadcasted_iota(jnp.int32, (n, width), 0)
    target = lax.broadcasted_iota(jnp.int32, (n, width), 1)
    picks = (target >= at) & (target < at + share) & (lax.rem(source, share) == target - at)
    spread = dot(both, picks.astype(F32).astype(BF))
    return spread[:devices] + spread[devices:]


def heads_grad_kernel(
    pos_at, scal, a_own, a_oth, own_early, own_late, oth_early, oth_late, kept_h, sent_h, sums_1, kept_e, sent_e, sums_2, *refs, devices
):
    outs, table = refs[:-1], refs[-1]
    x, y, z = (scal[pos_at + n] for n in range(3))
    width = outs[0].shape[-1]

    @pl.when(pl.program_id(0) == 0)
    def _():
        first_core = scal[pos_at - 1] == 0
        ordered = lambda kept, sent: [jnp.where(first_core, kept, sent), jnp.where(first_core, sent, kept)]
        sums_e = jnp.concatenate(ordered(kept_e[...], sent_e[...]), axis=1)
        of_heads = [part for n in range(3) for part in ordered(kept_h[n, 0:1], sent_h[n, 0:1])]
        total = jnp.zeros((devices, width), F32)
        at = 0
        for entries in (
            jnp.concatenate(of_heads[:4], axis=1), jnp.concatenate(of_heads[4:], axis=1), sums_1[2:3], sums_1[0:1], sums_1[1:2],
            sums_e, sums_2[2:3], sums_2[0:1], sums_2[1:2],
        ):
            total = total + share_lanes(entries, devices, at, width)
            at += entries.shape[1] // devices
        table[...] = total

    join = lambda early, late: jnp.concatenate(
        [jnp.concatenate([early[n], late[n]], axis=0) for n in range(early.shape[0])], axis=1
    )
    own, other = join(own_early, own_late), join(oth_early, oth_late)
    line = lax.broadcasted_iota(jnp.int32, (8, width), 0)
    for half in range(2):
        tz = 2 * pl.program_id(0) + half
        values = dot(a_own[half], own) + dot(a_oth[half], other)
        rows8 = table[pl.ds(pl.multiple_of(tz * 8, 8), 8)]
        extra = []
        for n in range(8):
            high, low = high_low(rows8[n : n + 1])
            extra.append(jnp.where(line == 0, high, jnp.where(line == 1, low, 0.0)))
        pieces = place(values, values.shape[0] // 8, tz, (0, 1), x, y, z, extra, outs)
        place_y(pieces, tz, (0, 1), x, y, z, outs)


class Ring:
    def __init__(self, n_dp):
        self.n_dp = n_dp
        self.devices = 2 * n_dp

    def swap(self, value, bits):
        return lax.ppermute(value, AXES, [(i, i ^ bits) for i in range(self.devices)])

    def core(self, value):
        return self.swap(value, 2)

    def x(self, value):
        return self.swap(value, 1)

    def y(self, value):
        return self.swap(value, 4)

    def z(self, value, step):
        return self.swap(value, 8 * step)


def add_first_kernel(scal, xk, xr, yk, yr, xn, yn):
    wide = lambda ref: ref[0].astype(F32)
    xn[...] = (wide(xk) + wide(xr)).astype(BF)
    yn[...] = (wide(yk) + wide(yr)).astype(BF)


def add_second_kernel(scal, xk, xr, xm, yk, yr, ym, own, z1, z2, z3):
    for n, (keep, got, more) in enumerate(((xk, xr, xm), (yk, yr, ym))):
        total = lambda k: keep[0, k].astype(F32) + got[0, k].astype(F32) + more[k].astype(F32)
        own[n] = total(0)
        for k, out in ((1, z1), (2, z2), (3, z3)):
            out[n] = total(k).astype(BF)


def add_last_kernel(core_at, scal, own, z1, z2, z3, keep, send):
    first = scal[core_at] == 0
    total = lambda n: own[n] + z1[n].astype(F32) + z2[n].astype(F32) + z3[n].astype(F32)
    of_first, of_second = total(0), total(1)
    keep[...] = jnp.where(first, of_first, of_second)
    send[...] = jnp.where(first, of_second, of_first)


def add_second_half_kernel(scal, xk, xr, xm, yk, yr, ym, kept, sent):
    for n, (keep, got, more) in enumerate(((xk, xr, xm), (yk, yr, ym))):
        total = lambda k: keep[0, k].astype(F32) + got[0, k].astype(F32) + more[k].astype(F32)
        for k in range(2):
            kept[k, n] = total(2 * k)
            sent[k, n] = total(2 * k + 1).astype(BF)


def add_third_half_kernel(scal, kept, got, own, sent):
    own[...] = kept[0] + got[0].astype(F32)
    sent[...] = (kept[1] + got[1].astype(F32)).astype(BF)


def add_last_half_kernel(core_at, scal, own, got, keep, send):
    first = scal[core_at] == 0
    of_first, of_second = (own[n] + got[n].astype(F32) for n in range(2))
    keep[...] = jnp.where(first, of_first, of_second)
    send[...] = jnp.where(first, of_second, of_first)


def add_near_kernel(scal, kept, got, own, far):
    own[...] = kept[0].astype(F32) + got[0].astype(F32)
    far[...] = (kept[1].astype(F32) + got[1].astype(F32)).astype(BF)


def add_far_kernel(scal, own, got, kept, sent):
    for n in range(2):
        kept[n] = own[n, 0] + got[n, 0].astype(F32)
        sent[n] = (own[n, 1] + got[n, 1].astype(F32)).astype(BF)


def add_side_kernel(scal, kept, got, own, sent):
    for n in range(2):
        own[n] = kept[n, 0] + got[n, 0].astype(F32)
        sent[n] = (kept[n, 1] + got[n, 1].astype(F32)).astype(BF)


def add_end_kernel(core_at, scal, own, got, keep, send):
    first = scal[core_at] == 0
    of_first, of_second = (own[n] + got[n].astype(F32) for n in range(2))
    keep[...] = jnp.where(first, of_first, of_second)
    send[...] = jnp.where(first, of_second, of_first)


class Scatter:
    def __init__(self, ring, core_at, name, sent):
        self.ring, self.core_at, self.name = ring, core_at, name
        self.xk, self.xs, self.yk, self.ys = sent

    def send(self, *others):
        self.xr, self.yr = self.ring.x(after(self.xs, *others)), self.ring.y(after(self.ys, *others))

    def first(self, scal, us=0.1):
        shape = self.xk.shape[1:]
        part = lambda a: (a, (1,) + shape, lambda j, s: (1, 0, 0, 0))
        xn, yn = call(
            add_first_kernel, self.name + "_add1", scal, (1,), [part(a) for a in (self.xk, self.xr, self.yk, self.yr)],
            [(shape, BF, None, None)] * 2, us=us,
        )
        self.xn, self.yn = xn, yn
        return xn

    def send_first(self, *others):
        self.xm, self.ym = self.ring.y(after(self.xn, *others)), self.ring.x(after(self.yn, *others))

    def second(self, scal):
        shape = self.xk.shape[1:]
        piece = (2,) + shape[1:]
        part = lambda a: (a, (1,) + shape, lambda j, s: (0, 0, 0, 0))
        whole = lambda a: (a, None, None)
        self.own, *self.sends = call(
            add_second_kernel, self.name + "_add2", scal, (1,),
            [part(self.xk), part(self.xr), whole(self.xm), part(self.yk), part(self.yr), whole(self.ym)],
            [(piece, F32, None, None)] + [(piece, BF, None, None)] * 3,
        )
        return self.own

    def send_second(self, *others):
        self.arrived = [self.ring.z(after(v, *others), k + 1) for k, v in enumerate(self.sends)]

    def last(self, scal):
        piece = self.own.shape[1:]
        keep, send = call(
            functools.partial(add_last_kernel, self.core_at), self.name + "_add3", scal, (1,),
            [(a, None, None) for a in (self.own, *self.arrived)], [(piece, F32, None, None)] * 2,
        )
        return keep, self.ring.core(send)


class HalvingScatter(Scatter):
    def second(self, scal):
        shape = self.xk.shape[1:]
        piece = (2, 2) + shape[1:]
        part = lambda a: (a, (1,) + shape, lambda j, s: (0, 0, 0, 0))
        whole = lambda a: (a, None, None)
        self.kept, self.near = call(
            add_second_half_kernel, self.name + "_add2", scal, (1,),
            [part(self.xk), part(self.xr), whole(self.xm), part(self.yk), part(self.yr), whole(self.ym)],
            [(piece, F32, None, None), (piece, BF, None, None)],
        )
        return self.kept

    def send_second(self):
        self.got = self.ring.z(self.near, 1)

    def third(self, scal):
        piece = self.kept.shape[1:]
        self.own, self.far = call(
            add_third_half_kernel, self.name + "_add3", scal, (1,),
            [(a, None, None) for a in (self.kept, self.got)], [(piece, F32, None, None), (piece, BF, None, None)],
        )
        return self.own

    def send_third(self):
        self.arrived = self.ring.z(self.far, 2)

    def last(self, scal):
        piece = self.own.shape[1:]
        keep, send = call(
            functools.partial(add_last_half_kernel, self.core_at), self.name + "_add4", scal, (1,),
            [(a, None, None) for a in (self.own, self.arrived)], [(piece, F32, None, None)] * 2,
        )
        return keep, self.ring.core(send)


class DepthScatter:
    def __init__(self, ring, core_at, name, sent):
        self.ring, self.core_at, self.name = ring, core_at, name
        self.kept, self.near = sent

    def call(self, kernel, step, scal, ins, outs):
        whole = lambda a: (a, None, None)
        return call(kernel, self.name + step, scal, (), [*map(whole, ins)], [(s, d, None, None) for s, d in outs])

    def send_near(self):
        self.got = self.ring.z(self.near, 1)

    def add_near(self, scal):
        shape = self.kept.shape[1:]
        self.own, self.far = self.call(add_near_kernel, "_add1", scal, (self.kept, self.got), [(shape, F32), (shape, BF)])
        return self.own

    def send_far(self):
        self.got = self.ring.z(self.far, 2)

    def add_far(self, scal):
        shape = self.own.shape[:1] + self.own.shape[2:]
        self.kept, self.side = self.call(add_far_kernel, "_add2", scal, (self.own, self.got), [(shape, F32), (shape, BF)])
        return self.kept

    def send_side(self):
        self.got = self.ring.x(self.side)

    def add_side(self, scal):
        shape = self.kept.shape[:1] + self.kept.shape[2:]
        self.own, sent = self.call(add_side_kernel, "_add3", scal, (self.kept, self.got), [(shape, F32), (shape, BF)])
        self.got = self.ring.y(sent)
        return self.own

    def last(self, scal):
        shape = self.own.shape[1:]
        keep, send = self.call(
            functools.partial(add_end_kernel, self.core_at), "_add4", scal, (self.own, self.got), [(shape, F32)] * 2
        )
        return keep, self.ring.core(send)


def after(value, *others):
    if not others:
        return value
    return lax.optimization_barrier((value,) + others)[0]


def side_by_side(core_at, scal, own, got):
    first = scal[core_at] == 0
    return [jnp.where(first, own, got), jnp.where(first, got, own)]


def finish_kernel(
    core_at, scal, own, got, reduce_own, reduce_got, expand_own, expand_got,
    heads_o, reduce_o, expand_o, merge_o, *shares_o,
):
    width = own.shape[1]
    rows = heads_o.shape[0]
    for n, part in enumerate(side_by_side(core_at, scal, reduce_own[...], reduce_got[...])):
        reduce_o[:, n * width : (n + 1) * width] = part
    blocks = expand_own.shape[0] // rows - 1
    for n, part in enumerate(side_by_side(core_at, scal, expand_own[...], expand_got[...])):
        for k in range(blocks):
            at = (n * blocks + k) * width
            expand_o[:, at : at + width] = part[k * rows : (k + 1) * rows]
        merge_o[:, n * width : (n + 1) * width] = part[blocks * rows :]
    for n, part in enumerate(side_by_side(core_at, scal, own[...], got[...])):
        for k in range(3):
            at = (2 * k + n) * width
            heads_o[:, at : at + width] = part[k * rows : (k + 1) * rows]
    entries = own[3 * rows :] + got[3 * rows :]
    entries = entries[0:1] + entries[1:2]
    at = 0
    for share in shares_o:
        n = share.shape[1]
        moved = entries if at == 0 else pltpu.roll(entries, width - at, 1)
        share[...] = moved[:, :n]
        at += n


def per_device(
    tokens, w_heads, b_heads, w_merge, b_merge, gain_first, bias_first, w_expand, b_expand,
    w_reduce, b_reduce, gain_second, bias_second, seq_lengths, cotangent,
):
    rows = tokens.shape[0]
    seqs = seq_lengths.shape[1]
    n_dp = lax.axis_size("dp")
    ring = Ring(n_dp)
    head = lax.axis_index("head")
    dp = lax.axis_index("dp")
    core = dp % 2
    place_of = jnp.stack([head, core, head, (dp // 2) % 2, dp // 4]).astype(jnp.int32)
    scal = jnp.concatenate([seq_lengths[0].astype(jnp.int32), place_of])
    head_at, core_at, pos_at = seqs, seqs + 1, seqs + 2
    first_core = core == 0
    line = lambda v: v.reshape(1, -1)
    b_heads, b_merge, gain_first, bias_first, b_expand, b_reduce, gain_second, bias_second = map(
        line, (b_heads, b_merge, gain_first, bias_first, b_expand, b_reduce, gain_second, bias_second)
    )
    wide_shape = (rows, D)
    quarter = 256

    turned = ((4, D // 4, rows), BF, None, None)
    rk, v, state, tcol, trow, tokens_t = call(
        functools.partial(kv_kernel, seqs), "keys_values", scal, (3,),
        [
            (tokens, None, None),
            (w_heads, (D, quarter), lambda j, s: (0, 3 + j)),
            (w_heads, (D, quarter), lambda j, s: (0, 6 + j)),
            (b_heads, (1, quarter), lambda j, s: (0, 3 + j)),
            (b_heads, (1, quarter), lambda j, s: (0, 6 + j)),
        ],
        [
            (wide_shape, BF, (rows, quarter), lambda j, s: (0, j)),
            (wide_shape, BF, (rows, quarter), lambda j, s: (0, j)),
            ((PAIRS + 1, LANES, LANES), BF, None, None),
            ((rows, LANES), F32, None, None),
            ((8, rows), F32, None, None), turned,
        ],
        [pltpu.VMEM((LANES, LANES), F32)],
        us=4,
    )
    prior = ring.x(state)

    fast = n_dp == 16
    order = scal
    if fast:
        tokens_o = ring.core(tokens_t)
    rq, num, den = call(
        local_kernel, "local_attention", scal, (3,),
        [
            (tokens, None, None),
            (w_heads, (D, quarter), lambda j, s: (0, j)),
            (b_heads, (1, quarter), lambda j, s: (0, j)),
            (rk, (rows, quarter), lambda j, s: (0, j)),
            (v, (rows, quarter), lambda j, s: (0, j)),
            (tcol, None, None),
            (trow, None, None),
        ],
        [
            (wide_shape, BF, (rows, quarter), lambda j, s: (0, j)),
            (wide_shape, F32, (rows, quarter), lambda j, s: (0, j)),
            (wide_shape, F32, (rows, quarter), lambda j, s: (0, j)),
        ],
        [pltpu.VMEM((rows, rows), F32)],
        us=6,
    )

    if fast:
        order = after(scal, tokens_o)
    att, inv, mixed, xhat, scale, normed, second, turned_own, act, slope = call(
        functools.partial(ffn_kernel, head_at), "feed_forward", order, (FFN_STEPS,),
        [
            (rq, None, None), (num, None, None), (den, None, None), (prior, None, None),
            (tcol, None, None), (tokens, None, None), (w_merge, None, None), (b_merge, None, None),
            (gain_first, None, None), (bias_first, None, None), (b_reduce, None, None),
            (w_expand, (D, FFN_BLOCK), lambda j, s: (0, j)),
            (b_expand, (1, FFN_BLOCK), lambda j, s: (0, j)),
            (w_reduce, (FFN_BLOCK, D), lambda j, s: (j, 0)),
        ],
        [
            (wide_shape, F32, None, None), (wide_shape, F32, None, None), (wide_shape, BF, None, None),
            (wide_shape, F32, None, None), ((rows, LANES), F32, None, None), (wide_shape, BF, None, None),
            (wide_shape, F32, None, None), ((2, 4, D // 4, rows), BF, None, None),
            ((rows, FF), BF, (rows, FFN_BLOCK), lambda j, s: (0, j)),
            ((rows, FF), BF, (rows, FFN_BLOCK), lambda j, s: (0, j)),
        ],
        us=11, vmem=VMEM_FFN,
    )

    half_shape = (rows, D // 2)
    result, grad_second, branch, bg_keep, bg_send, sums_second = call(
        functools.partial(second_kernel, core_at), "second_norm", scal, (1,),
        [(second, None, None), (cotangent, None, None), (gain_second, None, None), (bias_second, None, None)],
        [
            (wide_shape, BF, None, None), (wide_shape, F32, None, None), (wide_shape, BF, None, None),
            (half_shape, BF, None, None), (half_shape, BF, None, None), ((8, D), F32, None, None),
        ],
        us=2.6,
    )

    devices = ring.devices
    small, large = D // devices, FF // devices
    whole = lambda a: (a, None, None)
    part = lambda a, n: (a, (1, 2, D // 4, rows), lambda j, s: (n, j, 0, 0))
    by_z = lambda a: (a, (2, D // 4, rows), lambda j, s: (j, 0, 0))
    by_col = lambda a: (a, (rows, FF // 4), lambda j, s: (0, j))

    def group(kernel, name, scal, grid, ins, piece_rows, us, scratch=(), kind=Scatter):
        shape = (2, 4, piece_rows, D // 2)
        sent = call(
            functools.partial(kernel, pos_at), name, scal, grid, ins, [(shape, BF, None, None)] * 4, scratch, us
        )
        return kind(ring, core_at, name, sent)

    ff_half = FF_STEPS // 2
    in_hbm = lambda a: (a, None, pltpu.HBM)
    hidden = ((ff_half, rows, FF_BLOCK), BF, None, None)
    hidden_sums = ((1, FF // 2), F32, None, None)
    buffers = [
        pltpu.VMEM((ff_half, D, FF_BLOCK), BF), pltpu.VMEM((ff_half, FF_BLOCK, D), BF),
        pltpu.SemaphoreType.DMA((2, ff_half)),
    ]
    hidden_in = [whole(branch), whole(slope), in_hbm(w_expand), in_hbm(w_reduce)]
    pg_send, sum_sent, partial = call(
        functools.partial(back_sent_kernel, core_at), "feed_forward_back_sent", scal, (),
        [*hidden_in, whole(grad_second)],
        [hidden, hidden_sums, (wide_shape, F32, None, None)], buffers,
        us=5, vmem=VMEM_BACK,
    )
    order = scal
    if fast:
        pg_o = ring.core(pg_send)
        act_o, turned_other, bg_o = map(ring.core, (act, turned_own, bg_send))
        pieces = ((2, 2, 2, 2, large, D // 2), BF, None, None)
        sent = call(
            functools.partial(reduce_grad_kernel, pos_at), "grad_reduce", after(scal, partial, turned_other), (4,),
            [by_col(act), by_col(act_o), whole(bg_keep), whole(bg_o)], [pieces, pieces], us=6,
        )
        reduced = DepthScatter(ring, core_at, "grad_reduce", sent)
        reduced.send_near()
        order = after(scal, reduced.near)

    pg_keep, grad_first, mg_keep, mg_send, w_att, e_att, later, sum_kept, sums_first = call(
        functools.partial(back_kernel, core_at), "feed_forward_back", order, (),
        [
            *hidden_in,
            (partial, None, None), (gain_first, None, None), (xhat, None, None), (scale, None, None),
            (w_merge, None, None), (att, None, None), (inv, None, None), (rq, None, None), (tcol, None, None),
        ],
        [
            hidden, (wide_shape, F32, None, None), (half_shape, BF, None, None), (half_shape, BF, None, None),
            (wide_shape, BF, None, None), ((rows, LANES), BF, None, None),
            ((PAIRS + 1, LANES, LANES), BF, None, None), hidden_sums, ((8, D), F32, None, None),
        ],
        [pltpu.VMEM(wide_shape, F32), *buffers],
        us=COST_BACK, vmem=VMEM_BACK,
    )
    later = ring.x(later)

    if fast:
        mg_o = ring.core(mg_send)
        expanded = group(
            expand_grad_kernel, "grad_expand", scal, (2,),
            [
                part(turned_own, 1), part(turned_other, 1), whole(pg_keep), whole(pg_o),
                part(turned_own, 0), part(turned_other, 0), whole(mg_keep), whole(mg_o),
            ],
            5 * small, COST_EXPAND, kind=HalvingScatter,
        )
        expanded.send(later)
        order = after(scal, expanded.xs, later)

    by_pair = [*map(whole, (rq, rk, v, w_att))]
    both_states = [whole(e_att), whole(prior), whole(later), whole(tcol)]
    pj_out = [((3, rows // 2, D // 2), BF, None, None)] * 2
    pj_sums = ((3, 8, D // 2), F32, None, None)
    table = ((rows, rows), F32, None, None)
    *pj_send, sum_heads_sent, weights, weights_t = call(
        functools.partial(attn_sent_kernel, head_at, core_at), "attention_back_sent", order, (),
        [*by_pair, *both_states, whole(trow)], [*pj_out, pj_sums, table, table], us=COST_SENT, vmem=VMEM_ATTN,
    )
    order = scal
    if fast:
        pj_o = [ring.core(v) for v in pj_send]
        order = after(scal, reduced.add_near(after(scal, pj_send[0])))
        reduced.send_far()
    *pj_keep, sum_heads_kept = call(
        functools.partial(attn_kept_kernel, head_at, core_at), "attention_back_kept", order, (PAIRS // 2,),
        [*by_pair, *both_states, whole(weights), whole(weights_t)], [*pj_out, pj_sums], us=COST_KEPT, vmem=VMEM_ATTN,
    )

    if fast:
        order = after(scal, expanded.first(after(scal, pj_keep[0])))
        expanded.send_first()
        heads = group(
            functools.partial(heads_grad_kernel, devices=devices), "grad_heads", order, (2,),
            [
                by_z(tokens_t), by_z(tokens_o), *map(whole, (*pj_keep, *pj_o)),
                *map(whole, (sum_heads_kept, sum_heads_sent, sums_first, sum_kept, sum_sent, sums_second)),
            ],
            3 * small + 8, COST_HEADS, [pltpu.VMEM((devices, D // 2), F32)],
        )
        heads.send()
        order = after(scal, heads.xs)

    of_part = lambda a: (a, (1, rows // 2, D // 2), lambda j, s: (j, 0, 0))
    (input_grad,) = call(
        input_kernel, "input_grad", order, (3,),
        [
            whole(grad_first), *map(of_part, (*pj_keep, *pj_send)),
            (w_heads, (D, D // 2), lambda j, s: (0, 2 * j + s[core_at])),
            (w_heads, (D, D // 2), lambda j, s: (0, 2 * j + 1 - s[core_at])),
        ],
        [(wide_shape, F32, None, None)],
        us=COST_INPUT,
    )

    if fast:
        order = reduced.add_far(after(scal, input_grad))
        order = expanded.second(after(scal, order))
        expanded.send_second()
        reduced.send_side()
        order = heads.first(after(scal, order))
        heads.send_first()
        order = expanded.third(after(scal, order))
        expanded.send_third()
        order = heads.second(after(scal, order))
        heads.send_second()
        order = reduced.add_side(after(scal, order))
        expand_own, expand_got = expanded.last(after(scal, order))
        reduce_own, reduce_got = reduced.last(after(scal, expand_own))
        heads_own, heads_got = heads.last(after(scal, reduce_own))
        out = lambda n, m: ((n, m), F32, None, None)
        counts = (2 * small, small, small, small, small, large, small, small, small)
        w_heads_grad, w_reduce_grad, w_expand_grad, w_merge_grad, *shares = call(
            functools.partial(finish_kernel, core_at), "finish", scal, (),
            [*map(whole, (heads_own, heads_got, reduce_own, reduce_got, expand_own, expand_got))],
            [out(small, 3 * D), out(large, D), out(small, FF), out(small, D), *(out(1, n) for n in counts)],
        )
        shares = [share.reshape(-1) for share in shares]
        grads = (
            w_heads_grad, *shares[:2], w_merge_grad, *shares[2:5], w_expand_grad, shares[5], w_reduce_grad,
            *shares[6:],
        )
    else:
        by_core = lambda keep, send: jnp.concatenate(
            [jnp.where(first_core, keep, send), jnp.where(first_core, send, keep)], axis=1
        )
        flat = lambda v: v.transpose(1, 0, 2).reshape(rows, -1)
        by_heads = lambda keep, send: jnp.concatenate(
            [by_core(keep[n], send[n]) for n in range(3)], axis=1
        )
        pj_keep, pj_send = (jnp.concatenate(v, axis=1) for v in (pj_keep, pj_send))
        sum_heads = by_heads(sum_heads_kept, sum_heads_sent)[0]
        scatter = lambda v: lax.psum_scatter(v, AXES, scatter_dimension=0, tiled=True)
        grads = (
            scatter(dot_t(tokens, by_heads(pj_keep, pj_send))),
            scatter(sum_heads[: 2 * D]), scatter(sum_heads[2 * D :]),
            scatter(dot_t(mixed, by_core(mg_keep, mg_send))),
            scatter(sums_first[2]), scatter(sums_first[0]), scatter(sums_first[1]),
            scatter(dot_t(normed, by_core(flat(pg_keep), flat(pg_send)))),
            scatter(by_core(sum_kept, sum_sent)[0]),
            scatter(dot_t(act, branch)),
            scatter(sums_second[2]), scatter(sums_second[0]), scatter(sums_second[1]),
        )
    return (result, input_grad) + tuple(grads)


def solution(mesh):
    in_specs = (P(AXES, None),) + (P(),) * 12 + (P("dp", None), P(AXES, None))
    row, one = P(AXES, None), P(AXES)
    out_specs = (row, row, row, one, one, row, one, one, one, row, one, row, one, one, one)
    return jax.shard_map(
        per_device, mesh=mesh, in_specs=in_specs, out_specs=out_specs, check_vma=False
    )
```
